32 devices in a mesh: grp: 2 (over x), sv: 8 (over z, y), tv: 2 (over core).
Axes of the slice: x: 2, y: 2, z: 4, core: 2. Of those that a mesh axis runs over, the one named last changes fastest.
Arguments:
- teacher_probs: bfloat16 [256, 81920], P(('grp', 'sv'), 'tv'), parts along dimension 0, may hold values from 9.983778e-07 to 0.0099487305
- align_owner: int32 [640, 2], replicated, may hold values from 0 to 7, all different within a row; in each aligned block of 320 rows (0 to 319, 320 to 639, ...) at most 160 rows name the same one
- align_local: int32 [640, 2], replicated, may hold values from 0 to 31
- align_weight: bfloat16 [640, 2], replicated, may hold values from 0.099609375 to 1
- student_logits: bfloat16 [256, 32768], P(('grp', 'tv'), 'sv'), parts along dimension 0, may hold values from -15 to 250
- hidden: bfloat16 [256, 1920], P(('grp', 'sv', 'tv')), parts along dimension 0, may hold values from -6 to 6
Outputs:
- divergence: float32 [256], P(('grp', 'tv')), parts along dimension 0
- logit_grad: bfloat16 [256, 32768], P(('grp', 'tv'), 'sv'), parts along dimension 0
- weight_grad: bfloat16 [1920, 65536], P(None, ('grp', 'sv', 'tv')), parts along dimension 1
The draws below stay inside these ranges and needn't reach their ends.
There are 2 independent parts, one for each index of `grp`. The reference program is written for one: setup_inputs(seed, part) draws one part's arguments, and reference() takes and returns one part's arrays. A program takes and returns all parts, laid end to end along the dimension named above; an argument that names none is the same for every part. Nothing has to cross between parts.
Inputs may be any that keep to these rules, and one draw needn't show every extreme that they name: `align_owner`: the 2 entries of a row name different sv indices. Among the rows of one aligned block of 320 teacher blocks (one half of the teacher vocabulary) no index is named more than 160 times, and in some block an index is named exactly 160 times.
All inputs are finite; a program needn't handle non-finite values.
Results may differ from the reference program's by a relative error of at most 0.0053.
Values may be sent and summed in bfloat16 or wider, within the bound.
No kernel may reach another device: no remote copies, remote signals or barrier semaphores. Data moves between devices by JAX's collectives and lax.ppermute only.
A program may use at most 128 MiB of HBM per device.

```python
import math
import jax
import jax.numpy as jnp
import numpy as np

BLK = 128
TB = 640
TOPA = 2
SB_DEV = 32
H = 1920
TOK = 128
VT = 81920
VS = 32768
CAP = 160
N_SV = 8
N_TV = 2


def draw_student_logits(key, part):
    key = jax.random.fold_in(key, 7)
    values = jnp.clip(3.0 * jax.random.normal(key, (TOK, VS), jnp.float32), -15.0, 15.0)
    return values.astype(jnp.bfloat16)


def touch_ends(result, key, smallest, high):
    dims = result.shape
    index_at = [jax.random.randint(jax.random.fold_in(key, axis), (), 0, dims[axis]) for axis in range(len(dims))]
    result = result.at[tuple(index_at)].set(smallest)
    longest = dims.index(max(dims))
    index_at[longest] = (index_at[longest] + 1) % dims[longest]
    return result.at[tuple(index_at)].set(high)


def shard_levels(rng, extent, shards, smallest, high):
    level = 1.0
    for dim, blocks in shards:
        heights = jax.random.uniform(jax.random.fold_in(jax.random.fold_in(rng, 6), dim), (blocks,), jnp.float32, smallest / len(shards), high / len(shards))
        level = level * jnp.repeat(jnp.exp(heights), extent[dim] // blocks).reshape((-1,) + (1,) * (len(extent) - 1 - dim))
    return level


def assign_block(rng, own, number, rows, number_of, top, most, lean):
    order = jax.random.permutation(rng, number_of)
    packed, common = portions_of(number_of, rows * top, most, lean, True), portions_of(number_of, rows * top, most, lean, False)
    places = jnp.arange(number_of)

    def named(tallies, turn):
        used = int((tallies > 0).sum())
        fixed = max(1, used // 4)
        passed = fixed + (places - fixed + turn * (used - fixed)) % max(1, number_of - fixed)
        return jnp.zeros((number_of,), jnp.int32).at[order[jnp.where(places < fixed, places, passed)]].set(jnp.asarray(tallies, jnp.int32))

    tallies = jnp.where(number % 4 == 0, named(packed, number // 4), named(common, number - number // 4 - 1))
    mixed = jax.random.permutation(jax.random.fold_in(own, 3), number_of)
    giver, sink = mixed[0:number_of // 2 * 2:2], mixed[1:number_of // 2 * 2:2]
    slack = jnp.minimum(tallies[giver] - 1, most - tallies[sink]) // 2
    slack = jnp.where((giver == order[0]) | (sink == order[0]) | (tallies[sink] == 0), 0, jnp.maximum(slack, 0))
    passed = jax.random.randint(jax.random.fold_in(own, 4), (number_of // 2,), 0, 1 << 20) % (slack + 1)
    tallies = tallies.at[giver].add(-passed).at[sink].add(passed)
    members = jnp.searchsorted(jnp.cumsum(tallies), jnp.arange(rows * top), side="right").astype(jnp.int32)
    listing = members.reshape(top, rows).T
    listing = listing[jax.random.permutation(jax.random.fold_in(own, 1), rows)]
    turn = jax.random.randint(jax.random.fold_in(own, 2), (rows, 1), 0, top)
    return jnp.take_along_axis(listing, (jnp.arange(top)[None, :] + turn) % top, axis=1)


def portions_of(amount, total, reach, skew, full):
    portions = [(1 << 20) // math.isqrt(standing ** skew) + 1 for standing in range(1, amount + 1)]
    largest = reach if full else min(reach, max(-(-total // amount), total * portions[0] // sum(portions)))
    least = 1 if total - largest >= amount - 1 else 0
    given, surplus = [largest] + [least] * (amount - 1), total - largest - least * (amount - 1)
    while surplus > 0:
        movable = [i for i in range(1, amount) if given[i] < largest] or [i for i in range(1, amount) if given[i] < reach]
        whole, budget = sum([portions[i] for i in movable]), surplus
        for i in movable:
            more = min(reach - given[i], max(1, budget * portions[i] // whole), surplus)
            given[i] = given[i] + more
            surplus = surplus - more
    return np.array(given)


def bell_draw(stream_key, shape, spread, bound, cuts=(), kind=jnp.bfloat16):
    level = shard_levels(stream_key, shape, cuts, -0.22, 0.18) if cuts else 1.0
    values = jax.random.normal(stream_key, shape, jnp.float32) * spread * level
    return jnp.minimum(jnp.maximum(values, -bound), bound).astype(kind)


def setup_inputs(seed: int = 0, part: int = 0) -> dict:
    keys = jax.random.split(jax.random.key(seed), 7)
    part_splits = jax.random.split(jax.random.fold_in(keys[6], part), 7)
    teacher_probs = jnp.clip(jnp.exp(math.log(0.0099487305) - 9.2068237 * jax.random.uniform(part_splits[0], (TOK, VT), jnp.float32) ** shard_levels(part_splits[0], (TOK, VT), ((0, 8), (1, 2)), -0.2, 0.2)), 9.98377799987793e-07, 0.0099487305).astype(jnp.bfloat16)
    align_owner_keys = jax.random.split(jax.random.fold_in(keys[1], 1), TB // (TB // N_TV))
    align_owner_turns = jax.random.permutation(jax.random.fold_in(keys[1], 3), TB // (TB // N_TV))
    align_owner = jax.vmap(lambda own, number: assign_block(jax.random.fold_in(keys[1], 2), own, number, TB // N_TV, N_SV, TOPA, CAP, 2))(align_owner_keys, align_owner_turns).reshape((TB, TOPA))
    align_local = touch_ends(jax.random.randint(keys[2], (TB, TOPA), 0, SB_DEV), jax.random.fold_in(keys[2], 1), 0, SB_DEV - 1).astype(jnp.int32)
    align_weight = jnp.clip(jnp.exp(jax.random.uniform(keys[3], (TB, TOPA), jnp.float32, math.log(0.099609375), math.log(1.0))), 0.099609375, 1.0).astype(jnp.bfloat16)
    student_logits = draw_student_logits(jax.random.fold_in(jax.random.fold_in(keys[6], part), 71), part)
    hidden = bell_draw(part_splits[5], (TOK, H), 1.0, 6.0, ((0, 16),))
    return dict(teacher_probs=teacher_probs, align_owner=align_owner, align_local=align_local, align_weight=align_weight, student_logits=student_logits, hidden=hidden)


def reference(teacher_probs, align_owner, align_local, align_weight, student_logits, hidden):
    student_block = (align_owner * SB_DEV + align_local).reshape(-1).astype(jnp.int32)
    prob_tiles = teacher_probs.astype(jnp.float32).reshape(TOK, TB, 1, BLK)
    contrib = (prob_tiles * align_weight.astype(jnp.float32).reshape(1, TB, TOPA, 1)).reshape(TOK, TB * TOPA, BLK)
    mapped = jnp.zeros((TOK, SB_DEV * N_SV, BLK), jnp.float32).at[:, student_block, :].add(contrib)
    mapped = mapped.reshape(TOK, VS)
    mass_total = jnp.sum(mapped, axis=1, keepdims=True)
    target = mapped / mass_total
    logits = student_logits.astype(jnp.float32)
    peak_value = jnp.max(logits, axis=1, keepdims=True)
    log_norm = peak_value + jnp.log(jnp.sum(jnp.exp(logits - peak_value), axis=1, keepdims=True))
    log_probs = logits - log_norm
    positive = target > 0
    safe_target = jnp.where(positive, target, 1.0)
    divergence = jnp.sum(jnp.where(positive, target * (jnp.log(safe_target) - log_probs), 0.0), axis=1)
    logit_grad = ((jnp.exp(log_probs) - target) * float(VS)).astype(jnp.bfloat16)
    weight_grad = jnp.dot(hidden.T, logit_grad, preferred_element_type=jnp.float32).astype(jnp.bfloat16)
    return (divergence, logit_grad, weight_grad)
```

```python
import jax
import jax.numpy as jnp
from jax import lax
from jax.experimental import pallas as pl
from jax.experimental.pallas import tpu as pltpu
from jax.sharding import PartitionSpec as P

BLK = 128
TB = 640
MASS_ROWS = 16
VMEM_LIMIT = 48 * 1024 * 1024


def swap_halves(x):
    return lax.ppermute(x, "tv", [(0, 1), (1, 0)])


def block_weights(row_of, weight, rows):
    row_ids = lax.broadcasted_iota(jnp.int32, (rows + MASS_ROWS, row_of.shape[1]), 0)
    total = jnp.zeros(row_ids.shape, jnp.float32)
    for slot in range(row_of.shape[0]):
        hit = (row_ids == row_of[slot][None, :]) | (row_ids == rows + slot)
        total = total + jnp.where(hit, weight[slot].astype(jnp.float32)[None, :], 0.0)
    return total.astype(jnp.bfloat16)


def spread_tokens(t_ref, s_ref):
    tokens = t_ref.shape[0]
    count = t_ref.shape[1] // BLK
    step = 16

    def some(i, carry):
        for j in range(step):
            k = i * step + j
            tile = t_ref[:, pl.ds(pl.multiple_of(k * BLK, BLK), BLK)]
            s_ref[pl.ds(pl.multiple_of(k * tokens, tokens), tokens), :] = tile.astype(jnp.float32)
        return carry

    lax.fori_loop(0, count // step, some, 0)


def token_pair(s_ref, t, tokens):
    count = s_ref.shape[0] // tokens
    both = [s_ref[pl.ds(t + i, count, stride=tokens), :].astype(jnp.bfloat16) for i in range(2)]
    return jnp.concatenate(both, axis=1)


def map_own_kernel(w_ref, t_ref, o_ref, s_ref):
    tokens = t_ref.shape[0]
    spread_tokens(t_ref, s_ref)
    for t in range(0, tokens, 2):
        o_ref[:, t * BLK : (t + 2) * BLK] = jnp.dot(
            w_ref[...], token_pair(s_ref, t, tokens), preferred_element_type=jnp.float32
        )


def map_rest_kernel(w_ref, t_ref, p_ref, o_ref, s_ref, m_ref):
    tokens = t_ref.shape[0]
    owners, _, width = o_ref.shape
    rows = w_ref.shape[0] - MASS_ROWS
    spread_tokens(t_ref, s_ref)
    for t in range(0, tokens, 2):
        both = p_ref[:, t * BLK : (t + 2) * BLK] + jnp.dot(
            w_ref[...], token_pair(s_ref, t, tokens), preferred_element_type=jnp.float32
        )
        for i in range(2):
            one = both[:, i * BLK : (i + 1) * BLK]
            mass = jnp.sum(jnp.sum(one[rows : rows + 8], axis=0, keepdims=True), axis=1, keepdims=True)
            m_ref[pl.ds(t + i, rows, stride=tokens), :] = one[:rows] * (1.0 / mass)

    def owner(q, carry):
        for b in range(width // BLK):
            first = (q * (width // BLK) + b) * tokens
            tile = m_ref[pl.ds(pl.multiple_of(first, tokens), tokens), :]
            o_ref[q, :, b * BLK : (b + 1) * BLK] = tile.astype(jnp.bfloat16)
        return carry

    lax.fori_loop(0, owners, owner, 0)


def grad_kernel(scale, target_ref, logits_ref, norm_ref, grad_ref, part_ref):
    target = target_ref[...].astype(jnp.float32)
    log_probs = logits_ref[...].astype(jnp.float32) - norm_ref[...]
    grad_ref[...] = ((jnp.exp(log_probs) - target) * scale).astype(jnp.bfloat16)
    positive = target > 0
    terms = target * (jnp.log(jnp.where(positive, target, 1.0)) - log_probs)
    part_ref[...] = jnp.sum(jnp.where(positive, terms, 0.0), axis=1, keepdims=True)


def weight_kernel(hidden_ref, grad_ref, o_ref):
    o_ref[...] = jnp.dot(
        hidden_ref[...], grad_ref[...], preferred_element_type=jnp.float32
    ).astype(jnp.bfloat16)


def whole():
    return pl.BlockSpec(memory_space=pltpu.VMEM)


def params():
    return pltpu.CompilerParams(vmem_limit_bytes=VMEM_LIMIT)


def body(teacher_probs, align_owner, align_local, align_weight, student_logits, hidden):
    owners = lax.axis_size("sv")
    halves = lax.axis_size("tv")
    half_index = lax.axis_index("tv")
    tokens = teacher_probs.shape[0]
    columns = student_logits.shape[1]
    blocks = columns // BLK
    mine = blocks // halves
    width = mine * BLK
    rows = owners * mine
    per_half = TB // halves
    group_tokens = owners * tokens
    half_tokens = student_logits.shape[0]

    teacher_other = swap_halves(teacher_probs)

    logit_halves = student_logits.reshape(half_tokens, halves, width)
    keep = lax.dynamic_index_in_dim(logit_halves, half_index, 1, keepdims=False)
    give = lax.dynamic_index_in_dim(logit_halves, 1 - half_index, 1, keepdims=False)
    got = swap_halves(give)
    first = half_index == 0
    logits = jnp.concatenate([jnp.where(first, keep, got), jnp.where(first, got, keep)], axis=0)

    hidden_mine = lax.all_to_all(
        jnp.broadcast_to(hidden[None], (owners,) + hidden.shape), "sv", 0, 0, tiled=True
    )
    hidden_other = swap_halves(hidden_mine)
    hidden_pair = jnp.stack(
        [jnp.where(first, hidden_mine, hidden_other), jnp.where(first, hidden_other, hidden_mine)], axis=1
    )
    hidden_t = hidden_pair.reshape(group_tokens, hidden.shape[1]).T

    wide = student_logits.astype(jnp.float32)
    peak = jnp.max(wide, axis=1)
    sums = jnp.sum(jnp.exp(wide - peak[:, None]), axis=1)
    stats = jnp.broadcast_to(jnp.stack([peak, sums])[None], (owners * halves, 2, half_tokens))
    stats = lax.all_to_all(stats, ("sv", "tv"), 0, 0, tiled=True)
    stats = stats.reshape(owners, halves, 2, half_tokens)
    peaks, sums = stats[:, :, 0], stats[:, :, 1]
    top = jnp.max(peaks, axis=0)
    log_norm = top + jnp.log(jnp.sum(sums * jnp.exp(peaks - top[None]), axis=0))
    log_norm = log_norm.reshape(group_tokens, 1)

    local = align_local.T - half_index * mine
    row_of = jnp.where((local >= 0) & (local < mine), align_owner.T * mine + local, -1)
    weight = align_weight.T
    cut = lambda x, which: lax.dynamic_slice_in_dim(x, which * per_half, per_half, 1)
    w_own = block_weights(cut(row_of, half_index), cut(weight, half_index), rows)
    w_rest = block_weights(cut(row_of, 1 - half_index), cut(weight, 1 - half_index), rows)
    flops = 2 * (rows + MASS_ROWS) * per_half * tokens * BLK
    spread = pltpu.VMEM((per_half * tokens, BLK), jnp.float32)
    part = pl.pallas_call(
        map_own_kernel,
        out_shape=jax.ShapeDtypeStruct((rows + MASS_ROWS, tokens * BLK), jnp.float32),
        in_specs=[whole()] * 2,
        out_specs=whole(),
        scratch_shapes=[spread],
        compiler_params=params(),
        cost_estimate=pl.CostEstimate(flops=flops, bytes_accessed=3 << 20, transcendentals=0),
        name="map_own",
    )(w_own, teacher_probs)
    outgoing = pl.pallas_call(
        map_rest_kernel,
        out_shape=jax.ShapeDtypeStruct((owners, tokens, width), jnp.bfloat16),
        in_specs=[whole()] * 3,
        out_specs=whole(),
        scratch_shapes=[spread, pltpu.VMEM((rows * tokens, BLK), jnp.float32)],
        compiler_params=params(),
        cost_estimate=pl.CostEstimate(flops=flops, bytes_accessed=4 << 20, transcendentals=0),
        name="map_rest",
    )(w_rest, teacher_other, part)
    target = lax.all_to_all(outgoing, "sv", 0, 0, tiled=True).reshape(group_tokens, width)

    scale = float(columns * owners)
    grad, terms = pl.pallas_call(
        lambda *refs: grad_kernel(scale, *refs),
        out_shape=(
            jax.ShapeDtypeStruct((group_tokens, width), jnp.bfloat16),
            jax.ShapeDtypeStruct((group_tokens, 1), jnp.float32),
        ),
        in_specs=[whole()] * 3,
        out_specs=(whole(), whole()),
        compiler_params=params(),
        cost_estimate=pl.CostEstimate(
            flops=10 * group_tokens * width,
            bytes_accessed=6 * group_tokens * width,
            transcendentals=2 * group_tokens * width,
        ),
        name="logit_grad",
    )(target, logits, log_norm)

    grad_halves = grad.reshape(halves, half_tokens, width)
    keep = lax.dynamic_index_in_dim(grad_halves, half_index, 0, keepdims=False)
    give = lax.dynamic_index_in_dim(grad_halves, 1 - half_index, 0, keepdims=False)
    got = swap_halves(give)
    logit_grad = jnp.concatenate([jnp.where(first, keep, got), jnp.where(first, got, keep)], axis=1)

    terms = jnp.broadcast_to(terms.reshape(1, halves, half_tokens), (owners, halves, half_tokens))
    terms = lax.all_to_all(terms.reshape(owners * halves, half_tokens), ("sv", "tv"), 0, 0, tiled=True)
    divergence = jnp.sum(terms, axis=0)

    features = hidden.shape[1]
    tile = features // 8
    weight_grad = pl.pallas_call(
        weight_kernel,
        out_shape=jax.ShapeDtypeStruct((features, width), jnp.bfloat16),
        grid=(features // tile,),
        in_specs=[
            pl.BlockSpec((tile, group_tokens), lambda i: (i, 0)),
            pl.BlockSpec((group_tokens, width), lambda i: (0, 0)),
        ],
        out_specs=pl.BlockSpec((tile, width), lambda i: (i, 0)),
        compiler_params=params(),
        cost_estimate=pl.CostEstimate(
            flops=2 * features * group_tokens * width,
            bytes_accessed=2 * (features * width + group_tokens * (features + width)),
            transcendentals=0,
        ),
        name="weight_grad",
    )(hidden_t, grad)
    return (divergence, logit_grad, weight_grad)


def solution(mesh):
    return jax.shard_map(
        body,
        mesh=mesh,
        in_specs=(
            P(("grp", "sv"), "tv"),
            P(),
            P(),
            P(),
            P(("grp", "tv"), "sv"),
            P(("grp", "sv", "tv"), None),
        ),
        out_specs=(P(("grp", "tv")), P(("grp", "tv"), "sv"), P(None, ("grp", "sv", "tv"))),
        check_vma=False,
    )
```

```python
import jax
import jax.numpy as jnp
from jax import lax
from jax.experimental import pallas as pl
from jax.experimental.pallas import tpu as pltpu
from jax.sharding import PartitionSpec as P

BLK = 128
TB = 640
MASS_ROWS = 16
VMEM_LIMIT = 48 * 1024 * 1024


def swap_halves(x):
    return lax.ppermute(x, "tv", [(0, 1), (1, 0)])


def block_weights(row_of, weight, rows):
    row_ids = lax.broadcasted_iota(jnp.int32, (rows + MASS_ROWS, row_of.shape[1]), 0)
    total = jnp.zeros(row_ids.shape, jnp.float32)
    for slot in range(row_of.shape[0]):
        hit = (row_ids == row_of[slot][None, :]) | (row_ids == rows + slot)
        total = total + jnp.where(hit, weight[slot].astype(jnp.float32)[None, :], 0.0)
    return total.astype(jnp.bfloat16)


def spread_tokens(t_ref, s_ref):
    tokens = t_ref.shape[0]
    count = t_ref.shape[1] // BLK
    step = 16

    def some(i, carry):
        for j in range(step):
            k = i * step + j
            tile = t_ref[:, pl.ds(pl.multiple_of(k * BLK, BLK), BLK)]
            s_ref[pl.ds(pl.multiple_of(k * tokens, tokens), tokens), :] = tile.astype(jnp.float32)
        return carry

    lax.fori_loop(0, count // step, some, 0)


def token_pair(s_ref, t, tokens):
    count = s_ref.shape[0] // tokens
    both = [s_ref[pl.ds(t + i, count, stride=tokens), :].astype(jnp.bfloat16) for i in range(2)]
    return jnp.concatenate(both, axis=1)


def map_own_kernel(w_ref, t_ref, o_ref, s_ref):
    tokens = t_ref.shape[0]
    spread_tokens(t_ref, s_ref)
    for t in range(0, tokens, 2):
        o_ref[:, t * BLK : (t + 2) * BLK] = jnp.dot(
            w_ref[...], token_pair(s_ref, t, tokens), preferred_element_type=jnp.float32
        )


def map_rest_kernel(place_ref, w_ref, t_ref, p_ref, *refs):
    o_refs, (s_ref, m_ref) = refs[:-2], refs[-2:]
    tokens = t_ref.shape[0]
    mine = o_refs[0].shape[1] // BLK
    rows = w_ref.shape[0] - MASS_ROWS
    spread_tokens(t_ref, s_ref)
    for t in range(0, tokens, 2):
        both = p_ref[:, t * BLK : (t + 2) * BLK] + jnp.dot(
            w_ref[...], token_pair(s_ref, t, tokens), preferred_element_type=jnp.float32
        )
        for i in range(2):
            one = both[:, i * BLK : (i + 1) * BLK]
            mass = jnp.sum(jnp.sum(one[rows : rows + 8], axis=0, keepdims=True), axis=1, keepdims=True)
            m_ref[pl.ds(t + i, rows, stride=tokens), :] = one[:rows] * (1.0 / mass)
    for offset, o_ref in enumerate(o_refs):
        owner = place_ref[0] ^ offset
        for b in range(mine):
            first = pl.multiple_of((owner * mine + b) * tokens, tokens)
            o_ref[:, b * BLK : (b + 1) * BLK] = m_ref[pl.ds(first, tokens), :].astype(jnp.bfloat16)


def grad_kernel(scale, place_ref, logits_ref, norm_ref, *refs):
    target_refs, (grad_ref, part_ref, sum_ref) = refs[:-3], refs[-3:]
    tokens = target_refs[0].shape[0]
    for offset, target_ref in enumerate(target_refs):
        rows = pl.ds(pl.multiple_of((place_ref[0] ^ offset) * tokens, tokens), tokens)
        target = target_ref[...].astype(jnp.float32)
        log_probs = logits_ref[rows, :].astype(jnp.float32) - norm_ref[rows, :]
        grad_ref[rows, :] = ((jnp.exp(log_probs) - target) * scale).astype(jnp.bfloat16)
        positive = target > 0
        terms = target * (jnp.log(jnp.where(positive, target, 1.0)) - log_probs)
        total = jnp.sum(jnp.where(positive, terms, 0.0), axis=1, keepdims=True)
        sum_ref[rows, :] = jnp.broadcast_to(total, (tokens, BLK))
    for i in range(sum_ref.shape[0] // BLK):
        part_ref[:, i * BLK : (i + 1) * BLK] = sum_ref[i * BLK : (i + 1) * BLK, :].T[:1]


def hidden_kernel(place_ref, other_ref, *refs):
    own_refs, (o_ref, s_ref) = refs[:-2], refs[-2:]
    held = own_refs[0].shape[0]
    for offset, own_ref in enumerate(own_refs):
        first = (place_ref[0] ^ offset) * 2
        own = pl.ds(pl.multiple_of((first + place_ref[1]) * held, held), held)
        other = pl.ds(pl.multiple_of((first + 1 - place_ref[1]) * held, held), held)
        s_ref[own, :] = own_ref[...].astype(jnp.float32)
        s_ref[other, :] = other_ref[offset].astype(jnp.float32)
    for i in range(s_ref.shape[0] // BLK):
        for j in range(s_ref.shape[1] // BLK):
            tile = s_ref[i * BLK : (i + 1) * BLK, j * BLK : (j + 1) * BLK].T
            o_ref[j * BLK : (j + 1) * BLK, i * BLK : (i + 1) * BLK] = tile.astype(jnp.bfloat16)


def weight_kernel(hidden_ref, grad_ref, o_ref):
    o_ref[...] = jnp.dot(
        hidden_ref[...], grad_ref[...], preferred_element_type=jnp.float32
    ).astype(jnp.bfloat16)


def whole():
    return pl.BlockSpec(memory_space=pltpu.VMEM)


def params():
    return pltpu.CompilerParams(vmem_limit_bytes=VMEM_LIMIT)


def scalars():
    return pl.BlockSpec(memory_space=pltpu.SMEM)


def to_partner(x, offset, flip=False):
    owners = lax.axis_size("sv")
    pairs = [
        (s * 2 + h, (s ^ offset) * 2 + (h ^ int(flip))) for s in range(owners) for h in range(2)
    ]
    return lax.ppermute(x, ("sv", "tv"), pairs)


def body(teacher_probs, align_owner, align_local, align_weight, student_logits, hidden):
    owners = lax.axis_size("sv")
    halves = lax.axis_size("tv")
    owner_index = lax.axis_index("sv")
    half_index = lax.axis_index("tv")
    place = jnp.stack([owner_index, half_index]).astype(jnp.int32)
    tokens = teacher_probs.shape[0]
    columns = student_logits.shape[1]
    blocks = columns // BLK
    mine = blocks // halves
    width = mine * BLK
    rows = owners * mine
    per_half = TB // halves
    group_tokens = owners * tokens
    half_tokens = student_logits.shape[0]
    features = hidden.shape[1]
    first = half_index == 0

    teacher_other = swap_halves(teacher_probs)

    hidden_own = [hidden] + [to_partner(hidden, a) for a in range(1, owners)]
    hidden_other = swap_halves(jnp.stack(hidden_own))
    hidden_t = pl.pallas_call(
        hidden_kernel,
        out_shape=jax.ShapeDtypeStruct((features, group_tokens), jnp.bfloat16),
        in_specs=[scalars()] + [whole()] * (owners + 1),
        out_specs=whole(),
        scratch_shapes=[pltpu.VMEM((group_tokens, features), jnp.float32)],
        compiler_params=params(),
        cost_estimate=pl.CostEstimate(flops=0, bytes_accessed=4 * features * group_tokens, transcendentals=0),
        name="hidden_t",
    )(place, hidden_other, *hidden_own)

    keep = lax.dynamic_slice_in_dim(student_logits, half_index * width, width, 1)
    give = lax.dynamic_slice_in_dim(student_logits, (1 - half_index) * width, width, 1)
    got = swap_halves(give)
    logits = jnp.concatenate([jnp.where(first, keep, got), jnp.where(first, got, keep)], axis=0)

    wide = student_logits.astype(jnp.float32)
    peak = jnp.max(wide, axis=1)
    sums = jnp.sum(jnp.exp(wide - peak[:, None]), axis=1)
    stats = jnp.stack([peak, sums])
    stats_other = swap_halves(stats)
    stats = jnp.stack([jnp.where(first, stats, stats_other), jnp.where(first, stats_other, stats)])
    stats = jnp.stack([stats] + [to_partner(stats, a) for a in range(1, owners)])
    peaks, sums = stats[:, :, 0], stats[:, :, 1]
    top = jnp.max(peaks, axis=0)
    log_norm = top + jnp.log(jnp.sum(sums * jnp.exp(peaks - top[None]), axis=0))
    log_norm = log_norm.reshape(group_tokens, 1)

    local = align_local.T - half_index * mine
    row_of = jnp.where((local >= 0) & (local < mine), align_owner.T * mine + local, -1)
    weight = align_weight.T
    cut = lambda x, which: lax.dynamic_slice_in_dim(x, which * per_half, per_half, 1)
    w_own = block_weights(cut(row_of, half_index), cut(weight, half_index), rows)
    w_rest = block_weights(cut(row_of, 1 - half_index), cut(weight, 1 - half_index), rows)
    flops = 2 * (rows + MASS_ROWS) * per_half * tokens * BLK
    spread = pltpu.VMEM((per_half * tokens, BLK), jnp.float32)
    part = pl.pallas_call(
        map_own_kernel,
        out_shape=jax.ShapeDtypeStruct((rows + MASS_ROWS, tokens * BLK), jnp.float32),
        in_specs=[whole()] * 2,
        out_specs=whole(),
        scratch_shapes=[spread],
        compiler_params=params(),
        cost_estimate=pl.CostEstimate(flops=flops, bytes_accessed=3 << 20, transcendentals=0),
        name="map_own",
    )(w_own, teacher_probs)
    outgoing = pl.pallas_call(
        map_rest_kernel,
        out_shape=[jax.ShapeDtypeStruct((tokens, width), jnp.bfloat16)] * owners,
        in_specs=[scalars()] + [whole()] * 3,
        out_specs=[whole()] * owners,
        scratch_shapes=[spread, pltpu.VMEM((rows * tokens, BLK), jnp.float32)],
        compiler_params=params(),
        cost_estimate=pl.CostEstimate(flops=flops, bytes_accessed=4 << 20, transcendentals=0),
        name="map_rest",
    )(place, w_rest, teacher_other, part)
    targets = [outgoing[0]] + [to_partner(outgoing[a], a) for a in range(1, owners)]

    scale = float(columns * owners)
    grad, terms = pl.pallas_call(
        lambda *refs: grad_kernel(scale, *refs),
        out_shape=(
            jax.ShapeDtypeStruct((group_tokens, width), jnp.bfloat16),
            jax.ShapeDtypeStruct((1, group_tokens), jnp.float32),
        ),
        in_specs=[scalars()] + [whole()] * (owners + 2),
        out_specs=(whole(), whole()),
        scratch_shapes=[pltpu.VMEM((group_tokens, BLK), jnp.float32)],
        compiler_params=params(),
        cost_estimate=pl.CostEstimate(
            flops=10 * group_tokens * width,
            bytes_accessed=6 * group_tokens * width,
            transcendentals=2 * group_tokens * width,
        ),
        name="logit_grad",
    )(place, logits, log_norm, *targets)

    keep = lax.dynamic_slice_in_dim(grad, half_index * half_tokens, half_tokens, 0)
    give = lax.dynamic_slice_in_dim(grad, (1 - half_index) * half_tokens, half_tokens, 0)
    got = swap_halves(give)
    logit_grad = jnp.concatenate([jnp.where(first, keep, got), jnp.where(first, got, keep)], axis=1)

    terms_keep = lax.dynamic_slice_in_dim(terms, half_index * half_tokens, half_tokens, 1)
    terms_give = lax.dynamic_slice_in_dim(terms, (1 - half_index) * half_tokens, half_tokens, 1)
    pieces = [terms_keep] + [to_partner(terms_keep, a) for a in range(1, owners)]
    pieces += [to_partner(terms_give, a, True) for a in range(owners)]
    divergence = sum(pieces[1:], pieces[0]).reshape(half_tokens)

    tile = 256
    weight_grad = pl.pallas_call(
        weight_kernel,
        out_shape=jax.ShapeDtypeStruct((features, width), jnp.bfloat16),
        grid=(width // tile,),
        in_specs=[
            pl.BlockSpec((features, group_tokens), lambda i: (0, 0)),
            pl.BlockSpec((group_tokens, tile), lambda i: (0, i)),
        ],
        out_specs=pl.BlockSpec((features, tile), lambda i: (0, i)),
        compiler_params=params(),
        cost_estimate=pl.CostEstimate(
            flops=2 * features * group_tokens * width,
            bytes_accessed=2 * (features * width + group_tokens * (features + width)),
            transcendentals=0,
        ),
        name="weight_grad",
    )(hidden_t, grad)
    return (divergence, logit_grad, weight_grad)


def solution(mesh):
    return jax.shard_map(
        body,
        mesh=mesh,
        in_specs=(
            P(("grp", "sv"), "tv"),
            P(),
            P(),
            P(),
            P(("grp", "tv"), "sv"),
            P(("grp", "sv", "tv"), None),
        ),
        out_specs=(P(("grp", "tv")), P(("grp", "tv"), "sv"), P(None, ("grp", "sv", "tv"))),
        check_vma=False,
    )
```

```python
import jax
import jax.numpy as jnp
from jax import lax
from jax.experimental import pallas as pl
from jax.experimental.pallas import tpu as pltpu
from jax.sharding import PartitionSpec as P

BLK = 128
TB = 640
MASS_ROWS = 16
VMEM_LIMIT = 48 * 1024 * 1024


def swap_halves(x):
    return lax.ppermute(x, "tv", [(0, 1), (1, 0)])


def block_weights(row_of, weight, rows):
    row_ids = lax.broadcasted_iota(jnp.int32, (rows + MASS_ROWS, row_of.shape[1]), 0)
    total = jnp.zeros(row_ids.shape, jnp.float32)
    for slot in range(row_of.shape[0]):
        hit = (row_ids == row_of[slot][None, :]) | (row_ids == rows + slot)
        total = total + jnp.where(hit, weight[slot].astype(jnp.float32)[None, :], 0.0)
    return total.astype(jnp.bfloat16)


def spread_tokens(t_ref, s_ref):
    tokens = t_ref.shape[0]
    count = t_ref.shape[1] // BLK
    step = 16

    def some(i, carry):
        for j in range(step):
            k = i * step + j
            tile = t_ref[:, pl.ds(pl.multiple_of(k * BLK, BLK), BLK)]
            s_ref[pl.ds(pl.multiple_of(k * tokens, tokens), tokens), :] = tile.astype(jnp.float32)
        return carry

    lax.fori_loop(0, count // step, some, 0)


def token_pair(s_ref, t, tokens):
    count = s_ref.shape[0] // tokens
    both = [s_ref[pl.ds(t + i, count, stride=tokens), :].astype(jnp.bfloat16) for i in range(2)]
    return jnp.concatenate(both, axis=1)


def map_own_kernel(w_ref, t_ref, o_ref, s_ref):
    tokens = t_ref.shape[0]
    spread_tokens(t_ref, s_ref)
    for t in range(0, tokens, 2):
        o_ref[:, t * BLK : (t + 2) * BLK] = jnp.dot(
            w_ref[...], token_pair(s_ref, t, tokens), preferred_element_type=jnp.float32
        )


def three_parts(x):
    parts = []
    for _ in range(3):
        parts.append(x.astype(jnp.bfloat16).astype(jnp.float32))
        x = x - parts[-1]
    return parts


def map_rest_kernel(w_ref, t_ref, p_ref, stats_ref, o_ref, s_ref, m_ref):
    tokens = t_ref.shape[0]
    owners = o_ref.shape[0]
    rows = w_ref.shape[0] - MASS_ROWS
    mine = rows // owners
    spread_tokens(t_ref, s_ref)
    for t in range(0, tokens, 2):
        both = p_ref[:, t * BLK : (t + 2) * BLK] + jnp.dot(
            w_ref[...], token_pair(s_ref, t, tokens), preferred_element_type=jnp.float32
        )
        for i in range(2):
            m_ref[pl.ds(t + i, rows + 8, stride=tokens), :] = both[: rows + 8, i * BLK : (i + 1) * BLK]
    mass = m_ref[rows * tokens : (rows + 1) * tokens, :]
    for slot in range(1, 2):
        mass = mass + m_ref[(rows + slot) * tokens : (rows + slot + 1) * tokens, :]
    inverse = jnp.broadcast_to(1.0 / jnp.sum(mass, axis=1, keepdims=True), (tokens, BLK))
    stats = [stats_ref[0:1, :]] + three_parts(stats_ref[1:2, :])
    extra = jnp.zeros((tokens, stats_ref.shape[1]), jnp.float32)
    row_ids = lax.broadcasted_iota(jnp.int32, extra.shape, 0)
    for i, row in enumerate(stats):
        extra = jnp.where(row_ids == i, row, extra)
    extra = extra.astype(jnp.bfloat16)

    def owner(q, carry):
        for b in range(mine):
            first = pl.multiple_of((q * mine + b) * tokens, tokens)
            tile = m_ref[pl.ds(first, tokens), :] * inverse
            o_ref[q, :, b * BLK : (b + 1) * BLK] = tile.astype(jnp.bfloat16)
        o_ref[q, :, mine * BLK :] = extra
        return carry

    lax.fori_loop(0, owners, owner, 0)


def grad_kernel(scale, target_ref, logits_ref, grad_ref, part_ref):
    owners, tokens, _ = target_ref.shape
    group_tokens, width = logits_ref.shape
    stats = [target_ref[q, :, width:].astype(jnp.float32) for q in range(owners)]
    top = stats[0][0:1]
    for one in stats[1:]:
        top = jnp.maximum(top, one[0:1])
    total = jnp.zeros_like(top)
    for one in stats:
        total = total + (one[1:2] + one[2:3] + one[3:4]) * jnp.exp(one[0:1] - top)
    log_norm = top + jnp.log(total)
    for i in range(group_tokens // BLK):
        rows = slice(i * BLK, (i + 1) * BLK)
        group = slice(i * BLK // tokens, (i + 1) * BLK // tokens)
        norm = jnp.broadcast_to(log_norm[:, rows], (BLK, BLK)).T
        terms = jnp.zeros((BLK, BLK), jnp.float32)
        for b in range(width // BLK):
            lanes = slice(b * BLK, (b + 1) * BLK)
            target = target_ref[group, :, lanes].reshape(BLK, BLK).astype(jnp.float32)
            log_probs = logits_ref[rows, lanes].astype(jnp.float32) - norm
            grad_ref[rows, lanes] = ((jnp.exp(log_probs) - target) * scale).astype(jnp.bfloat16)
            positive = target > 0
            one = target * (jnp.log(jnp.where(positive, target, 1.0)) - log_probs)
            terms = terms + jnp.where(positive, one, 0.0)
        part_ref[:, rows] = jnp.sum(terms.T, axis=0, keepdims=True)


def weight_kernel(hidden_ref, grad_ref, o_ref, block_ref, sem):
    steps, tile, _ = block_ref.shape
    copies = []
    for i in range(steps):
        rows = slice(i * tile, (i + 1) * tile)
        block_ref[i] = jnp.dot(
            hidden_ref[rows, :], grad_ref[...], preferred_element_type=jnp.float32
        ).astype(jnp.bfloat16)
        copies.append(pltpu.make_async_copy(block_ref.at[i], o_ref.at[pl.ds(i * tile, tile), :], sem.at[i]))
        copies[-1].start()
    for copy in copies:
        copy.wait()


def whole():
    return pl.BlockSpec(memory_space=pltpu.VMEM)


def params():
    return pltpu.CompilerParams(vmem_limit_bytes=VMEM_LIMIT)


def body(teacher_probs, align_owner, align_local, align_weight, student_logits, hidden):
    owners = lax.axis_size("sv")
    halves = lax.axis_size("tv")
    half_index = lax.axis_index("tv")
    tokens = teacher_probs.shape[0]
    columns = student_logits.shape[1]
    blocks = columns // BLK
    mine = blocks // halves
    width = mine * BLK
    rows = owners * mine
    per_half = TB // halves
    group_tokens = owners * tokens
    half_tokens = student_logits.shape[0]
    features = hidden.shape[1]
    first = half_index == 0

    def in_order(own, other, axis):
        return jnp.concatenate([jnp.where(first, own, other), jnp.where(first, other, own)], axis=axis)

    teacher_other = swap_halves(teacher_probs)

    keep = lax.dynamic_slice_in_dim(student_logits, half_index * width, width, 1)
    give = lax.dynamic_slice_in_dim(student_logits, (1 - half_index) * width, width, 1)
    logits = in_order(keep, swap_halves(give), 0)

    wide = student_logits.astype(jnp.float32)
    peak = jnp.max(wide, axis=1)
    sums = jnp.sum(jnp.exp(wide - peak[:, None]), axis=1)
    stats = jnp.stack([peak, sums])
    stats = in_order(stats, swap_halves(stats), 1)

    local = align_local.T - half_index * mine
    row_of = jnp.where((local >= 0) & (local < mine), align_owner.T * mine + local, -1)
    weight = align_weight.T
    cut = lambda x, which: lax.dynamic_slice_in_dim(x, which * per_half, per_half, 1)
    w_own = block_weights(cut(row_of, half_index), cut(weight, half_index), rows)
    w_rest = block_weights(cut(row_of, 1 - half_index), cut(weight, 1 - half_index), rows)
    flops = 2 * (rows + MASS_ROWS) * per_half * tokens * BLK
    spread = pltpu.VMEM((per_half * tokens, BLK), jnp.float32)
    part = pl.pallas_call(
        map_own_kernel,
        out_shape=jax.ShapeDtypeStruct((rows + MASS_ROWS, tokens * BLK), jnp.float32),
        in_specs=[whole()] * 2,
        out_specs=whole(),
        scratch_shapes=[spread],
        compiler_params=params(),
        cost_estimate=pl.CostEstimate(flops=flops, bytes_accessed=3 << 20, transcendentals=0),
        name="map_own",
    )(w_own, teacher_probs)
    outgoing = pl.pallas_call(
        map_rest_kernel,
        out_shape=jax.ShapeDtypeStruct((owners, tokens, width + group_tokens), jnp.bfloat16),
        in_specs=[whole()] * 4,
        out_specs=whole(),
        scratch_shapes=[spread, pltpu.VMEM(((rows + 8) * tokens, BLK), jnp.float32)],
        compiler_params=params(),
        cost_estimate=pl.CostEstimate(flops=flops, bytes_accessed=4 << 20, transcendentals=0),
        name="map_rest",
    )(w_rest, teacher_other, part, stats)
    target = lax.all_to_all(outgoing, "sv", 0, 0, tiled=True)

    hidden, outgoing = lax.optimization_barrier((hidden, outgoing))
    hidden_own = lax.all_gather(hidden, "sv")
    hidden_other = swap_halves(hidden_own)
    hidden_t = in_order(hidden_own, hidden_other, 1).reshape(group_tokens, features).T

    scale = float(columns * owners)
    grad, terms = pl.pallas_call(
        lambda *refs: grad_kernel(scale, *refs),
        out_shape=(
            jax.ShapeDtypeStruct((group_tokens, width), jnp.bfloat16),
            jax.ShapeDtypeStruct((1, group_tokens), jnp.float32),
        ),
        in_specs=[whole()] * 2,
        out_specs=(whole(), whole()),
        compiler_params=params(),
        cost_estimate=pl.CostEstimate(
            flops=10 * group_tokens * width,
            bytes_accessed=6 * group_tokens * width,
            transcendentals=2 * group_tokens * width,
        ),
        name="logit_grad",
    )(target, logits)

    keep = lax.dynamic_slice_in_dim(grad, half_index * half_tokens, half_tokens, 0)
    give = lax.dynamic_slice_in_dim(grad, (1 - half_index) * half_tokens, half_tokens, 0)
    logit_grad = in_order(keep, swap_halves(give), 1)

    terms = jnp.broadcast_to(terms.reshape(1, halves, half_tokens), (owners, halves, half_tokens))
    terms = lax.all_to_all(terms.reshape(owners * halves, half_tokens), ("sv", "tv"), 0, 0, tiled=True)
    divergence = jnp.sum(terms, axis=0)

    steps = 8
    weight_grad = pl.pallas_call(
        weight_kernel,
        out_shape=jax.ShapeDtypeStruct((features, width), jnp.bfloat16),
        in_specs=[whole()] * 2,
        out_specs=pl.BlockSpec(memory_space=pl.ANY),
        scratch_shapes=[
            pltpu.VMEM((steps, features // steps, width), jnp.bfloat16),
            pltpu.SemaphoreType.DMA((steps,)),
        ],
        compiler_params=params(),
        cost_estimate=pl.CostEstimate(
            flops=2 * features * group_tokens * width,
            bytes_accessed=2 * (features * width + group_tokens * (features + width)),
            transcendentals=0,
        ),
        name="weight_grad",
    )(hidden_t, grad)
    return (divergence, logit_grad, weight_grad)


def solution(mesh):
    return jax.shard_map(
        body,
        mesh=mesh,
        in_specs=(
            P(("grp", "sv"), "tv"),
            P(),
            P(),
            P(),
            P(("grp", "tv"), "sv"),
            P(("grp", "sv", "tv"), None),
        ),
        out_specs=(P(("grp", "tv")), P(("grp", "tv"), "sv"), P(None, ("grp", "sv", "tv"))),
        check_vma=False,
    )
```

```python
import jax
import jax.numpy as jnp
from jax import lax
from jax.experimental import pallas as pl
from jax.experimental.pallas import tpu as pltpu
from jax.sharding import PartitionSpec as P

BLK = 128
TB = 640
MASS_ROWS = 16
VMEM_LIMIT = 48 * 1024 * 1024


def swap_halves(x):
    return lax.ppermute(x, "tv", [(0, 1), (1, 0)])


def block_weights(row_of, weight, rows):
    row_ids = lax.broadcasted_iota(jnp.int32, (rows + MASS_ROWS, row_of.shape[1]), 0)
    total = jnp.zeros(row_ids.shape, jnp.float32)
    for slot in range(row_of.shape[0]):
        hit = (row_ids == row_of[slot][None, :]) | (row_ids == rows + slot)
        total = total + jnp.where(hit, weight[slot].astype(jnp.float32)[None, :], 0.0)
    return total.astype(jnp.bfloat16)


def spread_tokens(t_ref, s_ref, start, count):
    tokens = t_ref.shape[0]
    step = 16

    def some(i, carry):
        for j in range(step):
            k = start + i * step + j
            tile = t_ref[:, pl.ds(pl.multiple_of(k * BLK, BLK), BLK)]
            s_ref[pl.ds(pl.multiple_of(k * tokens, tokens), tokens), :] = tile.astype(jnp.float32)
        return carry

    lax.fori_loop(0, count // step, some, 0)


def token_pair(s_ref, t, tokens):
    count = s_ref.shape[0] // tokens
    both = [s_ref[pl.ds(t + i, count, stride=tokens), :].astype(jnp.bfloat16) for i in range(2)]
    return jnp.concatenate(both, axis=1)


def map_own_kernel(w_ref, t_ref, o_ref, s_ref):
    tokens = t_ref.shape[0]
    spread_tokens(t_ref, s_ref, 0, t_ref.shape[1] // BLK)
    for t in range(0, tokens, 2):
        o_ref[:, t * BLK : (t + 2) * BLK] = jnp.dot(
            w_ref[...], token_pair(s_ref, t, tokens), preferred_element_type=jnp.float32
        )


def three_parts(x):
    parts = []
    for _ in range(3):
        parts.append(x.astype(jnp.bfloat16).astype(jnp.float32))
        x = x - parts[-1]
    return parts


def map_rest_kernel(w_ref, t_ref, p_ref, stats_ref, o_ref, t_buf, s_ref, m_ref, o_buf, in_sem, out_sem):
    tokens = t_ref.shape[0]
    owners = o_ref.shape[0]
    rows = w_ref.shape[0] - MASS_ROWS
    mine = rows // owners
    cuts = in_sem.shape[0]
    part = t_ref.shape[1] // cuts
    arriving = [
        pltpu.make_async_copy(
            t_ref.at[:, pl.ds(i * part, part)], t_buf.at[:, pl.ds(i * part, part)], in_sem.at[i]
        )
        for i in range(cuts)
    ]
    for copy in arriving:
        copy.start()
    stats = [stats_ref[0:1, :]] + three_parts(stats_ref[1:2, :])
    extra = jnp.zeros((tokens, stats_ref.shape[1]), jnp.float32)
    row_ids = lax.broadcasted_iota(jnp.int32, extra.shape, 0)
    for i, row in enumerate(stats):
        extra = jnp.where(row_ids == i, row, extra)
    extra = extra.astype(jnp.bfloat16)
    for i, copy in enumerate(arriving):
        copy.wait()
        spread_tokens(t_buf, s_ref, i * (part // BLK), part // BLK)
    for t in range(0, tokens, 2):
        both = p_ref[:, t * BLK : (t + 2) * BLK] + jnp.dot(
            w_ref[...], token_pair(s_ref, t, tokens), preferred_element_type=jnp.float32
        )
        for i in range(2):
            m_ref[pl.ds(t + i, rows + 8, stride=tokens), :] = both[: rows + 8, i * BLK : (i + 1) * BLK]
    mass = m_ref[rows * tokens : (rows + 1) * tokens, :]
    for slot in range(1, 2):
        mass = mass + m_ref[(rows + slot) * tokens : (rows + slot + 1) * tokens, :]
    inverse = jnp.broadcast_to(1.0 / jnp.sum(mass, axis=1, keepdims=True), (tokens, BLK))

    def leaving(q):
        return pltpu.make_async_copy(o_buf.at[q], o_ref.at[q], out_sem.at[q])

    def owner(q, carry):
        for b in range(mine):
            first = pl.multiple_of((q * mine + b) * tokens, tokens)
            tile = m_ref[pl.ds(first, tokens), :] * inverse
            o_buf[q, :, b * BLK : (b + 1) * BLK] = tile.astype(jnp.bfloat16)
        o_buf[q, :, mine * BLK :] = extra
        leaving(q).start()
        return carry

    def left(q, carry):
        leaving(q).wait()
        return carry

    lax.fori_loop(0, owners, owner, 0)
    lax.fori_loop(0, owners, left, 0)


def stats_kernel(logits_ref, o_ref):
    half_tokens, columns = logits_ref.shape
    for i in range(0, half_tokens, 64):
        rows = slice(i, i + 64)
        peak = logits_ref[rows, :BLK].astype(jnp.float32)
        for b in range(1, columns // BLK):
            peak = jnp.maximum(peak, logits_ref[rows, b * BLK : (b + 1) * BLK].astype(jnp.float32))
        peak = jnp.broadcast_to(jnp.max(peak, axis=1, keepdims=True), peak.shape)
        total = jnp.zeros_like(peak)
        for b in range(columns // BLK):
            total = total + jnp.exp(logits_ref[rows, b * BLK : (b + 1) * BLK].astype(jnp.float32) - peak)
        o_ref[0:1, rows] = peak.T[0:1]
        o_ref[1:2, rows] = jnp.sum(total.T, axis=0, keepdims=True)


def grad_kernel(scale, target_ref, logits_ref, grad_ref, part_ref):
    owners, tokens, _ = target_ref.shape
    group_tokens, width = logits_ref.shape
    stats = [target_ref[q, :, width:].astype(jnp.float32) for q in range(owners)]
    top = stats[0][0:1]
    for one in stats[1:]:
        top = jnp.maximum(top, one[0:1])
    total = jnp.zeros_like(top)
    for one in stats:
        total = total + (one[1:2] + one[2:3] + one[3:4]) * jnp.exp(one[0:1] - top)
    log_norm = top + jnp.log(total)
    for i in range(group_tokens // BLK):
        rows = slice(i * BLK, (i + 1) * BLK)
        group = slice(i * BLK // tokens, (i + 1) * BLK // tokens)
        norm = jnp.broadcast_to(log_norm[:, rows], (BLK, BLK)).T
        terms = jnp.zeros((BLK, BLK), jnp.float32)
        for b in range(width // BLK):
            lanes = slice(b * BLK, (b + 1) * BLK)
            target = target_ref[group, :, lanes].reshape(BLK, BLK).astype(jnp.float32)
            log_probs = logits_ref[rows, lanes].astype(jnp.float32) - norm
            grad_ref[rows, lanes] = ((jnp.exp(log_probs) - target) * scale).astype(jnp.bfloat16)
            positive = target > 0
            one = target * (jnp.log(jnp.where(positive, target, 1.0)) - log_probs)
            terms = terms + jnp.where(positive, one, 0.0)
        row = jnp.sum(terms.T, axis=0, keepdims=True)
        for q in range(part_ref.shape[0]):
            part_ref[q, :, rows] = jnp.broadcast_to(row, (part_ref.shape[1], BLK))


def hidden_kernel(place_ref, own_ref, other_ref, o_ref, s_ref):
    owners, held, features = own_ref.shape
    for i in range(owners):
        offset = sum(((i >> j) & 1) * (owners >> (j + 1)) for j in range(owners.bit_length() - 1))
        first = (place_ref[0] ^ offset) * 2
        own = pl.ds(pl.multiple_of((first + place_ref[1]) * held, held), held)
        other = pl.ds(pl.multiple_of((first + 1 - place_ref[1]) * held, held), held)
        s_ref[own, :] = own_ref[i].astype(jnp.float32)
        s_ref[other, :] = other_ref[i].astype(jnp.float32)
    for i in range(s_ref.shape[0] // BLK):
        for j in range(features // BLK):
            tile = s_ref[i * BLK : (i + 1) * BLK, j * BLK : (j + 1) * BLK].T
            o_ref[j * BLK : (j + 1) * BLK, i * BLK : (i + 1) * BLK] = tile.astype(jnp.bfloat16)


def finish_kernel(place_ref, grad_ref, got_ref, terms_ref, o_ref, d_ref, sem):
    half_tokens, width = got_ref.shape
    half = place_ref[1]
    kept_at = pl.ds(pl.multiple_of(half * width, width), width)
    got_at = pl.ds(pl.multiple_of((1 - half) * width, width), width)
    rows = pl.ds(pl.multiple_of(half * half_tokens, half_tokens), half_tokens)
    copies = [
        pltpu.make_async_copy(grad_ref.at[rows, :], o_ref.at[:, kept_at], sem.at[0]),
        pltpu.make_async_copy(got_ref, o_ref.at[:, got_at], sem.at[1]),
    ]
    for copy in copies:
        copy.start()
    total = terms_ref[0, 0:1, :]
    for q in range(1, terms_ref.shape[0]):
        total = total + terms_ref[q, 0:1, :]
    d_ref[...] = jnp.where(half == 0, total[:, :half_tokens], total[:, half_tokens:])
    for copy in copies:
        copy.wait()


def weight_kernel(hidden_ref, grad_ref, o_ref, block_ref, sem):
    steps, tile, _ = block_ref.shape
    copies = []
    for i in range(steps):
        rows = slice(i * tile, (i + 1) * tile)
        block_ref[i] = jnp.dot(
            hidden_ref[rows, :], grad_ref[...], preferred_element_type=jnp.float32
        ).astype(jnp.bfloat16)
        copies.append(pltpu.make_async_copy(block_ref.at[i], o_ref.at[pl.ds(i * tile, tile), :], sem.at[i]))
        copies[-1].start()
    for copy in copies:
        copy.wait()


def whole():
    return pl.BlockSpec(memory_space=pltpu.VMEM)


def params():
    return pltpu.CompilerParams(vmem_limit_bytes=VMEM_LIMIT)


def scalars():
    return pl.BlockSpec(memory_space=pltpu.SMEM)


def anywhere():
    return pl.BlockSpec(memory_space=pl.ANY)


def to_partner(x, offset):
    return lax.ppermute(x, "sv", [(s, s ^ offset) for s in range(lax.axis_size("sv"))])


def body(teacher_probs, align_owner, align_local, align_weight, student_logits, hidden):
    owners = lax.axis_size("sv")
    halves = lax.axis_size("tv")
    half_index = lax.axis_index("tv")
    place = jnp.stack([lax.axis_index("sv"), half_index]).astype(jnp.int32)
    tokens = teacher_probs.shape[0]
    columns = student_logits.shape[1]
    blocks = columns // BLK
    mine = blocks // halves
    width = mine * BLK
    rows = owners * mine
    per_half = TB // halves
    group_tokens = owners * tokens
    half_tokens = student_logits.shape[0]
    features = hidden.shape[1]
    first = half_index == 0

    def in_order(own, other, axis):
        return jnp.concatenate([jnp.where(first, own, other), jnp.where(first, other, own)], axis=axis)

    teacher_other = swap_halves(teacher_probs)

    stats = pl.pallas_call(
        stats_kernel,
        out_shape=jax.ShapeDtypeStruct((2, half_tokens), jnp.float32),
        in_specs=[whole()],
        out_specs=whole(),
        compiler_params=params(),
        cost_estimate=pl.CostEstimate(flops=0, bytes_accessed=0, transcendentals=0),
        name="stats",
    )(student_logits)
    stats = in_order(stats, swap_halves(stats), 1)

    local = align_local.T - half_index * mine
    row_of = jnp.where((local >= 0) & (local < mine), align_owner.T * mine + local, -1)
    weight = align_weight.T
    cut = lambda x, which: lax.dynamic_slice_in_dim(x, which * per_half, per_half, 1)
    w_own = block_weights(cut(row_of, half_index), cut(weight, half_index), rows)
    w_rest = block_weights(cut(row_of, 1 - half_index), cut(weight, 1 - half_index), rows)
    spread = pltpu.VMEM((per_half * tokens, BLK), jnp.float32)
    part = pl.pallas_call(
        map_own_kernel,
        out_shape=jax.ShapeDtypeStruct((rows + MASS_ROWS, tokens * BLK), jnp.float32),
        in_specs=[whole()] * 2,
        out_specs=whole(),
        scratch_shapes=[spread],
        compiler_params=params(),
        cost_estimate=pl.CostEstimate(flops=0, bytes_accessed=0, transcendentals=0),
        name="map_own",
    )(w_own, teacher_probs)
    chunk = (owners, tokens, width + group_tokens)
    cuts = 4
    outgoing = pl.pallas_call(
        map_rest_kernel,
        out_shape=jax.ShapeDtypeStruct(chunk, jnp.bfloat16),
        in_specs=[whole(), anywhere(), whole(), whole()],
        out_specs=anywhere(),
        scratch_shapes=[
            pltpu.VMEM((tokens, per_half * BLK), jnp.bfloat16),
            spread,
            pltpu.VMEM(((rows + 8) * tokens, BLK), jnp.float32),
            pltpu.VMEM(chunk, jnp.bfloat16),
            pltpu.SemaphoreType.DMA((cuts,)),
            pltpu.SemaphoreType.DMA((owners,)),
        ],
        compiler_params=params(),
        cost_estimate=pl.CostEstimate(
            flops=2 * (rows + MASS_ROWS) * per_half * tokens * BLK, bytes_accessed=4 << 20, transcendentals=0
        ),
        name="map_rest",
    )(w_rest, teacher_other, part, stats)
    target = lax.all_to_all(outgoing, "sv", 0, 0, tiled=True)

    hidden, late_logits, outgoing = lax.optimization_barrier((hidden, student_logits, outgoing))

    keep = lax.dynamic_slice_in_dim(late_logits, half_index * width, width, 1)
    give = lax.dynamic_slice_in_dim(late_logits, (1 - half_index) * width, width, 1)
    logits = in_order(keep, swap_halves(give), 0)

    hidden_own = hidden[None]
    offset = owners // 2
    while offset:
        hidden_own = jnp.concatenate([hidden_own, to_partner(hidden_own, offset)])
        offset //= 2
    hidden_t = pl.pallas_call(
        hidden_kernel,
        out_shape=jax.ShapeDtypeStruct((features, group_tokens), jnp.bfloat16),
        in_specs=[scalars(), whole(), whole()],
        out_specs=whole(),
        scratch_shapes=[pltpu.VMEM((group_tokens, features), jnp.float32)],
        compiler_params=params(),
        cost_estimate=pl.CostEstimate(flops=0, bytes_accessed=4 * features * group_tokens, transcendentals=0),
        name="hidden_t",
    )(place, hidden_own, swap_halves(hidden_own))

    scale = float(columns * owners)
    grad, terms = pl.pallas_call(
        lambda *refs: grad_kernel(scale, *refs),
        out_shape=(
            jax.ShapeDtypeStruct((group_tokens, width), jnp.bfloat16),
            jax.ShapeDtypeStruct((owners * halves, 8, group_tokens), jnp.float32),
        ),
        in_specs=[whole()] * 2,
        out_specs=(whole(), whole()),
        compiler_params=params(),
        cost_estimate=pl.CostEstimate(
            flops=10 * group_tokens * width,
            bytes_accessed=6 * group_tokens * width,
            transcendentals=2 * group_tokens * width,
        ),
        name="logit_grad",
    )(target, logits)

    terms = lax.all_to_all(terms, ("sv", "tv"), 0, 0, tiled=True)
    give = lax.dynamic_slice_in_dim(grad, (1 - half_index) * half_tokens, half_tokens, 0)
    got = swap_halves(give)

    steps = 8
    weight_grad = pl.pallas_call(
        weight_kernel,
        out_shape=jax.ShapeDtypeStruct((features, width), jnp.bfloat16),
        in_specs=[whole()] * 2,
        out_specs=anywhere(),
        scratch_shapes=[
            pltpu.VMEM((steps, features // steps, width), jnp.bfloat16),
            pltpu.SemaphoreType.DMA((steps,)),
        ],
        compiler_params=params(),
        cost_estimate=pl.CostEstimate(
            flops=2 * features * group_tokens * width,
            bytes_accessed=2 * (features * width + group_tokens * (features + width)),
            transcendentals=0,
        ),
        name="weight_grad",
    )(hidden_t, grad)

    logit_grad, divergence = pl.pallas_call(
        finish_kernel,
        out_shape=(
            jax.ShapeDtypeStruct((half_tokens, columns), jnp.bfloat16),
            jax.ShapeDtypeStruct((1, half_tokens), jnp.float32),
        ),
        in_specs=[scalars(), anywhere(), anywhere(), whole()],
        out_specs=(anywhere(), whole()),
        scratch_shapes=[pltpu.SemaphoreType.DMA((2,))],
        compiler_params=params(),
        cost_estimate=pl.CostEstimate(flops=0, bytes_accessed=4 * half_tokens * columns, transcendentals=0),
        name="finish",
    )(place, grad, got, terms)
    return (divergence.reshape(half_tokens), logit_grad, weight_grad)


def solution(mesh):
    return jax.shard_map(
        body,
        mesh=mesh,
        in_specs=(
            P(("grp", "sv"), "tv"),
            P(),
            P(),
            P(),
            P(("grp", "tv"), "sv"),
            P(("grp", "sv", "tv"), None),
        ),
        out_specs=(P(("grp", "tv")), P(("grp", "tv"), "sv"), P(None, ("grp", "sv", "tv"))),
        check_vma=False,
    )
```

```python
import jax
import jax.numpy as jnp
from jax import lax
from jax.experimental import pallas as pl
from jax.experimental.pallas import tpu as pltpu
from jax.sharding import PartitionSpec as P

BLK = 128
TB = 640
MASS_ROWS = 16
VMEM_LIMIT = 48 * 1024 * 1024


def swap_halves(x):
    return lax.ppermute(x, "tv", [(0, 1), (1, 0)])


def block_weights(place_ref, owner_ref, local_ref, weight_ref, which, rows, mine):
    count = owner_ref.shape[1] // 2
    halved = lambda x: jnp.where(which == 0, x[:, :count], x[:, count:])
    local = local_ref[...] - place_ref[1] * mine
    inside = (local >= 0) & (local < mine)
    row_of = halved(jnp.where(inside, owner_ref[...] * mine + local, -1))
    weight = halved(weight_ref[...].astype(jnp.float32))
    row_ids = lax.broadcasted_iota(jnp.int32, (rows + MASS_ROWS, count), 0)
    total = jnp.zeros(row_ids.shape, jnp.float32)
    for slot in range(row_of.shape[0]):
        hit = (row_ids == row_of[slot : slot + 1]) | (row_ids == rows + slot)
        total = total + jnp.where(hit, weight[slot : slot + 1], 0.0)
    return total.astype(jnp.bfloat16)


def spread_tokens(t_ref, s_ref, start, count):
    tokens = t_ref.shape[0]
    step = 16

    def some(i, carry):
        for j in range(step):
            k = start + i * step + j
            tile = t_ref[:, pl.ds(pl.multiple_of(k * BLK, BLK), BLK)]
            s_ref[pl.ds(pl.multiple_of(k * tokens, tokens), tokens), :] = tile.astype(jnp.float32)
        return carry

    lax.fori_loop(0, count // step, some, 0)


def token_pair(s_ref, t, tokens):
    count = s_ref.shape[0] // tokens
    both = [s_ref[pl.ds(t + i, count, stride=tokens), :].astype(jnp.bfloat16) for i in range(2)]
    return jnp.concatenate(both, axis=1)


def map_own_kernel(w_ref, t_ref, o_ref, s_ref):
    tokens = t_ref.shape[0]
    spread_tokens(t_ref, s_ref, 0, t_ref.shape[1] // BLK)
    for t in range(0, tokens, 2):
        o_ref[:, t * BLK : (t + 2) * BLK] = jnp.dot(
            w_ref[...], token_pair(s_ref, t, tokens), preferred_element_type=jnp.float32
        )


def three_parts(x):
    parts = []
    for _ in range(3):
        parts.append(x.astype(jnp.bfloat16).astype(jnp.float32))
        x = x - parts[-1]
    return parts


def map_rest_kernel(w_ref, t_ref, p_ref, stats_ref, o_ref, t_buf, s_ref, m_ref, o_buf, in_sem, out_sem):
    tokens = t_ref.shape[0]
    owners = o_ref.shape[0]
    rows = w_ref.shape[0] - MASS_ROWS
    mine = rows // owners
    cuts = in_sem.shape[0]
    part = t_ref.shape[1] // cuts
    arriving = [
        pltpu.make_async_copy(
            t_ref.at[:, pl.ds(i * part, part)], t_buf.at[:, pl.ds(i * part, part)], in_sem.at[i]
        )
        for i in range(cuts)
    ]
    for copy in arriving:
        copy.start()
    stats = [stats_ref[0:1, :]] + three_parts(stats_ref[1:2, :])
    extra = jnp.zeros((tokens, stats_ref.shape[1]), jnp.float32)
    row_ids = lax.broadcasted_iota(jnp.int32, extra.shape, 0)
    for i, row in enumerate(stats):
        extra = jnp.where(row_ids == i, row, extra)
    extra = extra.astype(jnp.bfloat16)
    for i, copy in enumerate(arriving):
        copy.wait()
        spread_tokens(t_buf, s_ref, i * (part // BLK), part // BLK)
    for t in range(0, tokens, 2):
        both = p_ref[:, t * BLK : (t + 2) * BLK] + jnp.dot(
            w_ref[...], token_pair(s_ref, t, tokens), preferred_element_type=jnp.float32
        )
        for i in range(2):
            m_ref[pl.ds(t + i, rows + 8, stride=tokens), :] = both[: rows + 8, i * BLK : (i + 1) * BLK]
    mass = m_ref[rows * tokens : (rows + 1) * tokens, :]
    for slot in range(1, 2):
        mass = mass + m_ref[(rows + slot) * tokens : (rows + slot + 1) * tokens, :]
    inverse = jnp.broadcast_to(1.0 / jnp.sum(mass, axis=1, keepdims=True), (tokens, BLK))

    def leaving(q):
        return pltpu.make_async_copy(o_buf.at[q], o_ref.at[q], out_sem.at[q])

    def owner(q, carry):
        for b in range(mine):
            first = pl.multiple_of((q * mine + b) * tokens, tokens)
            tile = m_ref[pl.ds(first, tokens), :] * inverse
            o_buf[q, :, b * BLK : (b + 1) * BLK] = tile.astype(jnp.bfloat16)
        o_buf[q, :, mine * BLK :] = extra
        leaving(q).start()
        return carry

    def left(q, carry):
        leaving(q).wait()
        return carry

    lax.fori_loop(0, owners, owner, 0)
    lax.fori_loop(0, owners, left, 0)


def prepare_kernel(
    place_ref, owner_ref, local_ref, weight_ref, logits_ref, t_ref, stats_ref, own_ref, rest_ref, held_ref, l_buf, sems
):
    half_tokens, columns = logits_ref.shape
    rows = own_ref.shape[0] - MASS_ROWS
    mine = columns // BLK // 2
    cuts = sems.shape[0] // 2
    wide, deep = columns // cuts, t_ref.shape[1] // cuts
    for_stats = [
        pltpu.make_async_copy(
            logits_ref.at[:, pl.ds(i * wide, wide)], l_buf.at[:, pl.ds(i * wide, wide)], sems.at[i]
        )
        for i in range(cuts)
    ]
    for_mapping = [
        pltpu.make_async_copy(
            t_ref.at[:, pl.ds(i * deep, deep)], held_ref.at[:, pl.ds(i * deep, deep)], sems.at[cuts + i]
        )
        for i in range(cuts)
    ]
    for copy in for_stats + for_mapping:
        copy.start()
    own_ref[...] = block_weights(place_ref, owner_ref, local_ref, weight_ref, place_ref[1], rows, mine)
    rest_ref[...] = block_weights(place_ref, owner_ref, local_ref, weight_ref, 1 - place_ref[1], rows, mine)
    for copy in for_stats:
        copy.wait()
    for i in range(0, half_tokens, 64):
        some = slice(i, i + 64)
        peak = l_buf[some, :BLK].astype(jnp.float32)
        for b in range(1, columns // BLK):
            peak = jnp.maximum(peak, l_buf[some, b * BLK : (b + 1) * BLK].astype(jnp.float32))
        peak = jnp.broadcast_to(jnp.max(peak, axis=1, keepdims=True), peak.shape)
        total = jnp.zeros_like(peak)
        for b in range(columns // BLK):
            total = total + jnp.exp(l_buf[some, b * BLK : (b + 1) * BLK].astype(jnp.float32) - peak)
        stats_ref[0:1, some] = peak.T[0:1]
        stats_ref[1:2, some] = jnp.sum(total.T, axis=0, keepdims=True)
    for copy in for_mapping:
        copy.wait()


def later_kernel(place_ref, sent_ref, hidden_ref, logits_ref, h_ref, give_ref):
    width = give_ref.shape[1]
    h_ref[...] = hidden_ref[...]
    give_ref[...] = jnp.where(place_ref[1] == 0, logits_ref[:, width:], logits_ref[:, :width])


def grad_kernel(scale, target_ref, logits_ref, grad_ref, part_ref):
    owners, tokens, _ = target_ref.shape
    group_tokens, width = logits_ref.shape
    stats = [target_ref[q, :, width:].astype(jnp.float32) for q in range(owners)]
    top = stats[0][0:1]
    for one in stats[1:]:
        top = jnp.maximum(top, one[0:1])
    total = jnp.zeros_like(top)
    for one in stats:
        total = total + (one[1:2] + one[2:3] + one[3:4]) * jnp.exp(one[0:1] - top)
    log_norm = top + jnp.log(total)
    for i in range(group_tokens // BLK):
        rows = slice(i * BLK, (i + 1) * BLK)
        group = slice(i * BLK // tokens, (i + 1) * BLK // tokens)
        norm = jnp.broadcast_to(log_norm[:, rows], (BLK, BLK)).T
        terms = jnp.zeros((BLK, BLK), jnp.float32)
        for b in range(width // BLK):
            lanes = slice(b * BLK, (b + 1) * BLK)
            target = target_ref[group, :, lanes].reshape(BLK, BLK).astype(jnp.float32)
            log_probs = logits_ref[rows, lanes].astype(jnp.float32) - norm
            grad_ref[rows, lanes] = ((jnp.exp(log_probs) - target) * scale).astype(jnp.bfloat16)
            positive = target > 0
            one = target * (jnp.log(jnp.where(positive, target, 1.0)) - log_probs)
            terms = terms + jnp.where(positive, one, 0.0)
        row = jnp.sum(terms.T, axis=0, keepdims=True)
        for q in range(part_ref.shape[0]):
            part_ref[q, :, rows] = jnp.broadcast_to(row, (part_ref.shape[1], BLK))


def hidden_kernel(place_ref, *refs):
    pieces, (o_ref, s_ref) = refs[:-2], refs[-2:]
    count = len(pieces) // 2
    _, held, features = pieces[0].shape
    owners = s_ref.shape[0] // (2 * held)
    i = 0
    for own_ref, other_ref in zip(pieces[:count], pieces[count:]):
        for j in range(own_ref.shape[0]):
            offset = sum(((i >> bit) & 1) * (owners >> (bit + 1)) for bit in range(owners.bit_length() - 1))
            first = (place_ref[0] ^ offset) * 2
            own = pl.ds(pl.multiple_of((first + place_ref[1]) * held, held), held)
            other = pl.ds(pl.multiple_of((first + 1 - place_ref[1]) * held, held), held)
            s_ref[own, :] = own_ref[j].astype(jnp.float32)
            s_ref[other, :] = other_ref[j].astype(jnp.float32)
            i += 1
    for i in range(s_ref.shape[0] // BLK):
        for j in range(features // BLK):
            tile = s_ref[i * BLK : (i + 1) * BLK, j * BLK : (j + 1) * BLK].T
            o_ref[j * BLK : (j + 1) * BLK, i * BLK : (i + 1) * BLK] = tile.astype(jnp.bfloat16)


def join_kernel(place_ref, grad_ref, got_ref, o_ref, sem):
    half_tokens, width = got_ref.shape
    half = place_ref[1]
    kept_at = pl.ds(pl.multiple_of(half * width, width), width)
    got_at = pl.ds(pl.multiple_of((1 - half) * width, width), width)
    rows = pl.ds(pl.multiple_of(half * half_tokens, half_tokens), half_tokens)
    copies = [
        pltpu.make_async_copy(grad_ref.at[rows, :], o_ref.at[:, kept_at], sem.at[0]),
        pltpu.make_async_copy(got_ref, o_ref.at[:, got_at], sem.at[1]),
    ]
    for copy in copies:
        copy.start()
    for copy in copies:
        copy.wait()


def sum_kernel(place_ref, terms_ref, joined_ref, d_ref):
    half_tokens = d_ref.shape[1]
    total = terms_ref[0, 0:1, :]
    for q in range(1, terms_ref.shape[0]):
        total = total + terms_ref[q, 0:1, :]
    d_ref[...] = jnp.where(place_ref[1] == 0, total[:, :half_tokens], total[:, half_tokens:])


def weight_kernel(hidden_ref, grad_ref, o_ref, block_ref, sem):
    steps, tile, _ = block_ref.shape
    copies = []
    for i in range(steps):
        rows = slice(i * tile, (i + 1) * tile)
        block_ref[i] = jnp.dot(
            hidden_ref[rows, :], grad_ref[...], preferred_element_type=jnp.float32
        ).astype(jnp.bfloat16)
        copies.append(pltpu.make_async_copy(block_ref.at[i], o_ref.at[pl.ds(i * tile, tile), :], sem.at[i]))
        copies[-1].start()
    for copy in copies:
        copy.wait()


def whole():
    return pl.BlockSpec(memory_space=pltpu.VMEM)


def params():
    return pltpu.CompilerParams(vmem_limit_bytes=VMEM_LIMIT)


def scalars():
    return pl.BlockSpec(memory_space=pltpu.SMEM)


def anywhere():
    return pl.BlockSpec(memory_space=pl.ANY)


def to_partner(x, offset):
    return lax.ppermute(x, "sv", [(s, s ^ offset) for s in range(lax.axis_size("sv"))])


def body(teacher_probs, align_owner, align_local, align_weight, student_logits, hidden):
    owners = lax.axis_size("sv")
    halves = lax.axis_size("tv")
    half_index = lax.axis_index("tv")
    place = jnp.stack([lax.axis_index("sv"), half_index]).astype(jnp.int32)
    tokens = teacher_probs.shape[0]
    columns = student_logits.shape[1]
    blocks = columns // BLK
    mine = blocks // halves
    width = mine * BLK
    rows = owners * mine
    per_half = TB // halves
    group_tokens = owners * tokens
    half_tokens = student_logits.shape[0]
    features = hidden.shape[1]
    first = half_index == 0

    def in_order(own, other, axis):
        return jnp.concatenate([jnp.where(first, own, other), jnp.where(first, other, own)], axis=axis)

    teacher_other = swap_halves(teacher_probs)

    weights = jax.ShapeDtypeStruct((rows + MASS_ROWS, per_half), jnp.bfloat16)
    cuts = 4
    stats, w_own, w_rest, teacher_own = pl.pallas_call(
        prepare_kernel,
        out_shape=(
            jax.ShapeDtypeStruct((2, half_tokens), jnp.float32),
            weights,
            weights,
            jax.ShapeDtypeStruct(teacher_probs.shape, jnp.bfloat16),
        ),
        in_specs=[scalars()] + [whole()] * 3 + [anywhere()] * 2,
        out_specs=[whole()] * 4,
        scratch_shapes=[pltpu.VMEM(student_logits.shape, jnp.bfloat16), pltpu.SemaphoreType.DMA((2 * cuts,))],
        compiler_params=params(),
        cost_estimate=pl.CostEstimate(flops=0, bytes_accessed=0, transcendentals=0),
        name="prepare",
    )(place, align_owner.T, align_local.T, align_weight.T, student_logits, teacher_probs)
    stats = in_order(stats, swap_halves(stats), 1)
    spread = pltpu.VMEM((per_half * tokens, BLK), jnp.float32)
    part = pl.pallas_call(
        map_own_kernel,
        out_shape=jax.ShapeDtypeStruct((rows + MASS_ROWS, tokens * BLK), jnp.float32),
        in_specs=[whole()] * 2,
        out_specs=whole(),
        scratch_shapes=[spread],
        compiler_params=params(),
        cost_estimate=pl.CostEstimate(flops=0, bytes_accessed=0, transcendentals=0),
        name="map_own",
    )(w_own, teacher_own)
    chunk = (owners, tokens, width + group_tokens)
    outgoing = pl.pallas_call(
        map_rest_kernel,
        out_shape=jax.ShapeDtypeStruct(chunk, jnp.bfloat16),
        in_specs=[whole(), anywhere(), whole(), whole()],
        out_specs=anywhere(),
        scratch_shapes=[
            pltpu.VMEM((tokens, per_half * BLK), jnp.bfloat16),
            spread,
            pltpu.VMEM(((rows + 8) * tokens, BLK), jnp.float32),
            pltpu.VMEM(chunk, jnp.bfloat16),
            pltpu.SemaphoreType.DMA((cuts,)),
            pltpu.SemaphoreType.DMA((owners,)),
        ],
        compiler_params=params(),
        cost_estimate=pl.CostEstimate(
            flops=2 * (rows + MASS_ROWS) * per_half * tokens * BLK, bytes_accessed=4 << 20, transcendentals=0
        ),
        name="map_rest",
    )(w_rest, teacher_other, part, stats)
    target = lax.all_to_all(outgoing, "sv", 0, 0, tiled=True)

    hidden, give = pl.pallas_call(
        later_kernel,
        out_shape=(
            jax.ShapeDtypeStruct(hidden.shape, jnp.bfloat16),
            jax.ShapeDtypeStruct((half_tokens, width), jnp.bfloat16),
        ),
        in_specs=[scalars(), anywhere(), whole(), whole()],
        out_specs=(whole(), whole()),
        compiler_params=params(),
        cost_estimate=pl.CostEstimate(flops=0, bytes_accessed=48 << 20, transcendentals=0),
        name="later",
    )(place, outgoing, hidden, student_logits)

    keep = lax.dynamic_slice_in_dim(student_logits, half_index * width, width, 1)
    logits = in_order(keep, swap_halves(give), 0)

    pieces = [hidden[None]]
    offset = owners // 2
    while offset:
        pieces.append(to_partner(jnp.concatenate(pieces), offset))
        offset //= 2
    hidden_t = pl.pallas_call(
        hidden_kernel,
        out_shape=jax.ShapeDtypeStruct((features, group_tokens), jnp.bfloat16),
        in_specs=[scalars()] + [whole()] * (2 * len(pieces)),
        out_specs=whole(),
        scratch_shapes=[pltpu.VMEM((group_tokens, features), jnp.float32)],
        compiler_params=params(),
        cost_estimate=pl.CostEstimate(flops=0, bytes_accessed=4 * features * group_tokens, transcendentals=0),
        name="hidden_t",
    )(place, *pieces, *[swap_halves(piece) for piece in pieces])

    scale = float(columns * owners)
    grad, terms = pl.pallas_call(
        lambda *refs: grad_kernel(scale, *refs),
        out_shape=(
            jax.ShapeDtypeStruct((group_tokens, width), jnp.bfloat16),
            jax.ShapeDtypeStruct((owners * halves, 8, group_tokens), jnp.float32),
        ),
        in_specs=[whole()] * 2,
        out_specs=(whole(), whole()),
        compiler_params=params(),
        cost_estimate=pl.CostEstimate(
            flops=10 * group_tokens * width,
            bytes_accessed=6 * group_tokens * width,
            transcendentals=2 * group_tokens * width,
        ),
        name="logit_grad",
    )(target, logits)

    terms = lax.all_to_all(terms, ("sv", "tv"), 0, 0, tiled=True)
    give = lax.dynamic_slice_in_dim(grad, (1 - half_index) * half_tokens, half_tokens, 0)
    got = swap_halves(give)

    steps = 8
    weight_grad = pl.pallas_call(
        weight_kernel,
        out_shape=jax.ShapeDtypeStruct((features, width), jnp.bfloat16),
        in_specs=[whole()] * 2,
        out_specs=anywhere(),
        scratch_shapes=[
            pltpu.VMEM((steps, features // steps, width), jnp.bfloat16),
            pltpu.SemaphoreType.DMA((steps,)),
        ],
        compiler_params=params(),
        cost_estimate=pl.CostEstimate(
            flops=2 * features * group_tokens * width,
            bytes_accessed=2 * (features * width + group_tokens * (features + width)),
            transcendentals=0,
        ),
        name="weight_grad",
    )(hidden_t, grad)

    logit_grad = pl.pallas_call(
        join_kernel,
        out_shape=jax.ShapeDtypeStruct((half_tokens, columns), jnp.bfloat16),
        in_specs=[scalars(), anywhere(), anywhere()],
        out_specs=anywhere(),
        scratch_shapes=[pltpu.SemaphoreType.DMA((2,))],
        compiler_params=params(),
        cost_estimate=pl.CostEstimate(flops=0, bytes_accessed=4 * half_tokens * columns, transcendentals=0),
        name="join",
    )(place, grad, got)
    divergence = pl.pallas_call(
        sum_kernel,
        out_shape=jax.ShapeDtypeStruct((1, half_tokens), jnp.float32),
        in_specs=[scalars(), whole(), anywhere()],
        out_specs=whole(),
        compiler_params=params(),
        cost_estimate=pl.CostEstimate(flops=0, bytes_accessed=0, transcendentals=0),
        name="divergence",
    )(place, terms, logit_grad)
    return (divergence.reshape(half_tokens), logit_grad, weight_grad)


def solution(mesh):
    return jax.shard_map(
        body,
        mesh=mesh,
        in_specs=(
            P(("grp", "sv"), "tv"),
            P(),
            P(),
            P(),
            P(("grp", "tv"), "sv"),
            P(("grp", "sv", "tv"), None),
        ),
        out_specs=(P(("grp", "tv")), P(("grp", "tv"), "sv"), P(None, ("grp", "sv", "tv"))),
        check_vma=False,
    )
```

```python
import jax
import jax.numpy as jnp
from jax import lax
from jax.experimental import pallas as pl
from jax.experimental.pallas import tpu as pltpu
from jax.sharding import PartitionSpec as P

BLK = 128
TB = 640
TOPA = 2
MASS_ROWS = 16
VMEM_LIMIT = 48 * 1024 * 1024


def swap_halves(x):
    return lax.ppermute(x, "tv", [(0, 1), (1, 0)])


def block_weights(row_of, weight, rows):
    row_ids = lax.broadcasted_iota(jnp.int32, (rows + MASS_ROWS, row_of.shape[1]), 0)
    total = jnp.zeros(row_ids.shape, jnp.float32)
    for slot in range(row_of.shape[0]):
        hit = (row_ids == row_of[slot][None, :]) | (row_ids == rows + slot)
        total = total + jnp.where(hit, weight[slot].astype(jnp.float32)[None, :], 0.0)
    return total.astype(jnp.bfloat16)


def spread_tokens(t_ref, s_ref, start, count):
    tokens = t_ref.shape[0]
    step = 16

    def some(i, carry):
        for j in range(step):
            k = start + i * step + j
            tile = t_ref[:, pl.ds(pl.multiple_of(k * BLK, BLK), BLK)]
            s_ref[pl.ds(pl.multiple_of(k * tokens, tokens), tokens), :] = tile.astype(jnp.float32)
        return carry

    lax.fori_loop(0, count // step, some, 0)


def token_pair(s_ref, t, tokens):
    count = s_ref.shape[0] // tokens
    both = [s_ref[pl.ds(t + i, count, stride=tokens), :].astype(jnp.bfloat16) for i in range(2)]
    return jnp.concatenate(both, axis=1)


def map_own_kernel(w_ref, t_ref, o_ref, s_ref):
    tokens = t_ref.shape[0]
    spread_tokens(t_ref, s_ref, 0, t_ref.shape[1] // BLK)
    for t in range(0, tokens, 2):
        o_ref[:, t * BLK : (t + 2) * BLK] = jnp.dot(
            w_ref[...], token_pair(s_ref, t, tokens), preferred_element_type=jnp.float32
        )


def three_parts(x):
    parts = []
    for _ in range(3):
        parts.append(x.astype(jnp.bfloat16).astype(jnp.float32))
        x = x - parts[-1]
    return parts


def map_rest_kernel(w_ref, t_ref, p_ref, stats_ref, o_ref, t_buf, s_ref, m_ref, o_buf, in_sem, out_sem):
    tokens = t_ref.shape[0]
    owners = o_ref.shape[0]
    rows = w_ref.shape[0] - MASS_ROWS
    mine = rows // owners
    cuts = in_sem.shape[0]
    part = t_ref.shape[1] // cuts
    arriving = [
        pltpu.make_async_copy(
            t_ref.at[:, pl.ds(i * part, part)], t_buf.at[:, pl.ds(i * part, part)], in_sem.at[i]
        )
        for i in range(cuts)
    ]
    for copy in arriving:
        copy.start()
    stats = [stats_ref[0:1, :]] + three_parts(stats_ref[1:2, :])
    extra = jnp.zeros((tokens, stats_ref.shape[1]), jnp.float32)
    row_ids = lax.broadcasted_iota(jnp.int32, extra.shape, 0)
    for i, row in enumerate(stats):
        extra = jnp.where(row_ids == i, row, extra)
    extra = extra.astype(jnp.bfloat16)
    for i, copy in enumerate(arriving):
        copy.wait()
        spread_tokens(t_buf, s_ref, i * (part // BLK), part // BLK)
    for t in range(0, tokens, 2):
        both = p_ref[:, t * BLK : (t + 2) * BLK] + jnp.dot(
            w_ref[...], token_pair(s_ref, t, tokens), preferred_element_type=jnp.float32
        )
        for i in range(2):
            m_ref[pl.ds(t + i, rows + 8, stride=tokens), :] = both[: rows + 8, i * BLK : (i + 1) * BLK]
    mass = m_ref[rows * tokens : (rows + 1) * tokens, :]
    for slot in range(1, TOPA):
        mass = mass + m_ref[(rows + slot) * tokens : (rows + slot + 1) * tokens, :]
    inverse = jnp.broadcast_to(1.0 / jnp.sum(mass, axis=1, keepdims=True), (tokens, BLK))

    def leaving(q):
        return pltpu.make_async_copy(o_buf.at[q], o_ref.at[q], out_sem.at[q])

    def owner(q, carry):
        for b in range(mine):
            first = pl.multiple_of((q * mine + b) * tokens, tokens)
            tile = m_ref[pl.ds(first, tokens), :] * inverse
            o_buf[q, :, b * BLK : (b + 1) * BLK] = tile.astype(jnp.bfloat16)
        o_buf[q, :, mine * BLK :] = extra
        leaving(q).start()
        return carry

    def left(q, carry):
        leaving(q).wait()
        return carry

    lax.fori_loop(0, owners, owner, 0)
    lax.fori_loop(0, owners, left, 0)


def stats_kernel(place_ref, logits_ref, o_ref, give_ref):
    half_tokens, columns = logits_ref.shape
    width = give_ref.shape[1]
    for i in range(0, half_tokens, 64):
        rows = slice(i, i + 64)
        peak = logits_ref[rows, :BLK].astype(jnp.float32)
        for b in range(1, columns // BLK):
            peak = jnp.maximum(peak, logits_ref[rows, b * BLK : (b + 1) * BLK].astype(jnp.float32))
        peak = jnp.broadcast_to(jnp.max(peak, axis=1, keepdims=True), peak.shape)
        total = jnp.zeros_like(peak)
        for b in range(columns // BLK):
            total = total + jnp.exp(logits_ref[rows, b * BLK : (b + 1) * BLK].astype(jnp.float32) - peak)
        o_ref[0:1, rows] = peak.T[0:1]
        o_ref[1:2, rows] = jnp.sum(total.T, axis=0, keepdims=True)
    give_ref[...] = jnp.where(place_ref[1] == 0, logits_ref[:, width:], logits_ref[:, :width])


def later_kernel(sent_ref, hidden_ref, h_ref):
    h_ref[...] = hidden_ref[...]


def grad_kernel(scale, target_ref, logits_ref, grad_ref, part_ref, row_ref):
    owners, tokens, _ = target_ref.shape
    group_tokens, width = logits_ref.shape
    stats = [target_ref[q, :, width:].astype(jnp.float32) for q in range(owners)]
    top = stats[0][0:1]
    for one in stats[1:]:
        top = jnp.maximum(top, one[0:1])
    total = jnp.zeros_like(top)
    for one in stats:
        total = total + (one[1:2] + one[2:3] + one[3:4]) * jnp.exp(one[0:1] - top)
    log_norm = top + jnp.log(total)
    for i in range(group_tokens // BLK):
        rows = slice(i * BLK, (i + 1) * BLK)
        group = slice(i * BLK // tokens, (i + 1) * BLK // tokens)
        norm = jnp.broadcast_to(log_norm[:, rows], (BLK, BLK)).T
        terms = jnp.zeros((BLK, BLK), jnp.float32)
        for b in range(width // BLK):
            lanes = slice(b * BLK, (b + 1) * BLK)
            target = target_ref[group, :, lanes].reshape(BLK, BLK).astype(jnp.float32)
            log_probs = logits_ref[rows, lanes].astype(jnp.float32) - norm
            grad_ref[rows, lanes] = ((jnp.exp(log_probs) - target) * scale).astype(jnp.bfloat16)
            positive = target > 0
            one = target * (jnp.log(jnp.where(positive, target, 1.0)) - log_probs)
            terms = terms + jnp.where(positive, one, 0.0)
        row_ref[:, rows] = jnp.sum(terms.T, axis=0, keepdims=True)
    half_tokens = part_ref.shape[2]
    for half in range(group_tokens // half_tokens):
        row = row_ref[:, half * half_tokens : (half + 1) * half_tokens]
        for q in range(owners):
            part_ref[2 * q + half] = jnp.broadcast_to(row, part_ref.shape[1:])


def hidden_kernel(place_ref, *refs):
    pieces, (o_ref, s_ref) = refs[:-2], refs[-2:]
    count = len(pieces) // 2
    _, held, features = pieces[0].shape
    owners = s_ref.shape[0] // (2 * held)
    i = 0
    for own_ref, other_ref in zip(pieces[:count], pieces[count:]):
        for j in range(own_ref.shape[0]):
            offset = sum(((i >> bit) & 1) * (owners >> (bit + 1)) for bit in range(owners.bit_length() - 1))
            first = (place_ref[0] ^ offset) * 2
            own = pl.ds(pl.multiple_of((first + place_ref[1]) * held, held), held)
            other = pl.ds(pl.multiple_of((first + 1 - place_ref[1]) * held, held), held)
            s_ref[own, :] = own_ref[j].astype(jnp.float32)
            s_ref[other, :] = other_ref[j].astype(jnp.float32)
            i += 1
    for i in range(s_ref.shape[0] // BLK):
        for j in range(features // BLK):
            tile = s_ref[i * BLK : (i + 1) * BLK, j * BLK : (j + 1) * BLK].T
            o_ref[j * BLK : (j + 1) * BLK, i * BLK : (i + 1) * BLK] = tile.astype(jnp.bfloat16)


def join_kernel(place_ref, grad_ref, got_ref, o_ref, sem):
    half_tokens, width = got_ref.shape
    half = place_ref[1]
    kept_at = pl.ds(pl.multiple_of(half * width, width), width)
    got_at = pl.ds(pl.multiple_of((1 - half) * width, width), width)
    rows = pl.ds(pl.multiple_of(half * half_tokens, half_tokens), half_tokens)
    copies = [
        pltpu.make_async_copy(grad_ref.at[rows, :], o_ref.at[:, kept_at], sem.at[0]),
        pltpu.make_async_copy(got_ref, o_ref.at[:, got_at], sem.at[1]),
    ]
    for copy in copies:
        copy.start()
    for copy in copies:
        copy.wait()


def weight_kernel(hidden_ref, grad_ref, o_ref, block_ref, sem):
    steps, tile, _ = block_ref.shape
    copies = []
    for i in range(steps):
        rows = slice(i * tile, (i + 1) * tile)
        block_ref[i] = jnp.dot(
            hidden_ref[rows, :], grad_ref[...], preferred_element_type=jnp.float32
        ).astype(jnp.bfloat16)
        copies.append(pltpu.make_async_copy(block_ref.at[i], o_ref.at[pl.ds(i * tile, tile), :], sem.at[i]))
        copies[-1].start()
    for copy in copies:
        copy.wait()


def whole():
    return pl.BlockSpec(memory_space=pltpu.VMEM)


def params():
    return pltpu.CompilerParams(vmem_limit_bytes=VMEM_LIMIT)


def scalars():
    return pl.BlockSpec(memory_space=pltpu.SMEM)


def anywhere():
    return pl.BlockSpec(memory_space=pl.ANY)


def in_hbm():
    return pl.BlockSpec(memory_space=pltpu.HBM)


def to_partner(x, offset):
    return lax.ppermute(x, "sv", [(s, s ^ offset) for s in range(lax.axis_size("sv"))])


def body(teacher_probs, align_owner, align_local, align_weight, student_logits, hidden):
    owners = lax.axis_size("sv")
    halves = lax.axis_size("tv")
    half_index = lax.axis_index("tv")
    place = jnp.stack([lax.axis_index("sv"), half_index]).astype(jnp.int32)
    tokens = teacher_probs.shape[0]
    columns = student_logits.shape[1]
    blocks = columns // BLK
    mine = blocks // halves
    width = mine * BLK
    rows = owners * mine
    per_half = TB // halves
    group_tokens = owners * tokens
    half_tokens = student_logits.shape[0]
    features = hidden.shape[1]
    first = half_index == 0

    def in_order(own, other, axis):
        return jnp.concatenate([jnp.where(first, own, other), jnp.where(first, other, own)], axis=axis)

    teacher_other = swap_halves(teacher_probs)

    stats, give = pl.pallas_call(
        stats_kernel,
        out_shape=(
            jax.ShapeDtypeStruct((2, half_tokens), jnp.float32),
            jax.ShapeDtypeStruct((half_tokens, width), jnp.bfloat16),
        ),
        in_specs=[scalars(), whole()],
        out_specs=(whole(), whole()),
        compiler_params=params(),
        cost_estimate=pl.CostEstimate(flops=0, bytes_accessed=8 << 20, transcendentals=0),
        name="stats",
    )(place, student_logits)
    stats = in_order(stats, swap_halves(stats), 1)

    keep = lax.dynamic_slice_in_dim(student_logits, half_index * width, width, 1)
    logits = in_order(keep, swap_halves(give), 0)

    local = align_local.T - half_index * mine
    row_of = jnp.where((local >= 0) & (local < mine), align_owner.T * mine + local, -1)
    weight = align_weight.T
    cut = lambda x, which: lax.dynamic_slice_in_dim(x, which * per_half, per_half, 1)
    w_own = block_weights(cut(row_of, half_index), cut(weight, half_index), rows)
    w_rest = block_weights(cut(row_of, 1 - half_index), cut(weight, 1 - half_index), rows)
    spread = pltpu.VMEM((per_half * tokens, BLK), jnp.float32)
    part = pl.pallas_call(
        map_own_kernel,
        out_shape=jax.ShapeDtypeStruct((rows + MASS_ROWS, tokens * BLK), jnp.float32),
        in_specs=[whole()] * 2,
        out_specs=whole(),
        scratch_shapes=[spread],
        compiler_params=params(),
        cost_estimate=pl.CostEstimate(
            flops=2 * (rows + MASS_ROWS) * per_half * tokens * BLK, bytes_accessed=3 << 20, transcendentals=0
        ),
        name="map_own",
    )(w_own, teacher_probs)
    cuts = 4
    chunk = (owners, tokens, width + group_tokens)
    outgoing = pl.pallas_call(
        map_rest_kernel,
        out_shape=jax.ShapeDtypeStruct(chunk, jnp.bfloat16),
        in_specs=[whole(), anywhere(), whole(), whole()],
        out_specs=anywhere(),
        scratch_shapes=[
            pltpu.VMEM((tokens, per_half * BLK), jnp.bfloat16),
            spread,
            pltpu.VMEM(((rows + 8) * tokens, BLK), jnp.float32),
            pltpu.VMEM(chunk, jnp.bfloat16),
            pltpu.SemaphoreType.DMA((cuts,)),
            pltpu.SemaphoreType.DMA((owners,)),
        ],
        compiler_params=params(),
        cost_estimate=pl.CostEstimate(
            flops=2 * (rows + MASS_ROWS) * per_half * tokens * BLK, bytes_accessed=4 << 20, transcendentals=0
        ),
        name="map_rest",
    )(w_rest, teacher_other, part, stats)
    target = lax.all_to_all(outgoing, "sv", 0, 0, tiled=True)

    hidden = pl.pallas_call(
        later_kernel,
        out_shape=jax.ShapeDtypeStruct(hidden.shape, jnp.bfloat16),
        in_specs=[in_hbm(), whole()],
        out_specs=whole(),
        compiler_params=params(),
        cost_estimate=pl.CostEstimate(flops=0, bytes_accessed=0, transcendentals=0),
        name="later",
    )(outgoing, hidden)

    pieces = [hidden[None]]
    offset = owners // 2
    while offset:
        pieces.append(to_partner(jnp.concatenate(pieces), offset))
        offset //= 2
    hidden_t = pl.pallas_call(
        hidden_kernel,
        out_shape=jax.ShapeDtypeStruct((features, group_tokens), jnp.bfloat16),
        in_specs=[scalars()] + [whole()] * (2 * len(pieces)),
        out_specs=whole(),
        scratch_shapes=[pltpu.VMEM((group_tokens, features), jnp.float32)],
        compiler_params=params(),
        cost_estimate=pl.CostEstimate(flops=0, bytes_accessed=4 * features * group_tokens, transcendentals=0),
        name="hidden_t",
    )(place, *pieces, *[swap_halves(piece) for piece in pieces])

    scale = float(columns * owners)
    grad, terms = pl.pallas_call(
        lambda *refs: grad_kernel(scale, *refs),
        out_shape=(
            jax.ShapeDtypeStruct((group_tokens, width), jnp.bfloat16),
            jax.ShapeDtypeStruct((owners * halves, 8, half_tokens), jnp.float32),
        ),
        in_specs=[whole()] * 2,
        out_specs=(whole(), whole()),
        scratch_shapes=[pltpu.VMEM((1, group_tokens), jnp.float32)],
        compiler_params=params(),
        cost_estimate=pl.CostEstimate(
            flops=10 * group_tokens * width,
            bytes_accessed=6 * group_tokens * width,
            transcendentals=2 * group_tokens * width,
        ),
        name="logit_grad",
    )(target, logits)

    terms = lax.all_to_all(terms, ("sv", "tv"), 0, 0, tiled=True)
    give = lax.dynamic_slice_in_dim(grad, (1 - half_index) * half_tokens, half_tokens, 0)
    got = swap_halves(give)

    steps = 8
    weight_grad = pl.pallas_call(
        weight_kernel,
        out_shape=jax.ShapeDtypeStruct((features, width), jnp.bfloat16),
        in_specs=[whole()] * 2,
        out_specs=anywhere(),
        scratch_shapes=[
            pltpu.VMEM((steps, features // steps, width), jnp.bfloat16),
            pltpu.SemaphoreType.DMA((steps,)),
        ],
        compiler_params=params(),
        cost_estimate=pl.CostEstimate(
            flops=2 * features * group_tokens * width,
            bytes_accessed=2 * (features * width + group_tokens * (features + width)),
            transcendentals=0,
        ),
        name="weight_grad",
    )(hidden_t, grad)

    logit_grad = pl.pallas_call(
        join_kernel,
        out_shape=jax.ShapeDtypeStruct((half_tokens, columns), jnp.bfloat16),
        in_specs=[scalars(), anywhere(), anywhere()],
        out_specs=anywhere(),
        scratch_shapes=[pltpu.SemaphoreType.DMA((2,))],
        compiler_params=params(),
        cost_estimate=pl.CostEstimate(flops=0, bytes_accessed=4 * half_tokens * columns, transcendentals=0),
        name="join",
    )(place, grad, got)
    terms, logit_grad = lax.optimization_barrier((terms, logit_grad))
    divergence = jnp.sum(terms[:, 0], axis=0)
    return (divergence, logit_grad, weight_grad)


def solution(mesh):
    return jax.shard_map(
        body,
        mesh=mesh,
        in_specs=(
            P(("grp", "sv"), "tv"),
            P(),
            P(),
            P(),
            P(("grp", "tv"), "sv"),
            P(("grp", "sv", "tv"), None),
        ),
        out_specs=(P(("grp", "tv")), P(("grp", "tv"), "sv"), P(None, ("grp", "sv", "tv"))),
        check_vma=False,
    )
```

```python
import jax
import jax.numpy as jnp
from jax import lax
from jax.experimental import pallas as pl
from jax.experimental.pallas import tpu as pltpu
from jax.sharding import PartitionSpec as P

BLK = 128
TB = 640
TOPA = 2
MASS_ROWS = 16
STEP = 16


def block_weights(place_ref, owner_ref, local_ref, weight_ref, which, rows, mine):
    count = owner_ref.shape[1] // 2
    halved = lambda x: jnp.where(which == 0, x[:, :count], x[:, count:])
    local = local_ref[...] - place_ref[1] * mine
    inside = (local >= 0) & (local < mine)
    row_of = halved(jnp.where(inside, owner_ref[...] * mine + local, -1))
    weight = halved(weight_ref[...].astype(jnp.float32))
    row_ids = lax.broadcasted_iota(jnp.int32, (rows + MASS_ROWS, count), 0)
    total = jnp.zeros(row_ids.shape, jnp.float32)
    for slot in range(row_of.shape[0]):
        hit = (row_ids == row_of[slot : slot + 1]) | (row_ids == rows + slot)
        total = total + jnp.where(hit, weight[slot : slot + 1], 0.0)
    return total.astype(jnp.bfloat16)


def column_copies(source, target, sems, first=0):
    cuts = sems.shape[0] - first
    wide = source.shape[1] // cuts
    at = [pl.ds(i * wide, wide) for i in range(cuts)]
    return [pltpu.make_async_copy(source.at[:, at[i]], target.at[:, at[i]], sems.at[first + i]) for i in range(cuts)]


def spread_tokens(t_ref, s_ref, start, count):
    tokens = t_ref.shape[0]

    def some(i, carry):
        for j in range(STEP):
            k = start + i * STEP + j
            tile = t_ref[:, pl.ds(pl.multiple_of(k * BLK, BLK), BLK)]
            s_ref[pl.ds(pl.multiple_of(k * tokens, tokens), tokens), :] = tile.astype(jnp.float32)
        return carry

    lax.fori_loop(0, count // STEP, some, 0)


def spread_arriving(copies, t_buf, s_ref):
    blocks = t_buf.shape[1] // BLK // len(copies)
    for i, copy in enumerate(copies):
        copy.wait()
        spread_tokens(t_buf, s_ref, i * blocks, blocks)


def token_pair(s_ref, t, tokens):
    count = s_ref.shape[0] // tokens
    both = [s_ref[pl.ds(t + i, count, stride=tokens), :].astype(jnp.bfloat16) for i in range(2)]
    return jnp.concatenate(both, axis=1)


def stats_kernel(place_ref, logits_ref, o_ref, give_ref, l_buf, sems, give_sem):
    half_tokens, columns = logits_ref.shape
    width = give_ref.shape[1]
    arriving = column_copies(logits_ref, l_buf, sems)
    for copy in arriving:
        copy.start()
    for copy in arriving:
        copy.wait()
    given = pl.ds(pl.multiple_of((1 - place_ref[1]) * width, width), width)
    give = pltpu.make_async_copy(l_buf.at[:, given], give_ref, give_sem)
    give.start()
    for i in range(0, half_tokens, 64):
        rows = slice(i, i + 64)
        peak = l_buf[rows, :BLK].astype(jnp.float32)
        for b in range(1, columns // BLK):
            peak = jnp.maximum(peak, l_buf[rows, b * BLK : (b + 1) * BLK].astype(jnp.float32))
        peak = jnp.broadcast_to(jnp.max(peak, axis=1, keepdims=True), peak.shape)
        total = jnp.zeros_like(peak)
        for b in range(columns // BLK):
            total = total + jnp.exp(l_buf[rows, b * BLK : (b + 1) * BLK].astype(jnp.float32) - peak)
        o_ref[0:1, rows] = peak.T[0:1]
        o_ref[1:2, rows] = jnp.sum(total.T, axis=0, keepdims=True)
    give.wait()


def map_own_kernel(mine, place_ref, *refs):
    tables, (t_ref, rest_ref, o_ref), scratch = refs[:3], refs[3:6], refs[6:]
    held, (t_buf, s_ref, o_buf, table_sems, in_sems, out_sems) = scratch[:3], scratch[3:]
    tokens = t_ref.shape[0]
    rows = rest_ref.shape[0] - MASS_ROWS
    for_weights = [pltpu.make_async_copy(x, y, table_sems.at[i]) for i, (x, y) in enumerate(zip(tables, held))]
    arriving = column_copies(t_ref, t_buf, in_sems)
    for copy in for_weights + arriving:
        copy.start()
    for copy in for_weights:
        copy.wait()
    own = block_weights(place_ref, *held, place_ref[1], rows, mine)
    rest_ref[...] = block_weights(place_ref, *held, 1 - place_ref[1], rows, mine)
    spread_arriving(arriving, t_buf, s_ref)
    leaving = column_copies(o_buf, o_ref, out_sems)
    for i, copy in enumerate(leaving):
        o_buf[:, 2 * i * BLK : 2 * (i + 1) * BLK] = jnp.dot(
            own, token_pair(s_ref, 2 * i, tokens), preferred_element_type=jnp.float32
        )
        copy.start()
    for copy in leaving:
        copy.wait()


def three_parts(x):
    parts = []
    for _ in range(3):
        parts.append(x.astype(jnp.bfloat16).astype(jnp.float32))
        x = x - parts[-1]
    return parts


def riding_tile(hidden, stats, lanes):
    held, features = hidden.shape
    wide = stats.shape[1]
    rows = [stats[0:1]] + three_parts(stats[1:2])
    corner = jnp.concatenate(rows + [jnp.zeros((held - len(rows), wide), jnp.float32)], axis=0)
    rest = features - lanes
    gap = lanes - rest - wide
    parts = [hidden[:, lanes:]] + ([jnp.zeros((held, gap), jnp.float32)] if gap else []) + [corner]
    return jnp.concatenate([hidden[:, :lanes], jnp.concatenate(parts, axis=1)], axis=0)


def map_rest_kernel(
    w_ref, t_ref, p_ref, stats_ref, hidden_ref, o_ref,
    w_buf, t_buf, p_buf, stats_buf, hidden_buf, s_ref, m_ref, o_buf, sems, in_sems, p_sems, out_sems,
):
    tokens = t_ref.shape[0]
    owners, _, chunk = o_ref.shape
    rows = w_ref.shape[0] - MASS_ROWS
    mine = rows // owners
    width = mine * BLK
    arriving = column_copies(t_ref, t_buf, in_sems)
    partial = column_copies(p_ref, p_buf, p_sems)
    small = [
        pltpu.make_async_copy(x, y, sems.at[i])
        for i, (x, y) in enumerate([(w_ref, w_buf), (stats_ref, stats_buf), (hidden_ref, hidden_buf)])
    ]
    for copy in arriving + small + partial:
        copy.start()
    spread_arriving(arriving, t_buf, s_ref)
    for copy in small:
        copy.wait()
    for i, copy in enumerate(partial):
        copy.wait()
        t = 2 * i
        both = p_buf[:, t * BLK : (t + 2) * BLK] + jnp.dot(
            w_buf[...], token_pair(s_ref, t, tokens), preferred_element_type=jnp.float32
        )
        for j in range(2):
            m_ref[pl.ds(t + j, rows + 8, stride=tokens), :] = both[: rows + 8, j * BLK : (j + 1) * BLK]
    mass = m_ref[rows * tokens : (rows + 1) * tokens, :]
    for slot in range(1, TOPA):
        mass = mass + m_ref[(rows + slot) * tokens : (rows + slot + 1) * tokens, :]
    inverse = jnp.broadcast_to(1.0 / jnp.sum(mass, axis=1, keepdims=True), (tokens, BLK))
    riding = riding_tile(hidden_buf[...].astype(jnp.float32), stats_buf[...], chunk - width).astype(jnp.bfloat16)

    def leaving(q):
        return pltpu.make_async_copy(o_buf.at[q], o_ref.at[q], out_sems.at[q])

    def owner(q, carry):
        for b in range(mine):
            first = pl.multiple_of((q * mine + b) * tokens, tokens)
            tile = m_ref[pl.ds(first, tokens), :] * inverse
            o_buf[q, :, b * BLK : (b + 1) * BLK] = tile.astype(jnp.bfloat16)
        o_buf[q, :, width:] = riding
        leaving(q).start()
        return carry

    def left(q, carry):
        leaving(q).wait()
        return carry

    lax.fori_loop(0, owners, owner, 0)
    lax.fori_loop(0, owners, left, 0)


def grad_kernel(scale, target_ref, logits_ref, grad_ref, terms_ref, hidden_ref, row_ref):
    owners, tokens, chunk = target_ref.shape
    group_tokens, width = logits_ref.shape
    stats = [target_ref[q, :, chunk - group_tokens :].astype(jnp.float32)[8:] for q in range(owners)]
    top = stats[0][0:1]
    for one in stats[1:]:
        top = jnp.maximum(top, one[0:1])
    total = jnp.zeros_like(top)
    for one in stats:
        total = total + (one[1:2] + one[2:3] + one[3:4]) * jnp.exp(one[0:1] - top)
    log_norm = top + jnp.log(total)
    for q in range(owners):
        hidden_ref[q] = target_ref[q, :, width:]
    for i in range(group_tokens // BLK):
        rows = slice(i * BLK, (i + 1) * BLK)
        group = slice(i * BLK // tokens, (i + 1) * BLK // tokens)
        norm = jnp.broadcast_to(log_norm[:, rows], (BLK, BLK)).T
        terms = jnp.zeros((BLK, BLK), jnp.float32)
        for b in range(width // BLK):
            lanes = slice(b * BLK, (b + 1) * BLK)
            target = target_ref[group, :, lanes].reshape(BLK, BLK).astype(jnp.float32)
            log_probs = logits_ref[rows, lanes].astype(jnp.float32) - norm
            grad_ref[rows, lanes] = ((jnp.exp(log_probs) - target) * scale).astype(jnp.bfloat16)
            positive = target > 0
            one = target * (jnp.log(jnp.where(positive, target, 1.0)) - log_probs)
            terms = terms + jnp.where(positive, one, 0.0)
        row_ref[:, rows] = jnp.sum(terms.T, axis=0, keepdims=True)
    half_tokens = group_tokens // 2
    for half in range(2):
        row = row_ref[:, half * half_tokens : (half + 1) * half_tokens]
        tile = jnp.concatenate([row] * (terms_ref.shape[2] // half_tokens), axis=1)
        for q in range(owners):
            terms_ref[2 * q + half] = jnp.broadcast_to(tile, terms_ref.shape[1:])


def join_kernel(place_ref, grad_ref, got_ref, o_ref, sem):
    half_tokens, width = got_ref.shape
    half = place_ref[1]
    kept_at = pl.ds(pl.multiple_of(half * width, width), width)
    got_at = pl.ds(pl.multiple_of((1 - half) * width, width), width)
    rows = pl.ds(pl.multiple_of(half * half_tokens, half_tokens), half_tokens)
    copies = [
        pltpu.make_async_copy(grad_ref.at[rows, :], o_ref.at[:, kept_at], sem.at[0]),
        pltpu.make_async_copy(got_ref, o_ref.at[:, got_at], sem.at[1]),
    ]
    for copy in copies:
        copy.start()
    for copy in copies:
        copy.wait()


def weight_kernel(place_ref, own_ref, other_ref, grad_ref, o_ref, s_ref, h_ref, block_ref, sem):
    owners, tokens, lanes = own_ref.shape
    held = tokens // 2
    features = s_ref.shape[1]
    for q in range(owners):
        for ref, half in ((own_ref, place_ref[1]), (other_ref, 1 - place_ref[1])):
            rows = pl.ds(pl.multiple_of((2 * q + half) * held, held), held)
            tile = ref[q].astype(jnp.float32)
            s_ref[rows, :lanes] = tile[:held]
            s_ref[rows, lanes:] = tile[held:, : features - lanes]
    for i in range(s_ref.shape[0] // BLK):
        for j in range(features // BLK):
            tile = s_ref[i * BLK : (i + 1) * BLK, j * BLK : (j + 1) * BLK].T
            h_ref[j * BLK : (j + 1) * BLK, i * BLK : (i + 1) * BLK] = tile.astype(jnp.bfloat16)
    steps, tile, _ = block_ref.shape
    copies = []
    for i in range(steps):
        rows = slice(i * tile, (i + 1) * tile)
        block_ref[i] = jnp.dot(
            h_ref[rows, :], grad_ref[...], preferred_element_type=jnp.float32
        ).astype(jnp.bfloat16)
        copies.append(pltpu.make_async_copy(block_ref.at[i], o_ref.at[pl.ds(i * tile, tile), :], sem.at[i]))
        copies[-1].start()
    for copy in copies:
        copy.wait()


def in_vmem():
    return pl.BlockSpec(memory_space=pltpu.VMEM)


def scalars():
    return pl.BlockSpec(memory_space=pltpu.SMEM)


def anywhere():
    return pl.BlockSpec(memory_space=pl.ANY)


def params(mib=48):
    return pltpu.CompilerParams(vmem_limit_bytes=mib << 20)


def cost(flops=0, bytes_accessed=0, transcendentals=0):
    return pl.CostEstimate(flops=flops, bytes_accessed=bytes_accessed, transcendentals=transcendentals)


def swap_halves(x):
    return lax.ppermute(x, "tv", [(0, 1), (1, 0)])


def body(teacher_probs, align_owner, align_local, align_weight, student_logits, hidden):
    owners = lax.axis_size("sv")
    halves = lax.axis_size("tv")
    half_index = lax.axis_index("tv")
    place = jnp.stack([lax.axis_index("sv"), half_index]).astype(jnp.int32)
    tokens = teacher_probs.shape[0]
    columns = student_logits.shape[1]
    blocks = columns // BLK
    mine = blocks // halves
    width = mine * BLK
    rows = owners * mine
    per_half = TB // halves
    group_tokens = owners * tokens
    half_tokens = student_logits.shape[0]
    features = hidden.shape[1]
    first = half_index == 0
    bf16, f32 = jnp.bfloat16, jnp.float32
    shape = jax.ShapeDtypeStruct
    dma = lambda count: pltpu.SemaphoreType.DMA((count,))

    def in_order(own, other, axis):
        return jnp.concatenate([jnp.where(first, own, other), jnp.where(first, other, own)], axis=axis)

    teacher_other = swap_halves(teacher_probs)

    cuts = 4
    stats, give = pl.pallas_call(
        stats_kernel,
        out_shape=(shape((2, half_tokens), f32), shape((half_tokens, width), bf16)),
        in_specs=[scalars(), anywhere()],
        out_specs=(in_vmem(), anywhere()),
        scratch_shapes=[pltpu.VMEM(student_logits.shape, bf16), dma(cuts), pltpu.SemaphoreType.DMA],
        compiler_params=params(60),
        cost_estimate=cost(),
        name="stats",
    )(place, student_logits)
    stats = in_order(stats, swap_halves(stats), 1)

    keep = lax.dynamic_slice_in_dim(student_logits, half_index * width, width, 1)
    logits = in_order(keep, swap_halves(give), 0)

    pairs = tokens // 2
    weights = shape((rows + MASS_ROWS, per_half), bf16)
    partial = shape((rows + MASS_ROWS, tokens * BLK), f32)
    spread = pltpu.VMEM((per_half * tokens, BLK), f32)
    teacher = pltpu.VMEM((tokens, per_half * BLK), bf16)
    tables = [align_owner.T, align_local.T, align_weight.T]
    w_rest, part = pl.pallas_call(
        lambda *refs: map_own_kernel(mine, *refs),
        out_shape=(weights, partial),
        in_specs=[scalars()] + [anywhere()] * 4,
        out_specs=(in_vmem(), anywhere()),
        scratch_shapes=[
            *[pltpu.VMEM(x.shape, x.dtype) for x in tables],
            teacher,
            spread,
            pltpu.VMEM(partial.shape, f32),
            dma(len(tables)),
            dma(cuts),
            dma(pairs),
        ],
        compiler_params=params(60),
        cost_estimate=cost(),
        name="map_own",
    )(place, *tables, teacher_probs)
    riding = -(-(features + group_tokens) // (2 * BLK)) * BLK
    chunk = (owners, tokens, width + riding)
    outgoing = pl.pallas_call(
        map_rest_kernel,
        out_shape=shape(chunk, bf16),
        in_specs=[anywhere()] * 5,
        out_specs=anywhere(),
        scratch_shapes=[
            pltpu.VMEM(weights.shape, bf16),
            teacher,
            pltpu.VMEM(partial.shape, f32),
            pltpu.VMEM(stats.shape, f32),
            pltpu.VMEM(hidden.shape, bf16),
            spread,
            pltpu.VMEM(((rows + 8) * tokens, BLK), f32),
            pltpu.VMEM(chunk, bf16),
            dma(3),
            dma(cuts),
            dma(pairs),
            dma(owners),
        ],
        compiler_params=params(48),
        cost_estimate=cost(2 * (rows + MASS_ROWS) * per_half * tokens * BLK, 4 << 20),
        name="map_rest",
    )(w_rest, teacher_other, part, stats, hidden)
    target = lax.all_to_all(outgoing, "sv", 0, 0, tiled=True)

    scale = float(columns * owners)
    lanes = -(-half_tokens // BLK) * BLK
    grad, terms, hidden_own = pl.pallas_call(
        lambda *refs: grad_kernel(scale, *refs),
        out_shape=(
            shape((group_tokens, width), bf16),
            shape((owners * halves, 8, lanes), f32),
            shape((owners, tokens, riding), bf16),
        ),
        in_specs=[in_vmem()] * 2,
        out_specs=[in_vmem()] * 3,
        scratch_shapes=[pltpu.VMEM((1, group_tokens), f32)],
        compiler_params=params(),
        cost_estimate=cost(
            10 * group_tokens * width, 6 * group_tokens * width, 2 * group_tokens * width
        ),
        name="logit_grad",
    )(target, logits)

    terms = lax.all_to_all(terms, ("sv", "tv"), 0, 0, tiled=True)
    give = lax.dynamic_slice_in_dim(grad, (1 - half_index) * half_tokens, half_tokens, 0)
    got = swap_halves(give)

    steps = 8
    weight_grad = pl.pallas_call(
        weight_kernel,
        out_shape=shape((features, width), bf16),
        in_specs=[scalars()] + [in_vmem()] * 3,
        out_specs=anywhere(),
        scratch_shapes=[
            pltpu.VMEM((group_tokens, features), f32),
            pltpu.VMEM((features, group_tokens), bf16),
            pltpu.VMEM((steps, features // steps, width), bf16),
            dma(steps),
        ],
        compiler_params=params(),
        cost_estimate=cost(
            2 * features * group_tokens * width,
            2 * (features * width + group_tokens * (features + width)),
        ),
        name="weight_grad",
    )(place, hidden_own, swap_halves(hidden_own), grad)

    logit_grad = pl.pallas_call(
        join_kernel,
        out_shape=shape((half_tokens, columns), bf16),
        in_specs=[scalars(), anywhere(), anywhere()],
        out_specs=anywhere(),
        scratch_shapes=[dma(2)],
        compiler_params=params(),
        cost_estimate=cost(0, 4 * half_tokens * columns),
        name="join",
    )(place, grad, got)
    terms, logit_grad = lax.optimization_barrier((terms, logit_grad))
    divergence = jnp.sum(terms[:, 0, :half_tokens], axis=0)
    return (divergence, logit_grad, weight_grad)


def solution(mesh):
    return jax.shard_map(
        body,
        mesh=mesh,
        in_specs=(
            P(("grp", "sv"), "tv"),
            P(),
            P(),
            P(),
            P(("grp", "tv"), "sv"),
            P(("grp", "sv", "tv"), None),
        ),
        out_specs=(P(("grp", "tv")), P(("grp", "tv"), "sv"), P(None, ("grp", "sv", "tv"))),
        check_vma=False,
    )
```

```python
import jax
import jax.numpy as jnp
from jax import lax
from jax.experimental import pallas as pl
from jax.experimental.pallas import tpu as pltpu
from jax.sharding import PartitionSpec as P

BLK = 128
TB = 640
TOPA = 2
MASS_ROWS = 16
STEP = 16


def block_weights(row_of, weight, rows):
    row_ids = lax.broadcasted_iota(jnp.int32, (rows + MASS_ROWS, row_of.shape[1]), 0)
    total = jnp.zeros(row_ids.shape, jnp.float32)
    for slot in range(row_of.shape[0]):
        hit = (row_ids == row_of[slot][None, :]) | (row_ids == rows + slot)
        total = total + jnp.where(hit, weight[slot].astype(jnp.float32)[None, :], 0.0)
    return total.astype(jnp.bfloat16)


def column_copies(source, target, sems, first=0):
    cuts = sems.shape[0] - first
    wide = source.shape[1] // cuts
    at = [pl.ds(i * wide, wide) for i in range(cuts)]
    return [pltpu.make_async_copy(source.at[:, at[i]], target.at[:, at[i]], sems.at[first + i]) for i in range(cuts)]


def spread_tokens(t_ref, s_ref, start, count):
    tokens = t_ref.shape[0]

    def some(i, carry):
        for j in range(STEP):
            k = start + i * STEP + j
            tile = t_ref[:, pl.ds(pl.multiple_of(k * BLK, BLK), BLK)]
            s_ref[pl.ds(pl.multiple_of(k * tokens, tokens), tokens), :] = tile.astype(jnp.float32)
        return carry

    lax.fori_loop(0, count // STEP, some, 0)


def spread_arriving(copies, t_buf, s_ref):
    blocks = t_buf.shape[1] // BLK // len(copies)
    for i, copy in enumerate(copies):
        copy.wait()
        spread_tokens(t_buf, s_ref, i * blocks, blocks)


def token_pair(s_ref, t, tokens):
    count = s_ref.shape[0] // tokens
    both = [s_ref[pl.ds(t + i, count, stride=tokens), :].astype(jnp.bfloat16) for i in range(2)]
    return jnp.concatenate(both, axis=1)


def map_own_kernel(w_ref, t_ref, first_ref, o_ref, s_ref):
    tokens = t_ref.shape[0]
    spread_tokens(t_ref, s_ref, 0, t_ref.shape[1] // BLK)
    for t in range(0, tokens, 2):
        o_ref[:, t * BLK : (t + 2) * BLK] = jnp.dot(
            w_ref[...], token_pair(s_ref, t, tokens), preferred_element_type=jnp.float32
        )


def three_parts(x):
    parts = []
    for _ in range(3):
        parts.append(x.astype(jnp.bfloat16).astype(jnp.float32))
        x = x - parts[-1]
    return parts


def map_rest_kernel(w_ref, t_ref, p_ref, stats_ref, o_ref, t_buf, s_ref, m_ref, o_buf, in_sem, out_sem):
    tokens = t_ref.shape[0]
    owners = o_ref.shape[0]
    rows = w_ref.shape[0] - MASS_ROWS
    mine = rows // owners
    arriving = column_copies(t_ref, t_buf, in_sem)
    for copy in arriving:
        copy.start()
    stats = [stats_ref[0:1, :]] + three_parts(stats_ref[1:2, :])
    extra = jnp.zeros((tokens, stats_ref.shape[1]), jnp.float32)
    row_ids = lax.broadcasted_iota(jnp.int32, extra.shape, 0)
    for i, row in enumerate(stats):
        extra = jnp.where(row_ids == i, row, extra)
    extra = extra.astype(jnp.bfloat16)
    spread_arriving(arriving, t_buf, s_ref)
    for t in range(0, tokens, 2):
        both = p_ref[:, t * BLK : (t + 2) * BLK] + jnp.dot(
            w_ref[...], token_pair(s_ref, t, tokens), preferred_element_type=jnp.float32
        )
        for i in range(2):
            m_ref[pl.ds(t + i, rows + 8, stride=tokens), :] = both[: rows + 8, i * BLK : (i + 1) * BLK]
    mass = m_ref[rows * tokens : (rows + 1) * tokens, :]
    for slot in range(1, TOPA):
        mass = mass + m_ref[(rows + slot) * tokens : (rows + slot + 1) * tokens, :]
    inverse = jnp.broadcast_to(1.0 / jnp.sum(mass, axis=1, keepdims=True), (tokens, BLK))

    def leaving(q):
        return pltpu.make_async_copy(o_buf.at[q], o_ref.at[q], out_sem.at[q])

    def owner(q, carry):
        for b in range(mine):
            first = pl.multiple_of((q * mine + b) * tokens, tokens)
            tile = m_ref[pl.ds(first, tokens), :] * inverse
            o_buf[q, :, b * BLK : (b + 1) * BLK] = tile.astype(jnp.bfloat16)
        o_buf[q, :, mine * BLK :] = extra
        leaving(q).start()
        return carry

    def left(q, carry):
        leaving(q).wait()
        return carry

    lax.fori_loop(0, owners, owner, 0)
    lax.fori_loop(0, owners, left, 0)


def grad_kernel(scale, target_ref, logits_ref, grad_ref, terms_ref, row_ref):
    owners, tokens, _ = target_ref.shape
    group_tokens, width = logits_ref.shape
    stats = [target_ref[q, :, width:].astype(jnp.float32) for q in range(owners)]
    top = stats[0][0:1]
    for one in stats[1:]:
        top = jnp.maximum(top, one[0:1])
    total = jnp.zeros_like(top)
    for one in stats:
        total = total + (one[1:2] + one[2:3] + one[3:4]) * jnp.exp(one[0:1] - top)
    log_norm = top + jnp.log(total)
    for i in range(group_tokens // BLK):
        rows = slice(i * BLK, (i + 1) * BLK)
        group = slice(i * BLK // tokens, (i + 1) * BLK // tokens)
        norm = jnp.broadcast_to(log_norm[:, rows], (BLK, BLK)).T
        terms = jnp.zeros((BLK, BLK), jnp.float32)
        for b in range(width // BLK):
            lanes = slice(b * BLK, (b + 1) * BLK)
            target = target_ref[group, :, lanes].reshape(BLK, BLK).astype(jnp.float32)
            log_probs = logits_ref[rows, lanes].astype(jnp.float32) - norm
            grad_ref[rows, lanes] = ((jnp.exp(log_probs) - target) * scale).astype(jnp.bfloat16)
            positive = target > 0
            one = target * (jnp.log(jnp.where(positive, target, 1.0)) - log_probs)
            terms = terms + jnp.where(positive, one, 0.0)
        row_ref[:, rows] = jnp.sum(terms.T, axis=0, keepdims=True)
    half_tokens = group_tokens // 2
    for half in range(2):
        row = row_ref[:, half * half_tokens : (half + 1) * half_tokens]
        tile = jnp.concatenate([row] * (terms_ref.shape[2] // half_tokens), axis=1)
        for q in range(owners):
            terms_ref[2 * q + half] = jnp.broadcast_to(tile, terms_ref.shape[1:])


def join_kernel(place_ref, grad_ref, got_ref, o_ref, sem):
    half_tokens, width = got_ref.shape
    half = place_ref[1]
    kept_at = pl.ds(pl.multiple_of(half * width, width), width)
    got_at = pl.ds(pl.multiple_of((1 - half) * width, width), width)
    rows = pl.ds(pl.multiple_of(half * half_tokens, half_tokens), half_tokens)
    copies = [
        pltpu.make_async_copy(grad_ref.at[rows, :], o_ref.at[:, kept_at], sem.at[0]),
        pltpu.make_async_copy(got_ref, o_ref.at[:, got_at], sem.at[1]),
    ]
    for copy in copies:
        copy.start()
    for copy in copies:
        copy.wait()


def weight_kernel(place_ref, *refs):
    pieces, (grad_ref, o_ref, s_ref, h_ref, block_ref, sem) = refs[:-6], refs[-6:]
    count = len(pieces) // 2
    _, held, features = pieces[0].shape
    owners = s_ref.shape[0] // (2 * held)
    i = 0
    for own_ref, other_ref in zip(pieces[:count], pieces[count:]):
        for j in range(own_ref.shape[0]):
            offset = sum(((i >> bit) & 1) * (owners >> (bit + 1)) for bit in range(owners.bit_length() - 1))
            first = (place_ref[0] ^ offset) * 2
            own = pl.ds(pl.multiple_of((first + place_ref[1]) * held, held), held)
            other = pl.ds(pl.multiple_of((first + 1 - place_ref[1]) * held, held), held)
            s_ref[own, :] = own_ref[j].astype(jnp.float32)
            s_ref[other, :] = other_ref[j].astype(jnp.float32)
            i += 1
    for i in range(s_ref.shape[0] // BLK):
        for j in range(features // BLK):
            tile = s_ref[i * BLK : (i + 1) * BLK, j * BLK : (j + 1) * BLK].T
            h_ref[j * BLK : (j + 1) * BLK, i * BLK : (i + 1) * BLK] = tile.astype(jnp.bfloat16)
    steps, tile, _ = block_ref.shape
    copies = []
    for i in range(steps):
        rows = slice(i * tile, (i + 1) * tile)
        block_ref[i] = jnp.dot(
            h_ref[rows, :], grad_ref[...], preferred_element_type=jnp.float32
        ).astype(jnp.bfloat16)
        copies.append(pltpu.make_async_copy(block_ref.at[i], o_ref.at[pl.ds(i * tile, tile), :], sem.at[i]))
        copies[-1].start()
    for copy in copies:
        copy.wait()


def in_vmem():
    return pl.BlockSpec(memory_space=pltpu.VMEM)


def scalars():
    return pl.BlockSpec(memory_space=pltpu.SMEM)


def anywhere():
    return pl.BlockSpec(memory_space=pl.ANY)


def params(mib=48):
    return pltpu.CompilerParams(vmem_limit_bytes=mib << 20)


def cost(flops=0, bytes_accessed=0, transcendentals=0):
    return pl.CostEstimate(flops=flops, bytes_accessed=bytes_accessed, transcendentals=transcendentals)


def swap_halves(x):
    return lax.ppermute(x, "tv", [(0, 1), (1, 0)])


def to_partner(x, offset):
    return lax.ppermute(x, "sv", [(s, s ^ offset) for s in range(lax.axis_size("sv"))])


def body(teacher_probs, align_owner, align_local, align_weight, student_logits, hidden):
    owners = lax.axis_size("sv")
    halves = lax.axis_size("tv")
    half_index = lax.axis_index("tv")
    place = jnp.stack([lax.axis_index("sv"), half_index]).astype(jnp.int32)
    tokens = teacher_probs.shape[0]
    columns = student_logits.shape[1]
    blocks = columns // BLK
    mine = blocks // halves
    width = mine * BLK
    rows = owners * mine
    per_half = TB // halves
    group_tokens = owners * tokens
    half_tokens = student_logits.shape[0]
    features = hidden.shape[1]
    first = half_index == 0
    bf16, f32 = jnp.bfloat16, jnp.float32
    shape = jax.ShapeDtypeStruct
    dma = lambda count: pltpu.SemaphoreType.DMA((count,))

    def in_order(own, other, axis):
        return jnp.concatenate([jnp.where(first, own, other), jnp.where(first, other, own)], axis=axis)

    teacher_other = swap_halves(teacher_probs)

    hidden = hidden[None]
    offset = owners // 2
    first_piece = to_partner(hidden, offset)

    wide = student_logits.astype(f32)
    peak = jnp.max(wide, axis=1)
    sums = jnp.sum(jnp.exp(wide - peak[:, None]), axis=1)
    stats = jnp.stack([peak, sums])
    stats = in_order(stats, swap_halves(stats), 1)

    local = align_local.T - half_index * mine
    row_of = jnp.where((local >= 0) & (local < mine), align_owner.T * mine + local, -1)
    weight = align_weight.T
    cut = lambda x, which: lax.dynamic_slice_in_dim(x, which * per_half, per_half, 1)
    w_own = block_weights(cut(row_of, half_index), cut(weight, half_index), rows)
    w_rest = block_weights(cut(row_of, 1 - half_index), cut(weight, 1 - half_index), rows)
    spread = pltpu.VMEM((per_half * tokens, BLK), f32)
    flops = 2 * (rows + MASS_ROWS) * per_half * tokens * BLK
    part = pl.pallas_call(
        map_own_kernel,
        out_shape=shape((rows + MASS_ROWS, tokens * BLK), f32),
        in_specs=[in_vmem(), in_vmem(), anywhere()],
        out_specs=in_vmem(),
        scratch_shapes=[spread],
        compiler_params=params(),
        cost_estimate=cost(flops, 3 << 20),
        name="map_own",
    )(w_own, teacher_probs, first_piece)
    cuts = 4
    chunk = (owners, tokens, width + group_tokens)
    outgoing = pl.pallas_call(
        map_rest_kernel,
        out_shape=shape(chunk, bf16),
        in_specs=[in_vmem(), anywhere(), in_vmem(), in_vmem()],
        out_specs=anywhere(),
        scratch_shapes=[
            pltpu.VMEM((tokens, per_half * BLK), bf16),
            spread,
            pltpu.VMEM(((rows + 8) * tokens, BLK), f32),
            pltpu.VMEM(chunk, bf16),
            dma(cuts),
            dma(owners),
        ],
        compiler_params=params(),
        cost_estimate=cost(flops, 4 << 20),
        name="map_rest",
    )(w_rest, teacher_other, part, stats)
    target = lax.all_to_all(outgoing, "sv", 0, 0, tiled=True)

    hidden, late_logits, outgoing = lax.optimization_barrier((hidden, student_logits, outgoing))

    keep = lax.dynamic_slice_in_dim(late_logits, half_index * width, width, 1)
    give = lax.dynamic_slice_in_dim(late_logits, (1 - half_index) * width, width, 1)
    logits = in_order(keep, swap_halves(give), 0)

    pieces = [hidden, first_piece]
    while offset > 1:
        offset //= 2
        pieces.append(to_partner(jnp.concatenate(pieces), offset))

    scale = float(columns * owners)
    lanes = -(-half_tokens // BLK) * BLK
    grad, terms = pl.pallas_call(
        lambda *refs: grad_kernel(scale, *refs),
        out_shape=(
            shape((group_tokens, width), bf16),
            shape((owners * halves, 8, lanes), f32),
        ),
        in_specs=[in_vmem()] * 2,
        out_specs=[in_vmem()] * 2,
        scratch_shapes=[pltpu.VMEM((1, group_tokens), f32)],
        compiler_params=params(),
        cost_estimate=cost(
            10 * group_tokens * width, 6 * group_tokens * width, 2 * group_tokens * width
        ),
        name="logit_grad",
    )(target, logits)

    terms = lax.all_to_all(terms, ("sv", "tv"), 0, 0, tiled=True)
    give = lax.dynamic_slice_in_dim(grad, (1 - half_index) * half_tokens, half_tokens, 0)
    got = swap_halves(give)

    steps = 8
    weight_grad = pl.pallas_call(
        weight_kernel,
        out_shape=shape((features, width), bf16),
        in_specs=[scalars()] + [in_vmem()] * (2 * len(pieces) + 1),
        out_specs=anywhere(),
        scratch_shapes=[
            pltpu.VMEM((group_tokens, features), f32),
            pltpu.VMEM((features, group_tokens), bf16),
            pltpu.VMEM((steps, features // steps, width), bf16),
            dma(steps),
        ],
        compiler_params=params(),
        cost_estimate=cost(
            2 * features * group_tokens * width,
            2 * (features * width + group_tokens * (features + width)),
        ),
        name="weight_grad",
    )(place, *pieces, *[swap_halves(piece) for piece in pieces], grad)

    logit_grad = pl.pallas_call(
        join_kernel,
        out_shape=shape((half_tokens, columns), bf16),
        in_specs=[scalars(), anywhere(), anywhere()],
        out_specs=anywhere(),
        scratch_shapes=[dma(2)],
        compiler_params=params(),
        cost_estimate=cost(0, 4 * half_tokens * columns),
        name="join",
    )(place, grad, got)
    terms, logit_grad, weight_grad = lax.optimization_barrier((terms, logit_grad, weight_grad))
    divergence = jnp.sum(terms[:, 0, :half_tokens], axis=0)
    return (divergence, logit_grad, weight_grad)


def solution(mesh):
    return jax.shard_map(
        body,
        mesh=mesh,
        in_specs=(
            P(("grp", "sv"), "tv"),
            P(),
            P(),
            P(),
            P(("grp", "tv"), "sv"),
            P(("grp", "sv", "tv"), None),
        ),
        out_specs=(P(("grp", "tv")), P(("grp", "tv"), "sv"), P(None, ("grp", "sv", "tv"))),
        check_vma=False,
    )
```

```python
import jax
import jax.numpy as jnp
from jax import lax
from jax.experimental import pallas as pl
from jax.experimental.pallas import tpu as pltpu
from jax.sharding import PartitionSpec as P

BLK = 128
TB = 640
TOPA = 2
MASS_ROWS = 16
STEP = 16


def block_weights(place_ref, table_ref, which, rows, mine):
    count = table_ref.shape[1] // 2
    table = jnp.where(which == 0, table_ref[:, :count], table_ref[:, count:])
    owner, local, weight = (table[i * TOPA : (i + 1) * TOPA] for i in range(3))
    local = local.astype(jnp.int32) - place_ref[1] * mine
    row_of = jnp.where((local >= 0) & (local < mine), owner.astype(jnp.int32) * mine + local, -1)
    row_ids = lax.broadcasted_iota(jnp.int32, (rows + MASS_ROWS, count), 0)
    total = jnp.zeros(row_ids.shape, jnp.float32)
    for slot in range(TOPA):
        hit = (row_ids == row_of[slot : slot + 1]) | (row_ids == rows + slot)
        total = total + jnp.where(hit, weight[slot : slot + 1], 0.0)
    return total.astype(jnp.bfloat16)


def column_copies(source, target, sems, first=0):
    cuts = sems.shape[0] - first
    wide = source.shape[1] // cuts
    at = [pl.ds(i * wide, wide) for i in range(cuts)]
    return [pltpu.make_async_copy(source.at[:, at[i]], target.at[:, at[i]], sems.at[first + i]) for i in range(cuts)]


def spread_tokens(t_ref, s_ref, start, count):
    tokens = t_ref.shape[0]

    def some(i, carry):
        for j in range(STEP):
            k = start + i * STEP + j
            tile = t_ref[:, pl.ds(pl.multiple_of(k * BLK, BLK), BLK)]
            s_ref[pl.ds(pl.multiple_of(k * tokens, tokens), tokens), :] = tile.astype(jnp.float32)
        return carry

    lax.fori_loop(0, count // STEP, some, 0)


def spread_arriving(copies, t_buf, s_ref):
    blocks = t_buf.shape[1] // BLK // len(copies)
    for i, copy in enumerate(copies):
        copy.wait()
        spread_tokens(t_buf, s_ref, i * blocks, blocks)


def token_pair(s_ref, t, tokens):
    count = s_ref.shape[0] // tokens
    both = [s_ref[pl.ds(t + i, count, stride=tokens), :].astype(jnp.bfloat16) for i in range(2)]
    return jnp.concatenate(both, axis=1)


def map_own_kernel(mine, place_ref, table_ref, t_ref, first_ref, o_ref, s_ref):
    tokens = t_ref.shape[0]
    weights = block_weights(place_ref, table_ref, place_ref[1], o_ref.shape[0] - MASS_ROWS, mine)
    spread_tokens(t_ref, s_ref, 0, t_ref.shape[1] // BLK)
    for t in range(0, tokens, 2):
        o_ref[:, t * BLK : (t + 2) * BLK] = jnp.dot(
            weights, token_pair(s_ref, t, tokens), preferred_element_type=jnp.float32
        )


def three_parts(x):
    parts = []
    for _ in range(3):
        parts.append(x.astype(jnp.bfloat16).astype(jnp.float32))
        x = x - parts[-1]
    return parts


def map_rest_kernel(mine, place_ref, table_ref, t_ref, p_ref, stats_ref, *refs):
    o_refs, (t_buf, s_ref, m_ref, in_sem) = refs[:-4], refs[-4:]
    tokens = t_ref.shape[0]
    rows = p_ref.shape[0] - MASS_ROWS
    arriving = column_copies(t_ref, t_buf, in_sem)
    for copy in arriving:
        copy.start()
    weights = block_weights(place_ref, table_ref, 1 - place_ref[1], rows, mine)
    stats = [stats_ref[0:1, :]] + three_parts(stats_ref[1:2, :])
    extra = jnp.zeros((tokens, stats_ref.shape[1]), jnp.float32)
    row_ids = lax.broadcasted_iota(jnp.int32, extra.shape, 0)
    for i, row in enumerate(stats):
        extra = jnp.where(row_ids == i, row, extra)
    extra = extra.astype(jnp.bfloat16)
    spread_arriving(arriving, t_buf, s_ref)
    for t in range(0, tokens, 2):
        both = p_ref[:, t * BLK : (t + 2) * BLK] + jnp.dot(
            weights, token_pair(s_ref, t, tokens), preferred_element_type=jnp.float32
        )
        for i in range(2):
            m_ref[pl.ds(t + i, rows + 8, stride=tokens), :] = both[: rows + 8, i * BLK : (i + 1) * BLK]
    mass = m_ref[rows * tokens : (rows + 1) * tokens, :]
    for slot in range(1, TOPA):
        mass = mass + m_ref[(rows + slot) * tokens : (rows + slot + 1) * tokens, :]
    inverse = jnp.broadcast_to(1.0 / jnp.sum(mass, axis=1, keepdims=True), (tokens, BLK))
    for offset, o_ref in enumerate(o_refs):
        owner = place_ref[0] ^ offset
        for b in range(mine):
            first = pl.multiple_of((owner * mine + b) * tokens, tokens)
            tile = m_ref[pl.ds(first, tokens), :] * inverse
            o_ref[:, b * BLK : (b + 1) * BLK] = tile.astype(jnp.bfloat16)
        o_ref[:, mine * BLK :] = extra


def grad_kernel(scale, place_ref, logits_ref, *refs):
    target_refs, (grad_ref, terms_ref, norm_ref, sum_ref, t_buf, sem) = refs[:-6], refs[-6:]
    tokens = target_refs[0].shape[0]
    group_tokens, width = logits_ref.shape
    stats = [ref[:, width:].astype(jnp.float32) for ref in target_refs]
    top = stats[0][0:1]
    for one in stats[1:]:
        top = jnp.maximum(top, one[0:1])
    total = jnp.zeros_like(top)
    for one in stats:
        total = total + (one[1:2] + one[2:3] + one[3:4]) * jnp.exp(one[0:1] - top)
    log_norm = top + jnp.log(total)
    for i in range(0, group_tokens, BLK):
        norm_ref[i : i + BLK, :] = jnp.broadcast_to(log_norm[:, i : i + BLK], (BLK, BLK)).T
    per = BLK // tokens
    at = [pl.ds(pl.multiple_of((place_ref[0] ^ a) * tokens, tokens), tokens) for a in range(len(target_refs))]

    def block(i, b):
        lanes = slice(b * BLK, (b + 1) * BLK)
        some = range(i * per, (i + 1) * per)
        target = jnp.concatenate([target_refs[a][:, lanes] for a in some], axis=0).astype(jnp.float32)
        logits = jnp.concatenate([logits_ref[at[a], lanes] for a in some], axis=0).astype(jnp.float32)
        return target, logits

    norms = []
    for i in range(group_tokens // BLK):
        norms.append(jnp.concatenate([norm_ref[at[a], :] for a in range(i * per, (i + 1) * per)], axis=0))
        terms = jnp.zeros((BLK, BLK), jnp.float32)
        for b in range(width // BLK):
            target, logits = block(i, b)
            positive = target > 0
            one = target * (jnp.log(jnp.where(positive, target, 1.0)) - (logits - norms[i]))
            terms = terms + jnp.where(positive, one, 0.0)
        for j in range(per):
            sum_ref[at[i * per + j], :] = terms[j * tokens : (j + 1) * tokens]
    owners, half_tokens = len(target_refs), group_tokens // 2
    row = jnp.concatenate(
        [jnp.sum(sum_ref[i : i + BLK, :].T, axis=0, keepdims=True) for i in range(0, group_tokens, BLK)], axis=1
    )
    for half in range(2):
        mine = row[:, half * half_tokens : (half + 1) * half_tokens]
        tile = jnp.concatenate([mine] * (t_buf.shape[2] // half_tokens), axis=1)
        for q in range(owners):
            t_buf[2 * q + half] = jnp.broadcast_to(tile, t_buf.shape[1:])
    leaving = pltpu.make_async_copy(t_buf, terms_ref, sem)
    leaving.start()
    for i in range(group_tokens // BLK):
        for b in range(width // BLK):
            target, logits = block(i, b)
            grad = (jnp.exp(logits - norms[i]) - target) * scale
            grad_ref[i * BLK : (i + 1) * BLK, b * BLK : (b + 1) * BLK] = grad.astype(jnp.bfloat16)
    leaving.wait()


def join_kernel(place_ref, grad_ref, got_ref, o_ref, sem):
    half_tokens, width = got_ref.shape
    count = sem.shape[0] // 2
    tokens = half_tokens // count
    owner, half = place_ref[0], place_ref[1]
    kept_at = pl.ds(pl.multiple_of(half * width, width), width)
    got_at = pl.ds(pl.multiple_of((1 - half) * width, width), width)
    kept = ((owner // count) ^ half) * half_tokens
    copies = []
    for j in range(count):
        to = pl.ds(pl.multiple_of(((owner % count) ^ j) * tokens, tokens), tokens)
        here = pl.ds(pl.multiple_of(kept + j * tokens, tokens), tokens)
        there = pl.ds(j * tokens, tokens)
        copies.append(pltpu.make_async_copy(grad_ref.at[here, :], o_ref.at[to, kept_at], sem.at[2 * j]))
        copies.append(pltpu.make_async_copy(got_ref.at[there, :], o_ref.at[to, got_at], sem.at[2 * j + 1]))
    for copy in copies:
        copy.start()
    for copy in copies:
        copy.wait()


def arrival_order(owners):
    bits = owners.bit_length() - 1
    return [sum(((i >> bit) & 1) * (owners >> (bit + 1)) for bit in range(bits)) for i in range(owners)]


def weight_kernel(place_ref, own_ref, other_ref, grad_ref, o_ref, s_ref, h_ref, block_ref, sem):
    owners, held, features = own_ref.shape
    for i, offset in enumerate(arrival_order(owners)):
        own = pl.ds(pl.multiple_of((offset * 2 + place_ref[1]) * held, held), held)
        other = pl.ds(pl.multiple_of((offset * 2 + 1 - place_ref[1]) * held, held), held)
        s_ref[own, :] = own_ref[i].astype(jnp.float32)
        s_ref[other, :] = other_ref[i].astype(jnp.float32)
    for i in range(s_ref.shape[0] // BLK):
        for j in range(features // BLK):
            tile = s_ref[i * BLK : (i + 1) * BLK, j * BLK : (j + 1) * BLK].T
            h_ref[j * BLK : (j + 1) * BLK, i * BLK : (i + 1) * BLK] = tile.astype(jnp.bfloat16)
    steps, tile, _ = block_ref.shape
    copies = []
    for i in range(steps):
        rows = slice(i * tile, (i + 1) * tile)
        block_ref[i] = jnp.dot(
            h_ref[rows, :], grad_ref[...], preferred_element_type=jnp.float32
        ).astype(jnp.bfloat16)
        copies.append(pltpu.make_async_copy(block_ref.at[i], o_ref.at[pl.ds(i * tile, tile), :], sem.at[i]))
        copies[-1].start()
    for copy in copies:
        copy.wait()


def in_vmem():
    return pl.BlockSpec(memory_space=pltpu.VMEM)


def scalars():
    return pl.BlockSpec(memory_space=pltpu.SMEM)


def anywhere():
    return pl.BlockSpec(memory_space=pl.ANY)


def params(mib=48):
    return pltpu.CompilerParams(vmem_limit_bytes=mib << 20)


def cost(flops=0, bytes_accessed=0, transcendentals=0):
    return pl.CostEstimate(flops=flops, bytes_accessed=bytes_accessed, transcendentals=transcendentals)


def swap_halves(x):
    return lax.ppermute(x, "tv", [(0, 1), (1, 0)])


def to_partner(x, offset):
    return lax.ppermute(x, "sv", [(s, s ^ offset) for s in range(lax.axis_size("sv"))])


def body(teacher_probs, align_owner, align_local, align_weight, student_logits, hidden):
    owners = lax.axis_size("sv")
    halves = lax.axis_size("tv")
    half_index = lax.axis_index("tv")
    place = jnp.stack([lax.axis_index("sv"), half_index]).astype(jnp.int32)
    tokens = teacher_probs.shape[0]
    columns = student_logits.shape[1]
    blocks = columns // BLK
    mine = blocks // halves
    width = mine * BLK
    rows = owners * mine
    per_half = TB // halves
    group_tokens = owners * tokens
    half_tokens = student_logits.shape[0]
    features = hidden.shape[1]
    first = half_index == 0
    bf16, f32 = jnp.bfloat16, jnp.float32
    shape = jax.ShapeDtypeStruct
    dma = lambda count: pltpu.SemaphoreType.DMA((count,))

    def in_order(own, other, axis):
        return jnp.concatenate([jnp.where(first, own, other), jnp.where(first, other, own)], axis=axis)

    teacher_other = swap_halves(teacher_probs)

    hidden = hidden[None]
    offset = owners // 2
    first_piece = to_partner(hidden, offset)

    def merge(one, two):
        top = jnp.maximum(one[0], two[0])
        return top, one[1] * jnp.exp(one[0] - top) + two[1] * jnp.exp(two[0] - top)

    wide = student_logits.astype(f32)
    low = jnp.float32(-1e38)
    stats = jnp.stack(lax.reduce((wide, jnp.ones_like(wide)), (low, jnp.float32(0)), merge, (1,)))
    stats = in_order(stats, swap_halves(stats), 1)

    tables = jnp.concatenate([x.T.astype(f32) for x in (align_owner, align_local, align_weight)])
    spread = pltpu.VMEM((per_half * tokens, BLK), f32)
    flops = 2 * (rows + MASS_ROWS) * per_half * tokens * BLK
    part = pl.pallas_call(
        lambda *refs: map_own_kernel(mine, *refs),
        out_shape=shape((rows + MASS_ROWS, tokens * BLK), f32),
        in_specs=[scalars(), in_vmem(), in_vmem(), anywhere()],
        out_specs=in_vmem(),
        scratch_shapes=[spread],
        compiler_params=params(),
        cost_estimate=cost(flops, 3 << 20),
        name="map_own",
    )(place, tables, teacher_probs, first_piece)
    cuts = 4
    outgoing = pl.pallas_call(
        lambda *refs: map_rest_kernel(mine, *refs),
        out_shape=[shape((tokens, width + group_tokens), bf16)] * owners,
        in_specs=[scalars(), in_vmem(), anywhere(), in_vmem(), in_vmem()],
        out_specs=[in_vmem()] * owners,
        scratch_shapes=[
            pltpu.VMEM((tokens, per_half * BLK), bf16),
            spread,
            pltpu.VMEM(((rows + 8) * tokens, BLK), f32),
            dma(cuts),
        ],
        compiler_params=params(),
        cost_estimate=cost(flops, 4 << 20),
        name="map_rest",
    )(place, tables, teacher_other, part, stats)
    targets = dict(enumerate(outgoing))
    for a in [*range(owners // 2, owners), *range(1, owners // 2)]:
        targets[a] = to_partner(outgoing[a], a)

    late_logits, _ = lax.optimization_barrier((student_logits, outgoing[0]))
    hidden, _ = lax.optimization_barrier((hidden, targets[owners // 2]))

    keep = lax.dynamic_slice_in_dim(late_logits, half_index * width, width, 1)
    give = lax.dynamic_slice_in_dim(late_logits, (1 - half_index) * width, width, 1)
    logits = in_order(keep, swap_halves(give), 0)

    hidden_own = jnp.concatenate([hidden, first_piece])
    while offset > 1:
        offset //= 2
        hidden_own = jnp.concatenate([hidden_own, to_partner(hidden_own, offset)])

    scale = float(columns * owners)
    lanes = -(-half_tokens // BLK) * BLK
    grad, terms = pl.pallas_call(
        lambda *refs: grad_kernel(scale, *refs),
        out_shape=(shape((group_tokens, width), bf16), shape((owners * halves, 8, lanes), f32)),
        in_specs=[scalars()] + [in_vmem()] * (owners + 1),
        out_specs=(in_vmem(), anywhere()),
        scratch_shapes=[
            pltpu.VMEM((group_tokens, BLK), f32),
            pltpu.VMEM((group_tokens, BLK), f32),
            pltpu.VMEM((owners * halves, 8, lanes), f32),
            pltpu.SemaphoreType.DMA,
        ],
        compiler_params=params(),
        cost_estimate=cost(
            10 * group_tokens * width, 6 * group_tokens * width, 2 * group_tokens * width
        ),
        name="logit_grad",
    )(place, logits, *[targets[a] for a in range(owners)])

    terms = lax.all_to_all(terms, ("sv", "tv"), 0, 0, tiled=True)
    count = half_tokens // tokens
    given = (lax.axis_index("sv") // count) ^ (1 - half_index)
    give = lax.dynamic_slice_in_dim(grad, given * half_tokens, half_tokens, 0)
    got = swap_halves(give)

    steps = 8
    weight_grad = pl.pallas_call(
        weight_kernel,
        out_shape=shape((features, width), bf16),
        in_specs=[scalars()] + [in_vmem()] * 3,
        out_specs=anywhere(),
        scratch_shapes=[
            pltpu.VMEM((group_tokens, features), f32),
            pltpu.VMEM((features, group_tokens), bf16),
            pltpu.VMEM((steps, features // steps, width), bf16),
            dma(steps),
        ],
        compiler_params=params(),
        cost_estimate=cost(
            2 * features * group_tokens * width,
            2 * (features * width + group_tokens * (features + width)),
        ),
        name="weight_grad",
    )(place, hidden_own, swap_halves(hidden_own), grad)

    logit_grad = pl.pallas_call(
        join_kernel,
        out_shape=shape((half_tokens, columns), bf16),
        in_specs=[scalars(), anywhere(), anywhere()],
        out_specs=anywhere(),
        scratch_shapes=[dma(2 * count)],
        compiler_params=params(),
        cost_estimate=cost(0, 4 * half_tokens * columns),
        name="join",
    )(place, grad, got)
    terms, logit_grad, weight_grad = lax.optimization_barrier((terms, logit_grad, weight_grad))
    divergence = jnp.sum(terms[:, 0, :half_tokens], axis=0)
    return (divergence, logit_grad, weight_grad)


def solution(mesh):
    return jax.shard_map(
        body,
        mesh=mesh,
        in_specs=(
            P(("grp", "sv"), "tv"),
            P(),
            P(),
            P(),
            P(("grp", "tv"), "sv"),
            P(("grp", "sv", "tv"), None),
        ),
        out_specs=(P(("grp", "tv")), P(("grp", "tv"), "sv"), P(None, ("grp", "sv", "tv"))),
        check_vma=False,
    )
```

```python
import jax
import jax.numpy as jnp
from jax import lax
from jax.experimental import pallas as pl
from jax.experimental.pallas import tpu as pltpu
from jax.sharding import PartitionSpec as P

BLK = 128
TB = 640
TOPA = 2
MASS_ROWS = 16
STEP = 16


def block_weights(row_of, weight, rows):
    row_ids = lax.broadcasted_iota(jnp.int32, (rows + MASS_ROWS, row_of.shape[1]), 0)
    total = jnp.zeros(row_ids.shape, jnp.float32)
    for slot in range(row_of.shape[0]):
        hit = (row_ids == row_of[slot][None, :]) | (row_ids == rows + slot)
        total = total + jnp.where(hit, weight[slot][None, :], 0.0)
    return total.astype(jnp.bfloat16)


def column_copies(source, target, sems, first=0):
    cuts = sems.shape[0] - first
    wide = source.shape[1] // cuts
    at = [pl.ds(i * wide, wide) for i in range(cuts)]
    return [pltpu.make_async_copy(source.at[:, at[i]], target.at[:, at[i]], sems.at[first + i]) for i in range(cuts)]


def spread_tokens(t_ref, s_ref, start, count):
    tokens = t_ref.shape[0]

    def some(i, carry):
        for j in range(STEP):
            k = start + i * STEP + j
            tile = t_ref[:, pl.ds(pl.multiple_of(k * BLK, BLK), BLK)]
            s_ref[pl.ds(pl.multiple_of(k * tokens, tokens), tokens), :] = tile.astype(jnp.float32)
        return carry

    lax.fori_loop(0, count // STEP, some, 0)


def spread_arriving(copies, t_buf, s_ref):
    blocks = t_buf.shape[1] // BLK // len(copies)
    for i, copy in enumerate(copies):
        copy.wait()
        spread_tokens(t_buf, s_ref, i * blocks, blocks)


def token_pair(s_ref, t, tokens):
    count = s_ref.shape[0] // tokens
    both = [s_ref[pl.ds(t + i, count, stride=tokens), :].astype(jnp.bfloat16) for i in range(2)]
    return jnp.concatenate(both, axis=1)


def map_own_kernel(w_ref, t_ref, first_ref, o_ref, s_ref):
    tokens = t_ref.shape[0]
    spread_tokens(t_ref, s_ref, 0, t_ref.shape[1] // BLK)
    for t in range(0, tokens, 2):
        o_ref[:, t * BLK : (t + 2) * BLK] = jnp.dot(
            w_ref[...], token_pair(s_ref, t, tokens), preferred_element_type=jnp.float32
        )


def three_parts(x):
    parts = []
    for _ in range(3):
        parts.append(x.astype(jnp.bfloat16).astype(jnp.float32))
        x = x - parts[-1]
    return parts


def map_rest_kernel(w_ref, t_ref, p_ref, stats_ref, o_ref, t_buf, s_ref, m_ref, o_buf, in_sem, out_sem):
    tokens = t_ref.shape[0]
    owners = o_ref.shape[0]
    rows = w_ref.shape[0] - MASS_ROWS
    mine = rows // owners
    arriving = column_copies(t_ref, t_buf, in_sem)
    for copy in arriving:
        copy.start()
    stats = [stats_ref[0:1, :]] + three_parts(stats_ref[1:2, :])
    extra = jnp.zeros((tokens, stats_ref.shape[1]), jnp.float32)
    row_ids = lax.broadcasted_iota(jnp.int32, extra.shape, 0)
    for i, row in enumerate(stats):
        extra = jnp.where(row_ids == i, row, extra)
    extra = extra.astype(jnp.bfloat16)
    spread_arriving(arriving, t_buf, s_ref)
    for t in range(0, tokens, 2):
        both = p_ref[:, t * BLK : (t + 2) * BLK] + jnp.dot(
            w_ref[...], token_pair(s_ref, t, tokens), preferred_element_type=jnp.float32
        )
        for i in range(2):
            m_ref[pl.ds(t + i, rows + 8, stride=tokens), :] = both[: rows + 8, i * BLK : (i + 1) * BLK]
    mass = m_ref[rows * tokens : (rows + 1) * tokens, :]
    for slot in range(1, TOPA):
        mass = mass + m_ref[(rows + slot) * tokens : (rows + slot + 1) * tokens, :]
    inverse = jnp.broadcast_to(1.0 / jnp.sum(mass, axis=1, keepdims=True), (tokens, BLK))

    def leaving(q):
        return pltpu.make_async_copy(o_buf.at[q], o_ref.at[q], out_sem.at[q])

    def owner(q, carry):
        for b in range(mine):
            first = pl.multiple_of((q * mine + b) * tokens, tokens)
            tile = m_ref[pl.ds(first, tokens), :] * inverse
            o_buf[q, :, b * BLK : (b + 1) * BLK] = tile.astype(jnp.bfloat16)
        o_buf[q, :, mine * BLK :] = extra
        leaving(q).start()
        return carry

    def left(q, carry):
        leaving(q).wait()
        return carry

    lax.fori_loop(0, owners, owner, 0)
    lax.fori_loop(0, owners, left, 0)


def grad_kernel(scale, target_ref, logits_ref, grad_ref, terms_ref, norm_ref, t_buf, sem):
    owners, tokens, _ = target_ref.shape
    group_tokens, width = logits_ref.shape
    stats = [target_ref[q, :, width:].astype(jnp.float32) for q in range(owners)]
    top = stats[0][0:1]
    for one in stats[1:]:
        top = jnp.maximum(top, one[0:1])
    total = jnp.zeros_like(top)
    for one in stats:
        total = total + (one[1:2] + one[2:3] + one[3:4]) * jnp.exp(one[0:1] - top)
    log_norm = top + jnp.log(total)

    def block(i, b):
        lanes = slice(b * BLK, (b + 1) * BLK)
        group = slice(i * BLK // tokens, (i + 1) * BLK // tokens)
        target = target_ref[group, :, lanes].reshape(BLK, BLK).astype(jnp.float32)
        return target, logits_ref[i * BLK : (i + 1) * BLK, lanes].astype(jnp.float32)

    sums = []
    for i in range(group_tokens // BLK):
        rows = slice(i * BLK, (i + 1) * BLK)
        norm = jnp.broadcast_to(log_norm[:, rows], (BLK, BLK)).T
        norm_ref[rows, :] = norm
        terms = jnp.zeros((BLK, BLK), jnp.float32)
        for b in range(width // BLK):
            target, logits = block(i, b)
            positive = target > 0
            one = target * (jnp.log(jnp.where(positive, target, 1.0)) - (logits - norm))
            terms = terms + jnp.where(positive, one, 0.0)
        sums.append(jnp.sum(terms.T, axis=0, keepdims=True))
    row = jnp.concatenate(sums, axis=1)
    half_tokens = group_tokens // 2
    for half in range(2):
        mine = row[:, half * half_tokens : (half + 1) * half_tokens]
        tile = jnp.concatenate([mine] * (t_buf.shape[2] // half_tokens), axis=1)
        for q in range(owners):
            t_buf[2 * q + half] = jnp.broadcast_to(tile, t_buf.shape[1:])
    leaving = pltpu.make_async_copy(t_buf, terms_ref, sem)
    leaving.start()
    for i in range(group_tokens // BLK):
        rows = slice(i * BLK, (i + 1) * BLK)
        for b in range(width // BLK):
            target, logits = block(i, b)
            grad = (jnp.exp(logits - norm_ref[rows, :]) - target) * scale
            grad_ref[rows, b * BLK : (b + 1) * BLK] = grad.astype(jnp.bfloat16)
    leaving.wait()


def join_kernel(place_ref, grad_ref, got_ref, o_ref, sem):
    half_tokens, width = got_ref.shape
    half = place_ref[1]
    kept_at = pl.ds(pl.multiple_of(half * width, width), width)
    got_at = pl.ds(pl.multiple_of((1 - half) * width, width), width)
    rows = pl.ds(pl.multiple_of(half * half_tokens, half_tokens), half_tokens)
    copies = [
        pltpu.make_async_copy(grad_ref.at[rows, :], o_ref.at[:, kept_at], sem.at[0]),
        pltpu.make_async_copy(got_ref, o_ref.at[:, got_at], sem.at[1]),
    ]
    for copy in copies:
        copy.start()
    for copy in copies:
        copy.wait()


def arrival_order(owners):
    bits = owners.bit_length() - 1
    return [sum(((i >> bit) & 1) * (owners >> (bit + 1)) for bit in range(bits)) for i in range(owners)]


def weight_kernel(place_ref, own_ref, other_ref, grad_ref, o_ref, s_ref, h_ref, block_ref, sem):
    owners, held, features = own_ref.shape
    for i, offset in enumerate(arrival_order(owners)):
        first = (place_ref[0] ^ offset) * 2
        own = pl.ds(pl.multiple_of((first + place_ref[1]) * held, held), held)
        other = pl.ds(pl.multiple_of((first + 1 - place_ref[1]) * held, held), held)
        s_ref[own, :] = own_ref[i].astype(jnp.float32)
        s_ref[other, :] = other_ref[i].astype(jnp.float32)
    for i in range(s_ref.shape[0] // BLK):
        for j in range(features // BLK):
            tile = s_ref[i * BLK : (i + 1) * BLK, j * BLK : (j + 1) * BLK].T
            h_ref[j * BLK : (j + 1) * BLK, i * BLK : (i + 1) * BLK] = tile.astype(jnp.bfloat16)
    steps, tile, _ = block_ref.shape
    copies = []
    for i in range(steps):
        rows = slice(i * tile, (i + 1) * tile)
        block_ref[i] = jnp.dot(
            h_ref[rows, :], grad_ref[...], preferred_element_type=jnp.float32
        ).astype(jnp.bfloat16)
        copies.append(pltpu.make_async_copy(block_ref.at[i], o_ref.at[pl.ds(i * tile, tile), :], sem.at[i]))
        copies[-1].start()
    for copy in copies:
        copy.wait()


def in_vmem():
    return pl.BlockSpec(memory_space=pltpu.VMEM)


def scalars():
    return pl.BlockSpec(memory_space=pltpu.SMEM)


def anywhere():
    return pl.BlockSpec(memory_space=pl.ANY)


def params(mib=48):
    return pltpu.CompilerParams(vmem_limit_bytes=mib << 20)


def cost(flops=0, bytes_accessed=0, transcendentals=0):
    return pl.CostEstimate(flops=flops, bytes_accessed=bytes_accessed, transcendentals=transcendentals)


def swap_halves(x):
    return lax.ppermute(x, "tv", [(0, 1), (1, 0)])


def to_partner(x, offset):
    return lax.ppermute(x, "sv", [(s, s ^ offset) for s in range(lax.axis_size("sv"))])


def body(teacher_probs, align_owner, align_local, align_weight, student_logits, hidden):
    owners = lax.axis_size("sv")
    halves = lax.axis_size("tv")
    half_index = lax.axis_index("tv")
    place = jnp.stack([lax.axis_index("sv"), half_index]).astype(jnp.int32)
    tokens = teacher_probs.shape[0]
    columns = student_logits.shape[1]
    blocks = columns // BLK
    mine = blocks // halves
    width = mine * BLK
    rows = owners * mine
    per_half = TB // halves
    group_tokens = owners * tokens
    half_tokens = student_logits.shape[0]
    features = hidden.shape[1]
    first = half_index == 0
    bf16, f32 = jnp.bfloat16, jnp.float32
    shape = jax.ShapeDtypeStruct
    dma = lambda count: pltpu.SemaphoreType.DMA((count,))

    def in_order(own, other, axis):
        return jnp.concatenate([jnp.where(first, own, other), jnp.where(first, other, own)], axis=axis)

    hidden = hidden[None]
    offset = owners // 2
    first_piece = to_partner(hidden, offset)

    def merge(one, two):
        top = jnp.maximum(one[0], two[0])
        return top, one[1] * jnp.exp(one[0] - top) + two[1] * jnp.exp(two[0] - top)

    wide = student_logits.astype(f32)
    low = jnp.float32(-1e38)
    stats = jnp.stack(lax.reduce((wide, jnp.ones_like(wide)), (low, jnp.float32(0)), merge, (1,)))
    teacher_given, stats = lax.optimization_barrier((teacher_probs, stats))
    teacher_other = swap_halves(teacher_given)
    stats = in_order(stats, swap_halves(stats), 1)

    local = align_local.T - half_index * mine
    row_of = jnp.where((local >= 0) & (local < mine), align_owner.T * mine + local, -1)
    weight = jnp.where(align_owner.T >= 0, align_weight.T.astype(f32), 0.0)
    cut = lambda x, which: lax.dynamic_slice_in_dim(x, which * per_half, per_half, 1)
    w_own = block_weights(cut(row_of, half_index), cut(weight, half_index), rows)
    w_rest = block_weights(cut(row_of, 1 - half_index), cut(weight, 1 - half_index), rows)
    spread = pltpu.VMEM((per_half * tokens, BLK), f32)
    flops = 2 * (rows + MASS_ROWS) * per_half * tokens * BLK
    part = pl.pallas_call(
        map_own_kernel,
        out_shape=shape((rows + MASS_ROWS, tokens * BLK), f32),
        in_specs=[in_vmem(), in_vmem(), anywhere()],
        out_specs=in_vmem(),
        scratch_shapes=[spread],
        compiler_params=params(),
        cost_estimate=cost(flops, 3 << 20),
        name="map_own",
    )(w_own, teacher_probs, first_piece)
    cuts = 4
    chunk = (owners, tokens, width + group_tokens)
    outgoing = pl.pallas_call(
        map_rest_kernel,
        out_shape=shape(chunk, bf16),
        in_specs=[in_vmem(), anywhere(), in_vmem(), in_vmem()],
        out_specs=anywhere(),
        scratch_shapes=[
            pltpu.VMEM((tokens, per_half * BLK), bf16),
            spread,
            pltpu.VMEM(((rows + 8) * tokens, BLK), f32),
            pltpu.VMEM(chunk, bf16),
            dma(cuts),
            dma(owners),
        ],
        compiler_params=params(),
        cost_estimate=cost(flops, 4 << 20),
        name="map_rest",
    )(w_rest, teacher_other, part, stats)
    target = lax.all_to_all(outgoing, "sv", 0, 0, tiled=True)

    hidden, late_logits, outgoing = lax.optimization_barrier((hidden, student_logits, outgoing))

    keep = lax.dynamic_slice_in_dim(late_logits, half_index * width, width, 1)
    give = lax.dynamic_slice_in_dim(late_logits, (1 - half_index) * width, width, 1)
    logits = in_order(keep, swap_halves(give), 0)

    hidden_own = jnp.concatenate([hidden, first_piece])
    while offset > 1:
        offset //= 2
        hidden_own = jnp.concatenate([hidden_own, to_partner(hidden_own, offset)])

    scale = float(columns * owners)
    lanes = -(-half_tokens // BLK) * BLK
    grad, terms = pl.pallas_call(
        lambda *refs: grad_kernel(scale, *refs),
        out_shape=(shape((group_tokens, width), bf16), shape((owners * halves, 8, lanes), f32)),
        in_specs=[in_vmem()] * 2,
        out_specs=(in_vmem(), anywhere()),
        scratch_shapes=[
            pltpu.VMEM((group_tokens, BLK), f32),
            pltpu.VMEM((owners * halves, 8, lanes), f32),
            pltpu.SemaphoreType.DMA,
        ],
        compiler_params=params(),
        cost_estimate=cost(
            10 * group_tokens * width, 6 * group_tokens * width, 2 * group_tokens * width
        ),
        name="logit_grad",
    )(target, logits)

    terms = lax.all_to_all(terms, ("sv", "tv"), 0, 0, tiled=True)
    give = lax.dynamic_slice_in_dim(grad, (1 - half_index) * half_tokens, half_tokens, 0)
    got = swap_halves(give)

    steps = 8
    weight_grad = pl.pallas_call(
        weight_kernel,
        out_shape=shape((features, width), bf16),
        in_specs=[scalars()] + [in_vmem()] * 3,
        out_specs=anywhere(),
        scratch_shapes=[
            pltpu.VMEM((group_tokens, features), f32),
            pltpu.VMEM((features, group_tokens), bf16),
            pltpu.VMEM((steps, features // steps, width), bf16),
            dma(steps),
        ],
        compiler_params=params(),
        cost_estimate=cost(
            2 * features * group_tokens * width,
            2 * (features * width + group_tokens * (features + width)),
        ),
        name="weight_grad",
    )(place, hidden_own, swap_halves(hidden_own), grad)

    logit_grad = pl.pallas_call(
        join_kernel,
        out_shape=shape((half_tokens, columns), bf16),
        in_specs=[scalars(), anywhere(), anywhere()],
        out_specs=anywhere(),
        scratch_shapes=[dma(2)],
        compiler_params=params(),
        cost_estimate=cost(0, 4 * half_tokens * columns),
        name="join",
    )(place, grad, got)
    terms, logit_grad, weight_grad = lax.optimization_barrier((terms, logit_grad, weight_grad))
    divergence = jnp.sum(terms[:, 0, :half_tokens], axis=0)
    return (divergence, logit_grad, weight_grad)


def solution(mesh):
    return jax.shard_map(
        body,
        mesh=mesh,
        in_specs=(
            P(("grp", "sv"), "tv"),
            P(),
            P(),
            P(),
            P(("grp", "tv"), "sv"),
            P(("grp", "sv", "tv"), None),
        ),
        out_specs=(P(("grp", "tv")), P(("grp", "tv"), "sv"), P(None, ("grp", "sv", "tv"))),
        check_vma=False,
    )
```

```python
import jax
import jax.numpy as jnp
from jax import lax
from jax.experimental import pallas as pl
from jax.experimental.pallas import tpu as pltpu
from jax.sharding import PartitionSpec as P

BLK = 128
TB = 640
TOPA = 2
MASS_ROWS = 16
STEP = 16


def block_weights(code, rows):
    row_ids = lax.broadcasted_iota(jnp.int32, (rows + MASS_ROWS, code.shape[1]), 0)
    total = jnp.zeros(row_ids.shape, jnp.float32)
    for slot in range(TOPA):
        row = jnp.floor(code[slot])
        weight = (code[slot] - row) * 2.0
        hit = (row_ids == row.astype(jnp.int32)[None, :]) | (row_ids == rows + slot)
        total = total + jnp.where(hit, weight[None, :], 0.0)
    return total.astype(jnp.bfloat16)


def column_copies(source, target, sems, first=0):
    cuts = sems.shape[0] - first
    wide = source.shape[1] // cuts
    at = [pl.ds(i * wide, wide) for i in range(cuts)]
    return [pltpu.make_async_copy(source.at[:, at[i]], target.at[:, at[i]], sems.at[first + i]) for i in range(cuts)]


def spread_tokens(t_ref, s_ref, start, count):
    tokens = t_ref.shape[0]

    def some(i, carry):
        for j in range(STEP):
            k = start + i * STEP + j
            tile = t_ref[:, pl.ds(pl.multiple_of(k * BLK, BLK), BLK)]
            s_ref[pl.ds(pl.multiple_of(k * tokens, tokens), tokens), :] = tile.astype(jnp.float32)
        return carry

    lax.fori_loop(0, count // STEP, some, 0)


def spread_arriving(copies, t_buf, s_ref):
    blocks = t_buf.shape[1] // BLK // len(copies)
    for i, copy in enumerate(copies):
        copy.wait()
        spread_tokens(t_buf, s_ref, i * blocks, blocks)


def token_pair(s_ref, t, tokens):
    count = s_ref.shape[0] // tokens
    both = [s_ref[pl.ds(t + i, count, stride=tokens), :].astype(jnp.bfloat16) for i in range(2)]
    return jnp.concatenate(both, axis=1)


def map_own_kernel(w_ref, t_ref, first_ref, o_ref, s_ref):
    tokens = t_ref.shape[0]
    spread_tokens(t_ref, s_ref, 0, t_ref.shape[1] // BLK)
    for t in range(0, tokens, 2):
        o_ref[:, t * BLK : (t + 2) * BLK] = jnp.dot(
            w_ref[...], token_pair(s_ref, t, tokens), preferred_element_type=jnp.float32
        )


def three_parts(x):
    parts = []
    for _ in range(3):
        parts.append(x.astype(jnp.bfloat16).astype(jnp.float32))
        x = x - parts[-1]
    return parts


def map_rest_kernel(w_ref, t_ref, p_ref, stats_ref, o_ref, t_buf, s_ref, m_ref, o_buf, in_sem, out_sem):
    tokens = t_ref.shape[0]
    owners = o_ref.shape[0]
    rows = w_ref.shape[0] - MASS_ROWS
    mine = rows // owners
    arriving = column_copies(t_ref, t_buf, in_sem)
    for copy in arriving:
        copy.start()
    stats = [stats_ref[0:1, :]] + three_parts(stats_ref[1:2, :])
    extra = jnp.zeros((tokens, stats_ref.shape[1]), jnp.float32)
    row_ids = lax.broadcasted_iota(jnp.int32, extra.shape, 0)
    for i, row in enumerate(stats):
        extra = jnp.where(row_ids == i, row, extra)
    extra = extra.astype(jnp.bfloat16)
    spread_arriving(arriving, t_buf, s_ref)
    for t in range(0, tokens, 2):
        both = p_ref[:, t * BLK : (t + 2) * BLK] + jnp.dot(
            w_ref[...], token_pair(s_ref, t, tokens), preferred_element_type=jnp.float32
        )
        for i in range(2):
            m_ref[pl.ds(t + i, rows + 8, stride=tokens), :] = both[: rows + 8, i * BLK : (i + 1) * BLK]
    mass = m_ref[rows * tokens : (rows + 1) * tokens, :]
    for slot in range(1, TOPA):
        mass = mass + m_ref[(rows + slot) * tokens : (rows + slot + 1) * tokens, :]
    inverse = jnp.broadcast_to(1.0 / jnp.sum(mass, axis=1, keepdims=True), (tokens, BLK))

    def leaving(q):
        return pltpu.make_async_copy(o_buf.at[q], o_ref.at[q], out_sem.at[q])

    def owner(q, carry):
        for b in range(mine):
            first = pl.multiple_of((q * mine + b) * tokens, tokens)
            tile = m_ref[pl.ds(first, tokens), :] * inverse
            o_buf[q, :, b * BLK : (b + 1) * BLK] = tile.astype(jnp.bfloat16)
        o_buf[q, :, mine * BLK :] = extra
        leaving(q).start()
        return carry

    def left(q, carry):
        leaving(q).wait()
        return carry

    lax.fori_loop(0, owners, owner, 0)
    lax.fori_loop(0, owners, left, 0)


def grad_kernel(scale, target_ref, logits_ref, grad_ref, terms_ref, norm_ref, t_buf, sem):
    owners, tokens, _ = target_ref.shape
    group_tokens, width = logits_ref.shape
    stats = [target_ref[q, :, width:].astype(jnp.float32) for q in range(owners)]
    top = stats[0][0:1]
    for one in stats[1:]:
        top = jnp.maximum(top, one[0:1])
    total = jnp.zeros_like(top)
    for one in stats:
        total = total + (one[1:2] + one[2:3] + one[3:4]) * jnp.exp(one[0:1] - top)
    log_norm = top + jnp.log(total)

    def block(i, b):
        lanes = slice(b * BLK, (b + 1) * BLK)
        group = slice(i * BLK // tokens, (i + 1) * BLK // tokens)
        target = target_ref[group, :, lanes].reshape(BLK, BLK).astype(jnp.float32)
        return target, logits_ref[i * BLK : (i + 1) * BLK, lanes].astype(jnp.float32)

    sums = []
    for i in range(group_tokens // BLK):
        rows = slice(i * BLK, (i + 1) * BLK)
        norm = jnp.broadcast_to(log_norm[:, rows], (BLK, BLK)).T
        norm_ref[rows, :] = norm
        terms = jnp.zeros((BLK, BLK), jnp.float32)
        for b in range(width // BLK):
            target, logits = block(i, b)
            positive = target > 0
            one = target * (jnp.log(jnp.where(positive, target, 1.0)) - (logits - norm))
            terms = terms + jnp.where(positive, one, 0.0)
        sums.append(jnp.sum(terms.T, axis=0, keepdims=True))
    row = jnp.concatenate(sums, axis=1)
    for q in range(owners):
        t_buf[q] = jnp.broadcast_to(row, t_buf.shape[1:])
    leaving = pltpu.make_async_copy(t_buf, terms_ref, sem)
    leaving.start()
    for i in range(group_tokens // BLK):
        rows = slice(i * BLK, (i + 1) * BLK)
        for b in range(width // BLK):
            target, logits = block(i, b)
            grad = (jnp.exp(logits - norm_ref[rows, :]) - target) * scale
            grad_ref[rows, b * BLK : (b + 1) * BLK] = grad.astype(jnp.bfloat16)
    leaving.wait()


def arrival_order(owners):
    return [a for b in range(owners // 2) for a in (b, b + owners // 2)]


def weight_blocks(h_ref, grad_ref, o_ref, block_ref, sems, first):
    steps, tile, _ = block_ref.shape
    copies = []
    for i in range(steps):
        block_ref[i] = jnp.dot(
            h_ref[i * tile : (i + 1) * tile, :], grad_ref[...], preferred_element_type=jnp.float32
        ).astype(jnp.bfloat16)
        rows = pl.ds(first + i * tile, tile)
        copies.append(pltpu.make_async_copy(block_ref.at[i], o_ref.at[rows, :], sems.at[i]))
        copies[-1].start()
    return copies


def first_weight_kernel(place_ref, own_ref, other_ref, grad_ref, o_ref, later_ref, s_ref, h_ref, block_ref, sems):
    owners, held, features = own_ref.shape
    for i, offset in enumerate(arrival_order(owners)):
        first = (place_ref[0] ^ offset) * 2
        own = pl.ds(pl.multiple_of((first + place_ref[1]) * held, held), held)
        other = pl.ds(pl.multiple_of((first + 1 - place_ref[1]) * held, held), held)
        s_ref[own, :] = own_ref[i].astype(jnp.float32)
        s_ref[other, :] = other_ref[i].astype(jnp.float32)
    for i in range(s_ref.shape[0] // BLK):
        for j in range(features // BLK):
            tile = s_ref[i * BLK : (i + 1) * BLK, j * BLK : (j + 1) * BLK].T
            h_ref[j * BLK : (j + 1) * BLK, i * BLK : (i + 1) * BLK] = tile.astype(jnp.bfloat16)
    copies = weight_blocks(h_ref, grad_ref, o_ref, block_ref, sems, 0)
    later_ref[...] = h_ref[features // 2 :, :]
    for copy in copies:
        copy.wait()


def second_weight_kernel(
    place_ref, h_ref, grad_ref, got_ref, sums_ref, half_ref, o_ref, joined_ref, block_ref, sems, join_sems
):
    half_tokens, width = got_ref.shape
    half = place_ref[1]
    kept_at = pl.ds(pl.multiple_of(half * width, width), width)
    got_at = pl.ds(pl.multiple_of((1 - half) * width, width), width)
    rows = pl.ds(pl.multiple_of(half * half_tokens, half_tokens), half_tokens)
    copies = [
        pltpu.make_async_copy(grad_ref.at[rows, :], joined_ref.at[:, kept_at], join_sems.at[0]),
        pltpu.make_async_copy(got_ref, joined_ref.at[:, got_at], join_sems.at[1]),
    ]
    for copy in copies:
        copy.start()
    for copy in copies + weight_blocks(h_ref, grad_ref, o_ref, block_ref, sems, h_ref.shape[0]):
        copy.wait()


def in_vmem():
    return pl.BlockSpec(memory_space=pltpu.VMEM)


def scalars():
    return pl.BlockSpec(memory_space=pltpu.SMEM)


def anywhere():
    return pl.BlockSpec(memory_space=pl.ANY)


def params(mib=48):
    return pltpu.CompilerParams(vmem_limit_bytes=mib << 20)


def cost(flops=0, bytes_accessed=0, transcendentals=0):
    return pl.CostEstimate(flops=flops, bytes_accessed=bytes_accessed, transcendentals=transcendentals)


def swap_halves(x):
    return lax.ppermute(x, "tv", [(0, 1), (1, 0)])


def to_partner(x, offset):
    return lax.ppermute(x, "sv", [(s, s ^ offset) for s in range(lax.axis_size("sv"))])


def body(teacher_probs, align_owner, align_local, align_weight, student_logits, hidden):
    owners = lax.axis_size("sv")
    halves = lax.axis_size("tv")
    half_index = lax.axis_index("tv")
    place = jnp.stack([lax.axis_index("sv"), half_index]).astype(jnp.int32)
    tokens = teacher_probs.shape[0]
    columns = student_logits.shape[1]
    blocks = columns // BLK
    mine = blocks // halves
    width = mine * BLK
    rows = owners * mine
    per_half = TB // halves
    group_tokens = owners * tokens
    half_tokens = student_logits.shape[0]
    features = hidden.shape[1]
    first = half_index == 0
    bf16, f32 = jnp.bfloat16, jnp.float32
    shape = jax.ShapeDtypeStruct
    dma = lambda count: pltpu.SemaphoreType.DMA((count,))

    def in_order(own, other, axis):
        return jnp.concatenate([jnp.where(first, own, other), jnp.where(first, other, own)], axis=axis)

    hidden = hidden[None]
    offset = owners // 2
    first_piece = to_partner(hidden, offset)

    def merge(one, two):
        top = jnp.maximum(one[0], two[0])
        return top, one[1] * jnp.exp(one[0] - top) + two[1] * jnp.exp(two[0] - top)

    wide = student_logits.astype(f32)
    low = jnp.float32(-1e38)
    stats = jnp.stack(lax.reduce((wide, jnp.ones_like(wide)), (low, jnp.float32(0)), merge, (1,)))
    teacher_given, stats = lax.optimization_barrier((teacher_probs, stats))
    teacher_other = swap_halves(teacher_given)
    stats = in_order(stats, swap_halves(stats), 1)

    local = align_local.T - half_index * mine
    row_of = jnp.where((local >= 0) & (local < mine), align_owner.T * mine + local, -1)
    code = row_of.astype(f32) + 0.5 * align_weight.T.astype(f32)
    cut = lambda which: lax.dynamic_slice_in_dim(code, which * per_half, per_half, 1)
    w_own = block_weights(cut(half_index), rows)
    w_rest = block_weights(cut(1 - half_index), rows)
    spread = pltpu.VMEM((per_half * tokens, BLK), f32)
    flops = 2 * (rows + MASS_ROWS) * per_half * tokens * BLK
    part = pl.pallas_call(
        map_own_kernel,
        out_shape=shape((rows + MASS_ROWS, tokens * BLK), f32),
        in_specs=[in_vmem(), in_vmem(), anywhere()],
        out_specs=in_vmem(),
        scratch_shapes=[spread],
        compiler_params=params(),
        cost_estimate=cost(flops, 3 << 20),
        name="map_own",
    )(w_own, teacher_probs, first_piece)
    cuts = 4
    chunk = (owners, tokens, width + group_tokens)
    outgoing = pl.pallas_call(
        map_rest_kernel,
        out_shape=shape(chunk, bf16),
        in_specs=[in_vmem(), anywhere(), in_vmem(), in_vmem()],
        out_specs=anywhere(),
        scratch_shapes=[
            pltpu.VMEM((tokens, per_half * BLK), bf16),
            spread,
            pltpu.VMEM(((rows + 8) * tokens, BLK), f32),
            pltpu.VMEM(chunk, bf16),
            dma(cuts),
            dma(owners),
        ],
        compiler_params=params(),
        cost_estimate=cost(flops, 4 << 20),
        name="map_rest",
    )(w_rest, teacher_other, part, stats)
    target = lax.all_to_all(outgoing, "sv", 0, 0, tiled=True)

    hidden, late_logits, outgoing = lax.optimization_barrier((hidden, student_logits, outgoing))

    keep = lax.dynamic_slice_in_dim(late_logits, half_index * width, width, 1)
    give = lax.dynamic_slice_in_dim(late_logits, (1 - half_index) * width, width, 1)
    logits = in_order(keep, swap_halves(give), 0)

    pieces = [jnp.concatenate([hidden, first_piece])]
    pieces += [to_partner(pieces[0], a) for a in range(1, offset)]
    hidden_own = jnp.concatenate(pieces)

    scale = float(columns * owners)
    grad, terms = pl.pallas_call(
        lambda *refs: grad_kernel(scale, *refs),
        out_shape=(shape((group_tokens, width), bf16), shape((owners, 8, group_tokens), f32)),
        in_specs=[in_vmem()] * 2,
        out_specs=(in_vmem(), anywhere()),
        scratch_shapes=[
            pltpu.VMEM((group_tokens, BLK), f32),
            pltpu.VMEM((owners, 8, group_tokens), f32),
            pltpu.SemaphoreType.DMA,
        ],
        compiler_params=params(),
        cost_estimate=cost(
            10 * group_tokens * width, 6 * group_tokens * width, 2 * group_tokens * width
        ),
        name="logit_grad",
    )(target, logits)

    terms = lax.all_to_all(terms, "sv", 0, 0, tiled=True)
    give = lax.dynamic_slice_in_dim(grad, (1 - half_index) * half_tokens, half_tokens, 0)
    got = swap_halves(give)

    steps = 4
    part_rows = features // 2
    blocks = pltpu.VMEM((steps, part_rows // steps, width), bf16)
    weight_cost = cost(
        features * group_tokens * width, features * width + group_tokens * (features + 2 * width)
    )
    weight_grad, hidden_t = pl.pallas_call(
        first_weight_kernel,
        out_shape=(shape((features, width), bf16), shape((part_rows, group_tokens), bf16)),
        in_specs=[scalars()] + [in_vmem()] * 3,
        out_specs=(anywhere(), in_vmem()),
        scratch_shapes=[
            pltpu.VMEM((group_tokens, features), f32),
            pltpu.VMEM((features, group_tokens), bf16),
            blocks,
            dma(steps),
        ],
        compiler_params=params(),
        cost_estimate=weight_cost,
        name="weight_grad_first",
    )(place, hidden_own, swap_halves(hidden_own), grad)

    sums = jnp.sum(terms[:, 0], axis=0)
    sums_other = swap_halves(sums)
    weight_grad, logit_grad = pl.pallas_call(
        second_weight_kernel,
        out_shape=(shape((features, width), bf16), shape((half_tokens, columns), bf16)),
        in_specs=[scalars(), in_vmem(), in_vmem(), anywhere(), anywhere(), anywhere()],
        out_specs=(anywhere(), anywhere()),
        scratch_shapes=[blocks, dma(steps), dma(2)],
        input_output_aliases={5: 0},
        compiler_params=params(),
        cost_estimate=weight_cost,
        name="weight_grad_second",
    )(place, hidden_t, grad, got, sums, weight_grad)
    sums_other, weight_grad, logit_grad = lax.optimization_barrier((sums_other, weight_grad, logit_grad))
    divergence = lax.dynamic_slice_in_dim(sums + sums_other, half_index * half_tokens, half_tokens, 0)
    return (divergence, logit_grad, weight_grad)


def solution(mesh):
    return jax.shard_map(
        body,
        mesh=mesh,
        in_specs=(
            P(("grp", "sv"), "tv"),
            P(),
            P(),
            P(),
            P(("grp", "tv"), "sv"),
            P(("grp", "sv", "tv"), None),
        ),
        out_specs=(P(("grp", "tv")), P(("grp", "tv"), "sv"), P(None, ("grp", "sv", "tv"))),
        check_vma=False,
    )
```

```python
import jax
import jax.numpy as jnp
from jax import lax
from jax.experimental import pallas as pl
from jax.experimental.pallas import tpu as pltpu
from jax.sharding import PartitionSpec as P

BLK = 128
TB = 640
TOPA = 2
MASS_ROWS = 16
STEP = 16


def block_weights(code, rows):
    row_ids = lax.broadcasted_iota(jnp.int32, (rows + MASS_ROWS, code.shape[1]), 0)
    total = jnp.zeros(row_ids.shape, jnp.float32)
    for slot in range(TOPA):
        row = jnp.floor(code[slot])
        weight = (code[slot] - row) * 2.0
        hit = (row_ids == row.astype(jnp.int32)[None, :]) | (row_ids == rows + slot)
        total = total + jnp.where(hit, weight[None, :], 0.0)
    return total.astype(jnp.bfloat16)


def spread_tokens(t_ref, s_ref, start, count):
    tokens = t_ref.shape[0]

    def some(i, carry):
        for j in range(STEP):
            k = start + i * STEP + j
            tile = t_ref[:, pl.ds(pl.multiple_of(k * BLK, BLK), BLK)]
            s_ref[pl.ds(pl.multiple_of(k * tokens, tokens), tokens), :] = tile.astype(jnp.float32)
        return carry

    lax.fori_loop(0, count // STEP, some, 0)


def token_pair(s_ref, t, tokens):
    count = s_ref.shape[0] // tokens
    both = [s_ref[pl.ds(t + i, count, stride=tokens), :].astype(jnp.bfloat16) for i in range(2)]
    return jnp.concatenate(both, axis=1)


def map_own_kernel(w_ref, t_ref, first_ref, o_ref, s_ref):
    tokens = t_ref.shape[0]
    spread_tokens(t_ref, s_ref, 0, t_ref.shape[1] // BLK)
    for t in range(0, tokens, 2):
        o_ref[:, t * BLK : (t + 2) * BLK] = jnp.dot(
            w_ref[...], token_pair(s_ref, t, tokens), preferred_element_type=jnp.float32
        )


def three_parts(x):
    parts = []
    for _ in range(3):
        parts.append(x.astype(jnp.bfloat16).astype(jnp.float32))
        x = x - parts[-1]
    return parts


def map_rest_kernel(w_ref, t_ref, p_ref, stats_ref, o_ref, s_ref, m_ref, o_buf, out_sem):
    tokens = t_ref.shape[0]
    owners = o_ref.shape[0]
    rows = w_ref.shape[0] - MASS_ROWS
    mine = rows // owners
    stats = [stats_ref[0:1, :]] + three_parts(stats_ref[1:2, :])
    extra = jnp.zeros((tokens, stats_ref.shape[1]), jnp.float32)
    row_ids = lax.broadcasted_iota(jnp.int32, extra.shape, 0)
    for i, row in enumerate(stats):
        extra = jnp.where(row_ids == i, row, extra)
    extra = extra.astype(jnp.bfloat16)
    spread_tokens(t_ref, s_ref, 0, t_ref.shape[1] // BLK)
    for t in range(0, tokens, 2):
        both = p_ref[:, t * BLK : (t + 2) * BLK] + jnp.dot(
            w_ref[...], token_pair(s_ref, t, tokens), preferred_element_type=jnp.float32
        )
        for i in range(2):
            m_ref[pl.ds(t + i, rows + 8, stride=tokens), :] = both[: rows + 8, i * BLK : (i + 1) * BLK]
    mass = m_ref[rows * tokens : (rows + 1) * tokens, :]
    for slot in range(1, TOPA):
        mass = mass + m_ref[(rows + slot) * tokens : (rows + slot + 1) * tokens, :]
    inverse = jnp.broadcast_to(1.0 / jnp.sum(mass, axis=1, keepdims=True), (tokens, BLK))

    def leaving(q):
        return pltpu.make_async_copy(o_buf.at[q], o_ref.at[q], out_sem.at[q])

    def owner(q, carry):
        for b in range(mine):
            first = pl.multiple_of((q * mine + b) * tokens, tokens)
            tile = m_ref[pl.ds(first, tokens), :] * inverse
            o_buf[q, :, b * BLK : (b + 1) * BLK] = tile.astype(jnp.bfloat16)
        o_buf[q, :, mine * BLK :] = extra
        leaving(q).start()
        return carry

    def left(q, carry):
        leaving(q).wait()
        return carry

    lax.fori_loop(0, owners, owner, 0)
    lax.fori_loop(0, owners, left, 0)


def grad_kernel(scale, target_ref, logits_ref, grad_ref, terms_ref, norm_ref, t_buf, sem):
    owners, tokens, _ = target_ref.shape
    group_tokens, width = logits_ref.shape
    stats = [target_ref[q, :, width:].astype(jnp.float32) for q in range(owners)]
    top = stats[0][0:1]
    for one in stats[1:]:
        top = jnp.maximum(top, one[0:1])
    total = jnp.zeros_like(top)
    for one in stats:
        total = total + (one[1:2] + one[2:3] + one[3:4]) * jnp.exp(one[0:1] - top)
    log_norm = top + jnp.log(total)

    def block(i, b):
        lanes = slice(b * BLK, (b + 1) * BLK)
        group = slice(i * BLK // tokens, (i + 1) * BLK // tokens)
        target = target_ref[group, :, lanes].reshape(BLK, BLK).astype(jnp.float32)
        return target, logits_ref[i * BLK : (i + 1) * BLK, lanes].astype(jnp.float32)

    sums = []
    for i in range(group_tokens // BLK):
        rows = slice(i * BLK, (i + 1) * BLK)
        norm = jnp.broadcast_to(log_norm[:, rows], (BLK, BLK)).T
        norm_ref[rows, :] = norm
        terms = jnp.zeros((BLK, BLK), jnp.float32)
        for b in range(width // BLK):
            target, logits = block(i, b)
            positive = target > 0
            one = target * (jnp.log(jnp.where(positive, target, 1.0)) - (logits - norm))
            terms = terms + jnp.where(positive, one, 0.0)
        sums.append(jnp.sum(terms.T, axis=0, keepdims=True))
    row = jnp.concatenate(sums, axis=1)
    half_tokens = group_tokens // 2
    for half in range(2):
        mine = row[:, half * half_tokens : (half + 1) * half_tokens]
        tile = jnp.concatenate([mine] * (t_buf.shape[2] // half_tokens), axis=1)
        for q in range(owners):
            t_buf[2 * q + half] = jnp.broadcast_to(tile, t_buf.shape[1:])
    leaving = pltpu.make_async_copy(t_buf, terms_ref, sem)
    leaving.start()
    for i in range(group_tokens // BLK):
        rows = slice(i * BLK, (i + 1) * BLK)
        for b in range(width // BLK):
            target, logits = block(i, b)
            grad = (jnp.exp(logits - norm_ref[rows, :]) - target) * scale
            grad_ref[rows, b * BLK : (b + 1) * BLK] = grad.astype(jnp.bfloat16)
    leaving.wait()


def arrival_order(owners):
    return [a for b in range(owners // 2) for a in (b, b + owners // 2)]


def weight_kernel(
    place_ref, own_ref, other_ref, grad_ref, got_ref, o_ref, joined_ref, s_ref, h_ref, block_ref, sems, join_sems
):
    half_tokens, width = got_ref.shape
    half = place_ref[1]
    kept_at = pl.ds(pl.multiple_of(half * width, width), width)
    got_at = pl.ds(pl.multiple_of((1 - half) * width, width), width)
    kept = pl.ds(pl.multiple_of(half * half_tokens, half_tokens), half_tokens)
    copies = [
        pltpu.make_async_copy(grad_ref.at[kept, :], joined_ref.at[:, kept_at], join_sems.at[0]),
        pltpu.make_async_copy(got_ref, joined_ref.at[:, got_at], join_sems.at[1]),
    ]
    for copy in copies:
        copy.start()
    owners, held, features = own_ref.shape
    for i, offset in enumerate(arrival_order(owners)):
        first = (place_ref[0] ^ offset) * 2
        own = pl.ds(pl.multiple_of((first + half) * held, held), held)
        other = pl.ds(pl.multiple_of((first + 1 - half) * held, held), held)
        s_ref[own, :] = own_ref[i].astype(jnp.float32)
        s_ref[other, :] = other_ref[i].astype(jnp.float32)
    for i in range(s_ref.shape[0] // BLK):
        for j in range(features // BLK):
            tile = s_ref[i * BLK : (i + 1) * BLK, j * BLK : (j + 1) * BLK].T
            h_ref[j * BLK : (j + 1) * BLK, i * BLK : (i + 1) * BLK] = tile.astype(jnp.bfloat16)
    steps, tile, _ = block_ref.shape
    for i in range(steps):
        rows = slice(i * tile, (i + 1) * tile)
        block_ref[i] = jnp.dot(
            h_ref[rows, :], grad_ref[...], preferred_element_type=jnp.float32
        ).astype(jnp.bfloat16)
        copies.append(pltpu.make_async_copy(block_ref.at[i], o_ref.at[pl.ds(i * tile, tile), :], sems.at[i]))
        copies[-1].start()
    for copy in copies:
        copy.wait()


def in_vmem():
    return pl.BlockSpec(memory_space=pltpu.VMEM)


def scalars():
    return pl.BlockSpec(memory_space=pltpu.SMEM)


def anywhere():
    return pl.BlockSpec(memory_space=pl.ANY)


def params(mib=48):
    return pltpu.CompilerParams(vmem_limit_bytes=mib << 20)


def cost(flops=0, bytes_accessed=0, transcendentals=0):
    return pl.CostEstimate(flops=flops, bytes_accessed=bytes_accessed, transcendentals=transcendentals)


def swap_halves(x):
    return lax.ppermute(x, "tv", [(0, 1), (1, 0)])


def to_partner(x, offset):
    return lax.ppermute(x, "sv", [(s, s ^ offset) for s in range(lax.axis_size("sv"))])


def body(teacher_probs, align_owner, align_local, align_weight, student_logits, hidden):
    owners = lax.axis_size("sv")
    halves = lax.axis_size("tv")
    half_index = lax.axis_index("tv")
    place = jnp.stack([lax.axis_index("sv"), half_index]).astype(jnp.int32)
    tokens = teacher_probs.shape[0]
    columns = student_logits.shape[1]
    blocks = columns // BLK
    mine = blocks // halves
    width = mine * BLK
    rows = owners * mine
    per_half = TB // halves
    group_tokens = owners * tokens
    half_tokens = student_logits.shape[0]
    features = hidden.shape[1]
    first = half_index == 0
    bf16, f32 = jnp.bfloat16, jnp.float32
    shape = jax.ShapeDtypeStruct
    dma = lambda count: pltpu.SemaphoreType.DMA((count,))

    def in_order(own, other, axis):
        return jnp.concatenate([jnp.where(first, own, other), jnp.where(first, other, own)], axis=axis)

    hidden = hidden[None]
    offset = owners // 2
    first_piece = to_partner(hidden, offset)

    def merge(one, two):
        top = jnp.maximum(one[0], two[0])
        return top, one[1] * jnp.exp(one[0] - top) + two[1] * jnp.exp(two[0] - top)

    wide = student_logits.astype(f32)
    low = jnp.float32(-1e38)
    stats = jnp.stack(lax.reduce((wide, jnp.ones_like(wide)), (low, jnp.float32(0)), merge, (1,)))
    teacher_given, stats = lax.optimization_barrier((teacher_probs, stats))
    teacher_other = swap_halves(teacher_given)
    stats = in_order(stats, swap_halves(stats), 1)

    local = align_local.T - half_index * mine
    row_of = jnp.where((local >= 0) & (local < mine), align_owner.T * mine + local, -1)
    code = row_of.astype(f32) + 0.5 * align_weight.T.astype(f32)
    cut = lambda which: lax.dynamic_slice_in_dim(code, which * per_half, per_half, 1)
    w_own = block_weights(cut(half_index), rows)
    w_rest = block_weights(cut(1 - half_index), rows)
    spread = pltpu.VMEM((per_half * tokens, BLK), f32)
    flops = 2 * (rows + MASS_ROWS) * per_half * tokens * BLK
    part = pl.pallas_call(
        map_own_kernel,
        out_shape=shape((rows + MASS_ROWS, tokens * BLK), f32),
        in_specs=[in_vmem(), in_vmem(), anywhere()],
        out_specs=in_vmem(),
        scratch_shapes=[spread],
        compiler_params=params(),
        cost_estimate=cost(flops, 3 << 20),
        name="map_own",
    )(w_own, teacher_probs, first_piece)
    chunk = (owners, tokens, width + group_tokens)
    outgoing = pl.pallas_call(
        map_rest_kernel,
        out_shape=shape(chunk, bf16),
        in_specs=[in_vmem()] * 4,
        out_specs=anywhere(),
        scratch_shapes=[
            spread,
            pltpu.VMEM(((rows + 8) * tokens, BLK), f32),
            pltpu.VMEM(chunk, bf16),
            dma(owners),
        ],
        compiler_params=params(),
        cost_estimate=cost(flops, 4 << 20),
        name="map_rest",
    )(w_rest, teacher_other, part, stats)
    target = lax.all_to_all(outgoing, "sv", 0, 0, tiled=True)

    hidden, late_logits, outgoing = lax.optimization_barrier((hidden, student_logits, outgoing))

    keep = lax.dynamic_slice_in_dim(late_logits, half_index * width, width, 1)
    give = lax.dynamic_slice_in_dim(late_logits, (1 - half_index) * width, width, 1)
    logits = in_order(keep, swap_halves(give), 0)

    pieces = [jnp.concatenate([hidden, first_piece])]
    pieces += [to_partner(pieces[0], a) for a in range(1, offset)]

    scale = float(columns * owners)
    lanes = -(-half_tokens // BLK) * BLK
    grad, terms = pl.pallas_call(
        lambda *refs: grad_kernel(scale, *refs),
        out_shape=(shape((group_tokens, width), bf16), shape((owners * halves, 8, lanes), f32)),
        in_specs=[in_vmem()] * 2,
        out_specs=(in_vmem(), anywhere()),
        scratch_shapes=[
            pltpu.VMEM((group_tokens, BLK), f32),
            pltpu.VMEM((owners * halves, 8, lanes), f32),
            pltpu.SemaphoreType.DMA,
        ],
        compiler_params=params(),
        cost_estimate=cost(
            10 * group_tokens * width, 6 * group_tokens * width, 2 * group_tokens * width
        ),
        name="logit_grad",
    )(target, logits)

    terms = lax.all_to_all(terms, ("sv", "tv"), 0, 0, tiled=True)
    give = lax.dynamic_slice_in_dim(grad, (1 - half_index) * half_tokens, half_tokens, 0)
    got = swap_halves(give)

    *pieces, grad = lax.optimization_barrier((*pieces, grad))
    hidden_own = jnp.concatenate(pieces)
    steps = 8
    weight_grad, logit_grad = pl.pallas_call(
        weight_kernel,
        out_shape=(shape((features, width), bf16), shape((half_tokens, columns), bf16)),
        in_specs=[scalars()] + [in_vmem()] * 4,
        out_specs=(anywhere(), anywhere()),
        scratch_shapes=[
            pltpu.VMEM((group_tokens, features), f32),
            pltpu.VMEM((features, group_tokens), bf16),
            pltpu.VMEM((steps, features // steps, width), bf16),
            dma(steps),
            dma(2),
        ],
        compiler_params=params(),
        cost_estimate=cost(
            2 * features * group_tokens * width,
            2 * (features * width + group_tokens * (features + width)),
        ),
        name="weight_grad",
    )(place, hidden_own, swap_halves(hidden_own), grad, got)
    terms, logit_grad, weight_grad = lax.optimization_barrier((terms, logit_grad, weight_grad))
    divergence = jnp.sum(terms[:, 0, :half_tokens], axis=0)
    return (divergence, logit_grad, weight_grad)


def solution(mesh):
    return jax.shard_map(
        body,
        mesh=mesh,
        in_specs=(
            P(("grp", "sv"), "tv"),
            P(),
            P(),
            P(),
            P(("grp", "tv"), "sv"),
            P(("grp", "sv", "tv"), None),
        ),
        out_specs=(P(("grp", "tv")), P(("grp", "tv"), "sv"), P(None, ("grp", "sv", "tv"))),
        check_vma=False,
    )
```

```python
import jax
import jax.numpy as jnp
from jax import lax
from jax.experimental import pallas as pl
from jax.experimental.pallas import tpu as pltpu
from jax.sharding import PartitionSpec as P

BLK = 128
TB = 640
TOPA = 2
MASS_ROWS = 16
STEP = 16


def block_weights(code, rows):
    row_ids = lax.broadcasted_iota(jnp.int32, (rows + MASS_ROWS, code.shape[1]), 0)
    total = jnp.zeros(row_ids.shape, jnp.float32)
    for slot in range(TOPA):
        row = jnp.floor(code[slot])
        weight = (code[slot] - row) * 2.0
        hit = (row_ids == row.astype(jnp.int32)[None, :]) | (row_ids == rows + slot)
        total = total + jnp.where(hit, weight[None, :], 0.0)
    return total.astype(jnp.bfloat16)


def spread_tokens(t_ref, s_ref, start, count):
    tokens = t_ref.shape[0]

    def some(i, carry):
        for j in range(STEP):
            k = start + i * STEP + j
            tile = t_ref[:, pl.ds(pl.multiple_of(k * BLK, BLK), BLK)]
            s_ref[pl.ds(pl.multiple_of(k * tokens, tokens), tokens), :] = tile.astype(jnp.float32)
        return carry

    lax.fori_loop(0, count // STEP, some, 0)


def token_pair(s_ref, t, tokens):
    count = s_ref.shape[0] // tokens
    both = [s_ref[pl.ds(t + i, count, stride=tokens), :].astype(jnp.bfloat16) for i in range(2)]
    return jnp.concatenate(both, axis=1)


def map_own_kernel(w_ref, t_ref, o_ref, s_ref):
    tokens = t_ref.shape[0]
    spread_tokens(t_ref, s_ref, 0, t_ref.shape[1] // BLK)
    for t in range(0, tokens, 2):
        o_ref[:, t * BLK : (t + 2) * BLK] = jnp.dot(
            w_ref[...], token_pair(s_ref, t, tokens), preferred_element_type=jnp.float32
        )


def three_parts(x):
    parts = []
    for _ in range(3):
        parts.append(x.astype(jnp.bfloat16).astype(jnp.float32))
        x = x - parts[-1]
    return parts


def map_rest_kernel(w_ref, t_ref, p_ref, stats_ref, o_ref, s_ref, m_ref, o_buf, out_sem):
    tokens = t_ref.shape[0]
    owners = o_ref.shape[0]
    rows = w_ref.shape[0] - MASS_ROWS
    mine = rows // owners
    stats = [stats_ref[0:1, :]] + three_parts(stats_ref[1:2, :])
    extra = jnp.zeros((tokens, stats_ref.shape[1]), jnp.float32)
    row_ids = lax.broadcasted_iota(jnp.int32, extra.shape, 0)
    for i, row in enumerate(stats):
        extra = jnp.where(row_ids == i, row, extra)
    extra = extra.astype(jnp.bfloat16)
    spread_tokens(t_ref, s_ref, 0, t_ref.shape[1] // BLK)
    for t in range(0, tokens, 2):
        both = p_ref[:, t * BLK : (t + 2) * BLK] + jnp.dot(
            w_ref[...], token_pair(s_ref, t, tokens), preferred_element_type=jnp.float32
        )
        for i in range(2):
            m_ref[pl.ds(t + i, rows + 8, stride=tokens), :] = both[: rows + 8, i * BLK : (i + 1) * BLK]
    mass = m_ref[rows * tokens : (rows + 1) * tokens, :]
    for slot in range(1, TOPA):
        mass = mass + m_ref[(rows + slot) * tokens : (rows + slot + 1) * tokens, :]
    inverse = jnp.broadcast_to(1.0 / jnp.sum(mass, axis=1, keepdims=True), (tokens, BLK))

    def leaving(q):
        return pltpu.make_async_copy(o_buf.at[q], o_ref.at[q], out_sem.at[q])

    def owner(q, carry):
        for b in range(mine):
            first = pl.multiple_of((q * mine + b) * tokens, tokens)
            tile = m_ref[pl.ds(first, tokens), :] * inverse
            o_buf[q, :, b * BLK : (b + 1) * BLK] = tile.astype(jnp.bfloat16)
        o_buf[q, :, mine * BLK :] = extra
        leaving(q).start()
        return carry

    def left(q, carry):
        leaving(q).wait()
        return carry

    lax.fori_loop(0, owners, owner, 0)
    lax.fori_loop(0, owners, left, 0)


def grad_kernel(scale, target_ref, logits_ref, grad_ref, terms_ref, norm_ref, t_buf, sem):
    owners, tokens, _ = target_ref.shape
    group_tokens, width = logits_ref.shape
    stats = [target_ref[q, :, width:].astype(jnp.float32) for q in range(owners)]
    top = stats[0][0:1]
    for one in stats[1:]:
        top = jnp.maximum(top, one[0:1])
    total = jnp.zeros_like(top)
    for one in stats:
        total = total + (one[1:2] + one[2:3] + one[3:4]) * jnp.exp(one[0:1] - top)
    log_norm = top + jnp.log(total)

    def block(i, b):
        lanes = slice(b * BLK, (b + 1) * BLK)
        group = slice(i * BLK // tokens, (i + 1) * BLK // tokens)
        target = target_ref[group, :, lanes].reshape(BLK, BLK).astype(jnp.float32)
        return target, logits_ref[i * BLK : (i + 1) * BLK, lanes].astype(jnp.float32)

    sums = []
    for i in range(group_tokens // BLK):
        rows = slice(i * BLK, (i + 1) * BLK)
        norm = jnp.broadcast_to(log_norm[:, rows], (BLK, BLK)).T
        norm_ref[rows, :] = norm
        terms = jnp.zeros((BLK, BLK), jnp.float32)
        for b in range(width // BLK):
            target, logits = block(i, b)
            positive = target > 0
            one = target * (jnp.log(jnp.where(positive, target, 1.0)) - (logits - norm))
            terms = terms + jnp.where(positive, one, 0.0)
        sums.append(jnp.sum(terms.T, axis=0, keepdims=True))
    row = jnp.concatenate(sums, axis=1)
    half_tokens = group_tokens // 2
    for half in range(2):
        mine = row[:, half * half_tokens : (half + 1) * half_tokens]
        tile = jnp.concatenate([mine] * (t_buf.shape[2] // half_tokens), axis=1)
        for q in range(owners):
            t_buf[2 * q + half] = jnp.broadcast_to(tile, t_buf.shape[1:])
    leaving = pltpu.make_async_copy(t_buf, terms_ref, sem)
    leaving.start()
    for i in range(group_tokens // BLK):
        rows = slice(i * BLK, (i + 1) * BLK)
        for b in range(width // BLK):
            target, logits = block(i, b)
            grad = (jnp.exp(logits - norm_ref[rows, :]) - target) * scale
            grad_ref[rows, b * BLK : (b + 1) * BLK] = grad.astype(jnp.bfloat16)
    leaving.wait()


def arrival_order(owners):
    return [a for b in range(owners // 2) for a in (b, b + owners // 2)]


def weight_kernel(
    place_ref, own_ref, other_ref, grad_ref, got_ref, o_ref, joined_ref, s_ref, h_ref, block_ref, sems, join_sems
):
    half_tokens, width = got_ref.shape
    half = place_ref[1]
    kept_at = pl.ds(pl.multiple_of(half * width, width), width)
    got_at = pl.ds(pl.multiple_of((1 - half) * width, width), width)
    kept = pl.ds(pl.multiple_of(half * half_tokens, half_tokens), half_tokens)
    copies = [
        pltpu.make_async_copy(grad_ref.at[kept, :], joined_ref.at[:, kept_at], join_sems.at[0]),
        pltpu.make_async_copy(got_ref, joined_ref.at[:, got_at], join_sems.at[1]),
    ]
    for copy in copies:
        copy.start()
    owners, held, features = own_ref.shape
    for i, offset in enumerate(arrival_order(owners)):
        first = (place_ref[0] ^ offset) * 2
        own = pl.ds(pl.multiple_of((first + half) * held, held), held)
        other = pl.ds(pl.multiple_of((first + 1 - half) * held, held), held)
        s_ref[own, :] = own_ref[i].astype(jnp.float32)
        s_ref[other, :] = other_ref[i].astype(jnp.float32)
    for i in range(s_ref.shape[0] // BLK):
        for j in range(features // BLK):
            tile = s_ref[i * BLK : (i + 1) * BLK, j * BLK : (j + 1) * BLK].T
            h_ref[j * BLK : (j + 1) * BLK, i * BLK : (i + 1) * BLK] = tile.astype(jnp.bfloat16)
    steps, tile, _ = block_ref.shape
    for i in range(steps):
        rows = slice(i * tile, (i + 1) * tile)
        block_ref[i] = jnp.dot(
            h_ref[rows, :], grad_ref[...], preferred_element_type=jnp.float32
        ).astype(jnp.bfloat16)
        copies.append(pltpu.make_async_copy(block_ref.at[i], o_ref.at[pl.ds(i * tile, tile), :], sems.at[i]))
        copies[-1].start()
    for copy in copies:
        copy.wait()


def in_vmem():
    return pl.BlockSpec(memory_space=pltpu.VMEM)


def scalars():
    return pl.BlockSpec(memory_space=pltpu.SMEM)


def anywhere():
    return pl.BlockSpec(memory_space=pl.ANY)


def params(mib=48):
    return pltpu.CompilerParams(vmem_limit_bytes=mib << 20)


def cost(flops=0, bytes_accessed=0, transcendentals=0):
    return pl.CostEstimate(flops=flops, bytes_accessed=bytes_accessed, transcendentals=transcendentals)


def swap_halves(x):
    return lax.ppermute(x, "tv", [(0, 1), (1, 0)])


def to_partner(x, offset):
    return lax.ppermute(x, "sv", [(s, s ^ offset) for s in range(lax.axis_size("sv"))])


def body(teacher_probs, align_owner, align_local, align_weight, student_logits, hidden):
    owners = lax.axis_size("sv")
    halves = lax.axis_size("tv")
    half_index = lax.axis_index("tv")
    place = jnp.stack([lax.axis_index("sv"), half_index]).astype(jnp.int32)
    tokens = teacher_probs.shape[0]
    columns = student_logits.shape[1]
    blocks = columns // BLK
    mine = blocks // halves
    width = mine * BLK
    rows = owners * mine
    per_half = TB // halves
    group_tokens = owners * tokens
    half_tokens = student_logits.shape[0]
    features = hidden.shape[1]
    first = half_index == 0
    bf16, f32 = jnp.bfloat16, jnp.float32
    shape = jax.ShapeDtypeStruct
    dma = lambda count: pltpu.SemaphoreType.DMA((count,))

    def in_order(own, other, axis):
        return jnp.concatenate([jnp.where(first, own, other), jnp.where(first, other, own)], axis=axis)

    hidden = hidden[None]
    offset = owners // 2
    first_piece = to_partner(hidden, offset)

    def merge(one, two):
        top = jnp.maximum(one[0], two[0])
        return top, one[1] * jnp.exp(one[0] - top) + two[1] * jnp.exp(two[0] - top)

    wide = student_logits.astype(f32)
    low = jnp.float32(-1e38)
    stats = jnp.stack(lax.reduce((wide, jnp.ones_like(wide)), (low, jnp.float32(0)), merge, (1,)))
    teacher_given, stats = lax.optimization_barrier((teacher_probs, stats))
    teacher_other = swap_halves(teacher_given)
    stats = in_order(stats, swap_halves(stats), 1)

    local = align_local.T - half_index * mine
    row_of = jnp.where((local >= 0) & (local < mine), align_owner.T * mine + local, -1)
    code = row_of.astype(f32) + 0.5 * align_weight.T.astype(f32)
    cut = lambda which: lax.dynamic_slice_in_dim(code, which * per_half, per_half, 1)
    w_own = block_weights(cut(half_index), rows)
    w_rest = block_weights(cut(1 - half_index), rows)
    spread = pltpu.VMEM((per_half * tokens, BLK), f32)
    flops = 2 * (rows + MASS_ROWS) * per_half * tokens * BLK
    part = pl.pallas_call(
        map_own_kernel,
        out_shape=shape((rows + MASS_ROWS, tokens * BLK), f32),
        in_specs=[in_vmem()] * 2,
        out_specs=in_vmem(),
        scratch_shapes=[spread],
        compiler_params=params(),
        cost_estimate=cost(flops, 3 << 20),
        name="map_own",
    )(w_own, teacher_probs)
    chunk = (owners, tokens, width + group_tokens)
    outgoing = pl.pallas_call(
        map_rest_kernel,
        out_shape=shape(chunk, bf16),
        in_specs=[in_vmem()] * 4,
        out_specs=anywhere(),
        scratch_shapes=[
            spread,
            pltpu.VMEM(((rows + 8) * tokens, BLK), f32),
            pltpu.VMEM(chunk, bf16),
            dma(owners),
        ],
        compiler_params=params(),
        cost_estimate=cost(flops, 4 << 20),
        name="map_rest",
    )(w_rest, teacher_other, part, stats)
    outgoing, first_piece = lax.optimization_barrier((outgoing, first_piece))
    target = lax.all_to_all(outgoing, "sv", 0, 0, tiled=True)

    hidden, late_logits, outgoing = lax.optimization_barrier((hidden, student_logits, outgoing))

    keep = lax.dynamic_slice_in_dim(late_logits, half_index * width, width, 1)
    give = lax.dynamic_slice_in_dim(late_logits, (1 - half_index) * width, width, 1)
    logits = in_order(keep, swap_halves(give), 0)

    pieces = [jnp.concatenate([hidden, first_piece])]
    pieces += [to_partner(pieces[0], a) for a in range(1, offset)]

    scale = float(columns * owners)
    lanes = -(-half_tokens // BLK) * BLK
    grad, terms = pl.pallas_call(
        lambda *refs: grad_kernel(scale, *refs),
        out_shape=(shape((group_tokens, width), bf16), shape((owners * halves, 8, lanes), f32)),
        in_specs=[in_vmem()] * 2,
        out_specs=(in_vmem(), anywhere()),
        scratch_shapes=[
            pltpu.VMEM((group_tokens, BLK), f32),
            pltpu.VMEM((owners * halves, 8, lanes), f32),
            pltpu.SemaphoreType.DMA,
        ],
        compiler_params=params(),
        cost_estimate=cost(
            10 * group_tokens * width, 6 * group_tokens * width, 2 * group_tokens * width
        ),
        name="logit_grad",
    )(target, logits)

    terms = lax.all_to_all(terms, ("sv", "tv"), 0, 0, tiled=True)
    give = lax.dynamic_slice_in_dim(grad, (1 - half_index) * half_tokens, half_tokens, 0)
    got = swap_halves(give)

    *pieces, grad = lax.optimization_barrier((*pieces, grad))
    hidden_own = jnp.concatenate(pieces)
    steps = 8
    weight_grad, logit_grad = pl.pallas_call(
        weight_kernel,
        out_shape=(shape((features, width), bf16), shape((half_tokens, columns), bf16)),
        in_specs=[scalars()] + [in_vmem()] * 4,
        out_specs=(anywhere(), anywhere()),
        scratch_shapes=[
            pltpu.VMEM((group_tokens, features), f32),
            pltpu.VMEM((features, group_tokens), bf16),
            pltpu.VMEM((steps, features // steps, width), bf16),
            dma(steps),
            dma(2),
        ],
        compiler_params=params(),
        cost_estimate=cost(
            2 * features * group_tokens * width,
            2 * (features * width + group_tokens * (features + width)),
        ),
        name="weight_grad",
    )(place, hidden_own, swap_halves(hidden_own), grad, got)
    terms, logit_grad, weight_grad = lax.optimization_barrier((terms, logit_grad, weight_grad))
    divergence = jnp.sum(terms[:, 0, :half_tokens], axis=0)
    return (divergence, logit_grad, weight_grad)


def solution(mesh):
    return jax.shard_map(
        body,
        mesh=mesh,
        in_specs=(
            P(("grp", "sv"), "tv"),
            P(),
            P(),
            P(),
            P(("grp", "tv"), "sv"),
            P(("grp", "sv", "tv"), None),
        ),
        out_specs=(P(("grp", "tv")), P(("grp", "tv"), "sv"), P(None, ("grp", "sv", "tv"))),
        check_vma=False,
    )
```

```python
import jax
import jax.numpy as jnp
from jax import lax
from jax.experimental import pallas as pl
from jax.experimental.pallas import tpu as pltpu
from jax.sharding import PartitionSpec as P

BLK = 128
TB = 640
TOPA = 2
MASS_ROWS = 16
STEP = 16


def block_weights(code, rows):
    row_ids = lax.broadcasted_iota(jnp.int32, (rows + MASS_ROWS, code.shape[1]), 0)
    total = jnp.zeros(row_ids.shape, jnp.float32)
    for slot in range(TOPA):
        row = jnp.floor(code[slot])
        weight = (code[slot] - row) * 2.0
        hit = (row_ids == row.astype(jnp.int32)[None, :]) | (row_ids == rows + slot)
        total = total + jnp.where(hit, weight[None, :], 0.0)
    return total.astype(jnp.bfloat16)


def spread_tokens(t_ref, s_ref, start, count):
    tokens = t_ref.shape[0]

    def some(i, carry):
        for j in range(STEP):
            k = start + i * STEP + j
            tile = t_ref[:, pl.ds(pl.multiple_of(k * BLK, BLK), BLK)]
            s_ref[pl.ds(pl.multiple_of(k * tokens, tokens), tokens), :] = tile.astype(jnp.float32)
        return carry

    lax.fori_loop(0, count // STEP, some, 0)


def token_pair(s_ref, t, tokens):
    count = s_ref.shape[0] // tokens
    both = [s_ref[pl.ds(t + i, count, stride=tokens), :].astype(jnp.bfloat16) for i in range(2)]
    return jnp.concatenate(both, axis=1)


def map_own_kernel(w_ref, t_ref, o_ref, s_ref):
    tokens = t_ref.shape[0]
    spread_tokens(t_ref, s_ref, 0, t_ref.shape[1] // BLK)
    for t in range(0, tokens, 2):
        o_ref[:, t * BLK : (t + 2) * BLK] = jnp.dot(
            w_ref[...], token_pair(s_ref, t, tokens), preferred_element_type=jnp.float32
        )


def three_parts(x):
    parts = []
    for _ in range(3):
        parts.append(x.astype(jnp.bfloat16).astype(jnp.float32))
        x = x - parts[-1]
    return parts


def map_rest_kernel(w_ref, t_ref, p_ref, stats_ref, first_ref, o_ref, s_ref, m_ref, o_buf, out_sem):
    tokens = t_ref.shape[0]
    owners = o_ref.shape[0]
    rows = w_ref.shape[0] - MASS_ROWS
    mine = rows // owners
    stats = [stats_ref[0:1, :]] + three_parts(stats_ref[1:2, :])
    extra = jnp.zeros((tokens, stats_ref.shape[1]), jnp.float32)
    row_ids = lax.broadcasted_iota(jnp.int32, extra.shape, 0)
    for i, row in enumerate(stats):
        extra = jnp.where(row_ids == i, row, extra)
    extra = extra.astype(jnp.bfloat16)
    spread_tokens(t_ref, s_ref, 0, t_ref.shape[1] // BLK)
    for t in range(0, tokens, 2):
        both = p_ref[:, t * BLK : (t + 2) * BLK] + jnp.dot(
            w_ref[...], token_pair(s_ref, t, tokens), preferred_element_type=jnp.float32
        )
        for i in range(2):
            m_ref[pl.ds(t + i, rows + 8, stride=tokens), :] = both[: rows + 8, i * BLK : (i + 1) * BLK]
    mass = m_ref[rows * tokens : (rows + 1) * tokens, :]
    for slot in range(1, TOPA):
        mass = mass + m_ref[(rows + slot) * tokens : (rows + slot + 1) * tokens, :]
    inverse = jnp.broadcast_to(1.0 / jnp.sum(mass, axis=1, keepdims=True), (tokens, BLK))

    def leaving(q):
        return pltpu.make_async_copy(o_buf.at[q], o_ref.at[q], out_sem.at[q])

    def owner(q, carry):
        for b in range(mine):
            first = pl.multiple_of((q * mine + b) * tokens, tokens)
            tile = m_ref[pl.ds(first, tokens), :] * inverse
            o_buf[q, :, b * BLK : (b + 1) * BLK] = tile.astype(jnp.bfloat16)
        o_buf[q, :, mine * BLK :] = extra
        leaving(q).start()
        return carry

    def left(q, carry):
        leaving(q).wait()
        return carry

    lax.fori_loop(0, owners, owner, 0)
    lax.fori_loop(0, owners, left, 0)


def grad_kernel(scale, target_ref, logits_ref, grad_ref, terms_ref, norm_ref, t_buf, sem):
    owners, tokens, _ = target_ref.shape
    group_tokens, width = logits_ref.shape
    stats = [target_ref[q, :, width:].astype(jnp.float32) for q in range(owners)]
    top = stats[0][0:1]
    for one in stats[1:]:
        top = jnp.maximum(top, one[0:1])
    total = jnp.zeros_like(top)
    for one in stats:
        total = total + (one[1:2] + one[2:3] + one[3:4]) * jnp.exp(one[0:1] - top)
    log_norm = top + jnp.log(total)

    def block(i, b):
        lanes = slice(b * BLK, (b + 1) * BLK)
        group = slice(i * BLK // tokens, (i + 1) * BLK // tokens)
        target = target_ref[group, :, lanes].reshape(BLK, BLK).astype(jnp.float32)
        return target, logits_ref[i * BLK : (i + 1) * BLK, lanes].astype(jnp.float32)

    sums = []
    for i in range(group_tokens // BLK):
        rows = slice(i * BLK, (i + 1) * BLK)
        norm = jnp.broadcast_to(log_norm[:, rows], (BLK, BLK)).T
        norm_ref[rows, :] = norm
        terms = jnp.zeros((BLK, BLK), jnp.float32)
        for b in range(width // BLK):
            target, logits = block(i, b)
            positive = target > 0
            one = target * (jnp.log(jnp.where(positive, target, 1.0)) - (logits - norm))
            terms = terms + jnp.where(positive, one, 0.0)
        sums.append(jnp.sum(terms.T, axis=0, keepdims=True))
    row = jnp.concatenate(sums, axis=1)
    half_tokens = group_tokens // 2
    for half in range(2):
        mine = row[:, half * half_tokens : (half + 1) * half_tokens]
        tile = jnp.concatenate([mine] * (t_buf.shape[2] // half_tokens), axis=1)
        for q in range(owners):
            t_buf[2 * q + half] = jnp.broadcast_to(tile, t_buf.shape[1:])
    leaving = pltpu.make_async_copy(t_buf, terms_ref, sem)
    leaving.start()
    for i in range(group_tokens // BLK):
        rows = slice(i * BLK, (i + 1) * BLK)
        for b in range(width // BLK):
            target, logits = block(i, b)
            grad = (jnp.exp(logits - norm_ref[rows, :]) - target) * scale
            grad_ref[rows, b * BLK : (b + 1) * BLK] = grad.astype(jnp.bfloat16)
    leaving.wait()


def arrival_order(owners):
    return [a for b in range(owners // 2) for a in (b, b + owners // 2)]


def weight_kernel(
    place_ref, own_ref, other_ref, grad_ref, got_ref, o_ref, joined_ref, s_ref, h_ref, block_ref, sems, join_sems
):
    half_tokens, width = got_ref.shape
    half = place_ref[1]
    kept_at = pl.ds(pl.multiple_of(half * width, width), width)
    got_at = pl.ds(pl.multiple_of((1 - half) * width, width), width)
    kept = pl.ds(pl.multiple_of(half * half_tokens, half_tokens), half_tokens)
    copies = [
        pltpu.make_async_copy(grad_ref.at[kept, :], joined_ref.at[:, kept_at], join_sems.at[0]),
        pltpu.make_async_copy(got_ref, joined_ref.at[:, got_at], join_sems.at[1]),
    ]
    for copy in copies:
        copy.start()
    owners, held, features = own_ref.shape
    for i, offset in enumerate(arrival_order(owners)):
        first = (place_ref[0] ^ offset) * 2
        own = pl.ds(pl.multiple_of((first + half) * held, held), held)
        other = pl.ds(pl.multiple_of((first + 1 - half) * held, held), held)
        s_ref[own, :] = own_ref[i].astype(jnp.float32)
        s_ref[other, :] = other_ref[i].astype(jnp.float32)
    for i in range(s_ref.shape[0] // BLK):
        for j in range(features // BLK):
            tile = s_ref[i * BLK : (i + 1) * BLK, j * BLK : (j + 1) * BLK].T
            h_ref[j * BLK : (j + 1) * BLK, i * BLK : (i + 1) * BLK] = tile.astype(jnp.bfloat16)
    steps, tile, _ = block_ref.shape
    for i in range(steps):
        rows = slice(i * tile, (i + 1) * tile)
        block_ref[i] = jnp.dot(
            h_ref[rows, :], grad_ref[...], preferred_element_type=jnp.float32
        ).astype(jnp.bfloat16)
        copies.append(pltpu.make_async_copy(block_ref.at[i], o_ref.at[pl.ds(i * tile, tile), :], sems.at[i]))
        copies[-1].start()
    for copy in copies:
        copy.wait()


def in_vmem():
    return pl.BlockSpec(memory_space=pltpu.VMEM)


def scalars():
    return pl.BlockSpec(memory_space=pltpu.SMEM)


def anywhere():
    return pl.BlockSpec(memory_space=pl.ANY)


def params(mib=24):
    return pltpu.CompilerParams(vmem_limit_bytes=mib << 20)


def cost(flops=0, bytes_accessed=0, transcendentals=0):
    return pl.CostEstimate(flops=flops, bytes_accessed=bytes_accessed, transcendentals=transcendentals)


def swap_halves(x):
    return lax.ppermute(x, "tv", [(0, 1), (1, 0)])


def to_partner(x, offset):
    return lax.ppermute(x, "sv", [(s, s ^ offset) for s in range(lax.axis_size("sv"))])


def body(teacher_probs, align_owner, align_local, align_weight, student_logits, hidden):
    owners = lax.axis_size("sv")
    halves = lax.axis_size("tv")
    half_index = lax.axis_index("tv")
    place = jnp.stack([lax.axis_index("sv"), half_index]).astype(jnp.int32)
    tokens = teacher_probs.shape[0]
    columns = student_logits.shape[1]
    blocks = columns // BLK
    mine = blocks // halves
    width = mine * BLK
    rows = owners * mine
    per_half = TB // halves
    group_tokens = owners * tokens
    half_tokens = student_logits.shape[0]
    features = hidden.shape[1]
    first = half_index == 0
    bf16, f32 = jnp.bfloat16, jnp.float32
    shape = jax.ShapeDtypeStruct
    dma = lambda count: pltpu.SemaphoreType.DMA((count,))

    def in_order(own, other, axis):
        return jnp.concatenate([jnp.where(first, own, other), jnp.where(first, other, own)], axis=axis)

    hidden = hidden[None]
    offset = owners // 2
    first_piece = to_partner(hidden, offset)

    def merge(one, two):
        top = jnp.maximum(one[0], two[0])
        return top, one[1] * jnp.exp(one[0] - top) + two[1] * jnp.exp(two[0] - top)

    wide = student_logits.astype(f32)
    low = jnp.float32(-1e38)
    stats = jnp.stack(lax.reduce((wide, jnp.ones_like(wide)), (low, jnp.float32(0)), merge, (1,)))
    teacher_given, stats = lax.optimization_barrier((teacher_probs, stats))
    teacher_other = swap_halves(teacher_given)
    stats = in_order(stats, swap_halves(stats), 1)

    local = align_local.T - half_index * mine
    row_of = jnp.where((local >= 0) & (local < mine), align_owner.T * mine + local, -1)
    code = row_of.astype(f32) + 0.5 * align_weight.T.astype(f32)
    cut = lambda which: lax.dynamic_slice_in_dim(code, which * per_half, per_half, 1)
    w_own = block_weights(cut(half_index), rows)
    w_rest = block_weights(cut(1 - half_index), rows)
    spread = pltpu.VMEM((per_half * tokens, BLK), f32)
    flops = 2 * (rows + MASS_ROWS) * per_half * tokens * BLK
    part = pl.pallas_call(
        map_own_kernel,
        out_shape=shape((rows + MASS_ROWS, tokens * BLK), f32),
        in_specs=[in_vmem()] * 2,
        out_specs=in_vmem(),
        scratch_shapes=[spread],
        compiler_params=params(),
        cost_estimate=cost(flops, 3 << 20),
        name="map_own",
    )(w_own, teacher_probs)
    chunk = (owners, tokens, width + group_tokens)
    outgoing = pl.pallas_call(
        map_rest_kernel,
        out_shape=shape(chunk, bf16),
        in_specs=[in_vmem()] * 4 + [anywhere()],
        out_specs=anywhere(),
        scratch_shapes=[
            spread,
            pltpu.VMEM(((rows + 8) * tokens, BLK), f32),
            pltpu.VMEM(chunk, bf16),
            dma(owners),
        ],
        compiler_params=params(),
        cost_estimate=cost(flops, 4 << 20),
        name="map_rest",
    )(w_rest, teacher_other, part, stats, first_piece)
    target = lax.all_to_all(outgoing, "sv", 0, 0, tiled=True)

    hidden, late_logits, outgoing = lax.optimization_barrier((hidden, student_logits, outgoing))

    keep = lax.dynamic_slice_in_dim(late_logits, half_index * width, width, 1)
    give = lax.dynamic_slice_in_dim(late_logits, (1 - half_index) * width, width, 1)
    logits = in_order(keep, swap_halves(give), 0)

    pieces = [jnp.concatenate([hidden, first_piece])]
    pieces += [to_partner(pieces[0], a) for a in range(1, offset)]

    scale = float(columns * owners)
    lanes = -(-half_tokens // BLK) * BLK
    grad, terms = pl.pallas_call(
        lambda *refs: grad_kernel(scale, *refs),
        out_shape=(shape((group_tokens, width), bf16), shape((owners * halves, 8, lanes), f32)),
        in_specs=[in_vmem()] * 2,
        out_specs=(in_vmem(), anywhere()),
        scratch_shapes=[
            pltpu.VMEM((group_tokens, BLK), f32),
            pltpu.VMEM((owners * halves, 8, lanes), f32),
            pltpu.SemaphoreType.DMA,
        ],
        compiler_params=params(),
        cost_estimate=cost(
            10 * group_tokens * width, 6 * group_tokens * width, 2 * group_tokens * width
        ),
        name="logit_grad",
    )(target, logits)

    terms = lax.all_to_all(terms, ("sv", "tv"), 0, 0, tiled=True)
    give = lax.dynamic_slice_in_dim(grad, (1 - half_index) * half_tokens, half_tokens, 0)
    got = swap_halves(give)

    *pieces, grad = lax.optimization_barrier((*pieces, grad))
    hidden_own = jnp.concatenate(pieces)
    steps = 8
    weight_grad, logit_grad = pl.pallas_call(
        weight_kernel,
        out_shape=(shape((features, width), bf16), shape((half_tokens, columns), bf16)),
        in_specs=[scalars()] + [in_vmem()] * 4,
        out_specs=(anywhere(), anywhere()),
        scratch_shapes=[
            pltpu.VMEM((group_tokens, features), f32),
            pltpu.VMEM((features, group_tokens), bf16),
            pltpu.VMEM((steps, features // steps, width), bf16),
            dma(steps),
            dma(2),
        ],
        compiler_params=params(32),
        cost_estimate=cost(
            2 * features * group_tokens * width,
            2 * (features * width + group_tokens * (features + width)),
        ),
        name="weight_grad",
    )(place, hidden_own, swap_halves(hidden_own), grad, got)
    terms, logit_grad, weight_grad = lax.optimization_barrier((terms, logit_grad, weight_grad))
    divergence = jnp.sum(terms[:, 0, :half_tokens], axis=0)
    return (divergence, logit_grad, weight_grad)


def solution(mesh):
    return jax.shard_map(
        body,
        mesh=mesh,
        in_specs=(
            P(("grp", "sv"), "tv"),
            P(),
            P(),
            P(),
            P(("grp", "tv"), "sv"),
            P(("grp", "sv", "tv"), None),
        ),
        out_specs=(P(("grp", "tv")), P(("grp", "tv"), "sv"), P(None, ("grp", "sv", "tv"))),
        check_vma=False,
    )
```

```python
import jax
import jax.numpy as jnp
from jax import lax
from jax.experimental import pallas as pl
from jax.experimental.pallas import tpu as pltpu
from jax.sharding import PartitionSpec as P

BLK = 128
TB = 640
TOPA = 2
MASS_ROWS = 16
STEP = 16


def block_weights(code, rows):
    row_ids = lax.broadcasted_iota(jnp.int32, (rows + MASS_ROWS, code.shape[1]), 0)
    total = jnp.zeros(row_ids.shape, jnp.float32)
    for slot in range(TOPA):
        row = jnp.floor(code[slot])
        weight = (code[slot] - row) * 2.0
        hit = (row_ids == row.astype(jnp.int32)[None, :]) | (row_ids == rows + slot)
        total = total + jnp.where(hit, weight[None, :], 0.0)
    return total.astype(jnp.bfloat16)


def spread_tokens(t_ref, s_ref, start, count):
    tokens = t_ref.shape[0]

    def some(i, carry):
        for j in range(STEP):
            k = start + i * STEP + j
            tile = t_ref[:, pl.ds(pl.multiple_of(k * BLK, BLK), BLK)]
            s_ref[pl.ds(pl.multiple_of(k * tokens, tokens), tokens), :] = tile.astype(jnp.float32)
        return carry

    lax.fori_loop(0, count // STEP, some, 0)


def token_pair(s_ref, t, tokens):
    count = s_ref.shape[0] // tokens
    both = [s_ref[pl.ds(t + i, count, stride=tokens), :].astype(jnp.bfloat16) for i in range(2)]
    return jnp.concatenate(both, axis=1)


def map_own_kernel(w_ref, t_ref, o_ref, s_ref):
    tokens = t_ref.shape[0]
    spread_tokens(t_ref, s_ref, 0, t_ref.shape[1] // BLK)
    for t in range(0, tokens, 2):
        o_ref[:, t * BLK : (t + 2) * BLK] = jnp.dot(
            w_ref[...], token_pair(s_ref, t, tokens), preferred_element_type=jnp.float32
        )


def three_parts(x):
    parts = []
    for _ in range(3):
        parts.append(x.astype(jnp.bfloat16).astype(jnp.float32))
        x = x - parts[-1]
    return parts


def map_rest_kernel(w_ref, t_ref, p_ref, stats_ref, first_ref, o_ref, s_ref, m_ref, o_buf, out_sem):
    tokens = t_ref.shape[0]
    owners = o_ref.shape[0]
    rows = w_ref.shape[0] - MASS_ROWS
    mine = rows // owners
    stats = [stats_ref[0:1, :]] + three_parts(stats_ref[1:2, :])
    extra = jnp.zeros((tokens, stats_ref.shape[1]), jnp.float32)
    row_ids = lax.broadcasted_iota(jnp.int32, extra.shape, 0)
    for i, row in enumerate(stats):
        extra = jnp.where(row_ids == i, row, extra)
    extra = extra.astype(jnp.bfloat16)
    spread_tokens(t_ref, s_ref, 0, t_ref.shape[1] // BLK)
    for t in range(0, tokens, 2):
        both = p_ref[:, t * BLK : (t + 2) * BLK] + jnp.dot(
            w_ref[...], token_pair(s_ref, t, tokens), preferred_element_type=jnp.float32
        )
        for i in range(2):
            m_ref[pl.ds(t + i, rows + 8, stride=tokens), :] = both[: rows + 8, i * BLK : (i + 1) * BLK]
    mass = m_ref[rows * tokens : (rows + 1) * tokens, :]
    for slot in range(1, TOPA):
        mass = mass + m_ref[(rows + slot) * tokens : (rows + slot + 1) * tokens, :]
    inverse = jnp.broadcast_to(1.0 / jnp.sum(mass, axis=1, keepdims=True), (tokens, BLK))

    def leaving(q):
        return pltpu.make_async_copy(o_buf.at[q], o_ref.at[q], out_sem.at[q])

    def owner(q, carry):
        for b in range(mine):
            first = pl.multiple_of((q * mine + b) * tokens, tokens)
            tile = m_ref[pl.ds(first, tokens), :] * inverse
            o_buf[q, :, b * BLK : (b + 1) * BLK] = tile.astype(jnp.bfloat16)
        o_buf[q, :, mine * BLK :] = extra
        leaving(q).start()
        return carry

    def left(q, carry):
        leaving(q).wait()
        return carry

    lax.fori_loop(0, owners, owner, 0)
    lax.fori_loop(0, owners, left, 0)


def grad_kernel(scale, target_ref, logits_ref, grad_ref, terms_ref, norm_ref, t_buf, sem):
    owners, tokens, _ = target_ref.shape
    group_tokens, width = logits_ref.shape
    stats = [target_ref[q, :, width:].astype(jnp.float32) for q in range(owners)]
    top = stats[0][0:1]
    for one in stats[1:]:
        top = jnp.maximum(top, one[0:1])
    total = jnp.zeros_like(top)
    for one in stats:
        total = total + (one[1:2] + one[2:3] + one[3:4]) * jnp.exp(one[0:1] - top)
    log_norm = top + jnp.log(total)

    def block(i, b):
        lanes = slice(b * BLK, (b + 1) * BLK)
        group = slice(i * BLK // tokens, (i + 1) * BLK // tokens)
        target = target_ref[group, :, lanes].reshape(BLK, BLK).astype(jnp.float32)
        return target, logits_ref[i * BLK : (i + 1) * BLK, lanes].astype(jnp.float32)

    sums = []
    for i in range(group_tokens // BLK):
        rows = slice(i * BLK, (i + 1) * BLK)
        norm = jnp.broadcast_to(log_norm[:, rows], (BLK, BLK)).T
        norm_ref[rows, :] = norm
        terms = jnp.zeros((BLK, BLK), jnp.float32)
        for b in range(width // BLK):
            target, logits = block(i, b)
            positive = target > 0
            one = target * (jnp.log(jnp.where(positive, target, 1.0)) - (logits - norm))
            terms = terms + jnp.where(positive, one, 0.0)
        sums.append(jnp.sum(terms.T, axis=0, keepdims=True))
    row = jnp.concatenate(sums, axis=1)
    half_tokens = group_tokens // 2
    for half in range(2):
        mine = row[:, half * half_tokens : (half + 1) * half_tokens]
        tile = jnp.concatenate([mine] * (t_buf.shape[2] // half_tokens), axis=1)
        for q in range(owners):
            t_buf[2 * q + half] = jnp.broadcast_to(tile, t_buf.shape[1:])
    leaving = pltpu.make_async_copy(t_buf, terms_ref, sem)
    leaving.start()
    for i in range(group_tokens // BLK):
        rows = slice(i * BLK, (i + 1) * BLK)
        for b in range(width // BLK):
            target, logits = block(i, b)
            grad = (jnp.exp(logits - norm_ref[rows, :]) - target) * scale
            grad_ref[rows, b * BLK : (b + 1) * BLK] = grad.astype(jnp.bfloat16)
    leaving.wait()


def arrival_order(owners):
    return [a for b in range(owners // 2) for a in (b, b + owners // 2)]


def weight_kernel(
    place_ref, own_ref, other_ref, grad_ref, got_ref, o_ref, joined_ref, s_ref, h_ref, block_ref, sems, join_sems
):
    half_tokens, width = got_ref.shape
    half = place_ref[1]
    kept_at = pl.ds(pl.multiple_of(half * width, width), width)
    got_at = pl.ds(pl.multiple_of((1 - half) * width, width), width)
    kept = pl.ds(pl.multiple_of(half * half_tokens, half_tokens), half_tokens)
    copies = [
        pltpu.make_async_copy(grad_ref.at[kept, :], joined_ref.at[:, kept_at], join_sems.at[0]),
        pltpu.make_async_copy(got_ref, joined_ref.at[:, got_at], join_sems.at[1]),
    ]
    for copy in copies:
        copy.start()
    owners, held, features = own_ref.shape
    for i, offset in enumerate(arrival_order(owners)):
        first = (place_ref[0] ^ offset) * 2
        own = pl.ds(pl.multiple_of((first + half) * held, held), held)
        other = pl.ds(pl.multiple_of((first + 1 - half) * held, held), held)
        s_ref[own, :] = own_ref[i].astype(jnp.float32)
        s_ref[other, :] = other_ref[i].astype(jnp.float32)
    for i in range(s_ref.shape[0] // BLK):
        for j in range(features // BLK):
            tile = s_ref[i * BLK : (i + 1) * BLK, j * BLK : (j + 1) * BLK].T
            h_ref[j * BLK : (j + 1) * BLK, i * BLK : (i + 1) * BLK] = tile.astype(jnp.bfloat16)
    steps, tile, _ = block_ref.shape
    for i in range(steps):
        rows = slice(i * tile, (i + 1) * tile)
        block_ref[i] = jnp.dot(
            h_ref[rows, :], grad_ref[...], preferred_element_type=jnp.float32
        ).astype(jnp.bfloat16)
        copies.append(pltpu.make_async_copy(block_ref.at[i], o_ref.at[pl.ds(i * tile, tile), :], sems.at[i]))
        copies[-1].start()
    for copy in copies:
        copy.wait()


def in_vmem():
    return pl.BlockSpec(memory_space=pltpu.VMEM)


def scalars():
    return pl.BlockSpec(memory_space=pltpu.SMEM)


def anywhere():
    return pl.BlockSpec(memory_space=pl.ANY)


def params(mib=48):
    return pltpu.CompilerParams(vmem_limit_bytes=mib << 20)


def cost(flops=0, bytes_accessed=0, transcendentals=0):
    return pl.CostEstimate(flops=flops, bytes_accessed=bytes_accessed, transcendentals=transcendentals)


def swap_halves(x):
    return lax.ppermute(x, "tv", [(0, 1), (1, 0)])


def to_partner(x, offset):
    return lax.ppermute(x, "sv", [(s, s ^ offset) for s in range(lax.axis_size("sv"))])


def body(teacher_probs, align_owner, align_local, align_weight, student_logits, hidden):
    owners = lax.axis_size("sv")
    halves = lax.axis_size("tv")
    half_index = lax.axis_index("tv")
    place = jnp.stack([lax.axis_index("sv"), half_index]).astype(jnp.int32)
    tokens = teacher_probs.shape[0]
    columns = student_logits.shape[1]
    blocks = columns // BLK
    mine = blocks // halves
    width = mine * BLK
    rows = owners * mine
    per_half = TB // halves
    group_tokens = owners * tokens
    half_tokens = student_logits.shape[0]
    features = hidden.shape[1]
    first = half_index == 0
    bf16, f32 = jnp.bfloat16, jnp.float32
    shape = jax.ShapeDtypeStruct
    dma = lambda count: pltpu.SemaphoreType.DMA((count,))

    def in_order(own, other, axis):
        return jnp.concatenate([jnp.where(first, own, other), jnp.where(first, other, own)], axis=axis)

    hidden = hidden[None]
    offset = owners // 2
    first_piece = to_partner(hidden, offset)

    def merge(one, two):
        top = jnp.maximum(one[0], two[0])
        return top, one[1] * jnp.exp(one[0] - top) + two[1] * jnp.exp(two[0] - top)

    wide = student_logits.astype(f32)
    low = jnp.float32(-1e38)
    stats = jnp.stack(lax.reduce((wide, jnp.ones_like(wide)), (low, jnp.float32(0)), merge, (1,)))
    teacher_given, stats = lax.optimization_barrier((teacher_probs, stats))
    teacher_other = swap_halves(teacher_given)
    stats = in_order(stats, swap_halves(stats), 1)

    local = align_local.T - half_index * mine
    row_of = jnp.where((local >= 0) & (local < mine), align_owner.T * mine + local, -1)
    code = row_of.astype(f32) + 0.5 * align_weight.T.astype(f32)
    cut = lambda which: lax.dynamic_slice_in_dim(code, which * per_half, per_half, 1)
    w_own = block_weights(cut(half_index), rows)
    w_rest = block_weights(cut(1 - half_index), rows)
    spread = pltpu.VMEM((per_half * tokens, BLK), f32)
    flops = 2 * (rows + MASS_ROWS) * per_half * tokens * BLK
    part = pl.pallas_call(
        map_own_kernel,
        out_shape=shape((rows + MASS_ROWS, tokens * BLK), f32),
        in_specs=[in_vmem()] * 2,
        out_specs=in_vmem(),
        scratch_shapes=[spread],
        compiler_params=params(),
        cost_estimate=cost(flops, 3 << 20),
        name="map_own",
    )(w_own, teacher_probs)
    chunk = (owners, tokens, width + group_tokens)
    outgoing = pl.pallas_call(
        map_rest_kernel,
        out_shape=shape(chunk, bf16),
        in_specs=[in_vmem()] * 4 + [anywhere()],
        out_specs=anywhere(),
        scratch_shapes=[
            spread,
            pltpu.VMEM(((rows + 8) * tokens, BLK), f32),
            pltpu.VMEM(chunk, bf16),
            dma(owners),
        ],
        compiler_params=params(),
        cost_estimate=cost(flops, 4 << 20),
        name="map_rest",
    )(w_rest, teacher_other, part, stats, first_piece)
    target = lax.all_to_all(outgoing, "sv", 0, 0, tiled=True)

    hidden, late_logits, outgoing = lax.optimization_barrier((hidden, student_logits, outgoing))

    keep = lax.dynamic_slice_in_dim(late_logits, half_index * width, width, 1)
    give = lax.dynamic_slice_in_dim(late_logits, (1 - half_index) * width, width, 1)
    logits = in_order(keep, swap_halves(give), 0)

    pieces = [jnp.concatenate([hidden, first_piece])]
    pieces += [to_partner(pieces[0], a) for a in range(1, offset)]

    scale = float(columns * owners)
    lanes = -(-half_tokens // BLK) * BLK
    grad, terms = pl.pallas_call(
        lambda *refs: grad_kernel(scale, *refs),
        out_shape=(shape((group_tokens, width), bf16), shape((owners * halves, 8, lanes), f32)),
        in_specs=[in_vmem()] * 2,
        out_specs=(in_vmem(), anywhere()),
        scratch_shapes=[
            pltpu.VMEM((group_tokens, BLK), f32),
            pltpu.VMEM((owners * halves, 8, lanes), f32),
            pltpu.SemaphoreType.DMA,
        ],
        compiler_params=params(),
        cost_estimate=cost(
            10 * group_tokens * width, 6 * group_tokens * width, 2 * group_tokens * width
        ),
        name="logit_grad",
    )(target, logits)

    terms = lax.all_to_all(terms, ("sv", "tv"), 0, 0, tiled=True)
    give = lax.dynamic_slice_in_dim(grad, (1 - half_index) * half_tokens, half_tokens, 0)
    got = swap_halves(give)

    *pieces, grad = lax.optimization_barrier((*pieces, grad))
    hidden_own = jnp.concatenate(pieces)
    steps = 8
    weight_grad, logit_grad = pl.pallas_call(
        weight_kernel,
        out_shape=(shape((features, width), bf16), shape((half_tokens, columns), bf16)),
        in_specs=[scalars()] + [in_vmem()] * 4,
        out_specs=(anywhere(), anywhere()),
        scratch_shapes=[
            pltpu.VMEM((group_tokens, features), f32),
            pltpu.VMEM((features, group_tokens), bf16),
            pltpu.VMEM((steps, features // steps, width), bf16),
            dma(steps),
            dma(2),
        ],
        compiler_params=params(),
        cost_estimate=cost(
            2 * features * group_tokens * width,
            2 * (features * width + group_tokens * (features + width)),
        ),
        name="weight_grad",
    )(place, hidden_own, swap_halves(hidden_own), grad, got)
    terms, logit_grad, weight_grad = lax.optimization_barrier((terms, logit_grad, weight_grad))
    divergence = jnp.sum(terms[:, 0, :half_tokens], axis=0)
    return (divergence, logit_grad, weight_grad)


def solution(mesh):
    return jax.shard_map(
        body,
        mesh=mesh,
        in_specs=(
            P(("grp", "sv"), "tv"),
            P(),
            P(),
            P(),
            P(("grp", "tv"), "sv"),
            P(("grp", "sv", "tv"), None),
        ),
        out_specs=(P(("grp", "tv")), P(("grp", "tv"), "sv"), P(None, ("grp", "sv", "tv"))),
        check_vma=False,
    )
```

```python
import jax
import jax.numpy as jnp
from jax import lax
from jax.experimental import pallas as pl
from jax.experimental.pallas import tpu as pltpu
from jax.sharding import PartitionSpec as P

BLK = 128
TB = 640
TOPA = 2
MASS_ROWS = 16
STEP = 16


def block_weights(code, rows):
    row_ids = lax.broadcasted_iota(jnp.int32, (rows + MASS_ROWS, code.shape[1]), 0)
    total = jnp.zeros(row_ids.shape, jnp.float32)
    for slot in range(TOPA):
        row = jnp.floor(code[slot])
        weight = (code[slot] - row) * 2.0
        hit = (row_ids == row.astype(jnp.int32)[None, :]) | (row_ids == rows + slot)
        total = total + jnp.where(hit, weight[None, :], 0.0)
    return total.astype(jnp.bfloat16)


def spread_tokens(t_ref, s_ref, start, count):
    tokens = t_ref.shape[0]

    def some(i, carry):
        for j in range(STEP):
            k = start + i * STEP + j
            tile = t_ref[:, pl.ds(pl.multiple_of(k * BLK, BLK), BLK)]
            s_ref[pl.ds(pl.multiple_of(k * tokens, tokens), tokens), :] = tile.astype(jnp.float32)
        return carry

    lax.fori_loop(0, count // STEP, some, 0)


def token_pair(s_ref, t, tokens):
    count = s_ref.shape[0] // tokens
    both = [s_ref[pl.ds(t + i, count, stride=tokens), :].astype(jnp.bfloat16) for i in range(2)]
    return jnp.concatenate(both, axis=1)


def map_own_kernel(w_ref, t_ref, stats_ref, o_ref, s_ref):
    tokens = t_ref.shape[0]
    spread_tokens(t_ref, s_ref, 0, t_ref.shape[1] // BLK)
    for t in range(0, tokens, 2):
        o_ref[:, t * BLK : (t + 2) * BLK] = jnp.dot(
            w_ref[...], token_pair(s_ref, t, tokens), preferred_element_type=jnp.float32
        )


def three_parts(x):
    parts = []
    for _ in range(3):
        parts.append(x.astype(jnp.bfloat16).astype(jnp.float32))
        x = x - parts[-1]
    return parts


def map_rest_kernel(w_ref, t_ref, p_ref, stats_ref, first_ref, o_ref, s_ref, m_ref, o_buf, out_sem):
    tokens = t_ref.shape[0]
    owners = o_ref.shape[0]
    rows = w_ref.shape[0] - MASS_ROWS
    mine = rows // owners
    stats = [stats_ref[0:1, :]] + three_parts(stats_ref[1:2, :])
    extra = jnp.zeros((tokens, stats_ref.shape[1]), jnp.float32)
    row_ids = lax.broadcasted_iota(jnp.int32, extra.shape, 0)
    for i, row in enumerate(stats):
        extra = jnp.where(row_ids == i, row, extra)
    extra = extra.astype(jnp.bfloat16)
    spread_tokens(t_ref, s_ref, 0, t_ref.shape[1] // BLK)
    for t in range(0, tokens, 2):
        both = p_ref[:, t * BLK : (t + 2) * BLK] + jnp.dot(
            w_ref[...], token_pair(s_ref, t, tokens), preferred_element_type=jnp.float32
        )
        for i in range(2):
            m_ref[pl.ds(t + i, rows + 8, stride=tokens), :] = both[: rows + 8, i * BLK : (i + 1) * BLK]
    mass = m_ref[rows * tokens : (rows + 1) * tokens, :]
    for slot in range(1, TOPA):
        mass = mass + m_ref[(rows + slot) * tokens : (rows + slot + 1) * tokens, :]
    inverse = jnp.broadcast_to(1.0 / jnp.sum(mass, axis=1, keepdims=True), (tokens, BLK))

    def leaving(q):
        return pltpu.make_async_copy(o_buf.at[q], o_ref.at[q], out_sem.at[q])

    def owner(q, carry):
        for b in range(mine):
            first = pl.multiple_of((q * mine + b) * tokens, tokens)
            tile = m_ref[pl.ds(first, tokens), :] * inverse
            o_buf[q, :, b * BLK : (b + 1) * BLK] = tile.astype(jnp.bfloat16)
        o_buf[q, :, mine * BLK :] = extra
        leaving(q).start()
        return carry

    def left(q, carry):
        leaving(q).wait()
        return carry

    lax.fori_loop(0, owners, owner, 0)
    lax.fori_loop(0, owners, left, 0)


def grad_kernel(scale, target_ref, logits_ref, grad_ref, terms_ref, norm_ref, t_buf, sem):
    owners, tokens, _ = target_ref.shape
    group_tokens, width = logits_ref.shape
    stats = [target_ref[q, :, width:].astype(jnp.float32) for q in range(owners)]
    top = stats[0][0:1]
    for one in stats[1:]:
        top = jnp.maximum(top, one[0:1])
    total = jnp.zeros_like(top)
    for one in stats:
        total = total + (one[1:2] + one[2:3] + one[3:4]) * jnp.exp(one[0:1] - top)
    log_norm = top + jnp.log(total)

    def block(i, b):
        lanes = slice(b * BLK, (b + 1) * BLK)
        group = slice(i * BLK // tokens, (i + 1) * BLK // tokens)
        target = target_ref[group, :, lanes].reshape(BLK, BLK).astype(jnp.float32)
        return target, logits_ref[i * BLK : (i + 1) * BLK, lanes].astype(jnp.float32)

    sums = []
    for i in range(group_tokens // BLK):
        rows = slice(i * BLK, (i + 1) * BLK)
        norm = jnp.broadcast_to(log_norm[:, rows], (BLK, BLK)).T
        norm_ref[rows, :] = norm
        terms = jnp.zeros((BLK, BLK), jnp.float32)
        for b in range(width // BLK):
            target, logits = block(i, b)
            positive = target > 0
            one = target * (jnp.log(jnp.where(positive, target, 1.0)) - (logits - norm))
            terms = terms + jnp.where(positive, one, 0.0)
        sums.append(jnp.sum(terms.T, axis=0, keepdims=True))
    row = jnp.concatenate(sums, axis=1)
    half_tokens = group_tokens // 2
    for half in range(2):
        mine = row[:, half * half_tokens : (half + 1) * half_tokens]
        tile = jnp.concatenate([mine] * (t_buf.shape[2] // half_tokens), axis=1)
        for q in range(owners):
            t_buf[2 * q + half] = jnp.broadcast_to(tile, t_buf.shape[1:])
    leaving = pltpu.make_async_copy(t_buf, terms_ref, sem)
    leaving.start()
    for i in range(group_tokens // BLK):
        rows = slice(i * BLK, (i + 1) * BLK)
        for b in range(width // BLK):
            target, logits = block(i, b)
            grad = (jnp.exp(logits - norm_ref[rows, :]) - target) * scale
            grad_ref[rows, b * BLK : (b + 1) * BLK] = grad.astype(jnp.bfloat16)
    leaving.wait()


def arrival_order(owners):
    return [a for b in range(owners // 2) for a in (b, b + owners // 2)]


def weight_kernel(
    place_ref, own_ref, other_ref, grad_ref, got_ref, o_ref, joined_ref, s_ref, h_ref, block_ref, sems, join_sems
):
    half_tokens, width = got_ref.shape
    half = place_ref[1]
    kept_at = pl.ds(pl.multiple_of(half * width, width), width)
    got_at = pl.ds(pl.multiple_of((1 - half) * width, width), width)
    kept = pl.ds(pl.multiple_of(half * half_tokens, half_tokens), half_tokens)
    copies = [
        pltpu.make_async_copy(grad_ref.at[kept, :], joined_ref.at[:, kept_at], join_sems.at[0]),
        pltpu.make_async_copy(got_ref, joined_ref.at[:, got_at], join_sems.at[1]),
    ]
    for copy in copies:
        copy.start()
    owners, held, features = own_ref.shape
    for i, offset in enumerate(arrival_order(owners)):
        first = (place_ref[0] ^ offset) * 2
        own = pl.ds(pl.multiple_of((first + half) * held, held), held)
        other = pl.ds(pl.multiple_of((first + 1 - half) * held, held), held)
        s_ref[own, :] = own_ref[i].astype(jnp.float32)
        s_ref[other, :] = other_ref[i].astype(jnp.float32)
    for i in range(s_ref.shape[0] // BLK):
        for j in range(features // BLK):
            tile = s_ref[i * BLK : (i + 1) * BLK, j * BLK : (j + 1) * BLK].T
            h_ref[j * BLK : (j + 1) * BLK, i * BLK : (i + 1) * BLK] = tile.astype(jnp.bfloat16)
    steps, tile, _ = block_ref.shape
    for i in range(steps):
        rows = slice(i * tile, (i + 1) * tile)
        block_ref[i] = jnp.dot(
            h_ref[rows, :], grad_ref[...], preferred_element_type=jnp.float32
        ).astype(jnp.bfloat16)
        copies.append(pltpu.make_async_copy(block_ref.at[i], o_ref.at[pl.ds(i * tile, tile), :], sems.at[i]))
        copies[-1].start()
    for copy in copies:
        copy.wait()


def in_vmem():
    return pl.BlockSpec(memory_space=pltpu.VMEM)


def scalars():
    return pl.BlockSpec(memory_space=pltpu.SMEM)


def anywhere():
    return pl.BlockSpec(memory_space=pl.ANY)


def params(mib=48):
    return pltpu.CompilerParams(vmem_limit_bytes=mib << 20)


def cost(flops=0, bytes_accessed=0, transcendentals=0):
    return pl.CostEstimate(flops=flops, bytes_accessed=bytes_accessed, transcendentals=transcendentals)


def swap_halves(x):
    return lax.ppermute(x, "tv", [(0, 1), (1, 0)])


def to_partner(x, offset):
    return lax.ppermute(x, "sv", [(s, s ^ offset) for s in range(lax.axis_size("sv"))])


def body(teacher_probs, align_owner, align_local, align_weight, student_logits, hidden):
    owners = lax.axis_size("sv")
    halves = lax.axis_size("tv")
    half_index = lax.axis_index("tv")
    place = jnp.stack([lax.axis_index("sv"), half_index]).astype(jnp.int32)
    tokens = teacher_probs.shape[0]
    columns = student_logits.shape[1]
    blocks = columns // BLK
    mine = blocks // halves
    width = mine * BLK
    rows = owners * mine
    per_half = TB // halves
    group_tokens = owners * tokens
    half_tokens = student_logits.shape[0]
    features = hidden.shape[1]
    first = half_index == 0
    bf16, f32 = jnp.bfloat16, jnp.float32
    shape = jax.ShapeDtypeStruct
    dma = lambda count: pltpu.SemaphoreType.DMA((count,))

    def in_order(own, other, axis):
        return jnp.concatenate([jnp.where(first, own, other), jnp.where(first, other, own)], axis=axis)

    hidden = hidden[None]
    offset = owners // 2
    first_piece = to_partner(hidden, offset)

    def merge(one, two):
        top = jnp.maximum(one[0], two[0])
        return top, one[1] * jnp.exp(one[0] - top) + two[1] * jnp.exp(two[0] - top)

    wide = student_logits.astype(f32)
    low = jnp.float32(-1e38)
    stats = jnp.stack(lax.reduce((wide, jnp.ones_like(wide)), (low, jnp.float32(0)), merge, (1,)))
    teacher_given, stats = lax.optimization_barrier((teacher_probs, stats))
    teacher_other = swap_halves(teacher_given)
    stats = in_order(stats, swap_halves(stats), 1)

    local = align_local.T - half_index * mine
    row_of = jnp.where((local >= 0) & (local < mine), align_owner.T * mine + local, -1)
    code = row_of.astype(f32) + 0.5 * align_weight.T.astype(f32)
    cut = lambda which: lax.dynamic_slice_in_dim(code, which * per_half, per_half, 1)
    w_own = block_weights(cut(half_index), rows)
    w_rest = block_weights(cut(1 - half_index), rows)
    spread = pltpu.VMEM((per_half * tokens, BLK), f32)
    flops = 2 * (rows + MASS_ROWS) * per_half * tokens * BLK
    part = pl.pallas_call(
        map_own_kernel,
        out_shape=shape((rows + MASS_ROWS, tokens * BLK), f32),
        in_specs=[in_vmem()] * 2 + [anywhere()],
        out_specs=in_vmem(),
        scratch_shapes=[spread],
        compiler_params=params(),
        cost_estimate=cost(flops, 3 << 20),
        name="map_own",
    )(w_own, teacher_probs, stats)
    chunk = (owners, tokens, width + group_tokens)
    outgoing = pl.pallas_call(
        map_rest_kernel,
        out_shape=shape(chunk, bf16),
        in_specs=[in_vmem()] * 4 + [anywhere()],
        out_specs=anywhere(),
        scratch_shapes=[
            spread,
            pltpu.VMEM(((rows + 8) * tokens, BLK), f32),
            pltpu.VMEM(chunk, bf16),
            dma(owners),
        ],
        compiler_params=params(),
        cost_estimate=cost(flops, 4 << 20),
        name="map_rest",
    )(w_rest, teacher_other, part, stats, first_piece)
    target = lax.all_to_all(outgoing, "sv", 0, 0, tiled=True)

    hidden, late_logits, outgoing = lax.optimization_barrier((hidden, student_logits, outgoing))

    keep = lax.dynamic_slice_in_dim(late_logits, half_index * width, width, 1)
    give = lax.dynamic_slice_in_dim(late_logits, (1 - half_index) * width, width, 1)
    logits = in_order(keep, swap_halves(give), 0)

    pieces = [jnp.concatenate([hidden, first_piece])]
    pieces += [to_partner(pieces[0], a) for a in range(1, offset)]

    scale = float(columns * owners)
    lanes = -(-half_tokens // BLK) * BLK
    grad, terms = pl.pallas_call(
        lambda *refs: grad_kernel(scale, *refs),
        out_shape=(shape((group_tokens, width), bf16), shape((owners * halves, 8, lanes), f32)),
        in_specs=[in_vmem()] * 2,
        out_specs=(in_vmem(), anywhere()),
        scratch_shapes=[
            pltpu.VMEM((group_tokens, BLK), f32),
            pltpu.VMEM((owners * halves, 8, lanes), f32),
            pltpu.SemaphoreType.DMA,
        ],
        compiler_params=params(),
        cost_estimate=cost(
            10 * group_tokens * width, 6 * group_tokens * width, 2 * group_tokens * width
        ),
        name="logit_grad",
    )(target, logits)

    terms = lax.all_to_all(terms, ("sv", "tv"), 0, 0, tiled=True)
    give = lax.dynamic_slice_in_dim(grad, (1 - half_index) * half_tokens, half_tokens, 0)
    got = swap_halves(give)

    *pieces, grad = lax.optimization_barrier((*pieces, grad))
    hidden_own = jnp.concatenate(pieces)
    steps = 8
    weight_grad, logit_grad = pl.pallas_call(
        weight_kernel,
        out_shape=(shape((features, width), bf16), shape((half_tokens, columns), bf16)),
        in_specs=[scalars()] + [in_vmem()] * 4,
        out_specs=(anywhere(), anywhere()),
        scratch_shapes=[
            pltpu.VMEM((group_tokens, features), f32),
            pltpu.VMEM((features, group_tokens), bf16),
            pltpu.VMEM((steps, features // steps, width), bf16),
            dma(steps),
            dma(2),
        ],
        compiler_params=params(),
        cost_estimate=cost(
            2 * features * group_tokens * width,
            2 * (features * width + group_tokens * (features + width)),
        ),
        name="weight_grad",
    )(place, hidden_own, swap_halves(hidden_own), grad, got)
    terms, logit_grad, weight_grad = lax.optimization_barrier((terms, logit_grad, weight_grad))
    divergence = jnp.sum(terms[:, 0, :half_tokens], axis=0)
    return (divergence, logit_grad, weight_grad)


def solution(mesh):
    return jax.shard_map(
        body,
        mesh=mesh,
        in_specs=(
            P(("grp", "sv"), "tv"),
            P(),
            P(),
            P(),
            P(("grp", "tv"), "sv"),
            P(("grp", "sv", "tv"), None),
        ),
        out_specs=(P(("grp", "tv")), P(("grp", "tv"), "sv"), P(None, ("grp", "sv", "tv"))),
        check_vma=False,
    )
```

```python
import jax
import jax.numpy as jnp
from jax import lax
from jax.experimental import pallas as pl
from jax.experimental.pallas import tpu as pltpu
from jax.sharding import PartitionSpec as P

BLK = 128
TB = 640
TOPA = 2
MASS_ROWS = 16
STEP = 16


def block_weights(code, rows):
    row_ids = lax.broadcasted_iota(jnp.int32, (rows + MASS_ROWS, code.shape[1]), 0)
    total = jnp.zeros(row_ids.shape, jnp.float32)
    for slot in range(TOPA):
        row = jnp.floor(code[slot])
        weight = (code[slot] - row) * 2.0
        hit = (row_ids == row.astype(jnp.int32)[None, :]) | (row_ids == rows + slot)
        total = total + jnp.where(hit, weight[None, :], 0.0)
    return total.astype(jnp.bfloat16)


def spread_tokens(t_ref, s_ref, start, count):
    tokens = t_ref.shape[0]

    def some(i, carry):
        for j in range(STEP):
            k = start + i * STEP + j
            tile = t_ref[:, pl.ds(pl.multiple_of(k * BLK, BLK), BLK)]
            s_ref[pl.ds(pl.multiple_of(k * tokens, tokens), tokens), :] = tile.astype(jnp.float32)
        return carry

    lax.fori_loop(0, count // STEP, some, 0)


def token_pair(s_ref, t, tokens):
    count = s_ref.shape[0] // tokens
    both = [s_ref[pl.ds(t + i, count, stride=tokens), :].astype(jnp.bfloat16) for i in range(2)]
    return jnp.concatenate(both, axis=1)


def map_own_kernel(w_ref, t_ref, stats_ref, o_ref, s_ref):
    tokens = t_ref.shape[0]
    spread_tokens(t_ref, s_ref, 0, t_ref.shape[1] // BLK)
    for t in range(0, tokens, 2):
        o_ref[:, t * BLK : (t + 2) * BLK] = jnp.dot(
            w_ref[...], token_pair(s_ref, t, tokens), preferred_element_type=jnp.float32
        )


def three_parts(x):
    parts = []
    for _ in range(3):
        parts.append(x.astype(jnp.bfloat16).astype(jnp.float32))
        x = x - parts[-1]
    return parts


def map_rest_kernel(w_ref, t_ref, p_ref, stats_ref, o_ref, s_ref, m_ref, o_buf, out_sem):
    tokens = t_ref.shape[0]
    owners = o_ref.shape[0]
    rows = w_ref.shape[0] - MASS_ROWS
    mine = rows // owners
    stats = [stats_ref[0:1, :]] + three_parts(stats_ref[1:2, :])
    extra = jnp.zeros((tokens, stats_ref.shape[1]), jnp.float32)
    row_ids = lax.broadcasted_iota(jnp.int32, extra.shape, 0)
    for i, row in enumerate(stats):
        extra = jnp.where(row_ids == i, row, extra)
    extra = extra.astype(jnp.bfloat16)
    spread_tokens(t_ref, s_ref, 0, t_ref.shape[1] // BLK)
    for t in range(0, tokens, 2):
        both = p_ref[:, t * BLK : (t + 2) * BLK] + jnp.dot(
            w_ref[...], token_pair(s_ref, t, tokens), preferred_element_type=jnp.float32
        )
        for i in range(2):
            m_ref[pl.ds(t + i, rows + 8, stride=tokens), :] = both[: rows + 8, i * BLK : (i + 1) * BLK]
    mass = m_ref[rows * tokens : (rows + 1) * tokens, :]
    for slot in range(1, TOPA):
        mass = mass + m_ref[(rows + slot) * tokens : (rows + slot + 1) * tokens, :]
    inverse = jnp.broadcast_to(1.0 / jnp.sum(mass, axis=1, keepdims=True), (tokens, BLK))

    def leaving(q):
        return pltpu.make_async_copy(o_buf.at[q], o_ref.at[q], out_sem.at[q])

    def owner(q, carry):
        for b in range(mine):
            first = pl.multiple_of((q * mine + b) * tokens, tokens)
            tile = m_ref[pl.ds(first, tokens), :] * inverse
            o_buf[q, :, b * BLK : (b + 1) * BLK] = tile.astype(jnp.bfloat16)
        o_buf[q, :, mine * BLK :] = extra
        leaving(q).start()
        return carry

    def left(q, carry):
        leaving(q).wait()
        return carry

    lax.fori_loop(0, owners, owner, 0)
    lax.fori_loop(0, owners, left, 0)


def grad_kernel(scale, target_ref, logits_ref, grad_ref, terms_ref, norm_ref, t_buf, sem):
    owners, tokens, _ = target_ref.shape
    group_tokens, width = logits_ref.shape
    stats = [target_ref[q, :, width:].astype(jnp.float32) for q in range(owners)]
    top = stats[0][0:1]
    for one in stats[1:]:
        top = jnp.maximum(top, one[0:1])
    total = jnp.zeros_like(top)
    for one in stats:
        total = total + (one[1:2] + one[2:3] + one[3:4]) * jnp.exp(one[0:1] - top)
    log_norm = top + jnp.log(total)

    def block(i, b):
        lanes = slice(b * BLK, (b + 1) * BLK)
        group = slice(i * BLK // tokens, (i + 1) * BLK // tokens)
        target = target_ref[group, :, lanes].reshape(BLK, BLK).astype(jnp.float32)
        return target, logits_ref[i * BLK : (i + 1) * BLK, lanes].astype(jnp.float32)

    sums = []
    for i in range(group_tokens // BLK):
        rows = slice(i * BLK, (i + 1) * BLK)
        norm = jnp.broadcast_to(log_norm[:, rows], (BLK, BLK)).T
        norm_ref[rows, :] = norm
        terms = jnp.zeros((BLK, BLK), jnp.float32)
        for b in range(width // BLK):
            target, logits = block(i, b)
            positive = target > 0
            one = target * (jnp.log(jnp.where(positive, target, 1.0)) - (logits - norm))
            terms = terms + jnp.where(positive, one, 0.0)
        sums.append(jnp.sum(terms.T, axis=0, keepdims=True))
    row = jnp.concatenate(sums, axis=1)
    half_tokens = group_tokens // 2
    for half in range(2):
        mine = row[:, half * half_tokens : (half + 1) * half_tokens]
        tile = jnp.concatenate([mine] * (t_buf.shape[2] // half_tokens), axis=1)
        for q in range(owners):
            t_buf[2 * q + half] = jnp.broadcast_to(tile, t_buf.shape[1:])
    leaving = pltpu.make_async_copy(t_buf, terms_ref, sem)
    leaving.start()
    for i in range(group_tokens // BLK):
        rows = slice(i * BLK, (i + 1) * BLK)
        for b in range(width // BLK):
            target, logits = block(i, b)
            grad = (jnp.exp(logits - norm_ref[rows, :]) - target) * scale
            grad_ref[rows, b * BLK : (b + 1) * BLK] = grad.astype(jnp.bfloat16)
    leaving.wait()


def arrival_order(owners):
    return [a for b in range(owners // 2) for a in (b, b + owners // 2)]


def weight_kernel(
    place_ref, own_ref, other_ref, grad_ref, got_ref, o_ref, joined_ref, s_ref, h_ref, block_ref, sems, join_sems
):
    half_tokens, width = got_ref.shape
    half = place_ref[1]
    kept_at = pl.ds(pl.multiple_of(half * width, width), width)
    got_at = pl.ds(pl.multiple_of((1 - half) * width, width), width)
    kept = pl.ds(pl.multiple_of(half * half_tokens, half_tokens), half_tokens)
    copies = [
        pltpu.make_async_copy(grad_ref.at[kept, :], joined_ref.at[:, kept_at], join_sems.at[0]),
        pltpu.make_async_copy(got_ref, joined_ref.at[:, got_at], join_sems.at[1]),
    ]
    for copy in copies:
        copy.start()
    owners, held, features = own_ref.shape
    for i, offset in enumerate(arrival_order(owners)):
        first = (place_ref[0] ^ offset) * 2
        own = pl.ds(pl.multiple_of((first + half) * held, held), held)
        other = pl.ds(pl.multiple_of((first + 1 - half) * held, held), held)
        s_ref[own, :] = own_ref[i].astype(jnp.float32)
        s_ref[other, :] = other_ref[i].astype(jnp.float32)
    for i in range(s_ref.shape[0] // BLK):
        for j in range(features // BLK):
            tile = s_ref[i * BLK : (i + 1) * BLK, j * BLK : (j + 1) * BLK].T
            h_ref[j * BLK : (j + 1) * BLK, i * BLK : (i + 1) * BLK] = tile.astype(jnp.bfloat16)
    steps, tile, _ = block_ref.shape
    for i in range(steps):
        rows = slice(i * tile, (i + 1) * tile)
        block_ref[i] = jnp.dot(
            h_ref[rows, :], grad_ref[...], preferred_element_type=jnp.float32
        ).astype(jnp.bfloat16)
        copies.append(pltpu.make_async_copy(block_ref.at[i], o_ref.at[pl.ds(i * tile, tile), :], sems.at[i]))
        copies[-1].start()
    for copy in copies:
        copy.wait()


def in_vmem():
    return pl.BlockSpec(memory_space=pltpu.VMEM)


def scalars():
    return pl.BlockSpec(memory_space=pltpu.SMEM)


def anywhere():
    return pl.BlockSpec(memory_space=pl.ANY)


def params(mib=48):
    return pltpu.CompilerParams(vmem_limit_bytes=mib << 20)


def cost(flops=0, bytes_accessed=0, transcendentals=0):
    return pl.CostEstimate(flops=flops, bytes_accessed=bytes_accessed, transcendentals=transcendentals)


def swap_halves(x):
    return lax.ppermute(x, "tv", [(0, 1), (1, 0)])


def to_partner(x, offset):
    return lax.ppermute(x, "sv", [(s, s ^ offset) for s in range(lax.axis_size("sv"))])


def body(teacher_probs, align_owner, align_local, align_weight, student_logits, hidden):
    owners = lax.axis_size("sv")
    halves = lax.axis_size("tv")
    half_index = lax.axis_index("tv")
    place = jnp.stack([lax.axis_index("sv"), half_index]).astype(jnp.int32)
    tokens = teacher_probs.shape[0]
    columns = student_logits.shape[1]
    blocks = columns // BLK
    mine = blocks // halves
    width = mine * BLK
    rows = owners * mine
    per_half = TB // halves
    group_tokens = owners * tokens
    half_tokens = student_logits.shape[0]
    features = hidden.shape[1]
    first = half_index == 0
    bf16, f32 = jnp.bfloat16, jnp.float32
    shape = jax.ShapeDtypeStruct
    dma = lambda count: pltpu.SemaphoreType.DMA((count,))

    def in_order(own, other, axis):
        return jnp.concatenate([jnp.where(first, own, other), jnp.where(first, other, own)], axis=axis)

    hidden = hidden[None]
    offset = owners // 2
    first_piece = to_partner(hidden, offset)

    def merge(one, two):
        top = jnp.maximum(one[0], two[0])
        return top, one[1] * jnp.exp(one[0] - top) + two[1] * jnp.exp(two[0] - top)

    wide = student_logits.astype(f32)
    low = jnp.float32(-1e38)
    stats = jnp.stack(lax.reduce((wide, jnp.ones_like(wide)), (low, jnp.float32(0)), merge, (1,)))
    teacher_given, stats = lax.optimization_barrier((teacher_probs, stats))
    teacher_other = swap_halves(teacher_given)
    stats = in_order(stats, swap_halves(stats), 1)

    local = align_local.T - half_index * mine
    row_of = jnp.where((local >= 0) & (local < mine), align_owner.T * mine + local, -1)
    code = row_of.astype(f32) + 0.5 * align_weight.T.astype(f32)
    cut = lambda which: lax.dynamic_slice_in_dim(code, which * per_half, per_half, 1)
    w_own = block_weights(cut(half_index), rows)
    w_rest = block_weights(cut(1 - half_index), rows)
    spread = pltpu.VMEM((per_half * tokens, BLK), f32)
    flops = 2 * (rows + MASS_ROWS) * per_half * tokens * BLK
    part = pl.pallas_call(
        map_own_kernel,
        out_shape=shape((rows + MASS_ROWS, tokens * BLK), f32),
        in_specs=[in_vmem()] * 2 + [anywhere()],
        out_specs=in_vmem(),
        scratch_shapes=[spread],
        compiler_params=params(),
        cost_estimate=cost(flops, 3 << 20),
        name="map_own",
    )(w_own, teacher_probs, stats)
    chunk = (owners, tokens, width + group_tokens)
    outgoing = pl.pallas_call(
        map_rest_kernel,
        out_shape=shape(chunk, bf16),
        in_specs=[in_vmem()] * 4,
        out_specs=anywhere(),
        scratch_shapes=[
            spread,
            pltpu.VMEM(((rows + 8) * tokens, BLK), f32),
            pltpu.VMEM(chunk, bf16),
            dma(owners),
        ],
        compiler_params=params(),
        cost_estimate=cost(flops, 4 << 20),
        name="map_rest",
    )(w_rest, teacher_other, part, stats)
    outgoing, first_piece = lax.optimization_barrier((outgoing, first_piece))
    target = lax.all_to_all(outgoing, "sv", 0, 0, tiled=True)

    hidden, late_logits, outgoing = lax.optimization_barrier((hidden, student_logits, outgoing))

    keep = lax.dynamic_slice_in_dim(late_logits, half_index * width, width, 1)
    give = lax.dynamic_slice_in_dim(late_logits, (1 - half_index) * width, width, 1)
    logits = in_order(keep, swap_halves(give), 0)

    pieces = [jnp.concatenate([hidden, first_piece])]
    pieces += [to_partner(pieces[0], a) for a in range(1, offset)]

    scale = float(columns * owners)
    lanes = -(-half_tokens // BLK) * BLK
    grad, terms = pl.pallas_call(
        lambda *refs: grad_kernel(scale, *refs),
        out_shape=(shape((group_tokens, width), bf16), shape((owners * halves, 8, lanes), f32)),
        in_specs=[in_vmem()] * 2,
        out_specs=(in_vmem(), anywhere()),
        scratch_shapes=[
            pltpu.VMEM((group_tokens, BLK), f32),
            pltpu.VMEM((owners * halves, 8, lanes), f32),
            pltpu.SemaphoreType.DMA,
        ],
        compiler_params=params(),
        cost_estimate=cost(
            10 * group_tokens * width, 6 * group_tokens * width, 2 * group_tokens * width
        ),
        name="logit_grad",
    )(target, logits)

    terms = lax.all_to_all(terms, ("sv", "tv"), 0, 0, tiled=True)
    give = lax.dynamic_slice_in_dim(grad, (1 - half_index) * half_tokens, half_tokens, 0)
    got = swap_halves(give)

    *pieces, grad = lax.optimization_barrier((*pieces, grad))
    hidden_own = jnp.concatenate(pieces)
    steps = 8
    weight_grad, logit_grad = pl.pallas_call(
        weight_kernel,
        out_shape=(shape((features, width), bf16), shape((half_tokens, columns), bf16)),
        in_specs=[scalars()] + [in_vmem()] * 4,
        out_specs=(anywhere(), anywhere()),
        scratch_shapes=[
            pltpu.VMEM((group_tokens, features), f32),
            pltpu.VMEM((features, group_tokens), bf16),
            pltpu.VMEM((steps, features // steps, width), bf16),
            dma(steps),
            dma(2),
        ],
        compiler_params=params(),
        cost_estimate=cost(
            2 * features * group_tokens * width,
            2 * (features * width + group_tokens * (features + width)),
        ),
        name="weight_grad",
    )(place, hidden_own, swap_halves(hidden_own), grad, got)
    terms, logit_grad, weight_grad = lax.optimization_barrier((terms, logit_grad, weight_grad))
    divergence = jnp.sum(terms[:, 0, :half_tokens], axis=0)
    return (divergence, logit_grad, weight_grad)


def solution(mesh):
    return jax.shard_map(
        body,
        mesh=mesh,
        in_specs=(
            P(("grp", "sv"), "tv"),
            P(),
            P(),
            P(),
            P(("grp", "tv"), "sv"),
            P(("grp", "sv", "tv"), None),
        ),
        out_specs=(P(("grp", "tv")), P(("grp", "tv"), "sv"), P(None, ("grp", "sv", "tv"))),
        check_vma=False,
    )
```

```python
import jax
import jax.numpy as jnp
from jax import lax
from jax.experimental import pallas as pl
from jax.experimental.pallas import tpu as pltpu
from jax.sharding import PartitionSpec as P

BLK = 128
TB = 640
TOPA = 2
MASS_ROWS = 16
STEP = 16


def block_weights(code, rows):
    row_ids = lax.broadcasted_iota(jnp.int32, (rows + MASS_ROWS, code.shape[1]), 0)
    total = jnp.zeros(row_ids.shape, jnp.float32)
    for slot in range(TOPA):
        row = jnp.floor(code[slot])
        weight = (code[slot] - row) * 2.0
        hit = (row_ids == row.astype(jnp.int32)[None, :]) | (row_ids == rows + slot)
        total = total + jnp.where(hit, weight[None, :], 0.0)
    return total.astype(jnp.bfloat16)


def spread_tokens(t_ref, s_ref, start, count):
    tokens = t_ref.shape[0]

    def some(i, carry):
        for j in range(STEP):
            k = start + i * STEP + j
            tile = t_ref[:, pl.ds(pl.multiple_of(k * BLK, BLK), BLK)]
            s_ref[pl.ds(pl.multiple_of(k * tokens, tokens), tokens), :] = tile.astype(jnp.float32)
        return carry

    lax.fori_loop(0, count // STEP, some, 0)


def token_pair(s_ref, t, tokens):
    count = s_ref.shape[0] // tokens
    both = [s_ref[pl.ds(t + i, count, stride=tokens), :].astype(jnp.bfloat16) for i in range(2)]
    return jnp.concatenate(both, axis=1)


def map_own_kernel(w_ref, t_ref, stats_ref, o_ref, s_ref):
    tokens = t_ref.shape[0]
    spread_tokens(t_ref, s_ref, 0, t_ref.shape[1] // BLK)
    for t in range(0, tokens, 2):
        o_ref[:, t * BLK : (t + 2) * BLK] = jnp.dot(
            w_ref[...], token_pair(s_ref, t, tokens), preferred_element_type=jnp.float32
        )


def three_parts(x):
    parts = []
    for _ in range(3):
        parts.append(x.astype(jnp.bfloat16).astype(jnp.float32))
        x = x - parts[-1]
    return parts


def map_rest_kernel(mine, place_ref, w_ref, t_ref, p_ref, stats_ref, *refs):
    o_refs, (s_ref, m_ref) = refs[:-2], refs[-2:]
    tokens = t_ref.shape[0]
    rows = w_ref.shape[0] - MASS_ROWS
    stats = [stats_ref[0:1, :]] + three_parts(stats_ref[1:2, :])
    extra = jnp.zeros((tokens, stats_ref.shape[1]), jnp.float32)
    row_ids = lax.broadcasted_iota(jnp.int32, extra.shape, 0)
    for i, row in enumerate(stats):
        extra = jnp.where(row_ids == i, row, extra)
    extra = extra.astype(jnp.bfloat16)
    spread_tokens(t_ref, s_ref, 0, t_ref.shape[1] // BLK)
    for t in range(0, tokens, 2):
        both = p_ref[:, t * BLK : (t + 2) * BLK] + jnp.dot(
            w_ref[...], token_pair(s_ref, t, tokens), preferred_element_type=jnp.float32
        )
        for i in range(2):
            m_ref[pl.ds(t + i, rows + 8, stride=tokens), :] = both[: rows + 8, i * BLK : (i + 1) * BLK]
    mass = m_ref[rows * tokens : (rows + 1) * tokens, :]
    for slot in range(1, TOPA):
        mass = mass + m_ref[(rows + slot) * tokens : (rows + slot + 1) * tokens, :]
    inverse = jnp.broadcast_to(1.0 / jnp.sum(mass, axis=1, keepdims=True), (tokens, BLK))

    for offset, o_ref in enumerate(o_refs):
        owner = place_ref[0] ^ offset
        for b in range(mine):
            first = pl.multiple_of((owner * mine + b) * tokens, tokens)
            tile = m_ref[pl.ds(first, tokens), :] * inverse
            o_ref[:, b * BLK : (b + 1) * BLK] = tile.astype(jnp.bfloat16)
        o_ref[:, mine * BLK :] = extra


def leaving_order(owners):
    near = list(range(1, owners // 2))
    return [*range(owners // 2, owners), *near[1:], *near[:1]]


def grad_kernel(scale, place_ref, logits_ref, *refs):
    own_ref, target_refs = refs[0], refs[1:-6]
    grad_ref, terms_ref, target_ref, norm_ref, t_buf, sem = refs[-6:]
    target_ref[place_ref[0]] = own_ref[...]
    for offset, ref in zip(leaving_order(target_ref.shape[0]), target_refs):
        target_ref[place_ref[0] ^ offset] = ref[...]
    owners, tokens, _ = target_ref.shape
    group_tokens, width = logits_ref.shape
    stats = [target_ref[q, :, width:].astype(jnp.float32) for q in range(owners)]
    top = stats[0][0:1]
    for one in stats[1:]:
        top = jnp.maximum(top, one[0:1])
    total = jnp.zeros_like(top)
    for one in stats:
        total = total + (one[1:2] + one[2:3] + one[3:4]) * jnp.exp(one[0:1] - top)
    log_norm = top + jnp.log(total)

    def block(i, b):
        lanes = slice(b * BLK, (b + 1) * BLK)
        group = slice(i * BLK // tokens, (i + 1) * BLK // tokens)
        target = target_ref[group, :, lanes].reshape(BLK, BLK).astype(jnp.float32)
        return target, logits_ref[i * BLK : (i + 1) * BLK, lanes].astype(jnp.float32)

    sums = []
    for i in range(group_tokens // BLK):
        rows = slice(i * BLK, (i + 1) * BLK)
        norm = jnp.broadcast_to(log_norm[:, rows], (BLK, BLK)).T
        norm_ref[rows, :] = norm
        terms = jnp.zeros((BLK, BLK), jnp.float32)
        for b in range(width // BLK):
            target, logits = block(i, b)
            positive = target > 0
            one = target * (jnp.log(jnp.where(positive, target, 1.0)) - (logits - norm))
            terms = terms + jnp.where(positive, one, 0.0)
        sums.append(jnp.sum(terms.T, axis=0, keepdims=True))
    row = jnp.concatenate(sums, axis=1)
    half_tokens = group_tokens // 2
    for half in range(2):
        mine = row[:, half * half_tokens : (half + 1) * half_tokens]
        tile = jnp.concatenate([mine] * (t_buf.shape[2] // half_tokens), axis=1)
        for q in range(owners):
            t_buf[2 * q + half] = jnp.broadcast_to(tile, t_buf.shape[1:])
    leaving = pltpu.make_async_copy(t_buf, terms_ref, sem)
    leaving.start()
    for i in range(group_tokens // BLK):
        rows = slice(i * BLK, (i + 1) * BLK)
        for b in range(width // BLK):
            target, logits = block(i, b)
            grad = (jnp.exp(logits - norm_ref[rows, :]) - target) * scale
            grad_ref[rows, b * BLK : (b + 1) * BLK] = grad.astype(jnp.bfloat16)
    leaving.wait()


def arrival_order(owners):
    return [a for b in range(owners // 2) for a in (b, b + owners // 2)]


def weight_kernel(
    place_ref, own_ref, other_ref, grad_ref, got_ref, o_ref, joined_ref, s_ref, h_ref, block_ref, sems, join_sems
):
    half_tokens, width = got_ref.shape
    half = place_ref[1]
    kept_at = pl.ds(pl.multiple_of(half * width, width), width)
    got_at = pl.ds(pl.multiple_of((1 - half) * width, width), width)
    kept = pl.ds(pl.multiple_of(half * half_tokens, half_tokens), half_tokens)
    copies = [
        pltpu.make_async_copy(grad_ref.at[kept, :], joined_ref.at[:, kept_at], join_sems.at[0]),
        pltpu.make_async_copy(got_ref, joined_ref.at[:, got_at], join_sems.at[1]),
    ]
    for copy in copies:
        copy.start()
    owners, held, features = own_ref.shape
    for i, offset in enumerate(arrival_order(owners)):
        first = (place_ref[0] ^ offset) * 2
        own = pl.ds(pl.multiple_of((first + half) * held, held), held)
        other = pl.ds(pl.multiple_of((first + 1 - half) * held, held), held)
        s_ref[own, :] = own_ref[i].astype(jnp.float32)
        s_ref[other, :] = other_ref[i].astype(jnp.float32)
    for i in range(s_ref.shape[0] // BLK):
        for j in range(features // BLK):
            tile = s_ref[i * BLK : (i + 1) * BLK, j * BLK : (j + 1) * BLK].T
            h_ref[j * BLK : (j + 1) * BLK, i * BLK : (i + 1) * BLK] = tile.astype(jnp.bfloat16)
    steps, tile, _ = block_ref.shape
    for i in range(steps):
        rows = slice(i * tile, (i + 1) * tile)
        block_ref[i] = jnp.dot(
            h_ref[rows, :], grad_ref[...], preferred_element_type=jnp.float32
        ).astype(jnp.bfloat16)
        copies.append(pltpu.make_async_copy(block_ref.at[i], o_ref.at[pl.ds(i * tile, tile), :], sems.at[i]))
        copies[-1].start()
    for copy in copies:
        copy.wait()


def in_vmem():
    return pl.BlockSpec(memory_space=pltpu.VMEM)


def scalars():
    return pl.BlockSpec(memory_space=pltpu.SMEM)


def anywhere():
    return pl.BlockSpec(memory_space=pl.ANY)


def params(mib=48):
    return pltpu.CompilerParams(vmem_limit_bytes=mib << 20)


def cost(flops=0, bytes_accessed=0, transcendentals=0):
    return pl.CostEstimate(flops=flops, bytes_accessed=bytes_accessed, transcendentals=transcendentals)


def swap_halves(x):
    return lax.ppermute(x, "tv", [(0, 1), (1, 0)])


def to_partner(x, offset):
    return lax.ppermute(x, "sv", [(s, s ^ offset) for s in range(lax.axis_size("sv"))])


def body(teacher_probs, align_owner, align_local, align_weight, student_logits, hidden):
    owners = lax.axis_size("sv")
    halves = lax.axis_size("tv")
    half_index = lax.axis_index("tv")
    place = jnp.stack([lax.axis_index("sv"), half_index]).astype(jnp.int32)
    tokens = teacher_probs.shape[0]
    columns = student_logits.shape[1]
    blocks = columns // BLK
    mine = blocks // halves
    width = mine * BLK
    rows = owners * mine
    per_half = TB // halves
    group_tokens = owners * tokens
    half_tokens = student_logits.shape[0]
    features = hidden.shape[1]
    first = half_index == 0
    bf16, f32 = jnp.bfloat16, jnp.float32
    shape = jax.ShapeDtypeStruct
    dma = lambda count: pltpu.SemaphoreType.DMA((count,))

    def in_order(own, other, axis):
        return jnp.concatenate([jnp.where(first, own, other), jnp.where(first, other, own)], axis=axis)

    hidden = hidden[None]
    offset = owners // 2
    first_piece = to_partner(hidden, offset)

    def merge(one, two):
        top = jnp.maximum(one[0], two[0])
        return top, one[1] * jnp.exp(one[0] - top) + two[1] * jnp.exp(two[0] - top)

    wide = student_logits.astype(f32)
    low = jnp.float32(-1e38)
    stats = jnp.stack(lax.reduce((wide, jnp.ones_like(wide)), (low, jnp.float32(0)), merge, (1,)))
    teacher_given, stats = lax.optimization_barrier((teacher_probs, stats))
    teacher_other = swap_halves(teacher_given)
    stats = in_order(stats, swap_halves(stats), 1)

    local = align_local.T - half_index * mine
    row_of = jnp.where((local >= 0) & (local < mine), align_owner.T * mine + local, -1)
    code = row_of.astype(f32) + 0.5 * align_weight.T.astype(f32)
    cut = lambda which: lax.dynamic_slice_in_dim(code, which * per_half, per_half, 1)
    w_own = block_weights(cut(half_index), rows)
    w_rest = block_weights(cut(1 - half_index), rows)
    spread = pltpu.VMEM((per_half * tokens, BLK), f32)
    flops = 2 * (rows + MASS_ROWS) * per_half * tokens * BLK
    part = pl.pallas_call(
        map_own_kernel,
        out_shape=shape((rows + MASS_ROWS, tokens * BLK), f32),
        in_specs=[in_vmem()] * 2 + [anywhere()],
        out_specs=in_vmem(),
        scratch_shapes=[spread],
        compiler_params=params(),
        cost_estimate=cost(flops, 3 << 20),
        name="map_own",
    )(w_own, teacher_probs, stats)
    chunk = (tokens, width + group_tokens)
    outgoing = pl.pallas_call(
        lambda *refs: map_rest_kernel(mine, *refs),
        out_shape=[shape(chunk, bf16)] * owners,
        in_specs=[scalars()] + [in_vmem()] * 4,
        out_specs=[in_vmem()] * owners,
        scratch_shapes=[spread, pltpu.VMEM(((rows + 8) * tokens, BLK), f32)],
        compiler_params=params(),
        cost_estimate=cost(flops, 4 << 20),
        name="map_rest",
    )(place, w_rest, teacher_other, part, stats)
    outgoing, first_piece = lax.optimization_barrier((outgoing, first_piece))
    targets = [to_partner(outgoing[a], a) for a in leaving_order(owners)]

    hidden, late_logits, _ = lax.optimization_barrier((hidden, student_logits, outgoing[0]))

    keep = lax.dynamic_slice_in_dim(late_logits, half_index * width, width, 1)
    give = lax.dynamic_slice_in_dim(late_logits, (1 - half_index) * width, width, 1)
    logits = in_order(keep, swap_halves(give), 0)

    pieces = [jnp.concatenate([hidden, first_piece])]
    pieces += [to_partner(pieces[0], a) for a in range(1, offset)]

    scale = float(columns * owners)
    lanes = -(-half_tokens // BLK) * BLK
    grad, terms = pl.pallas_call(
        lambda *refs: grad_kernel(scale, *refs),
        out_shape=(shape((group_tokens, width), bf16), shape((owners * halves, 8, lanes), f32)),
        in_specs=[scalars()] + [in_vmem()] * (owners + 1),
        out_specs=(in_vmem(), anywhere()),
        scratch_shapes=[
            pltpu.VMEM((owners, *chunk), bf16),
            pltpu.VMEM((group_tokens, BLK), f32),
            pltpu.VMEM((owners * halves, 8, lanes), f32),
            pltpu.SemaphoreType.DMA,
        ],
        compiler_params=params(),
        cost_estimate=cost(
            10 * group_tokens * width, 6 * group_tokens * width, 2 * group_tokens * width
        ),
        name="logit_grad",
    )(place, logits, outgoing[0], *targets)

    terms = lax.all_to_all(terms, ("sv", "tv"), 0, 0, tiled=True)
    give = lax.dynamic_slice_in_dim(grad, (1 - half_index) * half_tokens, half_tokens, 0)
    got = swap_halves(give)

    *pieces, grad = lax.optimization_barrier((*pieces, grad))
    hidden_own = jnp.concatenate(pieces)
    steps = 8
    weight_grad, logit_grad = pl.pallas_call(
        weight_kernel,
        out_shape=(shape((features, width), bf16), shape((half_tokens, columns), bf16)),
        in_specs=[scalars()] + [in_vmem()] * 4,
        out_specs=(anywhere(), anywhere()),
        scratch_shapes=[
            pltpu.VMEM((group_tokens, features), f32),
            pltpu.VMEM((features, group_tokens), bf16),
            pltpu.VMEM((steps, features // steps, width), bf16),
            dma(steps),
            dma(2),
        ],
        compiler_params=params(),
        cost_estimate=cost(
            2 * features * group_tokens * width,
            2 * (features * width + group_tokens * (features + width)),
        ),
        name="weight_grad",
    )(place, hidden_own, swap_halves(hidden_own), grad, got)
    terms, logit_grad, weight_grad = lax.optimization_barrier((terms, logit_grad, weight_grad))
    divergence = jnp.sum(terms[:, 0, :half_tokens], axis=0)
    return (divergence, logit_grad, weight_grad)


def solution(mesh):
    return jax.shard_map(
        body,
        mesh=mesh,
        in_specs=(
            P(("grp", "sv"), "tv"),
            P(),
            P(),
            P(),
            P(("grp", "tv"), "sv"),
            P(("grp", "sv", "tv"), None),
        ),
        out_specs=(P(("grp", "tv")), P(("grp", "tv"), "sv"), P(None, ("grp", "sv", "tv"))),
        check_vma=False,
    )
```

```python
import jax
import jax.numpy as jnp
from jax import lax
from jax.experimental import pallas as pl
from jax.experimental.pallas import tpu as pltpu
from jax.sharding import PartitionSpec as P

BLK = 128
TB = 640
TOPA = 2
MASS_ROWS = 16
STEP = 16


def block_weights(code, rows):
    row_ids = lax.broadcasted_iota(jnp.int32, (rows + MASS_ROWS, code.shape[1]), 0)
    total = jnp.zeros(row_ids.shape, jnp.float32)
    for slot in range(TOPA):
        row = jnp.floor(code[slot])
        weight = (code[slot] - row) * 2.0
        hit = (row_ids == row.astype(jnp.int32)[None, :]) | (row_ids == rows + slot)
        total = total + jnp.where(hit, weight[None, :], 0.0)
    return total.astype(jnp.bfloat16)


def spread_tokens(t_ref, s_ref, start, count):
    tokens = t_ref.shape[0]

    def some(i, carry):
        for j in range(STEP):
            k = start + i * STEP + j
            tile = t_ref[:, pl.ds(pl.multiple_of(k * BLK, BLK), BLK)]
            s_ref[pl.ds(pl.multiple_of(k * tokens, tokens), tokens), :] = tile.astype(jnp.float32)
        return carry

    lax.fori_loop(0, count // STEP, some, 0)


def token_pair(s_ref, t, tokens):
    count = s_ref.shape[0] // tokens
    both = [s_ref[pl.ds(t + i, count, stride=tokens), :].astype(jnp.bfloat16) for i in range(2)]
    return jnp.concatenate(both, axis=1)


def map_own_kernel(w_ref, t_ref, stats_ref, o_ref, s_ref):
    tokens = t_ref.shape[0]
    spread_tokens(t_ref, s_ref, 0, t_ref.shape[1] // BLK)
    for t in range(0, tokens, 2):
        o_ref[:, t * BLK : (t + 2) * BLK] = jnp.dot(
            w_ref[...], token_pair(s_ref, t, tokens), preferred_element_type=jnp.float32
        )


def three_parts(x):
    parts = []
    for _ in range(3):
        parts.append(x.astype(jnp.bfloat16).astype(jnp.float32))
        x = x - parts[-1]
    return parts


def map_rest_kernel(mine, place_ref, w_ref, t_ref, p_ref, stats_ref, *refs):
    o_refs, (s_ref, m_ref) = refs[:-2], refs[-2:]
    tokens = t_ref.shape[0]
    rows = w_ref.shape[0] - MASS_ROWS
    stats = [stats_ref[0:1, :]] + three_parts(stats_ref[1:2, :])
    extra = jnp.zeros((tokens, stats_ref.shape[1]), jnp.float32)
    row_ids = lax.broadcasted_iota(jnp.int32, extra.shape, 0)
    for i, row in enumerate(stats):
        extra = jnp.where(row_ids == i, row, extra)
    extra = extra.astype(jnp.bfloat16)
    spread_tokens(t_ref, s_ref, 0, t_ref.shape[1] // BLK)
    for t in range(0, tokens, 2):
        both = p_ref[:, t * BLK : (t + 2) * BLK] + jnp.dot(
            w_ref[...], token_pair(s_ref, t, tokens), preferred_element_type=jnp.float32
        )
        for i in range(2):
            m_ref[pl.ds(t + i, rows + 8, stride=tokens), :] = both[: rows + 8, i * BLK : (i + 1) * BLK]
    mass = m_ref[rows * tokens : (rows + 1) * tokens, :]
    for slot in range(1, TOPA):
        mass = mass + m_ref[(rows + slot) * tokens : (rows + slot + 1) * tokens, :]
    inverse = jnp.broadcast_to(1.0 / jnp.sum(mass, axis=1, keepdims=True), (tokens, BLK))

    for offset, o_ref in enumerate(o_refs):
        owner = place_ref[0] ^ offset
        for b in range(mine):
            first = pl.multiple_of((owner * mine + b) * tokens, tokens)
            tile = m_ref[pl.ds(first, tokens), :] * inverse
            o_ref[:, b * BLK : (b + 1) * BLK] = tile.astype(jnp.bfloat16)
        o_ref[:, mine * BLK :] = extra


def leaving_order(owners):
    near = list(range(1, owners // 2))
    return [*range(owners // 2, owners), *near[1:], *near[:1]]


def arrange_kernel(tokens, place_ref, keep_ref, got_ref, o_ref):
    count = keep_ref.shape[0] // tokens
    owner, half = place_ref[0], place_ref[1]
    for a in range(o_ref.shape[0] // tokens):
        rows = pl.ds(pl.multiple_of(((owner ^ a) % count) * tokens, tokens), tokens)
        kept = (owner ^ a) // count == half
        o_ref[a * tokens : (a + 1) * tokens, :] = jnp.where(kept, keep_ref[rows, :], got_ref[rows, :])


def grad_kernel(scale, place_ref, logits_ref, *refs):
    own_ref, far_refs = refs[0], refs[1:-6]
    grad_ref, terms_ref, norm_ref, sum_ref, t_buf, sem = refs[-6:]
    owners = len(far_refs) + 1
    tokens = own_ref.shape[0]
    group_tokens, width = logits_ref.shape
    target_refs = [own_ref] + [None] * (owners - 1)
    for offset, ref in zip(leaving_order(owners), far_refs):
        target_refs[offset] = ref
    stats = [ref[:, width:].astype(jnp.float32) for ref in target_refs]
    top = stats[0][0:1]
    for one in stats[1:]:
        top = jnp.maximum(top, one[0:1])
    total = jnp.zeros_like(top)
    for one in stats:
        total = total + (one[1:2] + one[2:3] + one[3:4]) * jnp.exp(one[0:1] - top)
    log_norm = top + jnp.log(total)
    for i in range(0, group_tokens, BLK):
        sum_ref[i : i + BLK, :] = jnp.broadcast_to(log_norm[:, i : i + BLK], (BLK, BLK)).T
    at = [pl.ds(pl.multiple_of((place_ref[0] ^ a) * tokens, tokens), tokens) for a in range(owners)]
    for a in range(owners):
        norm_ref[a * tokens : (a + 1) * tokens, :] = sum_ref[at[a], :]
    per = BLK // tokens

    def block(i, b):
        lanes = slice(b * BLK, (b + 1) * BLK)
        parts = [target_refs[a][:, lanes].astype(jnp.float32) for a in range(i * per, (i + 1) * per)]
        logits = logits_ref[i * BLK : (i + 1) * BLK, lanes].astype(jnp.float32)
        return jnp.concatenate(parts, axis=0), logits - norm_ref[i * BLK : (i + 1) * BLK, :]

    for i in range(group_tokens // BLK):
        terms = jnp.zeros((BLK, BLK), jnp.float32)
        for b in range(width // BLK):
            target, log_probs = block(i, b)
            positive = target > 0
            one = target * (jnp.log(jnp.where(positive, target, 1.0)) - log_probs)
            terms = terms + jnp.where(positive, one, 0.0)
        for j in range(per):
            sum_ref[at[i * per + j], :] = terms[j * tokens : (j + 1) * tokens]
    row = jnp.concatenate(
        [jnp.sum(sum_ref[i : i + BLK, :].T, axis=0, keepdims=True) for i in range(0, group_tokens, BLK)], axis=1
    )
    half_tokens = group_tokens // 2
    for half in range(2):
        mine = row[:, half * half_tokens : (half + 1) * half_tokens]
        tile = jnp.concatenate([mine] * (t_buf.shape[2] // half_tokens), axis=1)
        for q in range(owners):
            t_buf[2 * q + half] = jnp.broadcast_to(tile, t_buf.shape[1:])
    leaving = pltpu.make_async_copy(t_buf, terms_ref, sem)
    leaving.start()
    for i in range(group_tokens // BLK):
        for b in range(width // BLK):
            target, log_probs = block(i, b)
            grad = (jnp.exp(log_probs) - target) * scale
            grad_ref[i * BLK : (i + 1) * BLK, b * BLK : (b + 1) * BLK] = grad.astype(jnp.bfloat16)
    leaving.wait()


def arrival_order(owners):
    return [a for b in range(owners // 2) for a in (b, b + owners // 2)]


def weight_kernel(
    place_ref, own_ref, other_ref, grad_ref, got_ref, o_ref, joined_ref, s_ref, h_ref, block_ref, sems, join_sems
):
    half_tokens, width = got_ref.shape
    count = join_sems.shape[0] // 2
    tokens = half_tokens // count
    owner, half = place_ref[0], place_ref[1]
    kept_at = pl.ds(pl.multiple_of(half * width, width), width)
    got_at = pl.ds(pl.multiple_of((1 - half) * width, width), width)
    kept = ((owner // count) ^ half) * half_tokens
    copies = []
    for j in range(count):
        to = pl.ds(pl.multiple_of(((owner % count) ^ j) * tokens, tokens), tokens)
        here = pl.ds(pl.multiple_of(kept + j * tokens, tokens), tokens)
        there = pl.ds(j * tokens, tokens)
        copies.append(pltpu.make_async_copy(grad_ref.at[here, :], joined_ref.at[to, kept_at], join_sems.at[2 * j]))
        copies.append(pltpu.make_async_copy(got_ref.at[there, :], joined_ref.at[to, got_at], join_sems.at[2 * j + 1]))
    for copy in copies:
        copy.start()
    owners, held, features = own_ref.shape
    for i, offset in enumerate(arrival_order(owners)):
        own = pl.ds(pl.multiple_of((2 * offset + half) * held, held), held)
        other = pl.ds(pl.multiple_of((2 * offset + 1 - half) * held, held), held)
        s_ref[own, :] = own_ref[i].astype(jnp.float32)
        s_ref[other, :] = other_ref[i].astype(jnp.float32)
    for i in range(s_ref.shape[0] // BLK):
        for j in range(features // BLK):
            tile = s_ref[i * BLK : (i + 1) * BLK, j * BLK : (j + 1) * BLK].T
            h_ref[j * BLK : (j + 1) * BLK, i * BLK : (i + 1) * BLK] = tile.astype(jnp.bfloat16)
    steps, tile, _ = block_ref.shape
    for i in range(steps):
        rows = slice(i * tile, (i + 1) * tile)
        block_ref[i] = jnp.dot(
            h_ref[rows, :], grad_ref[...], preferred_element_type=jnp.float32
        ).astype(jnp.bfloat16)
        copies.append(pltpu.make_async_copy(block_ref.at[i], o_ref.at[pl.ds(i * tile, tile), :], sems.at[i]))
        copies[-1].start()
    for copy in copies:
        copy.wait()


def in_vmem():
    return pl.BlockSpec(memory_space=pltpu.VMEM)


def scalars():
    return pl.BlockSpec(memory_space=pltpu.SMEM)


def anywhere():
    return pl.BlockSpec(memory_space=pl.ANY)


def params(mib=48):
    return pltpu.CompilerParams(vmem_limit_bytes=mib << 20)


def cost(flops=0, bytes_accessed=0, transcendentals=0):
    return pl.CostEstimate(flops=flops, bytes_accessed=bytes_accessed, transcendentals=transcendentals)


def swap_halves(x):
    return lax.ppermute(x, "tv", [(0, 1), (1, 0)])


def to_partner(x, offset):
    return lax.ppermute(x, "sv", [(s, s ^ offset) for s in range(lax.axis_size("sv"))])


def body(teacher_probs, align_owner, align_local, align_weight, student_logits, hidden):
    owners = lax.axis_size("sv")
    halves = lax.axis_size("tv")
    half_index = lax.axis_index("tv")
    place = jnp.stack([lax.axis_index("sv"), half_index]).astype(jnp.int32)
    tokens = teacher_probs.shape[0]
    columns = student_logits.shape[1]
    blocks = columns // BLK
    mine = blocks // halves
    width = mine * BLK
    rows = owners * mine
    per_half = TB // halves
    group_tokens = owners * tokens
    half_tokens = student_logits.shape[0]
    features = hidden.shape[1]
    first = half_index == 0
    bf16, f32 = jnp.bfloat16, jnp.float32
    shape = jax.ShapeDtypeStruct
    dma = lambda count: pltpu.SemaphoreType.DMA((count,))

    def in_order(own, other, axis):
        return jnp.concatenate([jnp.where(first, own, other), jnp.where(first, other, own)], axis=axis)

    hidden = hidden[None]
    offset = owners // 2
    first_piece = to_partner(hidden, offset)

    def merge(one, two):
        top = jnp.maximum(one[0], two[0])
        return top, one[1] * jnp.exp(one[0] - top) + two[1] * jnp.exp(two[0] - top)

    wide = student_logits.astype(f32)
    low = jnp.float32(-1e38)
    stats = jnp.stack(lax.reduce((wide, jnp.ones_like(wide)), (low, jnp.float32(0)), merge, (1,)))
    teacher_given, stats = lax.optimization_barrier((teacher_probs, stats))
    teacher_other = swap_halves(teacher_given)
    stats = in_order(stats, swap_halves(stats), 1)

    local = align_local.T - half_index * mine
    row_of = jnp.where((local >= 0) & (local < mine), align_owner.T * mine + local, -1)
    code = row_of.astype(f32) + 0.5 * align_weight.T.astype(f32)
    cut = lambda which: lax.dynamic_slice_in_dim(code, which * per_half, per_half, 1)
    w_own = block_weights(cut(half_index), rows)
    w_rest = block_weights(cut(1 - half_index), rows)
    spread = pltpu.VMEM((per_half * tokens, BLK), f32)
    flops = 2 * (rows + MASS_ROWS) * per_half * tokens * BLK
    part = pl.pallas_call(
        map_own_kernel,
        out_shape=shape((rows + MASS_ROWS, tokens * BLK), f32),
        in_specs=[in_vmem()] * 2 + [anywhere()],
        out_specs=in_vmem(),
        scratch_shapes=[spread],
        compiler_params=params(),
        cost_estimate=cost(flops, 3 << 20),
        name="map_own",
    )(w_own, teacher_probs, stats)
    chunk = (tokens, width + group_tokens)
    outgoing = pl.pallas_call(
        lambda *refs: map_rest_kernel(mine, *refs),
        out_shape=[shape(chunk, bf16)] * owners,
        in_specs=[scalars()] + [in_vmem()] * 4,
        out_specs=[in_vmem()] * owners,
        scratch_shapes=[spread, pltpu.VMEM(((rows + 8) * tokens, BLK), f32)],
        compiler_params=params(),
        cost_estimate=cost(flops, 4 << 20),
        name="map_rest",
    )(place, w_rest, teacher_other, part, stats)
    outgoing, first_piece = lax.optimization_barrier((outgoing, first_piece))
    targets = [to_partner(outgoing[a], a) for a in leaving_order(owners)]

    late_logits, _ = lax.optimization_barrier((student_logits, outgoing[0]))
    hidden, _ = lax.optimization_barrier((hidden, targets[owners // 2 - 1]))

    keep = lax.dynamic_slice_in_dim(late_logits, half_index * width, width, 1)
    give = lax.dynamic_slice_in_dim(late_logits, (1 - half_index) * width, width, 1)
    logits = pl.pallas_call(
        lambda *refs: arrange_kernel(tokens, *refs),
        out_shape=shape((group_tokens, width), bf16),
        in_specs=[scalars()] + [in_vmem()] * 2,
        out_specs=in_vmem(),
        compiler_params=params(),
        cost_estimate=cost(0, 4 * group_tokens * width),
        name="arrange",
    )(place, keep, swap_halves(give))

    pieces = [jnp.concatenate([hidden, first_piece])]
    pieces += [to_partner(pieces[0], a) for a in range(1, offset)]

    scale = float(columns * owners)
    lanes = -(-half_tokens // BLK) * BLK
    grad, terms = pl.pallas_call(
        lambda *refs: grad_kernel(scale, *refs),
        out_shape=(shape((group_tokens, width), bf16), shape((owners * halves, 8, lanes), f32)),
        in_specs=[scalars()] + [in_vmem()] * (owners + 1),
        out_specs=(in_vmem(), anywhere()),
        scratch_shapes=[
            pltpu.VMEM((group_tokens, BLK), f32),
            pltpu.VMEM((group_tokens, BLK), f32),
            pltpu.VMEM((owners * halves, 8, lanes), f32),
            pltpu.SemaphoreType.DMA,
        ],
        compiler_params=params(),
        cost_estimate=cost(
            10 * group_tokens * width, 6 * group_tokens * width, 2 * group_tokens * width
        ),
        name="logit_grad",
    )(place, logits, outgoing[0], *targets)

    terms = lax.all_to_all(terms, ("sv", "tv"), 0, 0, tiled=True)
    count = half_tokens // tokens
    given = (lax.axis_index("sv") // count) ^ (1 - half_index)
    give = lax.dynamic_slice_in_dim(grad, given * half_tokens, half_tokens, 0)
    got = swap_halves(give)

    *pieces, grad = lax.optimization_barrier((*pieces, grad))
    hidden_own = jnp.concatenate(pieces)
    steps = 8
    weight_grad, logit_grad = pl.pallas_call(
        weight_kernel,
        out_shape=(shape((features, width), bf16), shape((half_tokens, columns), bf16)),
        in_specs=[scalars()] + [in_vmem()] * 4,
        out_specs=(anywhere(), anywhere()),
        scratch_shapes=[
            pltpu.VMEM((group_tokens, features), f32),
            pltpu.VMEM((features, group_tokens), bf16),
            pltpu.VMEM((steps, features // steps, width), bf16),
            dma(steps),
            dma(2 * count),
        ],
        compiler_params=params(),
        cost_estimate=cost(
            2 * features * group_tokens * width,
            2 * (features * width + group_tokens * (features + width)),
        ),
        name="weight_grad",
    )(place, hidden_own, swap_halves(hidden_own), grad, got)
    terms, logit_grad, weight_grad = lax.optimization_barrier((terms, logit_grad, weight_grad))
    divergence = jnp.sum(terms[:, 0, :half_tokens], axis=0)
    return (divergence, logit_grad, weight_grad)


def solution(mesh):
    return jax.shard_map(
        body,
        mesh=mesh,
        in_specs=(
            P(("grp", "sv"), "tv"),
            P(),
            P(),
            P(),
            P(("grp", "tv"), "sv"),
            P(("grp", "sv", "tv"), None),
        ),
        out_specs=(P(("grp", "tv")), P(("grp", "tv"), "sv"), P(None, ("grp", "sv", "tv"))),
        check_vma=False,
    )
```

```python
import jax
import jax.numpy as jnp
from jax import lax
from jax.experimental import pallas as pl
from jax.experimental.pallas import tpu as pltpu
from jax.sharding import PartitionSpec as P

BLK = 128
TB = 640
TOPA = 2
MASS_ROWS = 16
STEP = 16


def block_weights(code, rows):
    row_ids = lax.broadcasted_iota(jnp.int32, (rows + MASS_ROWS, code.shape[1]), 0)
    total = jnp.zeros(row_ids.shape, jnp.float32)
    for slot in range(TOPA):
        row = jnp.floor(code[slot])
        weight = (code[slot] - row) * 2.0
        hit = (row_ids == row.astype(jnp.int32)[None, :]) | (row_ids == rows + slot)
        total = total + jnp.where(hit, weight[None, :], 0.0)
    return total.astype(jnp.bfloat16)


def spread_tokens(t_ref, s_ref, start, count):
    tokens = t_ref.shape[0]

    def some(i, carry):
        for j in range(STEP):
            k = start + i * STEP + j
            tile = t_ref[:, pl.ds(pl.multiple_of(k * BLK, BLK), BLK)]
            s_ref[pl.ds(pl.multiple_of(k * tokens, tokens), tokens), :] = tile.astype(jnp.float32)
        return carry

    lax.fori_loop(0, count // STEP, some, 0)


def token_pair(s_ref, t, tokens):
    count = s_ref.shape[0] // tokens
    both = [s_ref[pl.ds(t + i, count, stride=tokens), :].astype(jnp.bfloat16) for i in range(2)]
    return jnp.concatenate(both, axis=1)


def map_own_kernel(w_ref, t_ref, stats_ref, o_ref, s_ref):
    tokens = t_ref.shape[0]
    spread_tokens(t_ref, s_ref, 0, t_ref.shape[1] // BLK)
    for t in range(0, tokens, 2):
        o_ref[:, t * BLK : (t + 2) * BLK] = jnp.dot(
            w_ref[...], token_pair(s_ref, t, tokens), preferred_element_type=jnp.float32
        )


def three_parts(x):
    parts = []
    for _ in range(3):
        parts.append(x.astype(jnp.bfloat16).astype(jnp.float32))
        x = x - parts[-1]
    return parts


def map_rest_kernel(mine, place_ref, w_ref, t_ref, p_ref, stats_ref, hidden_ref, first_ref, near_ref, *refs):
    far_refs, (s_ref, m_ref, o_buf, out_sem) = refs[:-4], refs[-4:]
    tokens = t_ref.shape[0]
    rows = w_ref.shape[0] - MASS_ROWS
    near = near_ref.shape[0]
    width = mine * BLK
    wide = far_refs[0].shape[1]
    riding = jnp.concatenate([hidden_ref[0].astype(jnp.float32), first_ref[0].astype(jnp.float32)], axis=0)
    riding = riding.astype(jnp.bfloat16)
    stats = [stats_ref[0:1, :]] + three_parts(stats_ref[1:2, :])
    extra = jnp.zeros((tokens, stats_ref.shape[1]), jnp.float32)
    row_ids = lax.broadcasted_iota(jnp.int32, extra.shape, 0)
    for i, row in enumerate(stats):
        extra = jnp.where(row_ids == i, row, extra)
    extra = extra.astype(jnp.bfloat16)
    spread_tokens(t_ref, s_ref, 0, t_ref.shape[1] // BLK)
    for t in range(0, tokens, 2):
        both = p_ref[:, t * BLK : (t + 2) * BLK] + jnp.dot(
            w_ref[...], token_pair(s_ref, t, tokens), preferred_element_type=jnp.float32
        )
        for i in range(2):
            m_ref[pl.ds(t + i, rows + 8, stride=tokens), :] = both[: rows + 8, i * BLK : (i + 1) * BLK]
    mass = m_ref[rows * tokens : (rows + 1) * tokens, :]
    for slot in range(1, TOPA):
        mass = mass + m_ref[(rows + slot) * tokens : (rows + slot + 1) * tokens, :]
    inverse = jnp.broadcast_to(1.0 / jnp.sum(mass, axis=1, keepdims=True), (tokens, BLK))

    def fill(o_ref, owner):
        for b in range(mine):
            first = pl.multiple_of((owner * mine + b) * tokens, tokens)
            tile = m_ref[pl.ds(first, tokens), :] * inverse
            o_ref[:, b * BLK : (b + 1) * BLK] = tile.astype(jnp.bfloat16)
        o_ref[:, width:wide] = extra

    copies = []
    for g in range(near):
        o_buf[g, :, wide:] = riding
        fill(o_buf.at[g], place_ref[0] // near * near + g)
        copies.append(pltpu.make_async_copy(o_buf.at[g], near_ref.at[g], out_sem.at[g]))
        copies[-1].start()
    for g, far_ref in enumerate(far_refs):
        fill(far_ref, place_ref[0] ^ (near + g))
    for copy in copies:
        copy.wait()


def grad_kernel(scale, place_ref, logits_ref, near_ref, *refs):
    far_refs, (grad_ref, terms_ref, far_buf, norm_ref, t_buf, sem) = refs[:-6], refs[-6:]
    near, tokens, _ = near_ref.shape
    owners = 2 * near
    group_tokens, width = logits_ref.shape
    half_tokens = group_tokens // 2
    for g, far_ref in enumerate(far_refs):
        far_buf[(place_ref[0] ^ g) % near] = far_ref[...]
    tiles = slice(width, width + group_tokens)
    stats = [near_ref[g, :, tiles].astype(jnp.float32) for g in range(near)]
    stats += [far_buf[g, :, tiles].astype(jnp.float32) for g in range(near)]
    top = stats[0][0:1]
    for one in stats[1:]:
        top = jnp.maximum(top, one[0:1])
    total = jnp.zeros_like(top)
    for one in stats:
        total = total + (one[1:2] + one[2:3] + one[3:4]) * jnp.exp(one[0:1] - top)

    def turned(row):
        other = jnp.concatenate([row[:, half_tokens:], row[:, :half_tokens]], axis=1)
        return jnp.where(place_ref[0] < near, row, other)

    log_norm = turned(top + jnp.log(total))
    per = BLK // tokens

    def block(i, b):
        lanes = slice(b * BLK, (b + 1) * BLK)
        chunks = range(i * per, (i + 1) * per)
        parts = [near_ref[c, :, lanes] if c < near else far_buf[c - near, :, lanes] for c in chunks]
        target = jnp.concatenate(parts, axis=0).astype(jnp.float32)
        return target, logits_ref[i * BLK : (i + 1) * BLK, lanes].astype(jnp.float32)

    sums = []
    for i in range(group_tokens // BLK):
        rows = slice(i * BLK, (i + 1) * BLK)
        norm = jnp.broadcast_to(log_norm[:, rows], (BLK, BLK)).T
        norm_ref[rows, :] = norm
        terms = jnp.zeros((BLK, BLK), jnp.float32)
        for b in range(width // BLK):
            target, logits = block(i, b)
            positive = target > 0
            one = target * (jnp.log(jnp.where(positive, target, 1.0)) - (logits - norm))
            terms = terms + jnp.where(positive, one, 0.0)
        sums.append(jnp.sum(terms.T, axis=0, keepdims=True))
    row = turned(jnp.concatenate(sums, axis=1))
    for half in range(2):
        mine = row[:, half * half_tokens : (half + 1) * half_tokens]
        tile = jnp.concatenate([mine] * (t_buf.shape[2] // half_tokens), axis=1)
        for q in range(owners):
            t_buf[2 * q + half] = jnp.broadcast_to(tile, t_buf.shape[1:])
    leaving = pltpu.make_async_copy(t_buf, terms_ref, sem)
    leaving.start()
    for i in range(group_tokens // BLK):
        rows = slice(i * BLK, (i + 1) * BLK)
        for b in range(width // BLK):
            target, logits = block(i, b)
            grad = (jnp.exp(logits - norm_ref[rows, :]) - target) * scale
            grad_ref[rows, b * BLK : (b + 1) * BLK] = grad.astype(jnp.bfloat16)
    leaving.wait()


def weight_kernel(
    place_ref, own_ref, other_ref, grad_ref, got_ref, o_ref, joined_ref, s_ref, h_ref, block_ref, sems, join_sems
):
    half_tokens, width = got_ref.shape
    half = place_ref[1]
    kept_at = pl.ds(pl.multiple_of(half * width, width), width)
    got_at = pl.ds(pl.multiple_of((1 - half) * width, width), width)
    near = own_ref.shape[0]
    kept = pl.ds(pl.multiple_of((place_ref[0] // near ^ half) * half_tokens, half_tokens), half_tokens)
    copies = [
        pltpu.make_async_copy(grad_ref.at[kept, :], joined_ref.at[:, kept_at], join_sems.at[0]),
        pltpu.make_async_copy(got_ref, joined_ref.at[:, got_at], join_sems.at[1]),
    ]
    for copy in copies:
        copy.start()
    near, tokens, features = own_ref.shape
    held = tokens // 2
    for ref, side in ((own_ref, half), (other_ref, 1 - half)):
        for g in range(near):
            tile = ref[g].astype(jnp.float32)
            for far in range(2):
                rows = pl.ds(pl.multiple_of((far * near + g) * tokens + side * held, held), held)
                s_ref[rows, :] = tile[far * held : (far + 1) * held]
    for i in range(s_ref.shape[0] // BLK):
        for j in range(features // BLK):
            tile = s_ref[i * BLK : (i + 1) * BLK, j * BLK : (j + 1) * BLK].T
            h_ref[j * BLK : (j + 1) * BLK, i * BLK : (i + 1) * BLK] = tile.astype(jnp.bfloat16)
    steps, tile, _ = block_ref.shape
    for i in range(steps):
        rows = slice(i * tile, (i + 1) * tile)
        block_ref[i] = jnp.dot(
            h_ref[rows, :], grad_ref[...], preferred_element_type=jnp.float32
        ).astype(jnp.bfloat16)
        copies.append(pltpu.make_async_copy(block_ref.at[i], o_ref.at[pl.ds(i * tile, tile), :], sems.at[i]))
        copies[-1].start()
    for copy in copies:
        copy.wait()


def in_vmem():
    return pl.BlockSpec(memory_space=pltpu.VMEM)


def scalars():
    return pl.BlockSpec(memory_space=pltpu.SMEM)


def anywhere():
    return pl.BlockSpec(memory_space=pl.ANY)


def params(mib=48):
    return pltpu.CompilerParams(vmem_limit_bytes=mib << 20)


def cost(flops=0, bytes_accessed=0, transcendentals=0):
    return pl.CostEstimate(flops=flops, bytes_accessed=bytes_accessed, transcendentals=transcendentals)


def swap_halves(x):
    return lax.ppermute(x, "tv", [(0, 1), (1, 0)])


def to_partner(x, offset):
    return lax.ppermute(x, "sv", [(s, s ^ offset) for s in range(lax.axis_size("sv"))])


def body(teacher_probs, align_owner, align_local, align_weight, student_logits, hidden):
    owners = lax.axis_size("sv")
    halves = lax.axis_size("tv")
    half_index = lax.axis_index("tv")
    place = jnp.stack([lax.axis_index("sv"), half_index]).astype(jnp.int32)
    tokens = teacher_probs.shape[0]
    columns = student_logits.shape[1]
    blocks = columns // BLK
    mine = blocks // halves
    width = mine * BLK
    rows = owners * mine
    per_half = TB // halves
    group_tokens = owners * tokens
    half_tokens = student_logits.shape[0]
    features = hidden.shape[1]
    first = half_index == 0
    bf16, f32 = jnp.bfloat16, jnp.float32
    shape = jax.ShapeDtypeStruct
    dma = lambda count: pltpu.SemaphoreType.DMA((count,))

    def in_order(own, other, axis):
        return jnp.concatenate([jnp.where(first, own, other), jnp.where(first, other, own)], axis=axis)

    hidden = hidden[None]
    offset = owners // 2
    first_piece = to_partner(hidden, offset)

    def merge(one, two):
        top = jnp.maximum(one[0], two[0])
        return top, one[1] * jnp.exp(one[0] - top) + two[1] * jnp.exp(two[0] - top)

    wide = student_logits.astype(f32)
    low = jnp.float32(-1e38)
    stats = jnp.stack(lax.reduce((wide, jnp.ones_like(wide)), (low, jnp.float32(0)), merge, (1,)))
    teacher_given, stats = lax.optimization_barrier((teacher_probs, stats))
    teacher_other = swap_halves(teacher_given)
    stats = in_order(stats, swap_halves(stats), 1)

    local = align_local.T - half_index * mine
    row_of = jnp.where((local >= 0) & (local < mine), align_owner.T * mine + local, -1)
    code = row_of.astype(f32) + 0.5 * align_weight.T.astype(f32)
    cut = lambda which: lax.dynamic_slice_in_dim(code, which * per_half, per_half, 1)
    w_own = block_weights(cut(half_index), rows)
    w_rest = block_weights(cut(1 - half_index), rows)
    spread = pltpu.VMEM((per_half * tokens, BLK), f32)
    flops = 2 * (rows + MASS_ROWS) * per_half * tokens * BLK
    part = pl.pallas_call(
        map_own_kernel,
        out_shape=shape((rows + MASS_ROWS, tokens * BLK), f32),
        in_specs=[in_vmem()] * 2 + [anywhere()],
        out_specs=in_vmem(),
        scratch_shapes=[spread],
        compiler_params=params(),
        cost_estimate=cost(flops, 3 << 20),
        name="map_own",
    )(w_own, teacher_probs, stats)
    near = owners // 2
    wide = width + group_tokens
    chunk = (near, tokens, wide + features)
    near_out, *far_out = pl.pallas_call(
        lambda *refs: map_rest_kernel(mine, *refs),
        out_shape=[shape(chunk, bf16)] + [shape((tokens, wide), bf16)] * near,
        in_specs=[scalars()] + [in_vmem()] * 6,
        out_specs=[anywhere()] + [in_vmem()] * near,
        scratch_shapes=[
            spread,
            pltpu.VMEM(((rows + 8) * tokens, BLK), f32),
            pltpu.VMEM(chunk, bf16),
            dma(near),
        ],
        compiler_params=params(),
        cost_estimate=cost(flops, 4 << 20),
        name="map_rest",
    )(place, w_rest, teacher_other, part, stats, hidden, first_piece)
    far_in = [to_partner(x, near + g) for g, x in enumerate(far_out)]
    groups = [list(range(near)), list(range(near, owners))]
    near_in = lax.all_to_all(near_out, "sv", 0, 0, axis_index_groups=groups, tiled=True)

    late_logits, _ = lax.optimization_barrier((student_logits, near_out))

    keep = lax.dynamic_slice_in_dim(late_logits, half_index * width, width, 1)
    give = lax.dynamic_slice_in_dim(late_logits, (1 - half_index) * width, width, 1)
    got = swap_halves(give)
    near_side = lax.axis_index("sv") // near
    near_own = half_index == near_side
    logits = jnp.concatenate([jnp.where(near_own, keep, got), jnp.where(near_own, got, keep)], axis=0)

    scale = float(columns * owners)
    lanes = -(-half_tokens // BLK) * BLK
    grad, terms = pl.pallas_call(
        lambda *refs: grad_kernel(scale, *refs),
        out_shape=(shape((group_tokens, width), bf16), shape((owners * halves, 8, lanes), f32)),
        in_specs=[scalars()] + [in_vmem()] * (near + 2),
        out_specs=(in_vmem(), anywhere()),
        scratch_shapes=[
            pltpu.VMEM((near, tokens, wide), bf16),
            pltpu.VMEM((group_tokens, BLK), f32),
            pltpu.VMEM((owners * halves, 8, lanes), f32),
            pltpu.SemaphoreType.DMA,
        ],
        compiler_params=params(),
        cost_estimate=cost(
            10 * group_tokens * width, 6 * group_tokens * width, 2 * group_tokens * width
        ),
        name="logit_grad",
    )(place, logits, near_in, *far_in)

    terms = lax.all_to_all(terms, ("sv", "tv"), 0, 0, tiled=True)
    given = near_side ^ (1 - half_index)
    give = lax.dynamic_slice_in_dim(grad, given * half_tokens, half_tokens, 0)
    got = swap_halves(give)

    hidden_own = near_in[:, :, wide:]
    steps = 8
    weight_grad, logit_grad = pl.pallas_call(
        weight_kernel,
        out_shape=(shape((features, width), bf16), shape((half_tokens, columns), bf16)),
        in_specs=[scalars()] + [in_vmem()] * 4,
        out_specs=(anywhere(), anywhere()),
        scratch_shapes=[
            pltpu.VMEM((group_tokens, features), f32),
            pltpu.VMEM((features, group_tokens), bf16),
            pltpu.VMEM((steps, features // steps, width), bf16),
            dma(steps),
            dma(2),
        ],
        compiler_params=params(),
        cost_estimate=cost(
            2 * features * group_tokens * width,
            2 * (features * width + group_tokens * (features + width)),
        ),
        name="weight_grad",
    )(place, hidden_own, swap_halves(hidden_own), grad, got)
    terms, logit_grad, weight_grad = lax.optimization_barrier((terms, logit_grad, weight_grad))
    divergence = jnp.sum(terms[:, 0, :half_tokens], axis=0)
    return (divergence, logit_grad, weight_grad)


def solution(mesh):
    return jax.shard_map(
        body,
        mesh=mesh,
        in_specs=(
            P(("grp", "sv"), "tv"),
            P(),
            P(),
            P(),
            P(("grp", "tv"), "sv"),
            P(("grp", "sv", "tv"), None),
        ),
        out_specs=(P(("grp", "tv")), P(("grp", "tv"), "sv"), P(None, ("grp", "sv", "tv"))),
        check_vma=False,
    )
```

```python
import jax
import jax.numpy as jnp
from jax import lax
from jax.experimental import pallas as pl
from jax.experimental.pallas import tpu as pltpu
from jax.sharding import PartitionSpec as P

BLK = 128
TB = 640
TOPA = 2
MASS_ROWS = 16
STEP = 16
GROUP = 8


def block_weights(code, rows):
    row_ids = lax.broadcasted_iota(jnp.int32, (rows + MASS_ROWS, code.shape[1]), 0)
    total = jnp.zeros(row_ids.shape, jnp.float32)
    for slot in range(TOPA):
        row = jnp.floor(code[slot])
        weight = (code[slot] - row) * 2.0
        hit = (row_ids == row.astype(jnp.int32)[None, :]) | (row_ids == rows + slot)
        total = total + jnp.where(hit, weight[None, :], 0.0)
    return total.astype(jnp.bfloat16)


def spread_tokens(t_ref, s_ref, start, count):
    tokens = t_ref.shape[0]

    def some(i, carry):
        for j in range(STEP):
            k = start + i * STEP + j
            tile = t_ref[:, pl.ds(pl.multiple_of(k * BLK, BLK), BLK)]
            s_ref[pl.ds(pl.multiple_of(k * tokens, tokens), tokens), :] = tile.astype(jnp.float32)
        return carry

    lax.fori_loop(0, count // STEP, some, 0)


def token_columns(s_ref, t, tokens):
    count = s_ref.shape[0] // tokens
    some = [s_ref[pl.ds(t + i, count, stride=tokens), :].astype(jnp.bfloat16) for i in range(GROUP)]
    return jnp.concatenate(some, axis=1)


def map_own_kernel(w_ref, t_ref, stats_ref, o_ref, s_ref):
    tokens = t_ref.shape[0]
    spread_tokens(t_ref, s_ref, 0, t_ref.shape[1] // BLK)
    for t in range(0, tokens, GROUP):
        o_ref[:, t * BLK : (t + GROUP) * BLK] = jnp.dot(
            w_ref[...], token_columns(s_ref, t, tokens), preferred_element_type=jnp.float32
        )


def three_parts(x):
    parts = []
    for _ in range(3):
        parts.append(x.astype(jnp.bfloat16).astype(jnp.float32))
        x = x - parts[-1]
    return parts


def map_rest_kernel(w_ref, t_ref, p_ref, stats_ref, o_ref, s_ref, m_ref, o_buf, out_sem):
    tokens = t_ref.shape[0]
    owners = o_ref.shape[0]
    rows = w_ref.shape[0] - MASS_ROWS
    mine = rows // owners
    stats = [stats_ref[0:1, :]] + three_parts(stats_ref[1:2, :])
    extra = jnp.zeros((tokens, stats_ref.shape[1]), jnp.float32)
    row_ids = lax.broadcasted_iota(jnp.int32, extra.shape, 0)
    for i, row in enumerate(stats):
        extra = jnp.where(row_ids == i, row, extra)
    extra = extra.astype(jnp.bfloat16)
    spread_tokens(t_ref, s_ref, 0, t_ref.shape[1] // BLK)
    for t in range(0, tokens, GROUP):
        both = p_ref[:, t * BLK : (t + GROUP) * BLK] + jnp.dot(
            w_ref[...], token_columns(s_ref, t, tokens), preferred_element_type=jnp.float32
        )
        for i in range(GROUP):
            m_ref[pl.ds(t + i, rows + 8, stride=tokens), :] = both[: rows + 8, i * BLK : (i + 1) * BLK]
    mass = m_ref[rows * tokens : (rows + 1) * tokens, :]
    for slot in range(1, TOPA):
        mass = mass + m_ref[(rows + slot) * tokens : (rows + slot + 1) * tokens, :]
    inverse = jnp.broadcast_to(1.0 / jnp.sum(mass, axis=1, keepdims=True), (tokens, BLK))

    def leaving(q):
        return pltpu.make_async_copy(o_buf.at[q], o_ref.at[q], out_sem.at[q])

    def owner(q, carry):
        for b in range(mine):
            first = pl.multiple_of((q * mine + b) * tokens, tokens)
            tile = m_ref[pl.ds(first, tokens), :] * inverse
            o_buf[q, :, b * BLK : (b + 1) * BLK] = tile.astype(jnp.bfloat16)
        o_buf[q, :, mine * BLK :] = extra
        leaving(q).start()
        return carry

    def left(q, carry):
        leaving(q).wait()
        return carry

    lax.fori_loop(0, owners, owner, 0)
    lax.fori_loop(0, owners, left, 0)


def grad_kernel(scale, target_ref, logits_ref, grad_ref, terms_ref, norm_ref, t_buf, sem):
    owners, tokens, _ = target_ref.shape
    group_tokens, width = logits_ref.shape
    stats = [target_ref[q, :, width:].astype(jnp.float32) for q in range(owners)]
    top = stats[0][0:1]
    for one in stats[1:]:
        top = jnp.maximum(top, one[0:1])
    total = jnp.zeros_like(top)
    for one in stats:
        total = total + (one[1:2] + one[2:3] + one[3:4]) * jnp.exp(one[0:1] - top)
    log_norm = top + jnp.log(total)

    def block(i, b):
        lanes = slice(b * BLK, (b + 1) * BLK)
        group = slice(i * BLK // tokens, (i + 1) * BLK // tokens)
        target = target_ref[group, :, lanes].reshape(BLK, BLK).astype(jnp.float32)
        return target, logits_ref[i * BLK : (i + 1) * BLK, lanes].astype(jnp.float32)

    sums = []
    for i in range(group_tokens // BLK):
        rows = slice(i * BLK, (i + 1) * BLK)
        norm = jnp.broadcast_to(log_norm[:, rows], (BLK, BLK)).T
        norm_ref[rows, :] = norm
        terms = jnp.zeros((BLK, BLK), jnp.float32)
        for b in range(width // BLK):
            target, logits = block(i, b)
            positive = target > 0
            one = target * (jnp.log(jnp.where(positive, target, 1.0)) - (logits - norm))
            terms = terms + jnp.where(positive, one, 0.0)
        sums.append(jnp.sum(terms.T, axis=0, keepdims=True))
    row = jnp.concatenate(sums, axis=1)
    half_tokens = group_tokens // 2
    for half in range(2):
        mine = row[:, half * half_tokens : (half + 1) * half_tokens]
        tile = jnp.concatenate([mine] * (t_buf.shape[2] // half_tokens), axis=1)
        for q in range(owners):
            t_buf[2 * q + half] = jnp.broadcast_to(tile, t_buf.shape[1:])
    leaving = pltpu.make_async_copy(t_buf, terms_ref, sem)
    leaving.start()
    for i in range(group_tokens // BLK):
        rows = slice(i * BLK, (i + 1) * BLK)
        for b in range(width // BLK):
            target, logits = block(i, b)
            grad = (jnp.exp(logits - norm_ref[rows, :]) - target) * scale
            grad_ref[rows, b * BLK : (b + 1) * BLK] = grad.astype(jnp.bfloat16)
    leaving.wait()


def arrival_order(owners):
    return [a for b in range(owners // 2) for a in (b, b + owners // 2)]


def weight_kernel(
    place_ref, own_ref, other_ref, grad_ref, got_ref, o_ref, joined_ref, s_ref, h_ref, block_ref, sems, join_sems
):
    half_tokens, width = got_ref.shape
    half = place_ref[1]
    kept_at = pl.ds(pl.multiple_of(half * width, width), width)
    got_at = pl.ds(pl.multiple_of((1 - half) * width, width), width)
    kept = pl.ds(pl.multiple_of(half * half_tokens, half_tokens), half_tokens)
    copies = [
        pltpu.make_async_copy(grad_ref.at[kept, :], joined_ref.at[:, kept_at], join_sems.at[0]),
        pltpu.make_async_copy(got_ref, joined_ref.at[:, got_at], join_sems.at[1]),
    ]
    for copy in copies:
        copy.start()
    owners, held, features = own_ref.shape
    for i, offset in enumerate(arrival_order(owners)):
        first = (place_ref[0] ^ offset) * 2
        own = pl.ds(pl.multiple_of((first + half) * held, held), held)
        other = pl.ds(pl.multiple_of((first + 1 - half) * held, held), held)
        s_ref[own, :] = own_ref[i].astype(jnp.float32)
        s_ref[other, :] = other_ref[i].astype(jnp.float32)
    for i in range(s_ref.shape[0] // BLK):
        for j in range(features // BLK):
            tile = s_ref[i * BLK : (i + 1) * BLK, j * BLK : (j + 1) * BLK].T
            h_ref[j * BLK : (j + 1) * BLK, i * BLK : (i + 1) * BLK] = tile.astype(jnp.bfloat16)
    steps, tile, _ = block_ref.shape
    for i in range(steps):
        rows = slice(i * tile, (i + 1) * tile)
        block_ref[i] = jnp.dot(
            h_ref[rows, :], grad_ref[...], preferred_element_type=jnp.float32
        ).astype(jnp.bfloat16)
        copies.append(pltpu.make_async_copy(block_ref.at[i], o_ref.at[pl.ds(i * tile, tile), :], sems.at[i]))
        copies[-1].start()
    for copy in copies:
        copy.wait()


def in_vmem():
    return pl.BlockSpec(memory_space=pltpu.VMEM)


def scalars():
    return pl.BlockSpec(memory_space=pltpu.SMEM)


def anywhere():
    return pl.BlockSpec(memory_space=pl.ANY)


def params(mib=48):
    return pltpu.CompilerParams(vmem_limit_bytes=mib << 20)


def cost(flops=0, bytes_accessed=0, transcendentals=0):
    return pl.CostEstimate(flops=flops, bytes_accessed=bytes_accessed, transcendentals=transcendentals)


def swap_halves(x):
    return lax.ppermute(x, "tv", [(0, 1), (1, 0)])


def to_partner(x, offset):
    return lax.ppermute(x, "sv", [(s, s ^ offset) for s in range(lax.axis_size("sv"))])


def body(teacher_probs, align_owner, align_local, align_weight, student_logits, hidden):
    owners = lax.axis_size("sv")
    halves = lax.axis_size("tv")
    half_index = lax.axis_index("tv")
    place = jnp.stack([lax.axis_index("sv"), half_index]).astype(jnp.int32)
    tokens = teacher_probs.shape[0]
    columns = student_logits.shape[1]
    blocks = columns // BLK
    mine = blocks // halves
    width = mine * BLK
    rows = owners * mine
    per_half = TB // halves
    group_tokens = owners * tokens
    half_tokens = student_logits.shape[0]
    features = hidden.shape[1]
    first = half_index == 0
    bf16, f32 = jnp.bfloat16, jnp.float32
    shape = jax.ShapeDtypeStruct
    dma = lambda count: pltpu.SemaphoreType.DMA((count,))

    def in_order(own, other, axis):
        return jnp.concatenate([jnp.where(first, own, other), jnp.where(first, other, own)], axis=axis)

    hidden = hidden[None]
    offset = owners // 2
    first_piece = to_partner(hidden, offset)

    def merge(one, two):
        top = jnp.maximum(one[0], two[0])
        return top, one[1] * jnp.exp(one[0] - top) + two[1] * jnp.exp(two[0] - top)

    wide = student_logits.astype(f32)
    low = jnp.float32(-1e38)
    stats = jnp.stack(lax.reduce((wide, jnp.ones_like(wide)), (low, jnp.float32(0)), merge, (1,)))
    teacher_given, stats = lax.optimization_barrier((teacher_probs, stats))
    teacher_other = swap_halves(teacher_given)
    stats = in_order(stats, swap_halves(stats), 1)

    local = align_local.T - half_index * mine
    row_of = jnp.where((local >= 0) & (local < mine), align_owner.T * mine + local, -1)
    code = row_of.astype(f32) + 0.5 * align_weight.T.astype(f32)
    cut = lambda which: lax.dynamic_slice_in_dim(code, which * per_half, per_half, 1)
    w_own = block_weights(cut(half_index), rows)
    w_rest = block_weights(cut(1 - half_index), rows)
    spread = pltpu.VMEM((per_half * tokens, BLK), f32)
    flops = 2 * (rows + MASS_ROWS) * per_half * tokens * BLK
    part = pl.pallas_call(
        map_own_kernel,
        out_shape=shape((rows + MASS_ROWS, tokens * BLK), f32),
        in_specs=[in_vmem()] * 2 + [anywhere()],
        out_specs=in_vmem(),
        scratch_shapes=[spread],
        compiler_params=params(),
        cost_estimate=cost(flops, 3 << 20),
        name="map_own",
    )(w_own, teacher_probs, stats)
    chunk = (owners, tokens, width + group_tokens)
    outgoing = pl.pallas_call(
        map_rest_kernel,
        out_shape=shape(chunk, bf16),
        in_specs=[in_vmem()] * 4,
        out_specs=anywhere(),
        scratch_shapes=[
            spread,
            pltpu.VMEM(((rows + 8) * tokens, BLK), f32),
            pltpu.VMEM(chunk, bf16),
            dma(owners),
        ],
        compiler_params=params(),
        cost_estimate=cost(flops, 4 << 20),
        name="map_rest",
    )(w_rest, teacher_other, part, stats)
    outgoing, first_piece = lax.optimization_barrier((outgoing, first_piece))
    target = lax.all_to_all(outgoing, "sv", 0, 0, tiled=True)

    hidden, late_logits, outgoing = lax.optimization_barrier((hidden, student_logits, outgoing))

    keep = lax.dynamic_slice_in_dim(late_logits, half_index * width, width, 1)
    give = lax.dynamic_slice_in_dim(late_logits, (1 - half_index) * width, width, 1)
    logits = in_order(keep, swap_halves(give), 0)

    pieces = [jnp.concatenate([hidden, first_piece])]
    pieces += [to_partner(pieces[0], a) for a in range(1, offset)]

    scale = float(columns * owners)
    lanes = -(-half_tokens // BLK) * BLK
    grad, terms = pl.pallas_call(
        lambda *refs: grad_kernel(scale, *refs),
        out_shape=(shape((group_tokens, width), bf16), shape((owners * halves, 8, lanes), f32)),
        in_specs=[in_vmem()] * 2,
        out_specs=(in_vmem(), anywhere()),
        scratch_shapes=[
            pltpu.VMEM((group_tokens, BLK), f32),
            pltpu.VMEM((owners * halves, 8, lanes), f32),
            pltpu.SemaphoreType.DMA,
        ],
        compiler_params=params(),
        cost_estimate=cost(
            10 * group_tokens * width, 6 * group_tokens * width, 2 * group_tokens * width
        ),
        name="logit_grad",
    )(target, logits)

    terms = lax.all_to_all(terms, ("sv", "tv"), 0, 0, tiled=True)
    give = lax.dynamic_slice_in_dim(grad, (1 - half_index) * half_tokens, half_tokens, 0)
    got = swap_halves(give)

    *pieces, grad = lax.optimization_barrier((*pieces, grad))
    hidden_own = jnp.concatenate(pieces)
    steps = 8
    weight_grad, logit_grad = pl.pallas_call(
        weight_kernel,
        out_shape=(shape((features, width), bf16), shape((half_tokens, columns), bf16)),
        in_specs=[scalars()] + [in_vmem()] * 4,
        out_specs=(anywhere(), anywhere()),
        scratch_shapes=[
            pltpu.VMEM((group_tokens, features), f32),
            pltpu.VMEM((features, group_tokens), bf16),
            pltpu.VMEM((steps, features // steps, width), bf16),
            dma(steps),
            dma(2),
        ],
        compiler_params=params(),
        cost_estimate=cost(
            2 * features * group_tokens * width,
            2 * (features * width + group_tokens * (features + width)),
        ),
        name="weight_grad",
    )(place, hidden_own, swap_halves(hidden_own), grad, got)
    terms, logit_grad, weight_grad = lax.optimization_barrier((terms, logit_grad, weight_grad))
    divergence = jnp.sum(terms[:, 0, :half_tokens], axis=0)
    return (divergence, logit_grad, weight_grad)


def solution(mesh):
    return jax.shard_map(
        body,
        mesh=mesh,
        in_specs=(
            P(("grp", "sv"), "tv"),
            P(),
            P(),
            P(),
            P(("grp", "tv"), "sv"),
            P(("grp", "sv", "tv"), None),
        ),
        out_specs=(P(("grp", "tv")), P(("grp", "tv"), "sv"), P(None, ("grp", "sv", "tv"))),
        check_vma=False,
    )
```

```python
import jax
import jax.numpy as jnp
from jax import lax
from jax.experimental import pallas as pl
from jax.experimental.pallas import tpu as pltpu
from jax.sharding import PartitionSpec as P

BLK = 128
TB = 640
TOPA = 2
MASS_ROWS = 16
STEP = 16


def block_weights(code, rows):
    row_ids = lax.broadcasted_iota(jnp.int32, (rows + MASS_ROWS, code.shape[1]), 0)
    total = jnp.zeros(row_ids.shape, jnp.float32)
    for slot in range(TOPA):
        row = jnp.floor(code[slot])
        weight = (code[slot] - row) * 2.0
        hit = (row_ids == row.astype(jnp.int32)[None, :]) | (row_ids == rows + slot)
        total = total + jnp.where(hit, weight[None, :], 0.0)
    return total.astype(jnp.bfloat16)


def turned_group(members):
    return [(i + members // 4) % members for i in range(members)]


def spread_tokens(t_ref, s_ref, start, count):
    tokens = t_ref.shape[0]

    def some(i, carry):
        for j in range(STEP):
            k = start + i * STEP + j
            tile = t_ref[:, pl.ds(pl.multiple_of(k * BLK, BLK), BLK)]
            s_ref[pl.ds(pl.multiple_of(k * tokens, tokens), tokens), :] = tile.astype(jnp.float32)
        return carry

    lax.fori_loop(0, count // STEP, some, 0)


def token_pair(s_ref, t, tokens):
    count = s_ref.shape[0] // tokens
    both = [s_ref[pl.ds(t + i, count, stride=tokens), :].astype(jnp.bfloat16) for i in range(2)]
    return jnp.concatenate(both, axis=1)


def map_own_kernel(w_ref, t_ref, stats_ref, o_ref, s_ref):
    tokens = t_ref.shape[0]
    spread_tokens(t_ref, s_ref, 0, t_ref.shape[1] // BLK)
    for t in range(0, tokens, 2):
        o_ref[:, t * BLK : (t + 2) * BLK] = jnp.dot(
            w_ref[...], token_pair(s_ref, t, tokens), preferred_element_type=jnp.float32
        )


def three_parts(x):
    parts = []
    for _ in range(3):
        parts.append(x.astype(jnp.bfloat16).astype(jnp.float32))
        x = x - parts[-1]
    return parts


def map_rest_kernel(w_ref, t_ref, p_ref, stats_ref, o_ref, s_ref, m_ref, o_buf, out_sem):
    tokens = t_ref.shape[0]
    owners = o_ref.shape[0]
    rows = w_ref.shape[0] - MASS_ROWS
    mine = rows // owners
    stats = [stats_ref[0:1, :]] + three_parts(stats_ref[1:2, :])
    extra = jnp.zeros((tokens, stats_ref.shape[1]), jnp.float32)
    row_ids = lax.broadcasted_iota(jnp.int32, extra.shape, 0)
    for i, row in enumerate(stats):
        extra = jnp.where(row_ids == i, row, extra)
    extra = extra.astype(jnp.bfloat16)
    spread_tokens(t_ref, s_ref, 0, t_ref.shape[1] // BLK)
    for t in range(0, tokens, 2):
        both = p_ref[:, t * BLK : (t + 2) * BLK] + jnp.dot(
            w_ref[...], token_pair(s_ref, t, tokens), preferred_element_type=jnp.float32
        )
        for i in range(2):
            m_ref[pl.ds(t + i, rows + 8, stride=tokens), :] = both[: rows + 8, i * BLK : (i + 1) * BLK]
    mass = m_ref[rows * tokens : (rows + 1) * tokens, :]
    for slot in range(1, TOPA):
        mass = mass + m_ref[(rows + slot) * tokens : (rows + slot + 1) * tokens, :]
    inverse = jnp.broadcast_to(1.0 / jnp.sum(mass, axis=1, keepdims=True), (tokens, BLK))

    def leaving(q):
        return pltpu.make_async_copy(o_buf.at[q], o_ref.at[q], out_sem.at[q])

    def owner(q, carry):
        member = lax.rem(q + owners // 4, owners)
        for b in range(mine):
            first = pl.multiple_of((member * mine + b) * tokens, tokens)
            tile = m_ref[pl.ds(first, tokens), :] * inverse
            o_buf[q, :, b * BLK : (b + 1) * BLK] = tile.astype(jnp.bfloat16)
        o_buf[q, :, mine * BLK :] = extra
        leaving(q).start()
        return carry

    def left(q, carry):
        leaving(q).wait()
        return carry

    lax.fori_loop(0, owners, owner, 0)
    lax.fori_loop(0, owners, left, 0)


def grad_kernel(scale, target_ref, logits_ref, grad_ref, terms_ref, norm_ref, t_buf, sem):
    owners, tokens, _ = target_ref.shape
    group_tokens, width = logits_ref.shape
    stats = [target_ref[q, :, width:].astype(jnp.float32) for q in range(owners)]
    top = stats[0][0:1]
    for one in stats[1:]:
        top = jnp.maximum(top, one[0:1])
    total = jnp.zeros_like(top)
    for one in stats:
        total = total + (one[1:2] + one[2:3] + one[3:4]) * jnp.exp(one[0:1] - top)
    log_norm = top + jnp.log(total)

    def block(i, b):
        lanes = slice(b * BLK, (b + 1) * BLK)
        first, count = i * BLK // tokens, BLK // tokens
        at = (first - owners // 4) % owners
        cut = min(count, owners - at)
        target = target_ref[at : at + cut, :, lanes].reshape(cut * tokens, BLK)
        if cut < count:
            rest = target_ref[: count - cut, :, lanes].reshape((count - cut) * tokens, BLK)
            target = jnp.concatenate([target, rest], axis=0)
        target = target.astype(jnp.float32)
        return target, logits_ref[i * BLK : (i + 1) * BLK, lanes].astype(jnp.float32)

    sums = []
    for i in range(group_tokens // BLK):
        rows = slice(i * BLK, (i + 1) * BLK)
        norm = jnp.broadcast_to(log_norm[:, rows], (BLK, BLK)).T
        norm_ref[rows, :] = norm
        terms = jnp.zeros((BLK, BLK), jnp.float32)
        for b in range(width // BLK):
            target, logits = block(i, b)
            positive = target > 0
            one = target * (jnp.log(jnp.where(positive, target, 1.0)) - (logits - norm))
            terms = terms + jnp.where(positive, one, 0.0)
        sums.append(jnp.sum(terms.T, axis=0, keepdims=True))
    row = jnp.concatenate(sums, axis=1)
    half_tokens = group_tokens // 2
    for half in range(2):
        mine = row[:, half * half_tokens : (half + 1) * half_tokens]
        tile = jnp.concatenate([mine] * (t_buf.shape[2] // half_tokens), axis=1)
        for q in range(owners):
            t_buf[2 * q + half] = jnp.broadcast_to(tile, t_buf.shape[1:])
    leaving = pltpu.make_async_copy(t_buf, terms_ref, sem)
    leaving.start()
    for i in range(group_tokens // BLK):
        rows = slice(i * BLK, (i + 1) * BLK)
        for b in range(width // BLK):
            target, logits = block(i, b)
            grad = (jnp.exp(logits - norm_ref[rows, :]) - target) * scale
            grad_ref[rows, b * BLK : (b + 1) * BLK] = grad.astype(jnp.bfloat16)
    leaving.wait()


def arrival_order(owners):
    return [a for b in range(owners // 2) for a in (b, b + owners // 2)]


def weight_kernel(
    place_ref, own_ref, other_ref, grad_ref, got_ref, o_ref, joined_ref, s_ref, h_ref, block_ref, sems, join_sems
):
    half_tokens, width = got_ref.shape
    half = place_ref[1]
    kept_at = pl.ds(pl.multiple_of(half * width, width), width)
    got_at = pl.ds(pl.multiple_of((1 - half) * width, width), width)
    kept = pl.ds(pl.multiple_of(half * half_tokens, half_tokens), half_tokens)
    copies = [
        pltpu.make_async_copy(grad_ref.at[kept, :], joined_ref.at[:, kept_at], join_sems.at[0]),
        pltpu.make_async_copy(got_ref, joined_ref.at[:, got_at], join_sems.at[1]),
    ]
    for copy in copies:
        copy.start()
    owners, held, features = own_ref.shape
    for i, offset in enumerate(arrival_order(owners)):
        first = (place_ref[0] ^ offset) * 2
        own = pl.ds(pl.multiple_of((first + half) * held, held), held)
        other = pl.ds(pl.multiple_of((first + 1 - half) * held, held), held)
        s_ref[own, :] = own_ref[i].astype(jnp.float32)
        s_ref[other, :] = other_ref[i].astype(jnp.float32)
    for i in range(s_ref.shape[0] // BLK):
        for j in range(features // BLK):
            tile = s_ref[i * BLK : (i + 1) * BLK, j * BLK : (j + 1) * BLK].T
            h_ref[j * BLK : (j + 1) * BLK, i * BLK : (i + 1) * BLK] = tile.astype(jnp.bfloat16)
    steps, tile, _ = block_ref.shape
    for i in range(steps):
        rows = slice(i * tile, (i + 1) * tile)
        block_ref[i] = jnp.dot(
            h_ref[rows, :], grad_ref[...], preferred_element_type=jnp.float32
        ).astype(jnp.bfloat16)
        copies.append(pltpu.make_async_copy(block_ref.at[i], o_ref.at[pl.ds(i * tile, tile), :], sems.at[i]))
        copies[-1].start()
    for copy in copies:
        copy.wait()


def in_vmem():
    return pl.BlockSpec(memory_space=pltpu.VMEM)


def scalars():
    return pl.BlockSpec(memory_space=pltpu.SMEM)


def anywhere():
    return pl.BlockSpec(memory_space=pl.ANY)


def params(mib=48):
    return pltpu.CompilerParams(vmem_limit_bytes=mib << 20)


def cost(flops=0, bytes_accessed=0, transcendentals=0):
    return pl.CostEstimate(flops=flops, bytes_accessed=bytes_accessed, transcendentals=transcendentals)


def swap_halves(x):
    return lax.ppermute(x, "tv", [(0, 1), (1, 0)])


def to_partner(x, offset):
    return lax.ppermute(x, "sv", [(s, s ^ offset) for s in range(lax.axis_size("sv"))])


def body(teacher_probs, align_owner, align_local, align_weight, student_logits, hidden):
    owners = lax.axis_size("sv")
    halves = lax.axis_size("tv")
    half_index = lax.axis_index("tv")
    place = jnp.stack([lax.axis_index("sv"), half_index]).astype(jnp.int32)
    tokens = teacher_probs.shape[0]
    columns = student_logits.shape[1]
    blocks = columns // BLK
    mine = blocks // halves
    width = mine * BLK
    rows = owners * mine
    per_half = TB // halves
    group_tokens = owners * tokens
    half_tokens = student_logits.shape[0]
    features = hidden.shape[1]
    first = half_index == 0
    bf16, f32 = jnp.bfloat16, jnp.float32
    shape = jax.ShapeDtypeStruct
    dma = lambda count: pltpu.SemaphoreType.DMA((count,))

    def in_order(own, other, axis):
        return jnp.concatenate([jnp.where(first, own, other), jnp.where(first, other, own)], axis=axis)

    hidden = hidden[None]
    offset = owners // 2
    first_piece = to_partner(hidden, offset)

    def merge(one, two):
        top = jnp.maximum(one[0], two[0])
        return top, one[1] * jnp.exp(one[0] - top) + two[1] * jnp.exp(two[0] - top)

    wide = student_logits.astype(f32)
    low = jnp.float32(-1e38)
    stats = jnp.stack(lax.reduce((wide, jnp.ones_like(wide)), (low, jnp.float32(0)), merge, (1,)))
    teacher_given, stats = lax.optimization_barrier((teacher_probs, stats))
    teacher_other = swap_halves(teacher_given)
    stats = in_order(stats, swap_halves(stats), 1)

    local = align_local.T - half_index * mine
    row_of = jnp.where((local >= 0) & (local < mine), align_owner.T * mine + local, -1)
    code = row_of.astype(f32) + 0.5 * align_weight.T.astype(f32)
    cut = lambda which: lax.dynamic_slice_in_dim(code, which * per_half, per_half, 1)
    w_own = block_weights(cut(half_index), rows)
    w_rest = block_weights(cut(1 - half_index), rows)
    spread = pltpu.VMEM((per_half * tokens, BLK), f32)
    flops = 2 * (rows + MASS_ROWS) * per_half * tokens * BLK
    part = pl.pallas_call(
        map_own_kernel,
        out_shape=shape((rows + MASS_ROWS, tokens * BLK), f32),
        in_specs=[in_vmem()] * 2 + [anywhere()],
        out_specs=in_vmem(),
        scratch_shapes=[spread],
        compiler_params=params(),
        cost_estimate=cost(flops, 3 << 20),
        name="map_own",
    )(w_own, teacher_probs, stats)
    chunk = (owners, tokens, width + group_tokens)
    outgoing = pl.pallas_call(
        map_rest_kernel,
        out_shape=shape(chunk, bf16),
        in_specs=[in_vmem()] * 4,
        out_specs=anywhere(),
        scratch_shapes=[
            spread,
            pltpu.VMEM(((rows + 8) * tokens, BLK), f32),
            pltpu.VMEM(chunk, bf16),
            dma(owners),
        ],
        compiler_params=params(),
        cost_estimate=cost(flops, 4 << 20),
        name="map_rest",
    )(w_rest, teacher_other, part, stats)
    outgoing, first_piece = lax.optimization_barrier((outgoing, first_piece))
    target = lax.all_to_all(outgoing, "sv", 0, 0, axis_index_groups=[turned_group(owners)], tiled=True)

    hidden, late_logits, outgoing = lax.optimization_barrier((hidden, student_logits, outgoing))

    keep = lax.dynamic_slice_in_dim(late_logits, half_index * width, width, 1)
    give = lax.dynamic_slice_in_dim(late_logits, (1 - half_index) * width, width, 1)
    logits = in_order(keep, swap_halves(give), 0)

    pieces = [jnp.concatenate([hidden, first_piece])]
    pieces += [to_partner(pieces[0], a) for a in range(1, offset)]

    scale = float(columns * owners)
    lanes = -(-half_tokens // BLK) * BLK
    grad, terms = pl.pallas_call(
        lambda *refs: grad_kernel(scale, *refs),
        out_shape=(shape((group_tokens, width), bf16), shape((owners * halves, 8, lanes), f32)),
        in_specs=[in_vmem()] * 2,
        out_specs=(in_vmem(), anywhere()),
        scratch_shapes=[
            pltpu.VMEM((group_tokens, BLK), f32),
            pltpu.VMEM((owners * halves, 8, lanes), f32),
            pltpu.SemaphoreType.DMA,
        ],
        compiler_params=params(),
        cost_estimate=cost(
            10 * group_tokens * width, 6 * group_tokens * width, 2 * group_tokens * width
        ),
        name="logit_grad",
    )(target, logits)

    everyone = [turned_group(owners * halves)]
    terms = lax.all_to_all(terms, ("sv", "tv"), 0, 0, axis_index_groups=everyone, tiled=True)
    give = lax.dynamic_slice_in_dim(grad, (1 - half_index) * half_tokens, half_tokens, 0)
    got = swap_halves(give)

    *pieces, grad = lax.optimization_barrier((*pieces, grad))
    hidden_own = jnp.concatenate(pieces)
    steps = 8
    weight_grad, logit_grad = pl.pallas_call(
        weight_kernel,
        out_shape=(shape((features, width), bf16), shape((half_tokens, columns), bf16)),
        in_specs=[scalars()] + [in_vmem()] * 4,
        out_specs=(anywhere(), anywhere()),
        scratch_shapes=[
            pltpu.VMEM((group_tokens, features), f32),
            pltpu.VMEM((features, group_tokens), bf16),
            pltpu.VMEM((steps, features // steps, width), bf16),
            dma(steps),
            dma(2),
        ],
        compiler_params=params(),
        cost_estimate=cost(
            2 * features * group_tokens * width,
            2 * (features * width + group_tokens * (features + width)),
        ),
        name="weight_grad",
    )(place, hidden_own, swap_halves(hidden_own), grad, got)
    terms, logit_grad, weight_grad = lax.optimization_barrier((terms, logit_grad, weight_grad))
    divergence = jnp.sum(terms[:, 0, :half_tokens], axis=0)
    return (divergence, logit_grad, weight_grad)


def solution(mesh):
    return jax.shard_map(
        body,
        mesh=mesh,
        in_specs=(
            P(("grp", "sv"), "tv"),
            P(),
            P(),
            P(),
            P(("grp", "tv"), "sv"),
            P(("grp", "sv", "tv"), None),
        ),
        out_specs=(P(("grp", "tv")), P(("grp", "tv"), "sv"), P(None, ("grp", "sv", "tv"))),
        check_vma=False,
    )
```

```python
import jax
import jax.numpy as jnp
from jax import lax
from jax.experimental import pallas as pl
from jax.experimental.pallas import tpu as pltpu
from jax.sharding import PartitionSpec as P

BLK = 128
TB = 640
TOPA = 2
MASS_ROWS = 16
STEP = 16


def block_weights(code, rows):
    row_ids = lax.broadcasted_iota(jnp.int32, (rows + MASS_ROWS, code.shape[1]), 0)
    total = jnp.zeros(row_ids.shape, jnp.float32)
    for slot in range(TOPA):
        row = jnp.floor(code[slot])
        weight = (code[slot] - row) * 2.0
        hit = (row_ids == row.astype(jnp.int32)[None, :]) | (row_ids == rows + slot)
        total = total + jnp.where(hit, weight[None, :], 0.0)
    return total.astype(jnp.bfloat16)


def turned_group(members, first):
    return [(i + first) % members for i in range(members)]


def spread_tokens(t_ref, s_ref, start, count):
    tokens = t_ref.shape[0]

    def some(i, carry):
        for j in range(STEP):
            k = start + i * STEP + j
            tile = t_ref[:, pl.ds(pl.multiple_of(k * BLK, BLK), BLK)]
            s_ref[pl.ds(pl.multiple_of(k * tokens, tokens), tokens), :] = tile.astype(jnp.float32)
        return carry

    lax.fori_loop(0, count // STEP, some, 0)


def token_pair(s_ref, t, tokens):
    count = s_ref.shape[0] // tokens
    both = [s_ref[pl.ds(t + i, count, stride=tokens), :].astype(jnp.bfloat16) for i in range(2)]
    return jnp.concatenate(both, axis=1)


def map_own_kernel(w_ref, t_ref, stats_ref, o_ref, s_ref):
    tokens = t_ref.shape[0]
    spread_tokens(t_ref, s_ref, 0, t_ref.shape[1] // BLK)
    for t in range(0, tokens, 2):
        o_ref[:, t * BLK : (t + 2) * BLK] = jnp.dot(
            w_ref[...], token_pair(s_ref, t, tokens), preferred_element_type=jnp.float32
        )


def three_parts(x):
    parts = []
    for _ in range(3):
        parts.append(x.astype(jnp.bfloat16).astype(jnp.float32))
        x = x - parts[-1]
    return parts


def map_rest_kernel(w_ref, t_ref, p_ref, stats_ref, o_ref, s_ref, m_ref, o_buf, out_sem):
    tokens = t_ref.shape[0]
    owners = o_ref.shape[0]
    rows = w_ref.shape[0] - MASS_ROWS
    mine = rows // owners
    stats = [stats_ref[0:1, :]] + three_parts(stats_ref[1:2, :])
    extra = jnp.zeros((tokens, stats_ref.shape[1]), jnp.float32)
    row_ids = lax.broadcasted_iota(jnp.int32, extra.shape, 0)
    for i, row in enumerate(stats):
        extra = jnp.where(row_ids == i, row, extra)
    extra = extra.astype(jnp.bfloat16)
    spread_tokens(t_ref, s_ref, 0, t_ref.shape[1] // BLK)
    for t in range(0, tokens, 2):
        both = p_ref[:, t * BLK : (t + 2) * BLK] + jnp.dot(
            w_ref[...], token_pair(s_ref, t, tokens), preferred_element_type=jnp.float32
        )
        for i in range(2):
            m_ref[pl.ds(t + i, rows + 8, stride=tokens), :] = both[: rows + 8, i * BLK : (i + 1) * BLK]
    mass = m_ref[rows * tokens : (rows + 1) * tokens, :]
    for slot in range(1, TOPA):
        mass = mass + m_ref[(rows + slot) * tokens : (rows + slot + 1) * tokens, :]
    inverse = jnp.broadcast_to(1.0 / jnp.sum(mass, axis=1, keepdims=True), (tokens, BLK))

    def leaving(q):
        return pltpu.make_async_copy(o_buf.at[q], o_ref.at[q], out_sem.at[q])

    def owner(q, carry):
        member = lax.rem(q + owners // 2, owners)
        for b in range(mine):
            first = pl.multiple_of((member * mine + b) * tokens, tokens)
            tile = m_ref[pl.ds(first, tokens), :] * inverse
            o_buf[q, :, b * BLK : (b + 1) * BLK] = tile.astype(jnp.bfloat16)
        o_buf[q, :, mine * BLK :] = extra
        leaving(q).start()
        return carry

    def left(q, carry):
        leaving(q).wait()
        return carry

    lax.fori_loop(0, owners, owner, 0)
    lax.fori_loop(0, owners, left, 0)


def grad_kernel(scale, target_ref, logits_ref, grad_ref, terms_ref, norm_ref, t_buf, sem):
    owners, tokens, _ = target_ref.shape
    group_tokens, width = logits_ref.shape
    stats = [target_ref[q, :, width:].astype(jnp.float32) for q in range(owners)]
    top = stats[0][0:1]
    for one in stats[1:]:
        top = jnp.maximum(top, one[0:1])
    total = jnp.zeros_like(top)
    for one in stats:
        total = total + (one[1:2] + one[2:3] + one[3:4]) * jnp.exp(one[0:1] - top)
    log_norm = top + jnp.log(total)

    def block(i, b):
        lanes = slice(b * BLK, (b + 1) * BLK)
        first, count = i * BLK // tokens, BLK // tokens
        at = (first - owners // 2) % owners
        cut = min(count, owners - at)
        target = target_ref[at : at + cut, :, lanes].reshape(cut * tokens, BLK)
        if cut < count:
            rest = target_ref[: count - cut, :, lanes].reshape((count - cut) * tokens, BLK)
            target = jnp.concatenate([target, rest], axis=0)
        target = target.astype(jnp.float32)
        return target, logits_ref[i * BLK : (i + 1) * BLK, lanes].astype(jnp.float32)

    sums = []
    for i in range(group_tokens // BLK):
        rows = slice(i * BLK, (i + 1) * BLK)
        norm = jnp.broadcast_to(log_norm[:, rows], (BLK, BLK)).T
        norm_ref[rows, :] = norm
        terms = jnp.zeros((BLK, BLK), jnp.float32)
        for b in range(width // BLK):
            target, logits = block(i, b)
            positive = target > 0
            one = target * (jnp.log(jnp.where(positive, target, 1.0)) - (logits - norm))
            terms = terms + jnp.where(positive, one, 0.0)
        sums.append(jnp.sum(terms.T, axis=0, keepdims=True))
    row = jnp.concatenate(sums, axis=1)
    half_tokens = group_tokens // 2
    for half in range(2):
        mine = row[:, half * half_tokens : (half + 1) * half_tokens]
        tile = jnp.concatenate([mine] * (t_buf.shape[2] // half_tokens), axis=1)
        for q in range(owners):
            t_buf[2 * q + half] = jnp.broadcast_to(tile, t_buf.shape[1:])
    leaving = pltpu.make_async_copy(t_buf, terms_ref, sem)
    leaving.start()
    for i in range(group_tokens // BLK):
        rows = slice(i * BLK, (i + 1) * BLK)
        for b in range(width // BLK):
            target, logits = block(i, b)
            grad = (jnp.exp(logits - norm_ref[rows, :]) - target) * scale
            grad_ref[rows, b * BLK : (b + 1) * BLK] = grad.astype(jnp.bfloat16)
    leaving.wait()


def arrival_order(owners):
    return [a for b in range(owners // 2) for a in (b, b + owners // 2)]


def weight_kernel(
    place_ref, own_ref, other_ref, grad_ref, got_ref, o_ref, joined_ref, s_ref, h_ref, block_ref, sems, join_sems
):
    half_tokens, width = got_ref.shape
    half = place_ref[1]
    kept_at = pl.ds(pl.multiple_of(half * width, width), width)
    got_at = pl.ds(pl.multiple_of((1 - half) * width, width), width)
    kept = pl.ds(pl.multiple_of(half * half_tokens, half_tokens), half_tokens)
    copies = [
        pltpu.make_async_copy(grad_ref.at[kept, :], joined_ref.at[:, kept_at], join_sems.at[0]),
        pltpu.make_async_copy(got_ref, joined_ref.at[:, got_at], join_sems.at[1]),
    ]
    for copy in copies:
        copy.start()
    owners, held, features = own_ref.shape
    for i, offset in enumerate(arrival_order(owners)):
        first = (place_ref[0] ^ offset) * 2
        own = pl.ds(pl.multiple_of((first + half) * held, held), held)
        other = pl.ds(pl.multiple_of((first + 1 - half) * held, held), held)
        s_ref[own, :] = own_ref[i].astype(jnp.float32)
        s_ref[other, :] = other_ref[i].astype(jnp.float32)
    for i in range(s_ref.shape[0] // BLK):
        for j in range(features // BLK):
            tile = s_ref[i * BLK : (i + 1) * BLK, j * BLK : (j + 1) * BLK].T
            h_ref[j * BLK : (j + 1) * BLK, i * BLK : (i + 1) * BLK] = tile.astype(jnp.bfloat16)
    steps, tile, _ = block_ref.shape
    for i in range(steps):
        rows = slice(i * tile, (i + 1) * tile)
        block_ref[i] = jnp.dot(
            h_ref[rows, :], grad_ref[...], preferred_element_type=jnp.float32
        ).astype(jnp.bfloat16)
        copies.append(pltpu.make_async_copy(block_ref.at[i], o_ref.at[pl.ds(i * tile, tile), :], sems.at[i]))
        copies[-1].start()
    for copy in copies:
        copy.wait()


def in_vmem():
    return pl.BlockSpec(memory_space=pltpu.VMEM)


def scalars():
    return pl.BlockSpec(memory_space=pltpu.SMEM)


def anywhere():
    return pl.BlockSpec(memory_space=pl.ANY)


def params(mib=48):
    return pltpu.CompilerParams(vmem_limit_bytes=mib << 20)


def cost(flops=0, bytes_accessed=0, transcendentals=0):
    return pl.CostEstimate(flops=flops, bytes_accessed=bytes_accessed, transcendentals=transcendentals)


def swap_halves(x):
    return lax.ppermute(x, "tv", [(0, 1), (1, 0)])


def to_partner(x, offset):
    return lax.ppermute(x, "sv", [(s, s ^ offset) for s in range(lax.axis_size("sv"))])


def body(teacher_probs, align_owner, align_local, align_weight, student_logits, hidden):
    owners = lax.axis_size("sv")
    halves = lax.axis_size("tv")
    half_index = lax.axis_index("tv")
    place = jnp.stack([lax.axis_index("sv"), half_index]).astype(jnp.int32)
    tokens = teacher_probs.shape[0]
    columns = student_logits.shape[1]
    blocks = columns // BLK
    mine = blocks // halves
    width = mine * BLK
    rows = owners * mine
    per_half = TB // halves
    group_tokens = owners * tokens
    half_tokens = student_logits.shape[0]
    features = hidden.shape[1]
    first = half_index == 0
    bf16, f32 = jnp.bfloat16, jnp.float32
    shape = jax.ShapeDtypeStruct
    dma = lambda count: pltpu.SemaphoreType.DMA((count,))

    def in_order(own, other, axis):
        return jnp.concatenate([jnp.where(first, own, other), jnp.where(first, other, own)], axis=axis)

    hidden = hidden[None]
    offset = owners // 2
    first_piece = to_partner(hidden, offset)

    def merge(one, two):
        top = jnp.maximum(one[0], two[0])
        return top, one[1] * jnp.exp(one[0] - top) + two[1] * jnp.exp(two[0] - top)

    wide = student_logits.astype(f32)
    low = jnp.float32(-1e38)
    stats = jnp.stack(lax.reduce((wide, jnp.ones_like(wide)), (low, jnp.float32(0)), merge, (1,)))
    teacher_given, stats = lax.optimization_barrier((teacher_probs, stats))
    teacher_other = swap_halves(teacher_given)
    stats = in_order(stats, swap_halves(stats), 1)

    local = align_local.T - half_index * mine
    row_of = jnp.where((local >= 0) & (local < mine), align_owner.T * mine + local, -1)
    code = row_of.astype(f32) + 0.5 * align_weight.T.astype(f32)
    cut = lambda which: lax.dynamic_slice_in_dim(code, which * per_half, per_half, 1)
    w_own = block_weights(cut(half_index), rows)
    w_rest = block_weights(cut(1 - half_index), rows)
    spread = pltpu.VMEM((per_half * tokens, BLK), f32)
    flops = 2 * (rows + MASS_ROWS) * per_half * tokens * BLK
    part = pl.pallas_call(
        map_own_kernel,
        out_shape=shape((rows + MASS_ROWS, tokens * BLK), f32),
        in_specs=[in_vmem()] * 2 + [anywhere()],
        out_specs=in_vmem(),
        scratch_shapes=[spread],
        compiler_params=params(),
        cost_estimate=cost(flops, 3 << 20),
        name="map_own",
    )(w_own, teacher_probs, stats)
    chunk = (owners, tokens, width + group_tokens)
    outgoing = pl.pallas_call(
        map_rest_kernel,
        out_shape=shape(chunk, bf16),
        in_specs=[in_vmem()] * 4,
        out_specs=anywhere(),
        scratch_shapes=[
            spread,
            pltpu.VMEM(((rows + 8) * tokens, BLK), f32),
            pltpu.VMEM(chunk, bf16),
            dma(owners),
        ],
        compiler_params=params(),
        cost_estimate=cost(flops, 4 << 20),
        name="map_rest",
    )(w_rest, teacher_other, part, stats)
    outgoing, first_piece = lax.optimization_barrier((outgoing, first_piece))
    target = lax.all_to_all(outgoing, "sv", 0, 0, axis_index_groups=[turned_group(owners, owners // 2)], tiled=True)

    hidden, late_logits, outgoing = lax.optimization_barrier((hidden, student_logits, outgoing))

    keep = lax.dynamic_slice_in_dim(late_logits, half_index * width, width, 1)
    give = lax.dynamic_slice_in_dim(late_logits, (1 - half_index) * width, width, 1)
    logits = in_order(keep, swap_halves(give), 0)

    pieces = [jnp.concatenate([hidden, first_piece])]
    pieces += [to_partner(pieces[0], a) for a in range(1, offset)]

    scale = float(columns * owners)
    lanes = -(-half_tokens // BLK) * BLK
    grad, terms = pl.pallas_call(
        lambda *refs: grad_kernel(scale, *refs),
        out_shape=(shape((group_tokens, width), bf16), shape((owners * halves, 8, lanes), f32)),
        in_specs=[in_vmem()] * 2,
        out_specs=(in_vmem(), anywhere()),
        scratch_shapes=[
            pltpu.VMEM((group_tokens, BLK), f32),
            pltpu.VMEM((owners * halves, 8, lanes), f32),
            pltpu.SemaphoreType.DMA,
        ],
        compiler_params=params(),
        cost_estimate=cost(
            10 * group_tokens * width, 6 * group_tokens * width, 2 * group_tokens * width
        ),
        name="logit_grad",
    )(target, logits)

    everyone = [turned_group(owners * halves, owners // 4 * halves)]
    terms = lax.all_to_all(terms, ("sv", "tv"), 0, 0, axis_index_groups=everyone, tiled=True)
    give = lax.dynamic_slice_in_dim(grad, (1 - half_index) * half_tokens, half_tokens, 0)
    got = swap_halves(give)

    *pieces, grad = lax.optimization_barrier((*pieces, grad))
    hidden_own = jnp.concatenate(pieces)
    steps = 8
    weight_grad, logit_grad = pl.pallas_call(
        weight_kernel,
        out_shape=(shape((features, width), bf16), shape((half_tokens, columns), bf16)),
        in_specs=[scalars()] + [in_vmem()] * 4,
        out_specs=(anywhere(), anywhere()),
        scratch_shapes=[
            pltpu.VMEM((group_tokens, features), f32),
            pltpu.VMEM((features, group_tokens), bf16),
            pltpu.VMEM((steps, features // steps, width), bf16),
            dma(steps),
            dma(2),
        ],
        compiler_params=params(),
        cost_estimate=cost(
            2 * features * group_tokens * width,
            2 * (features * width + group_tokens * (features + width)),
        ),
        name="weight_grad",
    )(place, hidden_own, swap_halves(hidden_own), grad, got)
    terms, logit_grad, weight_grad = lax.optimization_barrier((terms, logit_grad, weight_grad))
    divergence = jnp.sum(terms[:, 0, :half_tokens], axis=0)
    return (divergence, logit_grad, weight_grad)


def solution(mesh):
    return jax.shard_map(
        body,
        mesh=mesh,
        in_specs=(
            P(("grp", "sv"), "tv"),
            P(),
            P(),
            P(),
            P(("grp", "tv"), "sv"),
            P(("grp", "sv", "tv"), None),
        ),
        out_specs=(P(("grp", "tv")), P(("grp", "tv"), "sv"), P(None, ("grp", "sv", "tv"))),
        check_vma=False,
    )
```

```python
import jax
import jax.numpy as jnp
from jax import lax
from jax.experimental import pallas as pl
from jax.experimental.pallas import tpu as pltpu
from jax.sharding import PartitionSpec as P

BLK = 128
TB = 640
TOPA = 2
MASS_ROWS = 16
STEP = 16


def block_weights(code, rows):
    row_ids = lax.broadcasted_iota(jnp.int32, (rows + MASS_ROWS, code.shape[1]), 0)
    total = jnp.zeros(row_ids.shape, jnp.float32)
    for slot in range(TOPA):
        row = jnp.floor(code[slot])
        weight = (code[slot] - row) * 2.0
        hit = (row_ids == row.astype(jnp.int32)[None, :]) | (row_ids == rows + slot)
        total = total + jnp.where(hit, weight[None, :], 0.0)
    return total.astype(jnp.bfloat16)


def turned_group(members, first):
    return [(i + first) % members for i in range(members)]


def spread_tokens(t_ref, s_ref, start, count):
    tokens = t_ref.shape[0]

    def some(i, carry):
        for j in range(STEP):
            k = start + i * STEP + j
            tile = t_ref[:, pl.ds(pl.multiple_of(k * BLK, BLK), BLK)]
            s_ref[pl.ds(pl.multiple_of(k * tokens, tokens), tokens), :] = tile.astype(jnp.float32)
        return carry

    lax.fori_loop(0, count // STEP, some, 0)


def token_pair(s_ref, t, tokens):
    count = s_ref.shape[0] // tokens
    both = [s_ref[pl.ds(t + i, count, stride=tokens), :].astype(jnp.bfloat16) for i in range(2)]
    return jnp.concatenate(both, axis=1)


def map_own_kernel(w_ref, t_ref, stats_ref, o_ref, s_ref):
    tokens = t_ref.shape[0]
    spread_tokens(t_ref, s_ref, 0, t_ref.shape[1] // BLK)
    for t in range(0, tokens, 2):
        o_ref[:, t * BLK : (t + 2) * BLK] = jnp.dot(
            w_ref[...], token_pair(s_ref, t, tokens), preferred_element_type=jnp.float32
        )


def three_parts(x):
    parts = []
    for _ in range(3):
        parts.append(x.astype(jnp.bfloat16).astype(jnp.float32))
        x = x - parts[-1]
    return parts


def map_rest_kernel(w_ref, t_ref, p_ref, stats_ref, o_ref, s_ref, m_ref, o_buf, out_sem):
    tokens = t_ref.shape[0]
    owners = o_ref.shape[0]
    rows = w_ref.shape[0] - MASS_ROWS
    mine = rows // owners
    stats = [stats_ref[0:1, :]] + three_parts(stats_ref[1:2, :])
    extra = jnp.zeros((tokens, stats_ref.shape[1]), jnp.float32)
    row_ids = lax.broadcasted_iota(jnp.int32, extra.shape, 0)
    for i, row in enumerate(stats):
        extra = jnp.where(row_ids == i, row, extra)
    extra = extra.astype(jnp.bfloat16)
    spread_tokens(t_ref, s_ref, 0, t_ref.shape[1] // BLK)
    for t in range(0, tokens, 2):
        both = p_ref[:, t * BLK : (t + 2) * BLK] + jnp.dot(
            w_ref[...], token_pair(s_ref, t, tokens), preferred_element_type=jnp.float32
        )
        for i in range(2):
            m_ref[pl.ds(t + i, rows + 8, stride=tokens), :] = both[: rows + 8, i * BLK : (i + 1) * BLK]
    mass = m_ref[rows * tokens : (rows + 1) * tokens, :]
    for slot in range(1, TOPA):
        mass = mass + m_ref[(rows + slot) * tokens : (rows + slot + 1) * tokens, :]
    inverse = jnp.broadcast_to(1.0 / jnp.sum(mass, axis=1, keepdims=True), (tokens, BLK))

    def leaving(q):
        return pltpu.make_async_copy(o_buf.at[q], o_ref.at[q], out_sem.at[q])

    def owner(q, carry):
        member = lax.rem(q + owners // 2, owners)
        for b in range(mine):
            first = pl.multiple_of((member * mine + b) * tokens, tokens)
            tile = m_ref[pl.ds(first, tokens), :] * inverse
            o_buf[q, :, b * BLK : (b + 1) * BLK] = tile.astype(jnp.bfloat16)
        o_buf[q, :, mine * BLK :] = extra
        leaving(q).start()
        return carry

    def left(q, carry):
        leaving(q).wait()
        return carry

    lax.fori_loop(0, owners, owner, 0)
    lax.fori_loop(0, owners, left, 0)


def grad_kernel(scale, target_ref, logits_ref, grad_ref, terms_ref, norm_ref, t_buf, sem):
    owners, tokens, _ = target_ref.shape
    group_tokens, width = logits_ref.shape
    stats = [target_ref[q, :, width:].astype(jnp.float32) for q in range(owners)]
    top = stats[0][0:1]
    for one in stats[1:]:
        top = jnp.maximum(top, one[0:1])
    total = jnp.zeros_like(top)
    for one in stats:
        total = total + (one[1:2] + one[2:3] + one[3:4]) * jnp.exp(one[0:1] - top)
    log_norm = top + jnp.log(total)

    def block(i, b):
        lanes = slice(b * BLK, (b + 1) * BLK)
        first, count = i * BLK // tokens, BLK // tokens
        at = (first - owners // 2) % owners
        cut = min(count, owners - at)
        target = target_ref[at : at + cut, :, lanes].reshape(cut * tokens, BLK)
        if cut < count:
            rest = target_ref[: count - cut, :, lanes].reshape((count - cut) * tokens, BLK)
            target = jnp.concatenate([target, rest], axis=0)
        target = target.astype(jnp.float32)
        return target, logits_ref[i * BLK : (i + 1) * BLK, lanes].astype(jnp.float32)

    sums = []
    for i in range(group_tokens // BLK):
        rows = slice(i * BLK, (i + 1) * BLK)
        norm = jnp.broadcast_to(log_norm[:, rows], (BLK, BLK)).T
        norm_ref[rows, :] = norm
        terms = jnp.zeros((BLK, BLK), jnp.float32)
        for b in range(width // BLK):
            target, logits = block(i, b)
            positive = target > 0
            one = target * (jnp.log(jnp.where(positive, target, 1.0)) - (logits - norm))
            terms = terms + jnp.where(positive, one, 0.0)
        sums.append(jnp.sum(terms.T, axis=0, keepdims=True))
    row = jnp.concatenate(sums, axis=1)
    half_tokens = group_tokens // 2
    for half in range(2):
        mine = row[:, half * half_tokens : (half + 1) * half_tokens]
        tile = jnp.concatenate([mine] * (t_buf.shape[2] // half_tokens), axis=1)
        for q in range(owners):
            t_buf[2 * q + half] = jnp.broadcast_to(tile, t_buf.shape[1:])
    leaving = pltpu.make_async_copy(t_buf, terms_ref, sem)
    leaving.start()
    for i in range(group_tokens // BLK):
        rows = slice(i * BLK, (i + 1) * BLK)
        for b in range(width // BLK):
            target, logits = block(i, b)
            grad = (jnp.exp(logits - norm_ref[rows, :]) - target) * scale
            grad_ref[rows, b * BLK : (b + 1) * BLK] = grad.astype(jnp.bfloat16)
    leaving.wait()


def arrival_order(owners):
    return [a for b in range(owners // 2) for a in (b, b + owners // 2)]


def weight_kernel(
    place_ref, own_ref, got_ref, grad_ref, o_ref, joined_ref, s_ref, h_ref, block_ref, sems, join_sems
):
    half_tokens, width = got_ref.shape[0], grad_ref.shape[1]
    half = place_ref[1]
    kept_at = pl.ds(pl.multiple_of(half * width, width), width)
    got_at = pl.ds(pl.multiple_of((1 - half) * width, width), width)
    kept = pl.ds(pl.multiple_of(half * half_tokens, half_tokens), half_tokens)
    copies = [
        pltpu.make_async_copy(grad_ref.at[kept, :], joined_ref.at[:, kept_at], join_sems.at[0]),
        pltpu.make_async_copy(got_ref.at[:, pl.ds(0, width)], joined_ref.at[:, got_at], join_sems.at[1]),
    ]
    for copy in copies:
        copy.start()
    owners, held, features = own_ref.shape
    for i, offset in enumerate(arrival_order(owners)):
        first = (place_ref[0] ^ offset) * 2
        own = pl.ds(pl.multiple_of((first + half) * held, held), held)
        other = pl.ds(pl.multiple_of((first + 1 - half) * held, held), held)
        s_ref[own, :] = own_ref[i].astype(jnp.float32)
        pair = got_ref[i // 2 * 2 * held : (i // 2 + 1) * 2 * held, width:].astype(jnp.float32)
        s_ref[other, :] = pair[i % 2 * held : (i % 2 + 1) * held]
    for i in range(s_ref.shape[0] // BLK):
        for j in range(features // BLK):
            tile = s_ref[i * BLK : (i + 1) * BLK, j * BLK : (j + 1) * BLK].T
            h_ref[j * BLK : (j + 1) * BLK, i * BLK : (i + 1) * BLK] = tile.astype(jnp.bfloat16)
    steps, tile, _ = block_ref.shape
    for i in range(steps):
        rows = slice(i * tile, (i + 1) * tile)
        block_ref[i] = jnp.dot(
            h_ref[rows, :], grad_ref[...], preferred_element_type=jnp.float32
        ).astype(jnp.bfloat16)
        copies.append(pltpu.make_async_copy(block_ref.at[i], o_ref.at[pl.ds(i * tile, tile), :], sems.at[i]))
        copies[-1].start()
    for copy in copies:
        copy.wait()


def in_vmem():
    return pl.BlockSpec(memory_space=pltpu.VMEM)


def scalars():
    return pl.BlockSpec(memory_space=pltpu.SMEM)


def anywhere():
    return pl.BlockSpec(memory_space=pl.ANY)


def params(mib=48):
    return pltpu.CompilerParams(vmem_limit_bytes=mib << 20)


def cost(flops=0, bytes_accessed=0, transcendentals=0):
    return pl.CostEstimate(flops=flops, bytes_accessed=bytes_accessed, transcendentals=transcendentals)


def swap_halves(x):
    return lax.ppermute(x, "tv", [(0, 1), (1, 0)])


def to_partner(x, offset):
    return lax.ppermute(x, "sv", [(s, s ^ offset) for s in range(lax.axis_size("sv"))])


def body(teacher_probs, align_owner, align_local, align_weight, student_logits, hidden):
    owners = lax.axis_size("sv")
    halves = lax.axis_size("tv")
    half_index = lax.axis_index("tv")
    place = jnp.stack([lax.axis_index("sv"), half_index]).astype(jnp.int32)
    tokens = teacher_probs.shape[0]
    columns = student_logits.shape[1]
    blocks = columns // BLK
    mine = blocks // halves
    width = mine * BLK
    rows = owners * mine
    per_half = TB // halves
    group_tokens = owners * tokens
    half_tokens = student_logits.shape[0]
    features = hidden.shape[1]
    first = half_index == 0
    bf16, f32 = jnp.bfloat16, jnp.float32
    shape = jax.ShapeDtypeStruct
    dma = lambda count: pltpu.SemaphoreType.DMA((count,))

    def in_order(own, other, axis):
        return jnp.concatenate([jnp.where(first, own, other), jnp.where(first, other, own)], axis=axis)

    hidden = hidden[None]
    offset = owners // 2
    first_piece = to_partner(hidden, offset)

    def merge(one, two):
        top = jnp.maximum(one[0], two[0])
        return top, one[1] * jnp.exp(one[0] - top) + two[1] * jnp.exp(two[0] - top)

    wide = student_logits.astype(f32)
    low = jnp.float32(-1e38)
    stats = jnp.stack(lax.reduce((wide, jnp.ones_like(wide)), (low, jnp.float32(0)), merge, (1,)))
    teacher_given, stats = lax.optimization_barrier((teacher_probs, stats))
    teacher_other = swap_halves(teacher_given)
    stats = in_order(stats, swap_halves(stats), 1)

    local = align_local.T - half_index * mine
    row_of = jnp.where((local >= 0) & (local < mine), align_owner.T * mine + local, -1)
    code = row_of.astype(f32) + 0.5 * align_weight.T.astype(f32)
    cut = lambda which: lax.dynamic_slice_in_dim(code, which * per_half, per_half, 1)
    w_own = block_weights(cut(half_index), rows)
    w_rest = block_weights(cut(1 - half_index), rows)
    spread = pltpu.VMEM((per_half * tokens, BLK), f32)
    flops = 2 * (rows + MASS_ROWS) * per_half * tokens * BLK
    part = pl.pallas_call(
        map_own_kernel,
        out_shape=shape((rows + MASS_ROWS, tokens * BLK), f32),
        in_specs=[in_vmem()] * 2 + [anywhere()],
        out_specs=in_vmem(),
        scratch_shapes=[spread],
        compiler_params=params(),
        cost_estimate=cost(flops, 3 << 20),
        name="map_own",
    )(w_own, teacher_probs, stats)
    chunk = (owners, tokens, width + group_tokens)
    outgoing = pl.pallas_call(
        map_rest_kernel,
        out_shape=shape(chunk, bf16),
        in_specs=[in_vmem()] * 4,
        out_specs=anywhere(),
        scratch_shapes=[
            spread,
            pltpu.VMEM(((rows + 8) * tokens, BLK), f32),
            pltpu.VMEM(chunk, bf16),
            dma(owners),
        ],
        compiler_params=params(),
        cost_estimate=cost(flops, 4 << 20),
        name="map_rest",
    )(w_rest, teacher_other, part, stats)
    outgoing, first_piece = lax.optimization_barrier((outgoing, first_piece))
    target = lax.all_to_all(outgoing, "sv", 0, 0, axis_index_groups=[turned_group(owners, owners // 2)], tiled=True)

    hidden, late_logits, outgoing = lax.optimization_barrier((hidden, student_logits, outgoing))

    keep = lax.dynamic_slice_in_dim(late_logits, half_index * width, width, 1)
    give = lax.dynamic_slice_in_dim(late_logits, (1 - half_index) * width, width, 1)
    logits = in_order(keep, swap_halves(give), 0)

    pieces = [jnp.concatenate([hidden, first_piece])]
    pieces += [to_partner(pieces[0], a) for a in range(1, offset)]

    scale = float(columns * owners)
    lanes = -(-half_tokens // BLK) * BLK
    grad, terms = pl.pallas_call(
        lambda *refs: grad_kernel(scale, *refs),
        out_shape=(shape((group_tokens, width), bf16), shape((owners * halves, 8, lanes), f32)),
        in_specs=[in_vmem()] * 2,
        out_specs=(in_vmem(), anywhere()),
        scratch_shapes=[
            pltpu.VMEM((group_tokens, BLK), f32),
            pltpu.VMEM((owners * halves, 8, lanes), f32),
            pltpu.SemaphoreType.DMA,
        ],
        compiler_params=params(),
        cost_estimate=cost(
            10 * group_tokens * width, 6 * group_tokens * width, 2 * group_tokens * width
        ),
        name="logit_grad",
    )(target, logits)

    everyone = [turned_group(owners * halves, owners // 4 * halves)]
    terms = lax.all_to_all(terms, ("sv", "tv"), 0, 0, axis_index_groups=everyone, tiled=True)
    *pieces, grad = lax.optimization_barrier((*pieces, grad))
    give = lax.dynamic_slice_in_dim(grad, (1 - half_index) * half_tokens, half_tokens, 0)
    hidden_own = jnp.concatenate(pieces)
    got = swap_halves(jnp.concatenate([give, hidden_own.reshape(half_tokens, features)], axis=1))
    steps = 8
    weight_grad, logit_grad = pl.pallas_call(
        weight_kernel,
        out_shape=(shape((features, width), bf16), shape((half_tokens, columns), bf16)),
        in_specs=[scalars()] + [in_vmem()] * 3,
        out_specs=(anywhere(), anywhere()),
        scratch_shapes=[
            pltpu.VMEM((group_tokens, features), f32),
            pltpu.VMEM((features, group_tokens), bf16),
            pltpu.VMEM((steps, features // steps, width), bf16),
            dma(steps),
            dma(2),
        ],
        compiler_params=params(),
        cost_estimate=cost(
            2 * features * group_tokens * width,
            2 * (features * width + group_tokens * (features + width)),
        ),
        name="weight_grad",
    )(place, hidden_own, got, grad)
    terms, logit_grad, weight_grad = lax.optimization_barrier((terms, logit_grad, weight_grad))
    divergence = jnp.sum(terms[:, 0, :half_tokens], axis=0)
    return (divergence, logit_grad, weight_grad)


def solution(mesh):
    return jax.shard_map(
        body,
        mesh=mesh,
        in_specs=(
            P(("grp", "sv"), "tv"),
            P(),
            P(),
            P(),
            P(("grp", "tv"), "sv"),
            P(("grp", "sv", "tv"), None),
        ),
        out_specs=(P(("grp", "tv")), P(("grp", "tv"), "sv"), P(None, ("grp", "sv", "tv"))),
        check_vma=False,
    )
```

```python
import jax
import jax.numpy as jnp
from jax import lax
from jax.experimental import pallas as pl
from jax.experimental.pallas import tpu as pltpu
from jax.sharding import PartitionSpec as P

BLK = 128
TB = 640
TOPA = 2
MASS_ROWS = 16
STEP = 16


def block_weights(code, rows):
    row_ids = lax.broadcasted_iota(jnp.int32, (rows + MASS_ROWS, code.shape[1]), 0)
    total = jnp.zeros(row_ids.shape, jnp.float32)
    for slot in range(TOPA):
        row = jnp.floor(code[slot])
        weight = (code[slot] - row) * 2.0
        hit = (row_ids == row.astype(jnp.int32)[None, :]) | (row_ids == rows + slot)
        total = total + jnp.where(hit, weight[None, :], 0.0)
    return total.astype(jnp.bfloat16)


def turned_group(members, first):
    return [(i + first) % members for i in range(members)]


def spread_tokens(t_ref, s_ref, start, count):
    tokens = t_ref.shape[0]

    def some(i, carry):
        for j in range(STEP):
            k = start + i * STEP + j
            tile = t_ref[:, pl.ds(pl.multiple_of(k * BLK, BLK), BLK)]
            s_ref[pl.ds(pl.multiple_of(k * tokens, tokens), tokens), :] = tile.astype(jnp.float32)
        return carry

    lax.fori_loop(0, count // STEP, some, 0)


def token_pair(s_ref, t, tokens):
    count = s_ref.shape[0] // tokens
    both = [s_ref[pl.ds(t + i, count, stride=tokens), :].astype(jnp.bfloat16) for i in range(2)]
    return jnp.concatenate(both, axis=1)


def map_own_kernel(w_ref, t_ref, stats_ref, o_ref, s_ref):
    tokens = t_ref.shape[0]
    spread_tokens(t_ref, s_ref, 0, t_ref.shape[1] // BLK)
    for t in range(0, tokens, 2):
        o_ref[:, t * BLK : (t + 2) * BLK] = jnp.dot(
            w_ref[...], token_pair(s_ref, t, tokens), preferred_element_type=jnp.float32
        )


def three_parts(x):
    parts = []
    for _ in range(3):
        parts.append(x.astype(jnp.bfloat16).astype(jnp.float32))
        x = x - parts[-1]
    return parts


def map_rest_kernel(w_ref, t_ref, p_ref, stats_ref, o_ref, s_ref, m_ref, o_buf, out_sem):
    tokens = t_ref.shape[0]
    owners = o_ref.shape[0]
    rows = w_ref.shape[0] - MASS_ROWS
    mine = rows // owners
    stats = [stats_ref[0:1, :]] + three_parts(stats_ref[1:2, :])
    extra = jnp.zeros((tokens, stats_ref.shape[1]), jnp.float32)
    row_ids = lax.broadcasted_iota(jnp.int32, extra.shape, 0)
    for i, row in enumerate(stats):
        extra = jnp.where(row_ids == i, row, extra)
    extra = extra.astype(jnp.bfloat16)
    spread_tokens(t_ref, s_ref, 0, t_ref.shape[1] // BLK)
    for t in range(0, tokens, 2):
        both = p_ref[:, t * BLK : (t + 2) * BLK] + jnp.dot(
            w_ref[...], token_pair(s_ref, t, tokens), preferred_element_type=jnp.float32
        )
        for i in range(2):
            m_ref[pl.ds(t + i, rows + 8, stride=tokens), :] = both[: rows + 8, i * BLK : (i + 1) * BLK]
    mass = m_ref[rows * tokens : (rows + 1) * tokens, :]
    for slot in range(1, TOPA):
        mass = mass + m_ref[(rows + slot) * tokens : (rows + slot + 1) * tokens, :]
    inverse = jnp.broadcast_to(1.0 / jnp.sum(mass, axis=1, keepdims=True), (tokens, BLK))

    def leaving(q):
        return pltpu.make_async_copy(o_buf.at[q], o_ref.at[q], out_sem.at[q])

    def owner(q, carry):
        member = lax.rem(q + owners // 2, owners)
        for b in range(mine):
            first = pl.multiple_of((member * mine + b) * tokens, tokens)
            tile = m_ref[pl.ds(first, tokens), :] * inverse
            o_buf[q, :, b * BLK : (b + 1) * BLK] = tile.astype(jnp.bfloat16)
        o_buf[q, :, mine * BLK :] = extra
        leaving(q).start()
        return carry

    def left(q, carry):
        leaving(q).wait()
        return carry

    lax.fori_loop(0, owners, owner, 0)
    lax.fori_loop(0, owners, left, 0)


def grad_kernel(scale, target_ref, logits_ref, grad_ref, terms_ref, norm_ref, t_buf, sem):
    owners, tokens, _ = target_ref.shape
    group_tokens, width = logits_ref.shape
    stats = [target_ref[q, :, width:].astype(jnp.float32) for q in range(owners)]
    top = stats[0][0:1]
    for one in stats[1:]:
        top = jnp.maximum(top, one[0:1])
    total = jnp.zeros_like(top)
    for one in stats:
        total = total + (one[1:2] + one[2:3] + one[3:4]) * jnp.exp(one[0:1] - top)
    log_norm = top + jnp.log(total)

    def block(i, b):
        lanes = slice(b * BLK, (b + 1) * BLK)
        first, count = i * BLK // tokens, BLK // tokens
        at = (first - owners // 2) % owners
        cut = min(count, owners - at)
        target = target_ref[at : at + cut, :, lanes].reshape(cut * tokens, BLK)
        if cut < count:
            rest = target_ref[: count - cut, :, lanes].reshape((count - cut) * tokens, BLK)
            target = jnp.concatenate([target, rest], axis=0)
        target = target.astype(jnp.float32)
        return target, logits_ref[i * BLK : (i + 1) * BLK, lanes].astype(jnp.float32)

    sums = []
    for i in range(group_tokens // BLK):
        rows = slice(i * BLK, (i + 1) * BLK)
        norm = jnp.broadcast_to(log_norm[:, rows], (BLK, BLK)).T
        norm_ref[rows, :] = norm
        terms = jnp.zeros((BLK, BLK), jnp.float32)
        for b in range(width // BLK):
            target, logits = block(i, b)
            positive = target > 0
            one = target * (jnp.log(jnp.where(positive, target, 1.0)) - (logits - norm))
            terms = terms + jnp.where(positive, one, 0.0)
        sums.append(jnp.sum(terms.T, axis=0, keepdims=True))
    row = jnp.concatenate(sums, axis=1)
    half_tokens = group_tokens // 2
    for half in range(2):
        mine = row[:, half * half_tokens : (half + 1) * half_tokens]
        tile = jnp.concatenate([mine] * (t_buf.shape[2] // half_tokens), axis=1)
        for q in range(owners):
            t_buf[2 * q + half] = jnp.broadcast_to(tile, t_buf.shape[1:])
    leaving = pltpu.make_async_copy(t_buf, terms_ref, sem)
    leaving.start()
    for i in range(group_tokens // BLK):
        rows = slice(i * BLK, (i + 1) * BLK)
        for b in range(width // BLK):
            target, logits = block(i, b)
            grad = (jnp.exp(logits - norm_ref[rows, :]) - target) * scale
            grad_ref[rows, b * BLK : (b + 1) * BLK] = grad.astype(jnp.bfloat16)
    leaving.wait()


def arrival_order(owners):
    return [a for b in range(owners // 2) for a in (b, b + owners // 2)]


def weight_kernel(
    place_ref, own_ref, got_ref, grad_ref, o_ref, joined_ref, s_ref, h_ref, block_ref, sems, join_sems
):
    half_tokens, width = got_ref.shape[0], grad_ref.shape[1]
    half = place_ref[1]
    kept_at = pl.ds(pl.multiple_of(half * width, width), width)
    got_at = pl.ds(pl.multiple_of((1 - half) * width, width), width)
    kept = pl.ds(pl.multiple_of(half * half_tokens, half_tokens), half_tokens)
    copies = [
        pltpu.make_async_copy(grad_ref.at[kept, :], joined_ref.at[:, kept_at], join_sems.at[0]),
        pltpu.make_async_copy(got_ref.at[:, pl.ds(0, width)], joined_ref.at[:, got_at], join_sems.at[1]),
    ]
    for copy in copies:
        copy.start()
    owners, held, features = own_ref.shape
    for i, offset in enumerate(arrival_order(owners)):
        first = (place_ref[0] ^ offset) * 2
        own = pl.ds(pl.multiple_of((first + half) * held, held), held)
        other = pl.ds(pl.multiple_of((first + 1 - half) * held, held), held)
        s_ref[own, :] = own_ref[i].astype(jnp.float32)
        pair = got_ref[i // 2 * 2 * held : (i // 2 + 1) * 2 * held, width:].astype(jnp.float32)
        s_ref[other, :] = pair[i % 2 * held : (i % 2 + 1) * held]
    for i in range(s_ref.shape[0] // BLK):
        for j in range(features // BLK):
            tile = s_ref[i * BLK : (i + 1) * BLK, j * BLK : (j + 1) * BLK].T
            h_ref[j * BLK : (j + 1) * BLK, i * BLK : (i + 1) * BLK] = tile.astype(jnp.bfloat16)
    steps, tile, _ = block_ref.shape
    for i in range(steps):
        rows = slice(i * tile, (i + 1) * tile)
        block_ref[i] = jnp.dot(
            h_ref[rows, :], grad_ref[...], preferred_element_type=jnp.float32
        ).astype(jnp.bfloat16)
        copies.append(pltpu.make_async_copy(block_ref.at[i], o_ref.at[pl.ds(i * tile, tile), :], sems.at[i]))
        copies[-1].start()
    for copy in copies:
        copy.wait()


def in_vmem():
    return pl.BlockSpec(memory_space=pltpu.VMEM)


def scalars():
    return pl.BlockSpec(memory_space=pltpu.SMEM)


def anywhere():
    return pl.BlockSpec(memory_space=pl.ANY)


def params(mib=48):
    return pltpu.CompilerParams(vmem_limit_bytes=mib << 20)


def cost(flops=0, bytes_accessed=0, transcendentals=0):
    return pl.CostEstimate(flops=flops, bytes_accessed=bytes_accessed, transcendentals=transcendentals)


def swap_halves(x):
    return lax.ppermute(x, "tv", [(0, 1), (1, 0)])


def to_partner(x, offset):
    return lax.ppermute(x, "sv", [(s, s ^ offset) for s in range(lax.axis_size("sv"))])


def body(teacher_probs, align_owner, align_local, align_weight, student_logits, hidden):
    owners = lax.axis_size("sv")
    halves = lax.axis_size("tv")
    half_index = lax.axis_index("tv")
    place = jnp.stack([lax.axis_index("sv"), half_index]).astype(jnp.int32)
    tokens = teacher_probs.shape[0]
    columns = student_logits.shape[1]
    blocks = columns // BLK
    mine = blocks // halves
    width = mine * BLK
    rows = owners * mine
    per_half = TB // halves
    group_tokens = owners * tokens
    half_tokens = student_logits.shape[0]
    features = hidden.shape[1]
    first = half_index == 0
    bf16, f32 = jnp.bfloat16, jnp.float32
    shape = jax.ShapeDtypeStruct
    dma = lambda count: pltpu.SemaphoreType.DMA((count,))

    def in_order(own, other, axis):
        return jnp.concatenate([jnp.where(first, own, other), jnp.where(first, other, own)], axis=axis)

    hidden = hidden[None]
    offset = owners // 2
    first_piece = to_partner(hidden, offset)

    def merge(one, two):
        top = jnp.maximum(one[0], two[0])
        return top, one[1] * jnp.exp(one[0] - top) + two[1] * jnp.exp(two[0] - top)

    wide = student_logits.astype(f32)
    low = jnp.float32(-1e38)
    stats = jnp.stack(lax.reduce((wide, jnp.ones_like(wide)), (low, jnp.float32(0)), merge, (1,)))
    teacher_given, stats = lax.optimization_barrier((teacher_probs, stats))
    teacher_other = swap_halves(teacher_given)
    stats = in_order(stats, swap_halves(stats), 1)

    local = align_local.T - half_index * mine
    row_of = jnp.where((local >= 0) & (local < mine), align_owner.T * mine + local, -1)
    code = row_of.astype(f32) + 0.5 * align_weight.T.astype(f32)
    cut = lambda which: lax.dynamic_slice_in_dim(code, which * per_half, per_half, 1)
    w_own = block_weights(cut(half_index), rows)
    w_rest = block_weights(cut(1 - half_index), rows)
    spread = pltpu.VMEM((per_half * tokens, BLK), f32)
    flops = 2 * (rows + MASS_ROWS) * per_half * tokens * BLK
    part = pl.pallas_call(
        map_own_kernel,
        out_shape=shape((rows + MASS_ROWS, tokens * BLK), f32),
        in_specs=[in_vmem()] * 2 + [anywhere()],
        out_specs=in_vmem(),
        scratch_shapes=[spread],
        compiler_params=params(),
        cost_estimate=cost(flops, 3 << 20),
        name="map_own",
    )(w_own, teacher_probs, stats)
    chunk = (owners, tokens, width + group_tokens)
    outgoing = pl.pallas_call(
        map_rest_kernel,
        out_shape=shape(chunk, bf16),
        in_specs=[in_vmem()] * 4,
        out_specs=anywhere(),
        scratch_shapes=[
            spread,
            pltpu.VMEM(((rows + 8) * tokens, BLK), f32),
            pltpu.VMEM(chunk, bf16),
            dma(owners),
        ],
        compiler_params=params(),
        cost_estimate=cost(flops, 4 << 20),
        name="map_rest",
    )(w_rest, teacher_other, part, stats)
    outgoing, first_piece = lax.optimization_barrier((outgoing, first_piece))
    target = lax.all_to_all(outgoing, "sv", 0, 0, axis_index_groups=[turned_group(owners, owners // 2)], tiled=True)

    hidden, late_logits, outgoing = lax.optimization_barrier((hidden, student_logits, outgoing))

    keep = lax.dynamic_slice_in_dim(late_logits, half_index * width, width, 1)
    give = lax.dynamic_slice_in_dim(late_logits, (1 - half_index) * width, width, 1)
    logits = in_order(keep, swap_halves(give), 0)

    pieces = [jnp.concatenate([hidden, first_piece])]
    pieces += [to_partner(pieces[0], a) for a in range(1, offset)]

    scale = float(columns * owners)
    lanes = -(-half_tokens // BLK) * BLK
    grad, terms = pl.pallas_call(
        lambda *refs: grad_kernel(scale, *refs),
        out_shape=(shape((group_tokens, width), bf16), shape((owners * halves, 8, lanes), f32)),
        in_specs=[in_vmem()] * 2,
        out_specs=(in_vmem(), anywhere()),
        scratch_shapes=[
            pltpu.VMEM((group_tokens, BLK), f32),
            pltpu.VMEM((owners * halves, 8, lanes), f32),
            pltpu.SemaphoreType.DMA,
        ],
        compiler_params=params(),
        cost_estimate=cost(
            10 * group_tokens * width, 6 * group_tokens * width, 2 * group_tokens * width
        ),
        name="logit_grad",
    )(target, logits)

    everyone = [turned_group(owners * halves, owners // 2 * halves)]
    terms = lax.all_to_all(terms, ("sv", "tv"), 0, 0, axis_index_groups=everyone, tiled=True)
    *pieces, grad = lax.optimization_barrier((*pieces, grad))
    give = lax.dynamic_slice_in_dim(grad, (1 - half_index) * half_tokens, half_tokens, 0)
    hidden_own = jnp.concatenate(pieces)
    got = swap_halves(jnp.concatenate([give, hidden_own.reshape(half_tokens, features)], axis=1))
    steps = 8
    weight_grad, logit_grad = pl.pallas_call(
        weight_kernel,
        out_shape=(shape((features, width), bf16), shape((half_tokens, columns), bf16)),
        in_specs=[scalars()] + [in_vmem()] * 3,
        out_specs=(anywhere(), anywhere()),
        scratch_shapes=[
            pltpu.VMEM((group_tokens, features), f32),
            pltpu.VMEM((features, group_tokens), bf16),
            pltpu.VMEM((steps, features // steps, width), bf16),
            dma(steps),
            dma(2),
        ],
        compiler_params=params(),
        cost_estimate=cost(
            2 * features * group_tokens * width,
            2 * (features * width + group_tokens * (features + width)),
        ),
        name="weight_grad",
    )(place, hidden_own, got, grad)
    terms, logit_grad, weight_grad = lax.optimization_barrier((terms, logit_grad, weight_grad))
    divergence = jnp.sum(terms[:, 0, :half_tokens], axis=0)
    return (divergence, logit_grad, weight_grad)


def solution(mesh):
    return jax.shard_map(
        body,
        mesh=mesh,
        in_specs=(
            P(("grp", "sv"), "tv"),
            P(),
            P(),
            P(),
            P(("grp", "tv"), "sv"),
            P(("grp", "sv", "tv"), None),
        ),
        out_specs=(P(("grp", "tv")), P(("grp", "tv"), "sv"), P(None, ("grp", "sv", "tv"))),
        check_vma=False,
    )
```

```python
import jax
import jax.numpy as jnp
from jax import lax
from jax.experimental import pallas as pl
from jax.experimental.pallas import tpu as pltpu
from jax.sharding import PartitionSpec as P

BLK = 128
TB = 640
TOPA = 2
MASS_ROWS = 16
STEP = 16


def block_weights(code, rows):
    row_ids = lax.broadcasted_iota(jnp.int32, (rows + MASS_ROWS, code.shape[1]), 0)
    total = jnp.zeros(row_ids.shape, jnp.float32)
    for slot in range(TOPA):
        row = jnp.floor(code[slot])
        weight = (code[slot] - row) * 2.0
        hit = (row_ids == row.astype(jnp.int32)[None, :]) | (row_ids == rows + slot)
        total = total + jnp.where(hit, weight[None, :], 0.0)
    return total.astype(jnp.bfloat16)


def turned_group(members, first):
    return [(i + first) % members for i in range(members)]


def spread_tokens(t_ref, s_ref, start, count):
    tokens = t_ref.shape[0]

    def some(i, carry):
        for j in range(STEP):
            k = start + i * STEP + j
            tile = t_ref[:, pl.ds(pl.multiple_of(k * BLK, BLK), BLK)]
            s_ref[pl.ds(pl.multiple_of(k * tokens, tokens), tokens), :] = tile.astype(jnp.float32)
        return carry

    lax.fori_loop(0, count // STEP, some, 0)


def token_pair(s_ref, t, tokens):
    count = s_ref.shape[0] // tokens
    both = [s_ref[pl.ds(t + i, count, stride=tokens), :].astype(jnp.bfloat16) for i in range(2)]
    return jnp.concatenate(both, axis=1)


def map_own_kernel(w_ref, t_ref, stats_ref, o_ref, s_ref):
    tokens = t_ref.shape[0]
    spread_tokens(t_ref, s_ref, 0, t_ref.shape[1] // BLK)
    for t in range(0, tokens, 2):
        o_ref[:, t * BLK : (t + 2) * BLK] = jnp.dot(
            w_ref[...], token_pair(s_ref, t, tokens), preferred_element_type=jnp.float32
        )


def three_parts(x):
    parts = []
    for _ in range(3):
        parts.append(x.astype(jnp.bfloat16).astype(jnp.float32))
        x = x - parts[-1]
    return parts


def map_rest_kernel(w_ref, t_ref, p_ref, stats_ref, o_ref, s_ref, m_ref, o_buf, out_sem):
    tokens = t_ref.shape[0]
    owners = o_ref.shape[0]
    rows = w_ref.shape[0] - MASS_ROWS
    mine = rows // owners
    stats = [stats_ref[0:1, :]] + three_parts(stats_ref[1:2, :])
    extra = jnp.zeros((tokens, stats_ref.shape[1]), jnp.float32)
    row_ids = lax.broadcasted_iota(jnp.int32, extra.shape, 0)
    for i, row in enumerate(stats):
        extra = jnp.where(row_ids == i, row, extra)
    extra = extra.astype(jnp.bfloat16)
    spread_tokens(t_ref, s_ref, 0, t_ref.shape[1] // BLK)
    for t in range(0, tokens, 2):
        both = p_ref[:, t * BLK : (t + 2) * BLK] + jnp.dot(
            w_ref[...], token_pair(s_ref, t, tokens), preferred_element_type=jnp.float32
        )
        for i in range(2):
            m_ref[pl.ds(t + i, rows + 8, stride=tokens), :] = both[: rows + 8, i * BLK : (i + 1) * BLK]
    mass = m_ref[rows * tokens : (rows + 1) * tokens, :]
    for slot in range(1, TOPA):
        mass = mass + m_ref[(rows + slot) * tokens : (rows + slot + 1) * tokens, :]
    inverse = jnp.broadcast_to(1.0 / jnp.sum(mass, axis=1, keepdims=True), (tokens, BLK))

    def leaving(q):
        return pltpu.make_async_copy(o_buf.at[q], o_ref.at[q], out_sem.at[q])

    def owner(q, carry):
        member = lax.rem(q + owners // 2, owners)
        for b in range(mine):
            first = pl.multiple_of((member * mine + b) * tokens, tokens)
            tile = m_ref[pl.ds(first, tokens), :] * inverse
            o_buf[q, :, b * BLK : (b + 1) * BLK] = tile.astype(jnp.bfloat16)
        o_buf[q, :, mine * BLK :] = extra
        leaving(q).start()
        return carry

    def left(q, carry):
        leaving(q).wait()
        return carry

    lax.fori_loop(0, owners, owner, 0)
    lax.fori_loop(0, owners, left, 0)


def grad_kernel(scale, target_ref, logits_ref, grad_ref, terms_ref, norm_ref, t_buf, sem):
    owners, tokens, _ = target_ref.shape
    group_tokens, width = logits_ref.shape
    stats = [target_ref[q, :, width:].astype(jnp.float32) for q in range(owners)]
    top = stats[0][0:1]
    for one in stats[1:]:
        top = jnp.maximum(top, one[0:1])
    total = jnp.zeros_like(top)
    for one in stats:
        total = total + (one[1:2] + one[2:3] + one[3:4]) * jnp.exp(one[0:1] - top)
    log_norm = top + jnp.log(total)

    def block(i, b):
        lanes = slice(b * BLK, (b + 1) * BLK)
        first, count = i * BLK // tokens, BLK // tokens
        at = (first - owners // 2) % owners
        cut = min(count, owners - at)
        target = target_ref[at : at + cut, :, lanes].reshape(cut * tokens, BLK)
        if cut < count:
            rest = target_ref[: count - cut, :, lanes].reshape((count - cut) * tokens, BLK)
            target = jnp.concatenate([target, rest], axis=0)
        target = target.astype(jnp.float32)
        return target, logits_ref[i * BLK : (i + 1) * BLK, lanes].astype(jnp.float32)

    sums = []
    for i in range(group_tokens // BLK):
        rows = slice(i * BLK, (i + 1) * BLK)
        norm = jnp.broadcast_to(log_norm[:, rows], (BLK, BLK)).T
        norm_ref[rows, :] = norm
        terms = jnp.zeros((BLK, BLK), jnp.float32)
        for b in range(width // BLK):
            target, logits = block(i, b)
            positive = target > 0
            one = target * (jnp.log(jnp.where(positive, target, 1.0)) - (logits - norm))
            terms = terms + jnp.where(positive, one, 0.0)
        sums.append(jnp.sum(terms.T, axis=0, keepdims=True))
    row = jnp.concatenate(sums, axis=1)
    half_tokens = group_tokens // 2
    for half in range(2):
        mine = row[:, half * half_tokens : (half + 1) * half_tokens]
        tile = jnp.concatenate([mine] * (t_buf.shape[2] // half_tokens), axis=1)
        for q in range(owners):
            t_buf[2 * q + half] = jnp.broadcast_to(tile, t_buf.shape[1:])
    leaving = pltpu.make_async_copy(t_buf, terms_ref, sem)
    leaving.start()
    for i in range(group_tokens // BLK):
        rows = slice(i * BLK, (i + 1) * BLK)
        for b in range(width // BLK):
            target, logits = block(i, b)
            grad = (jnp.exp(logits - norm_ref[rows, :]) - target) * scale
            grad_ref[rows, b * BLK : (b + 1) * BLK] = grad.astype(jnp.bfloat16)
    leaving.wait()


def arrival_order(owners):
    return [a for b in range(owners // 2) for a in (b, b + owners // 2)]


def row_blocks(features):
    tiles = features // BLK
    sizes = [2] + [3] * ((tiles - 3) // 3)
    sizes.append(tiles - sum(sizes))
    return [size * BLK for size in sizes]


def weight_kernel(
    place_ref, own_ref, got_ref, grad_ref, o_ref, joined_ref, s_ref, h_ref, block_ref, sems, join_sems
):
    half_tokens, width = got_ref.shape[0], grad_ref.shape[1]
    half = place_ref[1]
    kept_at = pl.ds(pl.multiple_of(half * width, width), width)
    got_at = pl.ds(pl.multiple_of((1 - half) * width, width), width)
    kept = pl.ds(pl.multiple_of(half * half_tokens, half_tokens), half_tokens)
    copies = [
        pltpu.make_async_copy(grad_ref.at[kept, :], joined_ref.at[:, kept_at], join_sems.at[0]),
        pltpu.make_async_copy(got_ref.at[:, pl.ds(0, width)], joined_ref.at[:, got_at], join_sems.at[1]),
    ]
    for copy in copies:
        copy.start()
    owners, held, features = own_ref.shape
    for i, offset in enumerate(arrival_order(owners)):
        first = (place_ref[0] ^ offset) * 2
        own = pl.ds(pl.multiple_of((first + half) * held, held), held)
        other = pl.ds(pl.multiple_of((first + 1 - half) * held, held), held)
        s_ref[own, :] = own_ref[i].astype(jnp.float32)
        pair = got_ref[i // 2 * 2 * held : (i // 2 + 1) * 2 * held, width:].astype(jnp.float32)
        s_ref[other, :] = pair[i % 2 * held : (i % 2 + 1) * held]
    first = 0
    for i, size in enumerate(row_blocks(features)):
        rows = slice(first, first + size)
        for j in range(first, first + size, BLK):
            for t in range(0, s_ref.shape[0], BLK):
                h_ref[j : j + BLK, t : t + BLK] = s_ref[t : t + BLK, j : j + BLK].T.astype(jnp.bfloat16)
        block_ref[rows, :] = jnp.dot(
            h_ref[rows, :], grad_ref[...], preferred_element_type=jnp.float32
        ).astype(jnp.bfloat16)
        at = pl.ds(first, size)
        copies.append(pltpu.make_async_copy(block_ref.at[at, :], o_ref.at[at, :], sems.at[i]))
        copies[-1].start()
        first += size
    for copy in copies:
        copy.wait()


def in_vmem():
    return pl.BlockSpec(memory_space=pltpu.VMEM)


def scalars():
    return pl.BlockSpec(memory_space=pltpu.SMEM)


def anywhere():
    return pl.BlockSpec(memory_space=pl.ANY)


def params(mib=48):
    return pltpu.CompilerParams(vmem_limit_bytes=mib << 20)


def cost(flops=0, bytes_accessed=0, transcendentals=0):
    return pl.CostEstimate(flops=flops, bytes_accessed=bytes_accessed, transcendentals=transcendentals)


def swap_halves(x):
    return lax.ppermute(x, "tv", [(0, 1), (1, 0)])


def to_partner(x, offset):
    return lax.ppermute(x, "sv", [(s, s ^ offset) for s in range(lax.axis_size("sv"))])


def body(teacher_probs, align_owner, align_local, align_weight, student_logits, hidden):
    owners = lax.axis_size("sv")
    halves = lax.axis_size("tv")
    half_index = lax.axis_index("tv")
    place = jnp.stack([lax.axis_index("sv"), half_index]).astype(jnp.int32)
    tokens = teacher_probs.shape[0]
    columns = student_logits.shape[1]
    blocks = columns // BLK
    mine = blocks // halves
    width = mine * BLK
    rows = owners * mine
    per_half = TB // halves
    group_tokens = owners * tokens
    half_tokens = student_logits.shape[0]
    features = hidden.shape[1]
    first = half_index == 0
    bf16, f32 = jnp.bfloat16, jnp.float32
    shape = jax.ShapeDtypeStruct
    dma = lambda count: pltpu.SemaphoreType.DMA((count,))

    def in_order(own, other, axis):
        return jnp.concatenate([jnp.where(first, own, other), jnp.where(first, other, own)], axis=axis)

    hidden = hidden[None]
    offset = owners // 2
    first_piece = to_partner(hidden, offset)

    def merge(one, two):
        top = jnp.maximum(one[0], two[0])
        return top, one[1] * jnp.exp(one[0] - top) + two[1] * jnp.exp(two[0] - top)

    wide = student_logits.astype(f32)
    low = jnp.float32(-1e38)
    stats = jnp.stack(lax.reduce((wide, jnp.ones_like(wide)), (low, jnp.float32(0)), merge, (1,)))
    teacher_given, stats = lax.optimization_barrier((teacher_probs, stats))
    teacher_other = swap_halves(teacher_given)
    stats = in_order(stats, swap_halves(stats), 1)

    local = align_local.T - half_index * mine
    row_of = jnp.where((local >= 0) & (local < mine), align_owner.T * mine + local, -1)
    code = row_of.astype(f32) + 0.5 * align_weight.T.astype(f32)
    cut = lambda which: lax.dynamic_slice_in_dim(code, which * per_half, per_half, 1)
    w_own = block_weights(cut(half_index), rows)
    w_rest = block_weights(cut(1 - half_index), rows)
    spread = pltpu.VMEM((per_half * tokens, BLK), f32)
    flops = 2 * (rows + MASS_ROWS) * per_half * tokens * BLK
    part = pl.pallas_call(
        map_own_kernel,
        out_shape=shape((rows + MASS_ROWS, tokens * BLK), f32),
        in_specs=[in_vmem()] * 2 + [anywhere()],
        out_specs=in_vmem(),
        scratch_shapes=[spread],
        compiler_params=params(),
        cost_estimate=cost(flops, 3 << 20),
        name="map_own",
    )(w_own, teacher_probs, stats)
    chunk = (owners, tokens, width + group_tokens)
    outgoing = pl.pallas_call(
        map_rest_kernel,
        out_shape=shape(chunk, bf16),
        in_specs=[in_vmem()] * 4,
        out_specs=anywhere(),
        scratch_shapes=[
            spread,
            pltpu.VMEM(((rows + 8) * tokens, BLK), f32),
            pltpu.VMEM(chunk, bf16),
            dma(owners),
        ],
        compiler_params=params(),
        cost_estimate=cost(flops, 4 << 20),
        name="map_rest",
    )(w_rest, teacher_other, part, stats)
    outgoing, first_piece = lax.optimization_barrier((outgoing, first_piece))
    target = lax.all_to_all(outgoing, "sv", 0, 0, axis_index_groups=[turned_group(owners, owners // 2)], tiled=True)

    hidden, late_logits, outgoing = lax.optimization_barrier((hidden, student_logits, outgoing))

    keep = lax.dynamic_slice_in_dim(late_logits, half_index * width, width, 1)
    give = lax.dynamic_slice_in_dim(late_logits, (1 - half_index) * width, width, 1)
    logits = in_order(keep, swap_halves(give), 0)

    pieces = [jnp.concatenate([hidden, first_piece])]
    pieces += [to_partner(pieces[0], a) for a in range(1, offset)]

    scale = float(columns * owners)
    lanes = -(-half_tokens // BLK) * BLK
    grad, terms = pl.pallas_call(
        lambda *refs: grad_kernel(scale, *refs),
        out_shape=(shape((group_tokens, width), bf16), shape((owners * halves, 8, lanes), f32)),
        in_specs=[in_vmem()] * 2,
        out_specs=(in_vmem(), anywhere()),
        scratch_shapes=[
            pltpu.VMEM((group_tokens, BLK), f32),
            pltpu.VMEM((owners * halves, 8, lanes), f32),
            pltpu.SemaphoreType.DMA,
        ],
        compiler_params=params(),
        cost_estimate=cost(
            10 * group_tokens * width, 6 * group_tokens * width, 2 * group_tokens * width
        ),
        name="logit_grad",
    )(target, logits)

    everyone = [turned_group(owners * halves, owners // 2 * halves)]
    terms = lax.all_to_all(terms, ("sv", "tv"), 0, 0, axis_index_groups=everyone, tiled=True)
    *pieces, grad = lax.optimization_barrier((*pieces, grad))
    give = lax.dynamic_slice_in_dim(grad, (1 - half_index) * half_tokens, half_tokens, 0)
    hidden_own = jnp.concatenate(pieces)
    got = swap_halves(jnp.concatenate([give, hidden_own.reshape(half_tokens, features)], axis=1))
    weight_grad, logit_grad = pl.pallas_call(
        weight_kernel,
        out_shape=(shape((features, width), bf16), shape((half_tokens, columns), bf16)),
        in_specs=[scalars()] + [in_vmem()] * 3,
        out_specs=(anywhere(), anywhere()),
        scratch_shapes=[
            pltpu.VMEM((group_tokens, features), f32),
            pltpu.VMEM((features, group_tokens), bf16),
            pltpu.VMEM((features, width), bf16),
            dma(len(row_blocks(features))),
            dma(2),
        ],
        compiler_params=params(),
        cost_estimate=cost(
            2 * features * group_tokens * width,
            2 * (features * width + group_tokens * (features + width)),
        ),
        name="weight_grad",
    )(place, hidden_own, got, grad)
    terms, logit_grad, weight_grad = lax.optimization_barrier((terms, logit_grad, weight_grad))
    divergence = jnp.sum(terms[:, 0, :half_tokens], axis=0)
    return (divergence, logit_grad, weight_grad)


def solution(mesh):
    return jax.shard_map(
        body,
        mesh=mesh,
        in_specs=(
            P(("grp", "sv"), "tv"),
            P(),
            P(),
            P(),
            P(("grp", "tv"), "sv"),
            P(("grp", "sv", "tv"), None),
        ),
        out_specs=(P(("grp", "tv")), P(("grp", "tv"), "sv"), P(None, ("grp", "sv", "tv"))),
        check_vma=False,
    )
```

```python
import jax
import jax.numpy as jnp
from jax import lax
from jax.experimental import pallas as pl
from jax.experimental.pallas import tpu as pltpu
from jax.sharding import PartitionSpec as P

BLK = 128
TB = 640
TOPA = 2
MASS_ROWS = 16
STEP = 16


def block_weights(code, rows):
    row_ids = lax.broadcasted_iota(jnp.int32, (rows + MASS_ROWS, code.shape[1]), 0)
    total = jnp.zeros(row_ids.shape, jnp.float32)
    for slot in range(TOPA):
        row = jnp.floor(code[slot])
        weight = (code[slot] - row) * 2.0
        hit = (row_ids == row.astype(jnp.int32)[None, :]) | (row_ids == rows + slot)
        total = total + jnp.where(hit, weight[None, :], 0.0)
    return total.astype(jnp.bfloat16)


def turned_group(members, first):
    return [(i + first) % members for i in range(members)]


def spread_tokens(t_ref, s_ref, start, count):
    tokens = t_ref.shape[0]

    def some(i, carry):
        for j in range(STEP):
            k = start + i * STEP + j
            tile = t_ref[:, pl.ds(pl.multiple_of(k * BLK, BLK), BLK)]
            s_ref[pl.ds(pl.multiple_of(k * tokens, tokens), tokens), :] = tile.astype(jnp.float32)
        return carry

    lax.fori_loop(0, count // STEP, some, 0)


def token_pair(s_ref, t, tokens):
    count = s_ref.shape[0] // tokens
    both = [s_ref[pl.ds(t + i, count, stride=tokens), :].astype(jnp.bfloat16) for i in range(2)]
    return jnp.concatenate(both, axis=1)


def map_own_kernel(w_ref, t_ref, stats_ref, o_ref, s_ref):
    tokens = t_ref.shape[0]
    spread_tokens(t_ref, s_ref, 0, t_ref.shape[1] // BLK)
    for t in range(0, tokens, 2):
        o_ref[:, t * BLK : (t + 2) * BLK] = jnp.dot(
            w_ref[...], token_pair(s_ref, t, tokens), preferred_element_type=jnp.float32
        )


def three_parts(x):
    parts = []
    for _ in range(3):
        parts.append(x.astype(jnp.bfloat16).astype(jnp.float32))
        x = x - parts[-1]
    return parts


def map_rest_kernel(w_ref, t_ref, p_ref, stats_ref, o_ref, s_ref, m_ref, o_buf, out_sem):
    tokens = t_ref.shape[0]
    owners = o_ref.shape[0]
    rows = w_ref.shape[0] - MASS_ROWS
    mine = rows // owners
    stats = [stats_ref[0:1, :]] + three_parts(stats_ref[1:2, :])
    extra = jnp.zeros((tokens, stats_ref.shape[1]), jnp.float32)
    row_ids = lax.broadcasted_iota(jnp.int32, extra.shape, 0)
    for i, row in enumerate(stats):
        extra = jnp.where(row_ids == i, row, extra)
    extra = extra.astype(jnp.bfloat16)
    spread_tokens(t_ref, s_ref, 0, t_ref.shape[1] // BLK)
    for t in range(0, tokens, 2):
        both = p_ref[:, t * BLK : (t + 2) * BLK] + jnp.dot(
            w_ref[...], token_pair(s_ref, t, tokens), preferred_element_type=jnp.float32
        )
        for i in range(2):
            m_ref[pl.ds(t + i, rows + 8, stride=tokens), :] = both[: rows + 8, i * BLK : (i + 1) * BLK]
    mass = m_ref[rows * tokens : (rows + 1) * tokens, :]
    for slot in range(1, TOPA):
        mass = mass + m_ref[(rows + slot) * tokens : (rows + slot + 1) * tokens, :]
    inverse = jnp.broadcast_to(1.0 / jnp.sum(mass, axis=1, keepdims=True), (tokens, BLK))

    def leaving(q):
        return pltpu.make_async_copy(o_buf.at[q], o_ref.at[q], out_sem.at[q])

    def owner(q, carry):
        member = lax.rem(q + owners // 2, owners)
        for b in range(mine):
            first = pl.multiple_of((member * mine + b) * tokens, tokens)
            tile = m_ref[pl.ds(first, tokens), :] * inverse
            o_buf[q, :, b * BLK : (b + 1) * BLK] = tile.astype(jnp.bfloat16)
        o_buf[q, :, mine * BLK :] = extra
        leaving(q).start()
        return carry

    def left(q, carry):
        leaving(q).wait()
        return carry

    lax.fori_loop(0, owners, owner, 0)
    lax.fori_loop(0, owners, left, 0)


def grad_kernel(scale, target_ref, logits_ref, grad_ref, terms_ref, norm_ref, t_buf, sem):
    owners, tokens, _ = target_ref.shape
    group_tokens, width = logits_ref.shape
    stats = [target_ref[q, :, width:].astype(jnp.float32) for q in range(owners)]
    top = stats[0][0:1]
    for one in stats[1:]:
        top = jnp.maximum(top, one[0:1])
    total = jnp.zeros_like(top)
    for one in stats:
        total = total + (one[1:2] + one[2:3] + one[3:4]) * jnp.exp(one[0:1] - top)
    log_norm = top + jnp.log(total)

    def block(i, b):
        lanes = slice(b * BLK, (b + 1) * BLK)
        first, count = i * BLK // tokens, BLK // tokens
        at = (first - owners // 2) % owners
        cut = min(count, owners - at)
        target = target_ref[at : at + cut, :, lanes].reshape(cut * tokens, BLK)
        if cut < count:
            rest = target_ref[: count - cut, :, lanes].reshape((count - cut) * tokens, BLK)
            target = jnp.concatenate([target, rest], axis=0)
        target = target.astype(jnp.float32)
        return target, logits_ref[i * BLK : (i + 1) * BLK, lanes].astype(jnp.float32)

    sums = []
    for i in range(group_tokens // BLK):
        rows = slice(i * BLK, (i + 1) * BLK)
        norm = jnp.broadcast_to(log_norm[:, rows], (BLK, BLK)).T
        norm_ref[rows, :] = norm
        terms = jnp.zeros((BLK, BLK), jnp.float32)
        for b in range(width // BLK):
            target, logits = block(i, b)
            positive = target > 0
            one = target * (jnp.log(jnp.where(positive, target, 1.0)) - (logits - norm))
            terms = terms + jnp.where(positive, one, 0.0)
        sums.append(jnp.sum(terms.T, axis=0, keepdims=True))
    row = jnp.concatenate(sums, axis=1)
    half_tokens = group_tokens // 2
    for half in range(2):
        mine = row[:, half * half_tokens : (half + 1) * half_tokens]
        tile = jnp.concatenate([mine] * (t_buf.shape[2] // half_tokens), axis=1)
        for q in range(owners):
            t_buf[2 * q + half] = jnp.broadcast_to(tile, t_buf.shape[1:])
    leaving = pltpu.make_async_copy(t_buf, terms_ref, sem)
    leaving.start()
    for i in range(group_tokens // BLK):
        rows = slice(i * BLK, (i + 1) * BLK)
        for b in range(width // BLK):
            target, logits = block(i, b)
            grad = (jnp.exp(logits - norm_ref[rows, :]) - target) * scale
            grad_ref[rows, b * BLK : (b + 1) * BLK] = grad.astype(jnp.bfloat16)
    leaving.wait()


def arrival_order(owners):
    return [a for b in range(owners // 2) for a in (b, b + owners // 2)]


def row_blocks(features):
    tiles = features // BLK
    sizes = [2] + [3] * ((tiles - 3) // 3)
    sizes.append(tiles - sum(sizes))
    return [size * BLK for size in sizes]


def weight_kernel(
    place_ref, own_ref, got_ref, grad_ref, o_ref, joined_ref, s_ref, h_ref, block_ref, sems, join_sems
):
    half_tokens, width = got_ref.shape[0], grad_ref.shape[1]
    half = place_ref[1]
    kept_at = pl.ds(pl.multiple_of(half * width, width), width)
    got_at = pl.ds(pl.multiple_of((1 - half) * width, width), width)
    kept = pl.ds(pl.multiple_of(half * half_tokens, half_tokens), half_tokens)
    copies = [
        pltpu.make_async_copy(grad_ref.at[kept, :], joined_ref.at[:, kept_at], join_sems.at[0]),
        pltpu.make_async_copy(got_ref.at[:, pl.ds(0, width)], joined_ref.at[:, got_at], join_sems.at[1]),
    ]
    for copy in copies:
        copy.start()
    owners, held, features = own_ref.shape
    for i, offset in enumerate(arrival_order(owners)):
        first = (place_ref[0] ^ offset) * 2
        own = pl.ds(pl.multiple_of((first + half) * held, held), held)
        other = pl.ds(pl.multiple_of((first + 1 - half) * held, held), held)
        s_ref[own, :] = own_ref[i].astype(jnp.float32)
        pair = got_ref[i // 2 * 2 * held : (i // 2 + 1) * 2 * held, width:].astype(jnp.float32)
        s_ref[other, :] = pair[i % 2 * held : (i % 2 + 1) * held]
    first = 0
    for i, size in enumerate(row_blocks(features)):
        for j in range(first, first + size, BLK):
            rows = slice(j, j + BLK)
            for t in range(0, s_ref.shape[0], BLK):
                h_ref[rows, t : t + BLK] = s_ref[t : t + BLK, rows].T.astype(jnp.bfloat16)
            for n in range(0, width, 2 * BLK):
                tile = jnp.dot(
                    h_ref[rows, :], grad_ref[:, n : n + 2 * BLK], preferred_element_type=jnp.float32
                )
                block_ref[rows, n : n + 2 * BLK] = tile.astype(jnp.bfloat16)
        at = pl.ds(first, size)
        copies.append(pltpu.make_async_copy(block_ref.at[at, :], o_ref.at[at, :], sems.at[i]))
        copies[-1].start()
        first += size
    for copy in copies:
        copy.wait()


def in_vmem():
    return pl.BlockSpec(memory_space=pltpu.VMEM)


def scalars():
    return pl.BlockSpec(memory_space=pltpu.SMEM)


def anywhere():
    return pl.BlockSpec(memory_space=pl.ANY)


def params(mib=48):
    return pltpu.CompilerParams(vmem_limit_bytes=mib << 20)


def cost(flops=0, bytes_accessed=0, transcendentals=0):
    return pl.CostEstimate(flops=flops, bytes_accessed=bytes_accessed, transcendentals=transcendentals)


def swap_halves(x):
    return lax.ppermute(x, "tv", [(0, 1), (1, 0)])


def to_partner(x, offset):
    return lax.ppermute(x, "sv", [(s, s ^ offset) for s in range(lax.axis_size("sv"))])


def body(teacher_probs, align_owner, align_local, align_weight, student_logits, hidden):
    owners = lax.axis_size("sv")
    halves = lax.axis_size("tv")
    half_index = lax.axis_index("tv")
    place = jnp.stack([lax.axis_index("sv"), half_index]).astype(jnp.int32)
    tokens = teacher_probs.shape[0]
    columns = student_logits.shape[1]
    blocks = columns // BLK
    mine = blocks // halves
    width = mine * BLK
    rows = owners * mine
    per_half = TB // halves
    group_tokens = owners * tokens
    half_tokens = student_logits.shape[0]
    features = hidden.shape[1]
    first = half_index == 0
    bf16, f32 = jnp.bfloat16, jnp.float32
    shape = jax.ShapeDtypeStruct
    dma = lambda count: pltpu.SemaphoreType.DMA((count,))

    def in_order(own, other, axis):
        return jnp.concatenate([jnp.where(first, own, other), jnp.where(first, other, own)], axis=axis)

    hidden = hidden[None]
    offset = owners // 2
    first_piece = to_partner(hidden, offset)

    def merge(one, two):
        top = jnp.maximum(one[0], two[0])
        return top, one[1] * jnp.exp(one[0] - top) + two[1] * jnp.exp(two[0] - top)

    wide = student_logits.astype(f32)
    low = jnp.float32(-1e38)
    stats = jnp.stack(lax.reduce((wide, jnp.ones_like(wide)), (low, jnp.float32(0)), merge, (1,)))
    teacher_given, stats = lax.optimization_barrier((teacher_probs, stats))
    teacher_other = swap_halves(teacher_given)
    stats = in_order(stats, swap_halves(stats), 1)

    local = align_local.T - half_index * mine
    row_of = jnp.where((local >= 0) & (local < mine), align_owner.T * mine + local, -1)
    code = row_of.astype(f32) + 0.5 * align_weight.T.astype(f32)
    cut = lambda which: lax.dynamic_slice_in_dim(code, which * per_half, per_half, 1)
    w_own = block_weights(cut(half_index), rows)
    w_rest = block_weights(cut(1 - half_index), rows)
    spread = pltpu.VMEM((per_half * tokens, BLK), f32)
    flops = 2 * (rows + MASS_ROWS) * per_half * tokens * BLK
    part = pl.pallas_call(
        map_own_kernel,
        out_shape=shape((rows + MASS_ROWS, tokens * BLK), f32),
        in_specs=[in_vmem()] * 2 + [anywhere()],
        out_specs=in_vmem(),
        scratch_shapes=[spread],
        compiler_params=params(),
        cost_estimate=cost(flops, 3 << 20),
        name="map_own",
    )(w_own, teacher_probs, stats)
    chunk = (owners, tokens, width + group_tokens)
    outgoing = pl.pallas_call(
        map_rest_kernel,
        out_shape=shape(chunk, bf16),
        in_specs=[in_vmem()] * 4,
        out_specs=anywhere(),
        scratch_shapes=[
            spread,
            pltpu.VMEM(((rows + 8) * tokens, BLK), f32),
            pltpu.VMEM(chunk, bf16),
            dma(owners),
        ],
        compiler_params=params(),
        cost_estimate=cost(flops, 4 << 20),
        name="map_rest",
    )(w_rest, teacher_other, part, stats)
    outgoing, first_piece = lax.optimization_barrier((outgoing, first_piece))
    target = lax.all_to_all(outgoing, "sv", 0, 0, axis_index_groups=[turned_group(owners, owners // 2)], tiled=True)

    hidden, late_logits, outgoing = lax.optimization_barrier((hidden, student_logits, outgoing))

    keep = lax.dynamic_slice_in_dim(late_logits, half_index * width, width, 1)
    give = lax.dynamic_slice_in_dim(late_logits, (1 - half_index) * width, width, 1)
    logits = in_order(keep, swap_halves(give), 0)

    pieces = [jnp.concatenate([hidden, first_piece])]
    pieces += [to_partner(pieces[0], a) for a in range(1, offset)]

    scale = float(columns * owners)
    lanes = -(-half_tokens // BLK) * BLK
    grad, terms = pl.pallas_call(
        lambda *refs: grad_kernel(scale, *refs),
        out_shape=(shape((group_tokens, width), bf16), shape((owners * halves, 8, lanes), f32)),
        in_specs=[in_vmem()] * 2,
        out_specs=(in_vmem(), anywhere()),
        scratch_shapes=[
            pltpu.VMEM((group_tokens, BLK), f32),
            pltpu.VMEM((owners * halves, 8, lanes), f32),
            pltpu.SemaphoreType.DMA,
        ],
        compiler_params=params(),
        cost_estimate=cost(
            10 * group_tokens * width, 6 * group_tokens * width, 2 * group_tokens * width
        ),
        name="logit_grad",
    )(target, logits)

    everyone = [turned_group(owners * halves, owners // 2 * halves)]
    terms = lax.all_to_all(terms, ("sv", "tv"), 0, 0, axis_index_groups=everyone, tiled=True)
    *pieces, grad = lax.optimization_barrier((*pieces, grad))
    give = lax.dynamic_slice_in_dim(grad, (1 - half_index) * half_tokens, half_tokens, 0)
    hidden_own = jnp.concatenate(pieces)
    got = swap_halves(jnp.concatenate([give, hidden_own.reshape(half_tokens, features)], axis=1))
    weight_grad, logit_grad = pl.pallas_call(
        weight_kernel,
        out_shape=(shape((features, width), bf16), shape((half_tokens, columns), bf16)),
        in_specs=[scalars()] + [in_vmem()] * 3,
        out_specs=(anywhere(), anywhere()),
        scratch_shapes=[
            pltpu.VMEM((group_tokens, features), f32),
            pltpu.VMEM((features, group_tokens), bf16),
            pltpu.VMEM((features, width), bf16),
            dma(len(row_blocks(features))),
            dma(2),
        ],
        compiler_params=params(),
        cost_estimate=cost(
            2 * features * group_tokens * width,
            2 * (features * width + group_tokens * (features + width)),
        ),
        name="weight_grad",
    )(place, hidden_own, got, grad)
    terms, logit_grad, weight_grad = lax.optimization_barrier((terms, logit_grad, weight_grad))
    divergence = jnp.sum(terms[:, 0, :half_tokens], axis=0)
    return (divergence, logit_grad, weight_grad)


def solution(mesh):
    return jax.shard_map(
        body,
        mesh=mesh,
        in_specs=(
            P(("grp", "sv"), "tv"),
            P(),
            P(),
            P(),
            P(("grp", "tv"), "sv"),
            P(("grp", "sv", "tv"), None),
        ),
        out_specs=(P(("grp", "tv")), P(("grp", "tv"), "sv"), P(None, ("grp", "sv", "tv"))),
        check_vma=False,
    )
```

```python
import jax
import jax.numpy as jnp
from jax import lax
from jax.experimental import pallas as pl
from jax.experimental.pallas import tpu as pltpu
from jax.sharding import PartitionSpec as P

BLK = 128
TB = 640
TOPA = 2
MASS_ROWS = 16
STEP = 16


def block_weights(code, rows):
    row_ids = lax.broadcasted_iota(jnp.int32, (rows + MASS_ROWS, code.shape[1]), 0)
    total = jnp.zeros(row_ids.shape, jnp.float32)
    for slot in range(TOPA):
        row = jnp.floor(code[slot])
        weight = (code[slot] - row) * 2.0
        hit = (row_ids == row.astype(jnp.int32)[None, :]) | (row_ids == rows + slot)
        total = total + jnp.where(hit, weight[None, :], 0.0)
    return total.astype(jnp.bfloat16)


def turned_group(members, first):
    return [(i + first) % members for i in range(members)]


def spread_tokens(t_ref, s_ref, start, count):
    tokens = t_ref.shape[0]

    def some(i, carry):
        for j in range(STEP):
            k = start + i * STEP + j
            tile = t_ref[:, pl.ds(pl.multiple_of(k * BLK, BLK), BLK)]
            s_ref[pl.ds(pl.multiple_of(k * tokens, tokens), tokens), :] = tile.astype(jnp.float32)
        return carry

    lax.fori_loop(0, count // STEP, some, 0)


def token_pair(s_ref, t, tokens):
    count = s_ref.shape[0] // tokens
    both = [s_ref[pl.ds(t + i, count, stride=tokens), :].astype(jnp.bfloat16) for i in range(2)]
    return jnp.concatenate(both, axis=1)


def map_own_kernel(w_ref, t_ref, stats_ref, o_ref, s_ref):
    tokens = t_ref.shape[0]
    spread_tokens(t_ref, s_ref, 0, t_ref.shape[1] // BLK)
    for t in range(0, tokens, 2):
        o_ref[:, t * BLK : (t + 2) * BLK] = jnp.dot(
            w_ref[...], token_pair(s_ref, t, tokens), preferred_element_type=jnp.float32
        )


def three_parts(x):
    parts = []
    for _ in range(3):
        parts.append(x.astype(jnp.bfloat16).astype(jnp.float32))
        x = x - parts[-1]
    return parts


def map_rest_kernel(w_ref, t_ref, p_ref, stats_ref, o_ref, s_ref, m_ref, o_buf, out_sem):
    tokens = t_ref.shape[0]
    owners = o_ref.shape[0]
    rows = w_ref.shape[0] - MASS_ROWS
    mine = rows // owners
    stats = [stats_ref[0:1, :]] + three_parts(stats_ref[1:2, :])
    extra = jnp.zeros((tokens, stats_ref.shape[1]), jnp.float32)
    row_ids = lax.broadcasted_iota(jnp.int32, extra.shape, 0)
    for i, row in enumerate(stats):
        extra = jnp.where(row_ids == i, row, extra)
    extra = extra.astype(jnp.bfloat16)
    spread_tokens(t_ref, s_ref, 0, t_ref.shape[1] // BLK)
    for t in range(0, tokens, 2):
        both = p_ref[:, t * BLK : (t + 2) * BLK] + jnp.dot(
            w_ref[...], token_pair(s_ref, t, tokens), preferred_element_type=jnp.float32
        )
        for i in range(2):
            m_ref[pl.ds(t + i, rows + 8, stride=tokens), :] = both[: rows + 8, i * BLK : (i + 1) * BLK]
    mass = m_ref[rows * tokens : (rows + 1) * tokens, :]
    for slot in range(1, TOPA):
        mass = mass + m_ref[(rows + slot) * tokens : (rows + slot + 1) * tokens, :]
    inverse = jnp.broadcast_to(1.0 / jnp.sum(mass, axis=1, keepdims=True), (tokens, BLK))

    def leaving(q):
        return pltpu.make_async_copy(o_buf.at[q], o_ref.at[q], out_sem.at[q])

    def owner(q, carry):
        member = lax.rem(q + owners // 2, owners)
        for b in range(mine):
            first = pl.multiple_of((member * mine + b) * tokens, tokens)
            tile = m_ref[pl.ds(first, tokens), :] * inverse
            o_buf[q, :, b * BLK : (b + 1) * BLK] = tile.astype(jnp.bfloat16)
        o_buf[q, :, mine * BLK :] = extra
        leaving(q).start()
        return carry

    def left(q, carry):
        leaving(q).wait()
        return carry

    lax.fori_loop(0, owners, owner, 0)
    lax.fori_loop(0, owners, left, 0)


def grad_kernel(scale, target_ref, logits_ref, grad_ref, terms_ref, norm_ref, t_buf, sem):
    owners, tokens, _ = target_ref.shape
    group_tokens, width = logits_ref.shape
    stats = [target_ref[q, :, width:].astype(jnp.float32) for q in range(owners)]
    top = stats[0][0:1]
    for one in stats[1:]:
        top = jnp.maximum(top, one[0:1])
    total = jnp.zeros_like(top)
    for one in stats:
        total = total + (one[1:2] + one[2:3] + one[3:4]) * jnp.exp(one[0:1] - top)
    log_norm = top + jnp.log(total)

    def block(i, b):
        lanes = slice(b * BLK, (b + 1) * BLK)
        first, count = i * BLK // tokens, BLK // tokens
        at = (first - owners // 2) % owners
        cut = min(count, owners - at)
        target = target_ref[at : at + cut, :, lanes].reshape(cut * tokens, BLK)
        if cut < count:
            rest = target_ref[: count - cut, :, lanes].reshape((count - cut) * tokens, BLK)
            target = jnp.concatenate([target, rest], axis=0)
        target = target.astype(jnp.float32)
        return target, logits_ref[i * BLK : (i + 1) * BLK, lanes].astype(jnp.float32)

    sums = []
    for i in range(group_tokens // BLK):
        rows = slice(i * BLK, (i + 1) * BLK)
        norm = jnp.broadcast_to(log_norm[:, rows], (BLK, BLK)).T
        norm_ref[rows, :] = norm
        terms = jnp.zeros((BLK, BLK), jnp.float32)
        for b in range(width // BLK):
            target, logits = block(i, b)
            positive = target > 0
            one = target * (jnp.log(jnp.where(positive, target, 1.0)) - (logits - norm))
            terms = terms + jnp.where(positive, one, 0.0)
        sums.append(jnp.sum(terms.T, axis=0, keepdims=True))
    row = jnp.concatenate(sums, axis=1)
    half_tokens = group_tokens // 2
    for half in range(2):
        mine = row[:, half * half_tokens : (half + 1) * half_tokens]
        tile = jnp.concatenate([mine] * (t_buf.shape[2] // half_tokens), axis=1)
        for q in range(owners):
            t_buf[2 * q + half] = jnp.broadcast_to(tile, t_buf.shape[1:])
    leaving = pltpu.make_async_copy(t_buf, terms_ref, sem)
    leaving.start()
    for i in range(group_tokens // BLK):
        rows = slice(i * BLK, (i + 1) * BLK)
        for b in range(width // BLK):
            target, logits = block(i, b)
            grad = (jnp.exp(logits - norm_ref[rows, :]) - target) * scale
            grad_ref[rows, b * BLK : (b + 1) * BLK] = grad.astype(jnp.bfloat16)
    leaving.wait()


def arrival_order(owners):
    return [a for b in range(owners // 2) for a in (b, b + owners // 2)]


def row_blocks(features):
    tiles = features // BLK
    sizes = [2] + [3] * ((tiles - 3) // 3)
    sizes.append(tiles - sum(sizes))
    return [size * BLK for size in sizes]


def weight_kernel(
    place_ref, own_ref, got_ref, grad_ref, o_ref, joined_ref, s_ref, h_ref, block_ref, sems, join_sems
):
    half_tokens, width = got_ref.shape[0], grad_ref.shape[1]
    half = place_ref[1]
    kept_at = pl.ds(pl.multiple_of(half * width, width), width)
    got_at = pl.ds(pl.multiple_of((1 - half) * width, width), width)
    kept = pl.ds(pl.multiple_of(half * half_tokens, half_tokens), half_tokens)
    copies = [
        pltpu.make_async_copy(grad_ref.at[kept, :], joined_ref.at[:, kept_at], join_sems.at[0]),
        pltpu.make_async_copy(got_ref.at[:, pl.ds(0, width)], joined_ref.at[:, got_at], join_sems.at[1]),
    ]
    for copy in copies:
        copy.start()
    owners, held, features = own_ref.shape
    for i, offset in enumerate(arrival_order(owners)):
        first = (place_ref[0] ^ offset) * 2
        own = pl.ds(pl.multiple_of((first + half) * held, held), held)
        other = pl.ds(pl.multiple_of((first + 1 - half) * held, held), held)
        s_ref[own, :] = own_ref[i].astype(jnp.float32)
        pair = got_ref[i // 2 * 2 * held : (i // 2 + 1) * 2 * held, width:].astype(jnp.float32)
        s_ref[other, :] = pair[i % 2 * held : (i % 2 + 1) * held]
    first = 0
    for i, size in enumerate(row_blocks(features)):
        for j in range(first, first + size, BLK):
            rows = slice(j, j + BLK)
            for t in range(0, s_ref.shape[0], BLK):
                h_ref[rows, t : t + BLK] = s_ref[t : t + BLK, rows].T.astype(jnp.bfloat16)
            for n in range(0, width, 2 * BLK):
                tile = jnp.dot(
                    h_ref[rows, :], grad_ref[:, n : n + 2 * BLK], preferred_element_type=jnp.float32
                )
                block_ref[rows, n : n + 2 * BLK] = tile.astype(jnp.bfloat16)
        at = pl.ds(first, size)
        copies.append(pltpu.make_async_copy(block_ref.at[at, :], o_ref.at[at, :], sems.at[i]))
        copies[-1].start(priority=i % 2)
        first += size
    for copy in copies:
        copy.wait()


def in_vmem():
    return pl.BlockSpec(memory_space=pltpu.VMEM)


def scalars():
    return pl.BlockSpec(memory_space=pltpu.SMEM)


def anywhere():
    return pl.BlockSpec(memory_space=pl.ANY)


def params(mib=48):
    return pltpu.CompilerParams(vmem_limit_bytes=mib << 20)


def cost(flops=0, bytes_accessed=0, transcendentals=0):
    return pl.CostEstimate(flops=flops, bytes_accessed=bytes_accessed, transcendentals=transcendentals)


def swap_halves(x):
    return lax.ppermute(x, "tv", [(0, 1), (1, 0)])


def to_partner(x, offset):
    return lax.ppermute(x, "sv", [(s, s ^ offset) for s in range(lax.axis_size("sv"))])


def body(teacher_probs, align_owner, align_local, align_weight, student_logits, hidden):
    owners = lax.axis_size("sv")
    halves = lax.axis_size("tv")
    half_index = lax.axis_index("tv")
    place = jnp.stack([lax.axis_index("sv"), half_index]).astype(jnp.int32)
    tokens = teacher_probs.shape[0]
    columns = student_logits.shape[1]
    blocks = columns // BLK
    mine = blocks // halves
    width = mine * BLK
    rows = owners * mine
    per_half = TB // halves
    group_tokens = owners * tokens
    half_tokens = student_logits.shape[0]
    features = hidden.shape[1]
    first = half_index == 0
    bf16, f32 = jnp.bfloat16, jnp.float32
    shape = jax.ShapeDtypeStruct
    dma = lambda count: pltpu.SemaphoreType.DMA((count,))

    def in_order(own, other, axis):
        return jnp.concatenate([jnp.where(first, own, other), jnp.where(first, other, own)], axis=axis)

    hidden = hidden[None]
    offset = owners // 2
    first_piece = to_partner(hidden, offset)

    def merge(one, two):
        top = jnp.maximum(one[0], two[0])
        return top, one[1] * jnp.exp(one[0] - top) + two[1] * jnp.exp(two[0] - top)

    wide = student_logits.astype(f32)
    low = jnp.float32(-1e38)
    stats = jnp.stack(lax.reduce((wide, jnp.ones_like(wide)), (low, jnp.float32(0)), merge, (1,)))
    teacher_given, stats = lax.optimization_barrier((teacher_probs, stats))
    teacher_other = swap_halves(teacher_given)
    stats = in_order(stats, swap_halves(stats), 1)

    local = align_local.T - half_index * mine
    row_of = jnp.where((local >= 0) & (local < mine), align_owner.T * mine + local, -1)
    code = row_of.astype(f32) + 0.5 * align_weight.T.astype(f32)
    cut = lambda which: lax.dynamic_slice_in_dim(code, which * per_half, per_half, 1)
    w_own = block_weights(cut(half_index), rows)
    w_rest = block_weights(cut(1 - half_index), rows)
    spread = pltpu.VMEM((per_half * tokens, BLK), f32)
    flops = 2 * (rows + MASS_ROWS) * per_half * tokens * BLK
    part = pl.pallas_call(
        map_own_kernel,
        out_shape=shape((rows + MASS_ROWS, tokens * BLK), f32),
        in_specs=[in_vmem()] * 2 + [anywhere()],
        out_specs=in_vmem(),
        scratch_shapes=[spread],
        compiler_params=params(),
        cost_estimate=cost(flops, 3 << 20),
        name="map_own",
    )(w_own, teacher_probs, stats)
    chunk = (owners, tokens, width + group_tokens)
    outgoing = pl.pallas_call(
        map_rest_kernel,
        out_shape=shape(chunk, bf16),
        in_specs=[in_vmem()] * 4,
        out_specs=anywhere(),
        scratch_shapes=[
            spread,
            pltpu.VMEM(((rows + 8) * tokens, BLK), f32),
            pltpu.VMEM(chunk, bf16),
            dma(owners),
        ],
        compiler_params=params(),
        cost_estimate=cost(flops, 4 << 20),
        name="map_rest",
    )(w_rest, teacher_other, part, stats)
    outgoing, first_piece = lax.optimization_barrier((outgoing, first_piece))
    target = lax.all_to_all(outgoing, "sv", 0, 0, axis_index_groups=[turned_group(owners, owners // 2)], tiled=True)

    hidden, late_logits, outgoing = lax.optimization_barrier((hidden, student_logits, outgoing))

    keep = lax.dynamic_slice_in_dim(late_logits, half_index * width, width, 1)
    give = lax.dynamic_slice_in_dim(late_logits, (1 - half_index) * width, width, 1)
    logits = in_order(keep, swap_halves(give), 0)

    pieces = [jnp.concatenate([hidden, first_piece])]
    pieces += [to_partner(pieces[0], a) for a in range(1, offset)]

    scale = float(columns * owners)
    lanes = -(-half_tokens // BLK) * BLK
    grad, terms = pl.pallas_call(
        lambda *refs: grad_kernel(scale, *refs),
        out_shape=(shape((group_tokens, width), bf16), shape((owners * halves, 8, lanes), f32)),
        in_specs=[in_vmem()] * 2,
        out_specs=(in_vmem(), anywhere()),
        scratch_shapes=[
            pltpu.VMEM((group_tokens, BLK), f32),
            pltpu.VMEM((owners * halves, 8, lanes), f32),
            pltpu.SemaphoreType.DMA,
        ],
        compiler_params=params(),
        cost_estimate=cost(
            10 * group_tokens * width, 6 * group_tokens * width, 2 * group_tokens * width
        ),
        name="logit_grad",
    )(target, logits)

    everyone = [turned_group(owners * halves, owners // 2 * halves)]
    terms = lax.all_to_all(terms, ("sv", "tv"), 0, 0, axis_index_groups=everyone, tiled=True)
    *pieces, grad = lax.optimization_barrier((*pieces, grad))
    give = lax.dynamic_slice_in_dim(grad, (1 - half_index) * half_tokens, half_tokens, 0)
    hidden_own = jnp.concatenate(pieces)
    got = swap_halves(jnp.concatenate([give, hidden_own.reshape(half_tokens, features)], axis=1))
    weight_grad, logit_grad = pl.pallas_call(
        weight_kernel,
        out_shape=(shape((features, width), bf16), shape((half_tokens, columns), bf16)),
        in_specs=[scalars()] + [in_vmem()] * 3,
        out_specs=(anywhere(), anywhere()),
        scratch_shapes=[
            pltpu.VMEM((group_tokens, features), f32),
            pltpu.VMEM((features, group_tokens), bf16),
            pltpu.VMEM((features, width), bf16),
            dma(len(row_blocks(features))),
            dma(2),
        ],
        compiler_params=params(),
        cost_estimate=cost(
            2 * features * group_tokens * width,
            2 * (features * width + group_tokens * (features + width)),
        ),
        name="weight_grad",
    )(place, hidden_own, got, grad)
    terms, logit_grad, weight_grad = lax.optimization_barrier((terms, logit_grad, weight_grad))
    divergence = jnp.sum(terms[:, 0, :half_tokens], axis=0)
    return (divergence, logit_grad, weight_grad)


def solution(mesh):
    return jax.shard_map(
        body,
        mesh=mesh,
        in_specs=(
            P(("grp", "sv"), "tv"),
            P(),
            P(),
            P(),
            P(("grp", "tv"), "sv"),
            P(("grp", "sv", "tv"), None),
        ),
        out_specs=(P(("grp", "tv")), P(("grp", "tv"), "sv"), P(None, ("grp", "sv", "tv"))),
        check_vma=False,
    )
```

```python
import jax
import jax.numpy as jnp
from jax import lax
from jax.experimental import pallas as pl
from jax.experimental.pallas import tpu as pltpu
from jax.sharding import PartitionSpec as P

BLK = 128
TB = 640
TOPA = 2
MASS_ROWS = 16
STEP = 160


def block_weights(code, rows):
    row_ids = lax.broadcasted_iota(jnp.int32, (rows + MASS_ROWS, code.shape[1]), 0)
    total = jnp.zeros(row_ids.shape, jnp.float32)
    for slot in range(TOPA):
        row = jnp.floor(code[slot])
        weight = (code[slot] - row) * 2.0
        hit = (row_ids == row.astype(jnp.int32)[None, :]) | (row_ids == rows + slot)
        total = total + jnp.where(hit, weight[None, :], 0.0)
    return total.astype(jnp.bfloat16)


def turned_group(members, first):
    return [(i + first) % members for i in range(members)]


def spread_tokens(t_ref, s_ref, start, count):
    tokens = t_ref.shape[0]

    def some(i, carry):
        for j in range(STEP):
            k = start + i * STEP + j
            tile = t_ref[:, pl.ds(pl.multiple_of(k * BLK, BLK), BLK)]
            s_ref[pl.ds(pl.multiple_of(k * tokens, tokens), tokens), :] = tile.astype(jnp.float32)
        return carry

    lax.fori_loop(0, count // STEP, some, 0)


def token_pair(s_ref, t, tokens):
    count = s_ref.shape[0] // tokens
    both = [s_ref[pl.ds(t + i, count, stride=tokens), :].astype(jnp.bfloat16) for i in range(2)]
    return jnp.concatenate(both, axis=1)


def map_own_kernel(w_ref, t_ref, stats_ref, o_ref, s_ref):
    tokens = t_ref.shape[0]
    spread_tokens(t_ref, s_ref, 0, t_ref.shape[1] // BLK)
    for t in range(0, tokens, 2):
        o_ref[:, t * BLK : (t + 2) * BLK] = jnp.dot(
            w_ref[...], token_pair(s_ref, t, tokens), preferred_element_type=jnp.float32
        )


def three_parts(x):
    parts = []
    for _ in range(3):
        parts.append(x.astype(jnp.bfloat16).astype(jnp.float32))
        x = x - parts[-1]
    return parts


def map_rest_kernel(w_ref, t_ref, p_ref, stats_ref, o_ref, s_ref, m_ref, o_buf, out_sem):
    tokens = t_ref.shape[0]
    owners = o_ref.shape[0]
    rows = w_ref.shape[0] - MASS_ROWS
    mine = rows // owners
    stats = [stats_ref[0:1, :]] + three_parts(stats_ref[1:2, :])
    extra = jnp.zeros((tokens, stats_ref.shape[1]), jnp.float32)
    row_ids = lax.broadcasted_iota(jnp.int32, extra.shape, 0)
    for i, row in enumerate(stats):
        extra = jnp.where(row_ids == i, row, extra)
    extra = extra.astype(jnp.bfloat16)
    spread_tokens(t_ref, s_ref, 0, t_ref.shape[1] // BLK)
    for t in range(0, tokens, 2):
        both = p_ref[:, t * BLK : (t + 2) * BLK] + jnp.dot(
            w_ref[...], token_pair(s_ref, t, tokens), preferred_element_type=jnp.float32
        )
        for i in range(2):
            m_ref[pl.ds(t + i, rows + 8, stride=tokens), :] = both[: rows + 8, i * BLK : (i + 1) * BLK]
    mass = m_ref[rows * tokens : (rows + 1) * tokens, :]
    for slot in range(1, TOPA):
        mass = mass + m_ref[(rows + slot) * tokens : (rows + slot + 1) * tokens, :]
    inverse = jnp.broadcast_to(1.0 / jnp.sum(mass, axis=1, keepdims=True), (tokens, BLK))

    def leaving(q):
        return pltpu.make_async_copy(o_buf.at[q], o_ref.at[q], out_sem.at[q])

    def owner(q, carry):
        member = lax.rem(q + owners // 2, owners)
        for b in range(mine):
            first = pl.multiple_of((member * mine + b) * tokens, tokens)
            tile = m_ref[pl.ds(first, tokens), :] * inverse
            o_buf[q, :, b * BLK : (b + 1) * BLK] = tile.astype(jnp.bfloat16)
        o_buf[q, :, mine * BLK :] = extra
        leaving(q).start()
        return carry

    def left(q, carry):
        leaving(q).wait()
        return carry

    lax.fori_loop(0, owners, owner, 0)
    lax.fori_loop(0, owners, left, 0)


def grad_kernel(scale, target_ref, logits_ref, grad_ref, terms_ref, norm_ref, t_buf, sem):
    owners, tokens, _ = target_ref.shape
    group_tokens, width = logits_ref.shape
    stats = [target_ref[q, :, width:].astype(jnp.float32) for q in range(owners)]
    top = stats[0][0:1]
    for one in stats[1:]:
        top = jnp.maximum(top, one[0:1])
    total = jnp.zeros_like(top)
    for one in stats:
        total = total + (one[1:2] + one[2:3] + one[3:4]) * jnp.exp(one[0:1] - top)
    log_norm = top + jnp.log(total)

    def block(i, b):
        lanes = slice(b * BLK, (b + 1) * BLK)
        first, count = i * BLK // tokens, BLK // tokens
        at = (first - owners // 2) % owners
        cut = min(count, owners - at)
        target = target_ref[at : at + cut, :, lanes].reshape(cut * tokens, BLK)
        if cut < count:
            rest = target_ref[: count - cut, :, lanes].reshape((count - cut) * tokens, BLK)
            target = jnp.concatenate([target, rest], axis=0)
        target = target.astype(jnp.float32)
        return target, logits_ref[i * BLK : (i + 1) * BLK, lanes].astype(jnp.float32)

    sums = []
    for i in range(group_tokens // BLK):
        rows = slice(i * BLK, (i + 1) * BLK)
        norm = jnp.broadcast_to(log_norm[:, rows], (BLK, BLK)).T
        norm_ref[rows, :] = norm
        terms = jnp.zeros((BLK, BLK), jnp.float32)
        for b in range(width // BLK):
            target, logits = block(i, b)
            positive = target > 0
            one = target * (jnp.log(jnp.where(positive, target, 1.0)) - (logits - norm))
            terms = terms + jnp.where(positive, one, 0.0)
        sums.append(jnp.sum(terms.T, axis=0, keepdims=True))
    row = jnp.concatenate(sums, axis=1)
    half_tokens = group_tokens // 2
    for half in range(2):
        mine = row[:, half * half_tokens : (half + 1) * half_tokens]
        tile = jnp.concatenate([mine] * (t_buf.shape[2] // half_tokens), axis=1)
        for q in range(owners):
            t_buf[2 * q + half] = jnp.broadcast_to(tile, t_buf.shape[1:])
    leaving = pltpu.make_async_copy(t_buf, terms_ref, sem)
    leaving.start()
    for i in range(group_tokens // BLK):
        rows = slice(i * BLK, (i + 1) * BLK)
        for b in range(width // BLK):
            target, logits = block(i, b)
            grad = (jnp.exp(logits - norm_ref[rows, :]) - target) * scale
            grad_ref[rows, b * BLK : (b + 1) * BLK] = grad.astype(jnp.bfloat16)
    leaving.wait()


def arrival_order(owners):
    return [a for b in range(owners // 2) for a in (b, b + owners // 2)]


def row_blocks(features):
    tiles = features // BLK
    sizes = [2] + [3] * ((tiles - 3) // 3)
    sizes.append(tiles - sum(sizes))
    return [size * BLK for size in sizes]


def weight_kernel(
    place_ref, own_ref, got_ref, grad_ref, o_ref, joined_ref, s_ref, h_ref, block_ref, sems, join_sems
):
    half_tokens, width = got_ref.shape[0], grad_ref.shape[1]
    half = place_ref[1]
    kept_at = pl.ds(pl.multiple_of(half * width, width), width)
    got_at = pl.ds(pl.multiple_of((1 - half) * width, width), width)
    kept = pl.ds(pl.multiple_of(half * half_tokens, half_tokens), half_tokens)
    copies = [
        pltpu.make_async_copy(grad_ref.at[kept, :], joined_ref.at[:, kept_at], join_sems.at[0]),
        pltpu.make_async_copy(got_ref.at[:, pl.ds(0, width)], joined_ref.at[:, got_at], join_sems.at[1]),
    ]
    for copy in copies:
        copy.start()
    owners, held, features = own_ref.shape
    for i, offset in enumerate(arrival_order(owners)):
        first = (place_ref[0] ^ offset) * 2
        own = pl.ds(pl.multiple_of((first + half) * held, held), held)
        other = pl.ds(pl.multiple_of((first + 1 - half) * held, held), held)
        s_ref[own, :] = own_ref[i].astype(jnp.float32)
        pair = got_ref[i // 2 * 2 * held : (i // 2 + 1) * 2 * held, width:].astype(jnp.float32)
        s_ref[other, :] = pair[i % 2 * held : (i % 2 + 1) * held]
    first = 0
    for i, size in enumerate(row_blocks(features)):
        for j in range(first, first + size, BLK):
            rows = slice(j, j + BLK)
            for t in range(0, s_ref.shape[0], BLK):
                h_ref[rows, t : t + BLK] = s_ref[t : t + BLK, rows].T.astype(jnp.bfloat16)
            for n in range(0, width, 2 * BLK):
                tile = jnp.dot(
                    h_ref[rows, :], grad_ref[:, n : n + 2 * BLK], preferred_element_type=jnp.float32
                )
                block_ref[rows, n : n + 2 * BLK] = tile.astype(jnp.bfloat16)
        at = pl.ds(first, size)
        copies.append(pltpu.make_async_copy(block_ref.at[at, :], o_ref.at[at, :], sems.at[i]))
        copies[-1].start()
        first += size
    for copy in copies:
        copy.wait()


def in_vmem():
    return pl.BlockSpec(memory_space=pltpu.VMEM)


def scalars():
    return pl.BlockSpec(memory_space=pltpu.SMEM)


def anywhere():
    return pl.BlockSpec(memory_space=pl.ANY)


def params(mib=48):
    return pltpu.CompilerParams(vmem_limit_bytes=mib << 20)


def cost(flops=0, bytes_accessed=0, transcendentals=0):
    return pl.CostEstimate(flops=flops, bytes_accessed=bytes_accessed, transcendentals=transcendentals)


def swap_halves(x):
    return lax.ppermute(x, "tv", [(0, 1), (1, 0)])


def to_partner(x, offset):
    return lax.ppermute(x, "sv", [(s, s ^ offset) for s in range(lax.axis_size("sv"))])


def body(teacher_probs, align_owner, align_local, align_weight, student_logits, hidden):
    owners = lax.axis_size("sv")
    halves = lax.axis_size("tv")
    half_index = lax.axis_index("tv")
    place = jnp.stack([lax.axis_index("sv"), half_index]).astype(jnp.int32)
    tokens = teacher_probs.shape[0]
    columns = student_logits.shape[1]
    blocks = columns // BLK
    mine = blocks // halves
    width = mine * BLK
    rows = owners * mine
    per_half = TB // halves
    group_tokens = owners * tokens
    half_tokens = student_logits.shape[0]
    features = hidden.shape[1]
    first = half_index == 0
    bf16, f32 = jnp.bfloat16, jnp.float32
    shape = jax.ShapeDtypeStruct
    dma = lambda count: pltpu.SemaphoreType.DMA((count,))

    def in_order(own, other, axis):
        return jnp.concatenate([jnp.where(first, own, other), jnp.where(first, other, own)], axis=axis)

    hidden = hidden[None]
    offset = owners // 2
    first_piece = to_partner(hidden, offset)

    def merge(one, two):
        top = jnp.maximum(one[0], two[0])
        return top, one[1] * jnp.exp(one[0] - top) + two[1] * jnp.exp(two[0] - top)

    wide = student_logits.astype(f32)
    low = jnp.float32(-1e38)
    stats = jnp.stack(lax.reduce((wide, jnp.ones_like(wide)), (low, jnp.float32(0)), merge, (1,)))
    teacher_given, stats = lax.optimization_barrier((teacher_probs, stats))
    teacher_other = swap_halves(teacher_given)
    stats = in_order(stats, swap_halves(stats), 1)

    local = align_local.T - half_index * mine
    row_of = jnp.where((local >= 0) & (local < mine), align_owner.T * mine + local, -1)
    code = row_of.astype(f32) + 0.5 * align_weight.T.astype(f32)
    cut = lambda which: lax.dynamic_slice_in_dim(code, which * per_half, per_half, 1)
    w_own = block_weights(cut(half_index), rows)
    w_rest = block_weights(cut(1 - half_index), rows)
    spread = pltpu.VMEM((per_half * tokens, BLK), f32)
    flops = 2 * (rows + MASS_ROWS) * per_half * tokens * BLK
    part = pl.pallas_call(
        map_own_kernel,
        out_shape=shape((rows + MASS_ROWS, tokens * BLK), f32),
        in_specs=[in_vmem()] * 2 + [anywhere()],
        out_specs=in_vmem(),
        scratch_shapes=[spread],
        compiler_params=params(),
        cost_estimate=cost(flops, 3 << 20),
        name="map_own",
    )(w_own, teacher_probs, stats)
    chunk = (owners, tokens, width + group_tokens)
    outgoing = pl.pallas_call(
        map_rest_kernel,
        out_shape=shape(chunk, bf16),
        in_specs=[in_vmem()] * 4,
        out_specs=anywhere(),
        scratch_shapes=[
            spread,
            pltpu.VMEM(((rows + 8) * tokens, BLK), f32),
            pltpu.VMEM(chunk, bf16),
            dma(owners),
        ],
        compiler_params=params(),
        cost_estimate=cost(flops, 4 << 20),
        name="map_rest",
    )(w_rest, teacher_other, part, stats)
    outgoing, first_piece = lax.optimization_barrier((outgoing, first_piece))
    target = lax.all_to_all(outgoing, "sv", 0, 0, axis_index_groups=[turned_group(owners, owners // 2)], tiled=True)

    hidden, late_logits, outgoing = lax.optimization_barrier((hidden, student_logits, outgoing))

    keep = lax.dynamic_slice_in_dim(late_logits, half_index * width, width, 1)
    give = lax.dynamic_slice_in_dim(late_logits, (1 - half_index) * width, width, 1)
    logits = in_order(keep, swap_halves(give), 0)

    pieces = [jnp.concatenate([hidden, first_piece])]
    pieces += [to_partner(pieces[0], a) for a in range(1, offset)]

    scale = float(columns * owners)
    lanes = -(-half_tokens // BLK) * BLK
    grad, terms = pl.pallas_call(
        lambda *refs: grad_kernel(scale, *refs),
        out_shape=(shape((group_tokens, width), bf16), shape((owners * halves, 8, lanes), f32)),
        in_specs=[in_vmem()] * 2,
        out_specs=(in_vmem(), anywhere()),
        scratch_shapes=[
            pltpu.VMEM((group_tokens, BLK), f32),
            pltpu.VMEM((owners * halves, 8, lanes), f32),
            pltpu.SemaphoreType.DMA,
        ],
        compiler_params=params(),
        cost_estimate=cost(
            10 * group_tokens * width, 6 * group_tokens * width, 2 * group_tokens * width
        ),
        name="logit_grad",
    )(target, logits)

    everyone = [turned_group(owners * halves, owners // 2 * halves)]
    terms = lax.all_to_all(terms, ("sv", "tv"), 0, 0, axis_index_groups=everyone, tiled=True)
    *pieces, grad = lax.optimization_barrier((*pieces, grad))
    give = lax.dynamic_slice_in_dim(grad, (1 - half_index) * half_tokens, half_tokens, 0)
    hidden_own = jnp.concatenate(pieces)
    got = swap_halves(jnp.concatenate([give, hidden_own.reshape(half_tokens, features)], axis=1))
    weight_grad, logit_grad = pl.pallas_call(
        weight_kernel,
        out_shape=(shape((features, width), bf16), shape((half_tokens, columns), bf16)),
        in_specs=[scalars()] + [in_vmem()] * 3,
        out_specs=(anywhere(), anywhere()),
        scratch_shapes=[
            pltpu.VMEM((group_tokens, features), f32),
            pltpu.VMEM((features, group_tokens), bf16),
            pltpu.VMEM((features, width), bf16),
            dma(len(row_blocks(features))),
            dma(2),
        ],
        compiler_params=params(),
        cost_estimate=cost(
            2 * features * group_tokens * width,
            2 * (features * width + group_tokens * (features + width)),
        ),
        name="weight_grad",
    )(place, hidden_own, got, grad)
    terms, logit_grad, weight_grad = lax.optimization_barrier((terms, logit_grad, weight_grad))
    divergence = jnp.sum(terms[:, 0, :half_tokens], axis=0)
    return (divergence, logit_grad, weight_grad)


def solution(mesh):
    return jax.shard_map(
        body,
        mesh=mesh,
        in_specs=(
            P(("grp", "sv"), "tv"),
            P(),
            P(),
            P(),
            P(("grp", "tv"), "sv"),
            P(("grp", "sv", "tv"), None),
        ),
        out_specs=(P(("grp", "tv")), P(("grp", "tv"), "sv"), P(None, ("grp", "sv", "tv"))),
        check_vma=False,
    )
```

```python
import jax
import jax.numpy as jnp
from jax import lax
from jax.experimental import pallas as pl
from jax.experimental.pallas import tpu as pltpu
from jax.sharding import PartitionSpec as P

BLK = 128
TB = 640
TOPA = 2
MASS_ROWS = 16
STEP = 160


def block_weights(code, rows):
    row_ids = lax.broadcasted_iota(jnp.int32, (rows + MASS_ROWS, code.shape[1]), 0)
    total = jnp.zeros(row_ids.shape, jnp.float32)
    for slot in range(TOPA):
        row = jnp.floor(code[slot])
        weight = (code[slot] - row) * 2.0
        hit = (row_ids == row.astype(jnp.int32)[None, :]) | (row_ids == rows + slot)
        total = total + jnp.where(hit, weight[None, :], 0.0)
    return total.astype(jnp.bfloat16)


def turned_group(members, first):
    return [(i + first) % members for i in range(members)]


def spread_tokens(t_ref, s_ref, start, count):
    tokens = t_ref.shape[0]

    def some(i, carry):
        for j in range(STEP):
            k = start + i * STEP + j
            tile = t_ref[:, pl.ds(pl.multiple_of(k * BLK, BLK), BLK)]
            s_ref[pl.ds(pl.multiple_of(k * tokens, tokens), tokens), :] = tile.astype(jnp.float32)
        return carry

    lax.fori_loop(0, count // STEP, some, 0)


def token_pair(s_ref, t, tokens):
    count = s_ref.shape[0] // tokens
    both = [s_ref[pl.ds(t + i, count, stride=tokens), :].astype(jnp.bfloat16) for i in range(2)]
    return jnp.concatenate(both, axis=1)


def map_own_kernel(w_ref, t_ref, stats_ref, o_ref, s_ref):
    tokens = t_ref.shape[0]
    spread_tokens(t_ref, s_ref, 0, t_ref.shape[1] // BLK)
    for t in range(0, tokens, 2):
        o_ref[:, t * BLK : (t + 2) * BLK] = jnp.dot(
            w_ref[...], token_pair(s_ref, t, tokens), preferred_element_type=jnp.float32
        )


def three_parts(x):
    parts = []
    for _ in range(3):
        parts.append(x.astype(jnp.bfloat16).astype(jnp.float32))
        x = x - parts[-1]
    return parts


def map_rest_kernel(w_ref, t_ref, p_ref, stats_ref, o_ref, s_ref, m_ref, o_buf, out_sem):
    tokens = t_ref.shape[0]
    owners = o_ref.shape[0]
    rows = w_ref.shape[0] - MASS_ROWS
    mine = rows // owners
    stats = [stats_ref[0:1, :]] + three_parts(stats_ref[1:2, :])
    extra = jnp.zeros((tokens, stats_ref.shape[1]), jnp.float32)
    row_ids = lax.broadcasted_iota(jnp.int32, extra.shape, 0)
    for i, row in enumerate(stats):
        extra = jnp.where(row_ids == i, row, extra)
    extra = extra.astype(jnp.bfloat16)
    spread_tokens(t_ref, s_ref, 0, t_ref.shape[1] // BLK)
    for t in range(0, tokens, 2):
        both = p_ref[:, t * BLK : (t + 2) * BLK] + jnp.dot(
            w_ref[...], token_pair(s_ref, t, tokens), preferred_element_type=jnp.float32
        )
        for i in range(2):
            m_ref[pl.ds(t + i, rows + 8, stride=tokens), :] = both[: rows + 8, i * BLK : (i + 1) * BLK]
    mass = m_ref[rows * tokens : (rows + 1) * tokens, :]
    for slot in range(1, TOPA):
        mass = mass + m_ref[(rows + slot) * tokens : (rows + slot + 1) * tokens, :]
    inverse = jnp.broadcast_to(1.0 / jnp.sum(mass, axis=1, keepdims=True), (tokens, BLK))

    def leaving(q):
        return pltpu.make_async_copy(o_buf.at[q], o_ref.at[q], out_sem.at[q])

    def owner(q, carry):
        member = (q + owners // 2) % owners
        for b in range(mine):
            first = (member * mine + b) * tokens
            tile = m_ref[first : first + tokens, :] * inverse
            o_buf[q, :, b * BLK : (b + 1) * BLK] = tile.astype(jnp.bfloat16)
        o_buf[q, :, mine * BLK :] = extra
        leaving(q).start()
        return carry

    def left(q, carry):
        leaving(q).wait()
        return carry

    for q in range(owners):
        owner(q, 0)
    for q in range(owners):
        left(q, 0)


def grad_kernel(scale, target_ref, logits_ref, grad_ref, terms_ref, norm_ref, t_buf, sem):
    owners, tokens, _ = target_ref.shape
    group_tokens, width = logits_ref.shape
    stats = [target_ref[q, :, width:].astype(jnp.float32) for q in range(owners)]
    top = stats[0][0:1]
    for one in stats[1:]:
        top = jnp.maximum(top, one[0:1])
    total = jnp.zeros_like(top)
    for one in stats:
        total = total + (one[1:2] + one[2:3] + one[3:4]) * jnp.exp(one[0:1] - top)
    log_norm = top + jnp.log(total)

    def block(i, b):
        lanes = slice(b * BLK, (b + 1) * BLK)
        first, count = i * BLK // tokens, BLK // tokens
        at = (first - owners // 2) % owners
        cut = min(count, owners - at)
        target = target_ref[at : at + cut, :, lanes].reshape(cut * tokens, BLK)
        if cut < count:
            rest = target_ref[: count - cut, :, lanes].reshape((count - cut) * tokens, BLK)
            target = jnp.concatenate([target, rest], axis=0)
        target = target.astype(jnp.float32)
        return target, logits_ref[i * BLK : (i + 1) * BLK, lanes].astype(jnp.float32)

    sums = []
    for i in range(group_tokens // BLK):
        rows = slice(i * BLK, (i + 1) * BLK)
        norm = jnp.broadcast_to(log_norm[:, rows], (BLK, BLK)).T
        norm_ref[rows, :] = norm
        terms = jnp.zeros((BLK, BLK), jnp.float32)
        for b in range(width // BLK):
            target, logits = block(i, b)
            positive = target > 0
            one = target * (jnp.log(jnp.where(positive, target, 1.0)) - (logits - norm))
            terms = terms + jnp.where(positive, one, 0.0)
        sums.append(jnp.sum(terms.T, axis=0, keepdims=True))
    row = jnp.concatenate(sums, axis=1)
    half_tokens = group_tokens // 2
    for half in range(2):
        mine = row[:, half * half_tokens : (half + 1) * half_tokens]
        tile = jnp.concatenate([mine] * (t_buf.shape[2] // half_tokens), axis=1)
        for q in range(owners):
            t_buf[2 * q + half] = jnp.broadcast_to(tile, t_buf.shape[1:])
    leaving = pltpu.make_async_copy(t_buf, terms_ref, sem)
    leaving.start()
    for i in range(group_tokens // BLK):
        rows = slice(i * BLK, (i + 1) * BLK)
        for b in range(width // BLK):
            target, logits = block(i, b)
            grad = (jnp.exp(logits - norm_ref[rows, :]) - target) * scale
            grad_ref[rows, b * BLK : (b + 1) * BLK] = grad.astype(jnp.bfloat16)
    leaving.wait()


def arrival_order(owners):
    return [a for b in range(owners // 2) for a in (b, b + owners // 2)]


def row_blocks(features):
    tiles = features // BLK
    sizes = [2] + [3] * ((tiles - 3) // 3)
    sizes.append(tiles - sum(sizes))
    return [size * BLK for size in sizes]


def weight_kernel(
    place_ref, own_ref, got_ref, grad_ref, o_ref, joined_ref, s_ref, h_ref, block_ref, sems, join_sems
):
    half_tokens, width = got_ref.shape[0], grad_ref.shape[1]
    half = place_ref[1]
    kept_at = pl.ds(pl.multiple_of(half * width, width), width)
    got_at = pl.ds(pl.multiple_of((1 - half) * width, width), width)
    kept = pl.ds(pl.multiple_of(half * half_tokens, half_tokens), half_tokens)
    copies = [
        pltpu.make_async_copy(grad_ref.at[kept, :], joined_ref.at[:, kept_at], join_sems.at[0]),
        pltpu.make_async_copy(got_ref.at[:, pl.ds(0, width)], joined_ref.at[:, got_at], join_sems.at[1]),
    ]
    for copy in copies:
        copy.start()
    owners, held, features = own_ref.shape
    for i, offset in enumerate(arrival_order(owners)):
        first = (place_ref[0] ^ offset) * 2
        own = pl.ds(pl.multiple_of((first + half) * held, held), held)
        other = pl.ds(pl.multiple_of((first + 1 - half) * held, held), held)
        s_ref[own, :] = own_ref[i].astype(jnp.float32)
        pair = got_ref[i // 2 * 2 * held : (i // 2 + 1) * 2 * held, width:].astype(jnp.float32)
        s_ref[other, :] = pair[i % 2 * held : (i % 2 + 1) * held]
    first = 0
    for i, size in enumerate(row_blocks(features)):
        for j in range(first, first + size, BLK):
            rows = slice(j, j + BLK)
            for t in range(0, s_ref.shape[0], BLK):
                h_ref[rows, t : t + BLK] = s_ref[t : t + BLK, rows].T.astype(jnp.bfloat16)
            for n in range(0, width, 2 * BLK):
                tile = jnp.dot(
                    h_ref[rows, :], grad_ref[:, n : n + 2 * BLK], preferred_element_type=jnp.float32
                )
                block_ref[rows, n : n + 2 * BLK] = tile.astype(jnp.bfloat16)
        at = pl.ds(first, size)
        copies.append(pltpu.make_async_copy(block_ref.at[at, :], o_ref.at[at, :], sems.at[i]))
        copies[-1].start()
        first += size
    for copy in copies:
        copy.wait()


def in_vmem():
    return pl.BlockSpec(memory_space=pltpu.VMEM)


def scalars():
    return pl.BlockSpec(memory_space=pltpu.SMEM)


def anywhere():
    return pl.BlockSpec(memory_space=pl.ANY)


def params(mib=48):
    return pltpu.CompilerParams(vmem_limit_bytes=mib << 20)


def cost(flops=0, bytes_accessed=0, transcendentals=0):
    return pl.CostEstimate(flops=flops, bytes_accessed=bytes_accessed, transcendentals=transcendentals)


def swap_halves(x):
    return lax.ppermute(x, "tv", [(0, 1), (1, 0)])


def to_partner(x, offset):
    return lax.ppermute(x, "sv", [(s, s ^ offset) for s in range(lax.axis_size("sv"))])


def body(teacher_probs, align_owner, align_local, align_weight, student_logits, hidden):
    owners = lax.axis_size("sv")
    halves = lax.axis_size("tv")
    half_index = lax.axis_index("tv")
    place = jnp.stack([lax.axis_index("sv"), half_index]).astype(jnp.int32)
    tokens = teacher_probs.shape[0]
    columns = student_logits.shape[1]
    blocks = columns // BLK
    mine = blocks // halves
    width = mine * BLK
    rows = owners * mine
    per_half = TB // halves
    group_tokens = owners * tokens
    half_tokens = student_logits.shape[0]
    features = hidden.shape[1]
    first = half_index == 0
    bf16, f32 = jnp.bfloat16, jnp.float32
    shape = jax.ShapeDtypeStruct
    dma = lambda count: pltpu.SemaphoreType.DMA((count,))

    def in_order(own, other, axis):
        return jnp.concatenate([jnp.where(first, own, other), jnp.where(first, other, own)], axis=axis)

    hidden = hidden[None]
    offset = owners // 2
    first_piece = to_partner(hidden, offset)

    def merge(one, two):
        top = jnp.maximum(one[0], two[0])
        return top, one[1] * jnp.exp(one[0] - top) + two[1] * jnp.exp(two[0] - top)

    wide = student_logits.astype(f32)
    low = jnp.float32(-1e38)
    stats = jnp.stack(lax.reduce((wide, jnp.ones_like(wide)), (low, jnp.float32(0)), merge, (1,)))
    teacher_given, stats = lax.optimization_barrier((teacher_probs, stats))
    teacher_other = swap_halves(teacher_given)
    stats = in_order(stats, swap_halves(stats), 1)

    local = align_local.T - half_index * mine
    row_of = jnp.where((local >= 0) & (local < mine), align_owner.T * mine + local, -1)
    code = row_of.astype(f32) + 0.5 * align_weight.T.astype(f32)
    cut = lambda which: lax.dynamic_slice_in_dim(code, which * per_half, per_half, 1)
    w_own = block_weights(cut(half_index), rows)
    w_rest = block_weights(cut(1 - half_index), rows)
    spread = pltpu.VMEM((per_half * tokens, BLK), f32)
    flops = 2 * (rows + MASS_ROWS) * per_half * tokens * BLK
    part = pl.pallas_call(
        map_own_kernel,
        out_shape=shape((rows + MASS_ROWS, tokens * BLK), f32),
        in_specs=[in_vmem()] * 2 + [anywhere()],
        out_specs=in_vmem(),
        scratch_shapes=[spread],
        compiler_params=params(),
        cost_estimate=cost(flops, 3 << 20),
        name="map_own",
    )(w_own, teacher_probs, stats)
    chunk = (owners, tokens, width + group_tokens)
    outgoing = pl.pallas_call(
        map_rest_kernel,
        out_shape=shape(chunk, bf16),
        in_specs=[in_vmem()] * 4,
        out_specs=anywhere(),
        scratch_shapes=[
            spread,
            pltpu.VMEM(((rows + 8) * tokens, BLK), f32),
            pltpu.VMEM(chunk, bf16),
            dma(owners),
        ],
        compiler_params=params(),
        cost_estimate=cost(flops, 4 << 20),
        name="map_rest",
    )(w_rest, teacher_other, part, stats)
    outgoing, first_piece = lax.optimization_barrier((outgoing, first_piece))
    target = lax.all_to_all(outgoing, "sv", 0, 0, axis_index_groups=[turned_group(owners, owners // 2)], tiled=True)

    hidden, late_logits, outgoing = lax.optimization_barrier((hidden, student_logits, outgoing))

    keep = lax.dynamic_slice_in_dim(late_logits, half_index * width, width, 1)
    give = lax.dynamic_slice_in_dim(late_logits, (1 - half_index) * width, width, 1)
    logits = in_order(keep, swap_halves(give), 0)

    pieces = [jnp.concatenate([hidden, first_piece])]
    pieces += [to_partner(pieces[0], a) for a in range(1, offset)]

    scale = float(columns * owners)
    lanes = -(-half_tokens // BLK) * BLK
    grad, terms = pl.pallas_call(
        lambda *refs: grad_kernel(scale, *refs),
        out_shape=(shape((group_tokens, width), bf16), shape((owners * halves, 8, lanes), f32)),
        in_specs=[in_vmem()] * 2,
        out_specs=(in_vmem(), anywhere()),
        scratch_shapes=[
            pltpu.VMEM((group_tokens, BLK), f32),
            pltpu.VMEM((owners * halves, 8, lanes), f32),
            pltpu.SemaphoreType.DMA,
        ],
        compiler_params=params(),
        cost_estimate=cost(
            10 * group_tokens * width, 6 * group_tokens * width, 2 * group_tokens * width
        ),
        name="logit_grad",
    )(target, logits)

    everyone = [turned_group(owners * halves, owners // 2 * halves)]
    terms = lax.all_to_all(terms, ("sv", "tv"), 0, 0, axis_index_groups=everyone, tiled=True)
    *pieces, grad = lax.optimization_barrier((*pieces, grad))
    give = lax.dynamic_slice_in_dim(grad, (1 - half_index) * half_tokens, half_tokens, 0)
    hidden_own = jnp.concatenate(pieces)
    got = swap_halves(jnp.concatenate([give, hidden_own.reshape(half_tokens, features)], axis=1))
    weight_grad, logit_grad = pl.pallas_call(
        weight_kernel,
        out_shape=(shape((features, width), bf16), shape((half_tokens, columns), bf16)),
        in_specs=[scalars()] + [in_vmem()] * 3,
        out_specs=(anywhere(), anywhere()),
        scratch_shapes=[
            pltpu.VMEM((group_tokens, features), f32),
            pltpu.VMEM((features, group_tokens), bf16),
            pltpu.VMEM((features, width), bf16),
            dma(len(row_blocks(features))),
            dma(2),
        ],
        compiler_params=params(),
        cost_estimate=cost(
            2 * features * group_tokens * width,
            2 * (features * width + group_tokens * (features + width)),
        ),
        name="weight_grad",
    )(place, hidden_own, got, grad)
    terms, logit_grad, weight_grad = lax.optimization_barrier((terms, logit_grad, weight_grad))
    divergence = jnp.sum(terms[:, 0, :half_tokens], axis=0)
    return (divergence, logit_grad, weight_grad)


def solution(mesh):
    return jax.shard_map(
        body,
        mesh=mesh,
        in_specs=(
            P(("grp", "sv"), "tv"),
            P(),
            P(),
            P(),
            P(("grp", "tv"), "sv"),
            P(("grp", "sv", "tv"), None),
        ),
        out_specs=(P(("grp", "tv")), P(("grp", "tv"), "sv"), P(None, ("grp", "sv", "tv"))),
        check_vma=False,
    )
```
